32 devices in a mesh: rep: 2 (over y), ep: 16 (over z, x, core).
Axes of the slice: x: 2, y: 2, z: 4, core: 2. Of those that a mesh axis runs over, the one named last changes fastest.
Arguments:
- tokens: bfloat16 [32768, 1536], P(('rep', 'ep')), may hold values from -6 to 6
- routes: int32 [32768, 8], P(('rep', 'ep')), may hold values from 0 to 15, all different within a row; in each aligned block of 512 rows (0 to 511, 512 to 1023, ...) at most 320 rows name the same one
- pieces: int32 [32, 2], P(('rep', 'ep')), may hold values from 0 to 768, as said below
- attn_gain: float32 [1536], replicated, may hold values from 0.1 to 1.9
- w_query: bfloat16 [1536, 1536], replicated, may hold values from -0.15625 to 0.15625
- w_key: bfloat16 [1536, 512], replicated, may hold values from -0.15625 to 0.15625
- w_value: bfloat16 [1536, 512], replicated, may hold values from -0.15625 to 0.15625
- w_out: bfloat16 [1536, 1536], replicated, may hold values from -1.75 to 1.75
- ffn_gain: float32 [1536], replicated, may hold values from 0.1 to 1.9
- w_router: bfloat16 [1536, 16], replicated, may hold values from -0.078125 to 0.078125
- expert_gate: bfloat16 [16, 1536, 512], P('ep'), may hold values from -0.15625 to 0.15625
- expert_up: bfloat16 [16, 1536, 512], P('ep'), may hold values from -0.15625 to 0.15625
- expert_down: bfloat16 [16, 512, 1536], P('ep'), may hold values from -1 to 1
- cotangent: bfloat16 [32768, 1536], P(('rep', 'ep')), may hold values from -6 to 6
Outputs:
- output: bfloat16 [32768, 1536], P(('rep', 'ep'))
- d_tokens: float32 [32768, 1536], P(('rep', 'ep'))
- d_attn_gain: float32 [1536], P('ep')
- d_query: float32 [1536, 1536], P('ep')
- d_key: float32 [1536, 512], P('ep')
- d_value: float32 [1536, 512], P('ep')
- d_out: float32 [1536, 1536], P('ep')
- d_ffn_gain: float32 [1536], P('ep')
- d_router: float32 [1536, 16], P('ep')
- d_expert_gate: float32 [16, 1536, 512], P('ep')
- d_expert_up: float32 [16, 1536, 512], P('ep')
- d_expert_down: float32 [16, 512, 1536], P('ep')
The draws below stay inside these ranges and needn't reach their ends.
Inputs may be any that keep to these rules, and one draw needn't show every extreme that they name: `routes`: each row names 8 different experts; in each aligned block of 512 rows no expert is named by more than 320 rows, a bound that some block reaches. A sequence's 2 pieces of 256 positions start in increasing order and do not intersect.
All inputs are finite; a program needn't handle non-finite values.
Results may differ from the reference program's by a relative error of at most 0.025.
Values may be sent and summed in bfloat16 or wider, within the bound.
No kernel may reach another device: no remote copies, remote signals or barrier semaphores. Data moves between devices by JAX's collectives and lax.ppermute only.
A program may use at most 640 MiB of HBM per device.

```python
import math
import jax
import jax.numpy as jnp
import numpy as np
from jax import lax

D = 1536
HEADS = 24
KV = 8
HEAD = 64
FF = 512
TOP = 8
LEN = 1024
PIECE = 256
PIECES = 2
BLOCK = 512
EXPERTS = 16
CAP = 320
SEQS = 32
TOKENS = 32768


def draw_pieces(key, part):
    key = jax.random.fold_in(key, 11)
    slack = LEN - PIECES * PIECE
    cuts = jax.random.randint(key, (SEQS, PIECES), 0, slack + 1, dtype=jnp.int32)
    cuts = jnp.sort(cuts, axis=1)
    return (cuts + jnp.arange(PIECES, dtype=jnp.int32)[None, :] * PIECE).astype(jnp.int32)


def levels(rng, dims, shards, smallest, top_value):
    def one(dim, shards_of):
        draws = jax.random.uniform(jax.random.fold_in(jax.random.fold_in(rng, 6), dim), (shards_of,), jnp.float32, smallest / len(shards), top_value / len(shards))
        return jnp.repeat(jnp.exp(draws), dims[dim] // shards_of).reshape((-1,) + (1,) * (len(dims) - dim - 1))

    level = one(*shards[0])
    for cut in shards[1:]:
        level = level * one(*cut)
    return level


def routed_block(rng, own, number, rows, number_of, top, limit, skew):
    sequence = jax.random.permutation(rng, number_of)
    crowded, common = shares(number_of, rows * top, limit, skew, True), shares(number_of, rows * top, limit, skew, False)
    places = jnp.arange(number_of)

    def named(lengths, turn):
        used = int((lengths > 0).sum())
        fixed = max(1, used // 4)
        passed = fixed + (places - fixed + turn * (used - fixed)) % max(1, number_of - fixed)
        return jnp.zeros((number_of,), jnp.int32).at[sequence[jnp.where(places < fixed, places, passed)]].set(jnp.asarray(lengths, jnp.int32))

    lengths = jnp.where(number % 4 == 0, named(crowded, number // 4), named(common, number - number // 4 - 1))
    mixed = jax.random.permutation(jax.random.fold_in(own, 3), number_of)
    donor, receiver = mixed[0:number_of // 2 * 2:2], mixed[1:number_of // 2 * 2:2]
    room = jnp.minimum(lengths[donor] - 1, limit - lengths[receiver]) // 2
    room = jnp.where((donor == sequence[0]) | (receiver == sequence[0]) | (lengths[receiver] == 0), 0, jnp.maximum(room, 0))
    passed = jax.random.randint(jax.random.fold_in(own, 4), (number_of // 2,), 0, 1 << 20) % (room + 1)
    lengths = lengths.at[donor].add(-passed).at[receiver].add(passed)
    items = jnp.searchsorted(jnp.cumsum(lengths), jnp.arange(rows * top), side="right").astype(jnp.int32)
    table = items.reshape(top, rows).T
    table = table[jax.random.permutation(jax.random.fold_in(own, 1), rows)]
    turn = jax.random.randint(jax.random.fold_in(own, 2), (rows, 1), 0, top)
    return jnp.take_along_axis(table, (jnp.arange(top)[None, :] + turn) % top, axis=1)


def shares(amount, total, limit, skew, full):
    loads = [(1 << 20) // math.isqrt(standing ** skew) + 1 for standing in range(1, amount + 1)]
    largest = limit if full else min(limit, max(-(-total // amount), total * loads[0] // sum(loads)))
    least = 1 if total - largest >= amount - 1 else 0
    counts, surplus = [largest] + [least] * (amount - 1), total - largest - least * (amount - 1)
    while surplus > 0:
        free = [i for i in range(1, amount) if counts[i] < largest] or [i for i in range(1, amount) if counts[i] < limit]
        whole, left = sum([loads[i] for i in free]), surplus
        for i in free:
            more = min(limit - counts[i], max(1, left * loads[i] // whole), surplus)
            counts[i] = counts[i] + more
            surplus = surplus - more
    return np.array(counts)


def scatter_about(key, extent, deviation, limit, shards=(), held_as=jnp.bfloat16):
    values = jax.random.normal(key, extent, jnp.float32) * deviation
    if len(shards) > 0:
        values = levels(key, extent, shards, -0.22, 0.18) * values
    return jnp.clip(values, min=-limit, max=limit).astype(held_as)


def setup_inputs(seed: int = 0) -> dict:
    keys = jax.random.split(jax.random.key(seed), 15)
    tokens = scatter_about(keys[0], (TOKENS, D), 1.0, 6.0, ((0, 32),))
    routes_keys = jax.random.split(jax.random.fold_in(keys[1], 1), TOKENS // BLOCK)
    routes_turns = jax.random.permutation(jax.random.fold_in(keys[1], 3), TOKENS // BLOCK)
    routes = jax.vmap(lambda own, number: routed_block(jax.random.fold_in(keys[1], 2), own, number, BLOCK, EXPERTS, TOP, CAP, 1))(routes_keys, routes_turns).reshape((TOKENS, TOP))
    pieces = draw_pieces(jax.random.fold_in(keys[14], 71), 0)
    attn_gain = jnp.clip(1.0 + 0.18 * jax.random.normal(keys[3], (D,), jnp.float32), 0.1, 1.9)
    w_query = scatter_about(keys[4], (D, D), D ** -0.5, 0.15625)
    w_key = scatter_about(keys[5], (D, KV * HEAD), D ** -0.5, 0.15625)
    w_value = scatter_about(keys[6], (D, KV * HEAD), D ** -0.5, 0.15625)
    w_out = scatter_about(keys[7], (D, D), (max(D // 128, 4)) ** -0.5, 1.75)
    ffn_gain = jnp.clip(1.0 + 0.18 * jax.random.normal(keys[8], (D,), jnp.float32), 0.1, 1.9)
    w_router = scatter_about(keys[9], (D, EXPERTS), (4 * D) ** -0.5, 0.078125)
    expert_gate = scatter_about(keys[10], (EXPERTS, D, FF), D ** -0.5, 0.15625, ((0, 16),))
    expert_up = scatter_about(keys[11], (EXPERTS, D, FF), D ** -0.5, 0.15625, ((0, 16),))
    expert_down = scatter_about(keys[12], (EXPERTS, FF, D), (FF // 16) ** -0.5, 1.0, ((0, 16),))
    cotangent = scatter_about(keys[13], (TOKENS, D), 1.0, 6.0, ((0, 32),))
    return dict(tokens=tokens, routes=routes, pieces=pieces, attn_gain=attn_gain, w_query=w_query, w_key=w_key, w_value=w_value, w_out=w_out, ffn_gain=ffn_gain, w_router=w_router, expert_gate=expert_gate, expert_up=expert_up, expert_down=expert_down, cotangent=cotangent)


@jax.custom_vjp
def low(v):
    return lax.optimization_barrier(v.astype(jnp.bfloat16)).astype(jnp.float32)

@jax.custom_vjp
def low_back(v):
    return v

def low_keep(v):
    return (low(v), None)

def low_pass(kept, grad):
    return (grad,)

def back_keep(v):
    return (v, None)

def back_low(kept, grad):
    return (low(grad),)
low.defvjp(low_keep, low_pass)
low_back.defvjp(back_keep, back_low)
eps = 1e-06
theta_base = 10000.0
masked_score = -1e+30

def rms_scale(values):
    return lax.rsqrt(lax.optimization_barrier(jnp.mean(values * values, axis=-1, keepdims=True)) + eps)

def rotary_tables(length, head_size):
    half_head = head_size // 2
    frequency = theta_base ** (-(jnp.arange(half_head, dtype=jnp.float32) * 2.0) / head_size)
    angles = jnp.arange(length, dtype=jnp.float32)[:, None] * frequency[None, :]
    cosine = jnp.concatenate([jnp.cos(angles), jnp.cos(angles)], axis=-1)
    sine = jnp.concatenate([jnp.sin(angles), jnp.sin(angles)], axis=-1)
    return (cosine, sine)

def rotate_half(values):
    half_head = values.shape[-1] // 2
    return jnp.concatenate([-values[..., half_head:], values[..., :half_head]], axis=-1)

def piece_labels(starts, length):
    position = jnp.arange(length, dtype=jnp.int32)
    inside = (position[:, None] >= starts[None, :]) & (position[:, None] < starts[None, :] + PIECE)
    numbers = jnp.arange(1, starts.shape[0] + 1, dtype=jnp.int32)
    return lax.optimization_barrier(jnp.sum(inside.astype(jnp.int32) * numbers[None, :], axis=1))

def allowed_pairs(starts):
    position = jnp.arange(LEN, dtype=jnp.int32)
    labels = piece_labels(starts, LEN)
    same_piece = (labels[:, None] == labels[None, :]) & (labels[:, None] > 0)
    return (position[None, :] <= position[:, None]) | same_piece

def layer_sequence(inputs, route_rows, starts, params):
    attn_gain, w_query, w_key, w_value, w_out, ffn_gain, w_router, expert_gate, expert_up, expert_down = params
    highest = lax.Precision.HIGHEST
    query_group = HEADS // KV
    normed_one = low(inputs * rms_scale(inputs) * attn_gain)
    query = low_back(jnp.dot(normed_one, w_query, precision=highest))
    key_proj = low_back(jnp.dot(normed_one, w_key, precision=highest))
    value_low = low(low_back(jnp.dot(normed_one, w_value, precision=highest)))
    cosine, sine = rotary_tables(LEN, HEAD)
    query_heads = query.reshape(LEN, HEADS, HEAD)
    query_rot = low(query_heads * cosine[:, None, :] + rotate_half(query_heads) * sine[:, None, :])
    query_rot = query_rot.reshape(LEN, KV, query_group, HEAD)
    key_heads = key_proj.reshape(LEN, KV, HEAD)
    key_rot = low(key_heads * cosine[:, None, :] + rotate_half(key_heads) * sine[:, None, :])
    value_heads = value_low.reshape(LEN, KV, HEAD)
    scores = low_back(HEAD ** (-0.5) * jnp.einsum('qkgh,lkh->kgql', query_rot, key_rot, precision=highest))
    scores = jnp.where(allowed_pairs(starts), scores, masked_score)
    prob_low = low(jax.nn.softmax(scores, axis=-1))
    mixed_heads = jnp.einsum('kgql,lkh->qkgh', prob_low, value_heads, precision=highest).reshape(LEN, D)
    attn = low(low_back(mixed_heads))
    residual = inputs + low_back(jnp.dot(attn, w_out, precision=highest))
    normed_two = low(residual * rms_scale(residual) * ffn_gain)
    logits = low_back(jnp.dot(normed_two, w_router, precision=highest))
    gate_share = jax.nn.softmax(jnp.take_along_axis(logits, route_rows, axis=1), axis=-1)

    def one_expert(carry, packed):
        expert_id, gate_weight, up_weight, down_weight = packed
        share = lax.optimization_barrier(jnp.sum(gate_share * (route_rows == expert_id).astype(gate_share.dtype), axis=1))
        routed_in = low_back(normed_two)
        gate_act = low_back(jnp.dot(routed_in, gate_weight, precision=highest))
        up_act = low_back(jnp.dot(routed_in, up_weight, precision=highest))
        hidden = low(jax.nn.silu(gate_act) * up_act)
        result = low(low_back(jnp.dot(hidden, down_weight, precision=highest)))
        return (carry + share[:, None] * result, None)
    expert_ids = jnp.arange(EXPERTS, dtype=jnp.int32)
    mixture, _ = lax.scan(jax.checkpoint(one_expert), jnp.zeros_like(residual), (expert_ids, expert_gate, expert_up, expert_down))
    return residual + mixture

def reference(tokens, routes, pieces, attn_gain, w_query, w_key, w_value, w_out, ffn_gain, w_router, expert_gate, expert_up, expert_down, cotangent):
    params = (attn_gain.astype(jnp.float32), w_query.astype(jnp.float32), w_key.astype(jnp.float32), w_value.astype(jnp.float32), w_out.astype(jnp.float32), ffn_gain.astype(jnp.float32), w_router.astype(jnp.float32), expert_gate.astype(jnp.float32), expert_up.astype(jnp.float32), expert_down.astype(jnp.float32))
    inputs = tokens.astype(jnp.float32)
    route_seqs = routes.reshape(SEQS, LEN, TOP)

    def forward(layer_in, layer_params):

        def step(carry, packed):
            seq_in, seq_routes, seq_starts = packed
            return (carry, layer_sequence(seq_in, seq_routes, seq_starts, layer_params))
        _, layer_out = lax.scan(jax.checkpoint(step), jnp.zeros((), layer_in.dtype), (layer_in.reshape(SEQS, LEN, D), route_seqs, pieces))
        return layer_out.reshape(TOKENS, D)
    combined, pullback = jax.vjp(forward, inputs, params)
    d_inputs, grads = pullback(cotangent.astype(combined.dtype))
    d_attn_gain, d_query, d_key, d_value, d_out, d_ffn_gain, d_router, d_expert_gate, d_expert_up, d_expert_down = grads
    return (combined.astype(jnp.bfloat16), d_inputs, d_attn_gain, d_query, d_key, d_value, d_out, d_ffn_gain, d_router, d_expert_gate, d_expert_up, d_expert_down)
```

```python
import functools
import math

import jax
import jax.numpy as jnp
import numpy as np
from jax import lax
from jax.experimental import pallas as pl
from jax.experimental.pallas import tpu as pltpu
from jax.sharding import PartitionSpec as P

D = 1536
HEADS = 24
KV = 8
HEAD = 64
LEN = 1024
PIECE = 256
QUERIES = HEADS // KV
WIDE = 256
TILE = 256
GROUP = 4

eps = 1e-06
theta_base = 10000.0
masked_score = -1e30
score_scale = HEAD ** (-0.5)
two_scale = score_scale * math.log2(math.e)

F32 = jnp.float32
BF16 = jnp.bfloat16
NN = (((1,), (0,)), ((), ()))
NT = (((1,), (1,)), ((), ()))
TN = (((0,), (0,)), ((), ()))
ANY = pl.BlockSpec(memory_space=pl.ANY)
SMEM = pl.BlockSpec(memory_space=pltpu.SMEM)


def dot(left, right, dims):
    return lax.dot_general(left, right, dims, preferred_element_type=F32)


def shaped(shape, dtype):
    return jax.ShapeDtypeStruct(shape, dtype)


def rms_scale(values):
    return lax.rsqrt(jnp.mean(values * values, axis=-1, keepdims=True) + eps)


def rotary_tables():
    half_head = HEAD // 2
    frequency = theta_base ** (-(np.arange(half_head, dtype=np.float64) * 2.0) / HEAD)
    angles = frequency[:, None] * np.arange(LEN, dtype=np.float64)[None, :]
    return np.cos(angles).astype(np.float32), np.sin(angles).astype(np.float32)


def turn(values, cosine, sine):
    first, second = values[: HEAD // 2], values[HEAD // 2 :]
    return jnp.concatenate([first * cosine - second * sine, second * cosine + first * sine], axis=0)


def turn_back(grads, cosine, sine):
    first, second = grads[: HEAD // 2], grads[HEAD // 2 :]
    return jnp.concatenate([first * cosine + second * sine, second * cosine - first * sine], axis=0)


def fill_bias(pieces, bias):
    for block in range(LEN // WIDE):
        first = block * WIDE
        shape = bias.shape[1:]
        key = lax.broadcasted_iota(jnp.int32, shape, 0) + first
        query = lax.broadcasted_iota(jnp.int32, shape, 1) + first
        allowed = key <= query
        for piece in range(pieces.shape[1]):
            start = pieces[0, piece]
            low, high = jnp.minimum(key, query), jnp.maximum(key, query)
            allowed = allowed | ((low >= start) & (high < start + PIECE))
        bias[block] = jnp.where(allowed, 0.0, masked_score)


def key_span(block):
    return block * WIDE, min((block + 2) * WIDE, LEN)


def masked_scores(keys, queries, bias, block):
    first, last = key_span(block)
    scores = dot(keys[:last], queries, NN)
    masked = scores[first:] + bias[block, : last - first]
    return masked if first == 0 else jnp.concatenate([scores[:first], masked], axis=0)


def attend_kernel(pieces, q_in, k_in, v_in, cosine, sine, attn, q_out, k_out, v_out, lse, bias):
    @pl.when(pl.program_id(0) == 0)
    def _():
        fill_bias(pieces, bias)

    cos, sin = cosine[...], sine[...]
    k_rot = turn(k_in[...], cos, sin)
    k_out[...] = k_rot.astype(BF16)
    keys = k_rot.T.astype(BF16)
    values = v_in[...].astype(BF16)
    v_out[...] = values
    for head in range(QUERIES):
        rows = pl.ds(head * HEAD, HEAD)
        q_rot = turn(q_in[rows, :], cos, sin).astype(BF16)
        q_out[rows, :] = q_rot
        for block in range(LEN // WIDE):
            columns = pl.ds(block * WIDE, WIDE)
            last = key_span(block)[1]
            scores = masked_scores(keys, q_rot[:, block * WIDE : (block + 1) * WIDE], bias, block)
            highest = jnp.max(scores, axis=0, keepdims=True) * two_scale
            weights = jnp.exp2(scores * two_scale - highest)
            total = jnp.sum(weights, axis=0, keepdims=True)
            mixed = dot(values[:, :last], weights.astype(BF16), NN) / total
            attn[rows, columns] = mixed.astype(BF16)
            lse[head : head + 1, columns] = highest + jnp.log2(total)


def attend_call(pieces, q_in, k_in, v_in, cosine, sine):
    width = QUERIES * HEAD
    rows = lambda count: pl.BlockSpec((count, LEN), lambda i: (i, 0))
    table = pl.BlockSpec((HEAD // 2, LEN), lambda i: (0, 0))
    return pl.pallas_call(
        attend_kernel,
        grid=(KV,),
        in_specs=[SMEM, rows(width), rows(HEAD), rows(HEAD), table, table],
        out_specs=[rows(width), rows(width), rows(HEAD), rows(HEAD), rows(8)],
        out_shape=[
            shaped((D, LEN), BF16),
            shaped((D, LEN), BF16),
            shaped((KV * HEAD, LEN), BF16),
            shaped((KV * HEAD, LEN), BF16),
            shaped((KV * 8, LEN), F32),
        ],
        scratch_shapes=[pltpu.VMEM((LEN // WIDE, 2 * WIDE, WIDE), F32)],
        compiler_params=pltpu.CompilerParams(vmem_limit_bytes=48 << 20),
        cost_estimate=pl.CostEstimate(
            flops=16 * HEADS * LEN * LEN * HEAD, bytes_accessed=30 << 20, transcendentals=HEADS * LEN * LEN
        ),
        name="attend",
    )(pieces, q_in, k_in, v_in, cosine, sine)


def attend_back_kernel(
    pieces, q_in, k_in, v_in, do_in, lse, cosine, sine, dq, dk, dv, bias, dk_sum, dv_sum
):
    @pl.when(pl.program_id(0) == 0)
    def _():
        fill_bias(pieces, bias)

    cos, sin = cosine[...], sine[...]
    k_cols = k_in[...]
    keys = k_cols.astype(F32).T.astype(BF16)
    values = v_in[...].astype(F32).T.astype(BF16)
    dk_sum[...] = jnp.zeros_like(dk_sum)
    dv_sum[...] = jnp.zeros_like(dv_sum)
    for head in range(QUERIES):
        rows = pl.ds(head * HEAD, HEAD)
        q_cols, do_cols = q_in[rows, :], do_in[rows, :]
        q_rows = q_cols.astype(F32).T.astype(BF16)
        do_rows = do_cols.astype(F32).T.astype(BF16)
        for block in range(LEN // WIDE):
            columns = pl.ds(block * WIDE, WIDE)
            part = slice(block * WIDE, (block + 1) * WIDE)
            last = key_span(block)[1]
            scores = masked_scores(keys, q_cols[:, part], bias, block)
            probs = jnp.exp2(scores * two_scale - lse[head : head + 1, columns])
            d_probs = dot(values[:last], do_cols[:, part], NN)
            product = probs * d_probs
            delta = jnp.sum(product, axis=0, keepdims=True)
            d_scores = (product - probs * delta).astype(BF16)
            dv_sum[:last] += dot(probs.astype(BF16), do_rows[part], NN)
            dk_sum[:last] += dot(d_scores, q_rows[part], NN)
            d_query = dot(k_cols[:, :last], d_scores, NN) * score_scale
            dq[rows, columns] = turn_back(d_query, cos[:, part], sin[:, part]).astype(BF16)
    dk[...] = turn_back(dk_sum[...].T * score_scale, cos, sin).astype(BF16)
    dv[...] = dv_sum[...].T.astype(BF16)


def attend_back_call(pieces, q_in, k_in, v_in, do_in, lse, cosine, sine):
    width = QUERIES * HEAD
    rows = lambda count: pl.BlockSpec((count, LEN), lambda i: (i, 0))
    table = pl.BlockSpec((HEAD // 2, LEN), lambda i: (0, 0))
    return pl.pallas_call(
        attend_back_kernel,
        grid=(KV,),
        in_specs=[SMEM, rows(width), rows(HEAD), rows(HEAD), rows(width), rows(8), table, table],
        out_specs=[rows(width), rows(HEAD), rows(HEAD)],
        out_shape=[
            shaped((D, LEN), BF16),
            shaped((KV * HEAD, LEN), BF16),
            shaped((KV * HEAD, LEN), BF16),
        ],
        scratch_shapes=[
            pltpu.VMEM((LEN // WIDE, 2 * WIDE, WIDE), F32),
            pltpu.VMEM((LEN, HEAD), F32),
            pltpu.VMEM((LEN, HEAD), F32),
        ],
        compiler_params=pltpu.CompilerParams(vmem_limit_bytes=48 << 20),
        cost_estimate=pl.CostEstimate(
            flops=40 * HEADS * LEN * LEN * HEAD, bytes_accessed=30 << 20, transcendentals=HEADS * LEN * LEN
        ),
        name="attend_back",
    )(pieces, q_in, k_in, v_in, do_in, lse, cosine, sine)


def expert_kernel(first, fresh, steps, expert, n2, up, gate, *rest):
    rest = list(rest)
    w_in = rest[:2]
    del rest[:2]
    if not fresh:
        sums_in = rest[:2]
        del rest[:2]
    if not first:
        mix_in, dx_in, share_in = rest[:3]
        del rest[:3]
    mix, dx, share_out, sums_a, sums_b, weights, sums, sem = rest
    half = weights.shape[0] // 6
    width = 2 * half
    step = pl.program_id(0)

    def pieces_of(halves, whole):
        return [
            (ref.at[pl.ds(kind * half, half)], whole.at[pl.ds((2 * kind + part) * half, half)])
            for kind in range(3)
            for part, ref in enumerate(halves)
        ]

    def copy_all(pairs):
        copies = [pltpu.make_async_copy(a, b, sem.at[n]) for n, (a, b) in enumerate(pairs)]
        for copy in copies:
            copy.start()
        for copy in copies:
            copy.wait()

    @pl.when(step == 0)
    def _():
        if fresh:
            copy_all(pieces_of(w_in, weights))
            sums[...] = jnp.zeros_like(sums)
        else:
            copy_all(pieces_of(w_in, weights) + pieces_of(sums_in, sums))

    rows, grads = n2[...], up[...]
    hit = lax.broadcasted_iota(jnp.int32, gate.shape, 1) == expert[0]
    share = jnp.sum(jnp.where(hit, gate[...], 0.0), axis=1, keepdims=True)
    w_gate, w_up, w_down = weights[:width], weights[width : 2 * width], weights[2 * width :]
    gate_act = dot(rows, w_gate, NT)
    up_act = dot(rows, w_up, NT)
    d_plain = dot(grads, w_down, NT)
    sigmoid = 1.0 / (1.0 + jnp.exp(-gate_act))
    silu = gate_act * sigmoid
    hidden = silu * up_act
    shared = (share * hidden).astype(BF16)
    d_share = jnp.sum(hidden * d_plain, axis=1, keepdims=True)
    d_hidden = share * d_plain
    d_gate = (d_hidden * up_act * (sigmoid + silu * (1.0 - sigmoid))).astype(BF16)
    d_up = (d_hidden * silu).astype(BF16)
    mixed = dot(shared, w_down, NN)
    d_rows = dot(d_gate, w_gate, NN) + dot(d_up, w_up, NN)
    d_share = jnp.where(hit, d_share, 0.0)
    if first:
        mix[...], dx[...], share_out[...] = mixed, d_rows, d_share
    else:
        mix[...] = mix_in[...] + mixed
        dx[...] = dx_in[...] + d_rows
        share_out[...] = share_in[...] + d_share
    sums[:width] += dot(d_gate, rows, TN)
    sums[width : 2 * width] += dot(d_up, rows, TN)
    sums[2 * width :] += dot(shared, grads, TN)

    @pl.when(step == steps - 1)
    def _():
        copy_all([(b, a) for a, b in pieces_of((sums_a, sums_b), sums)])


def expert_call(expert, n2, up, gate, weights, sums=None, carry=None):
    tokens, experts, height = n2.shape[0], gate.shape[1], weights[0].shape[0]
    steps = tokens // TILE
    rows = lambda count: pl.BlockSpec((TILE, count), lambda i: (i, 0))
    ins = [expert, n2, up, gate, *weights]
    specs = [SMEM, rows(D), rows(D), rows(experts), ANY, ANY]
    aliases = {}
    if sums is not None:
        aliases.update({len(ins): 3, len(ins) + 1: 4})
        ins += sums
        specs += [ANY, ANY]
    if carry is not None:
        aliases.update({len(ins) + k: k for k in range(3)})
        ins += carry
        specs += [rows(D), rows(D), rows(experts)]
    out = pl.pallas_call(
        functools.partial(expert_kernel, carry is None, sums is None, steps),
        grid=(steps,),
        in_specs=specs,
        out_specs=[rows(D), rows(D), rows(experts), ANY, ANY],
        out_shape=[
            shaped((tokens, D), F32),
            shaped((tokens, D), F32),
            shaped((tokens, experts), F32),
            shaped((height, D), F32),
            shaped((height, D), F32),
        ],
        scratch_shapes=[
            pltpu.VMEM((2 * height, D), BF16),
            pltpu.VMEM((2 * height, D), F32),
            pltpu.SemaphoreType.DMA((12,)),
        ],
        input_output_aliases=aliases,
        compiler_params=pltpu.CompilerParams(vmem_limit_bytes=56 << 20),
        cost_estimate=pl.CostEstimate(
            flops=12 * tokens * D * height, bytes_accessed=24 * tokens * D, transcendentals=tokens * height
        ),
        name="expert",
    )(*ins)
    return list(out[:3]), list(out[3:])


def local(
    tokens,
    routes,
    pieces,
    attn_gain,
    w_query,
    w_key,
    w_value,
    w_out,
    ffn_gain,
    w_router,
    expert_gate,
    expert_up,
    expert_down,
    cotangent,
):
    shards, reps = lax.axis_size("ep"), lax.axis_size("rep")
    experts = w_router.shape[1]
    slots = shards // GROUP
    place = lax.axis_index("ep")
    side = lax.axis_index("rep") % 2

    def swap(values, bits):
        return lax.ppermute(values, "ep", [(i, i ^ bits) for i in range(shards)])

    def swap_rep(values, bits=1):
        return lax.ppermute(values, "rep", [(i, i ^ bits) for i in range(reps)])

    with jax.named_scope("weights_out"):
        half = expert_gate.shape[2] // 2
        whole = [expert_gate[0].T, expert_up[0].T, expert_down[0]]
        halves = [jnp.concatenate([w[k * half : (k + 1) * half] for w in whole]) for k in range(2)]
        mine = jnp.where(side == 0, halves[0], halves[1])
        weights = [(mine, jnp.where(side == 0, halves[1], halves[0]))]
        for slot in range(1, slots):
            landed = swap(mine, slot * GROUP)
            weights.append((landed, swap_rep(landed)))
    ids = [((place // GROUP) ^ slot) * GROUP + place % GROUP for slot in range(slots)]
    ids = [expert.astype(jnp.int32).reshape(1) for expert in ids]

    def share_chip(values):
        return jnp.concatenate([values, swap(values, 1)])

    def share_out(values):
        return [share_chip(values), share_chip(swap(values, 2))]

    with jax.named_scope("cotangent_out"):
        grads_in = share_out(cotangent)

    with jax.named_scope("attention"):
        inputs = tokens.astype(F32)
        scale_one = rms_scale(inputs)
        norm_one = inputs * scale_one
        normed_one = (norm_one * attn_gain).astype(BF16)
        w_dims = (((0,), (1,)), ((), ()))
        query, key, value = [dot(w, normed_one, w_dims) for w in (w_query, w_key, w_value)]
        cosine, sine = [jnp.asarray(table) for table in rotary_tables()]
        attn, query_rot, key_rot, value_low, lse = attend_call(pieces, query, key, value, cosine, sine)

    with jax.named_scope("routing"):
        residual = inputs + dot(attn, w_out, TN)
        scale_two = rms_scale(residual)
        norm_two = residual * scale_two
        normed_two = (norm_two * ffn_gain).astype(BF16)
        logits = jnp.dot(normed_two, w_router, preferred_element_type=F32)
        chosen = jnp.any(routes[:, :, None] == jnp.arange(experts, dtype=jnp.int32), axis=1)
        gate_share = jax.nn.softmax(jnp.where(chosen, logits, masked_score), axis=-1)
        rows_in, gates_in = share_out(normed_two), share_out(gate_share)

    with jax.named_scope("experts"):
        carry = [None, None]
        sums = [None] * slots
        order = [(slot, chip) for slot in range(slots - 2) for chip in (0, 1)]
        order += [(slots - 2, 1), (slots - 1, 1), (slots - 2, 0), (slots - 1, 0)]
        for slot, chip in order:
            carry[chip], sums[slot] = expert_call(
                ids[slot], rows_in[chip], grads_in[chip], gates_in[chip], weights[slot], sums[slot], carry[chip]
            )

    def bring_home(item, dtype):
        here, there = carry[0][item], carry[1][item]
        there = there[:LEN] + swap(there[LEN:].astype(dtype), 1).astype(F32)
        here = here[:LEN] + swap(here[LEN:].astype(dtype), 1).astype(F32)
        return here + swap(there.astype(dtype), 2).astype(F32)

    with jax.named_scope("routing_back"):
        d_rows = bring_home(1, BF16)
        d_share = bring_home(2, F32)
        upstream = cotangent.astype(F32)
        d_chosen = gate_share * (d_share - jnp.sum(gate_share * d_share, axis=-1, keepdims=True))
        d_logits = d_chosen.astype(BF16)
        d_router = dot(normed_two, d_logits, TN)
        d_normed_two = dot(d_logits, w_router, NT) + d_rows
        d_ffn_gain = jnp.sum(d_normed_two * norm_two, axis=0)
        scaled_two = d_normed_two * ffn_gain
        d_residual = upstream + scale_two * (
            scaled_two - norm_two * jnp.mean(scaled_two * norm_two, axis=-1, keepdims=True)
        )
        d_mixed = d_residual.astype(BF16)
        d_out = dot(attn, d_mixed, NN)
        d_attn = dot(w_out, d_mixed, NT).astype(BF16)

    with jax.named_scope("combine"):
        output = (residual + bring_home(0, BF16)).astype(BF16)

    with jax.named_scope("attention_back"):
        d_query, d_key, d_value = attend_back_call(
            pieces, query_rot, key_rot, value_low, d_attn, lse, cosine, sine
        )
        in_dims = (((0,), (1,)), ((), ()))
        d_weights = [dot(normed_one, g, in_dims) for g in (d_query, d_key, d_value)]
        back_dims = (((0,), (1,)), ((), ()))
        d_normed_one = sum(
            dot(g, w, back_dims) for g, w in ((d_query, w_query), (d_key, w_key), (d_value, w_value))
        )
        scaled_one = d_normed_one * attn_gain
        d_tokens = d_residual + scale_one * (
            scaled_one - norm_one * jnp.mean(scaled_one * norm_one, axis=-1, keepdims=True)
        )

    def reduce_rows(values):
        values = values.reshape(shards, -1, values.shape[1])
        bits = 1
        while bits < shards:
            values = values.reshape(values.shape[0] // 2, 2, *values.shape[1:])
            bit = (place // bits) % 2
            kept, sent = [
                lax.dynamic_index_in_dim(values, index, axis=1, keepdims=False) for index in (bit, 1 - bit)
            ]
            values = kept.astype(F32) + swap(sent.astype(BF16), bits).astype(F32)
            bits *= 2
        return reduce_reps(values[0])

    def reduce_reps(values, bits=1):
        while bits < reps:
            values = values.astype(BF16)
            values = values.astype(F32) + swap_rep(values, bits).astype(F32)
            bits *= 2
        return values

    with jax.named_scope("sums_out"):
        pad = jnp.zeros((D, 128 - experts - 1), F32)
        packed = jnp.concatenate([d_out, d_router, d_ffn_gain[:, None], pad], axis=1)
        packed = reduce_rows(packed)
        s_out, s_router, s_ffn = packed[:, :D], packed[:, D : D + experts], packed[:, D + experts]

    with jax.named_scope("sums_experts"):
        total = None
        for slot in range(slots):
            own, other = sums[slot]
            own = own + swap_rep(other.astype(BF16)).astype(F32)
            if slot > 0:
                own = swap(own.astype(BF16), slot * GROUP).astype(F32)
            total = own if total is None else total + own
        total = reduce_reps(total, 2).astype(BF16)
        other = swap_rep(total)
        joined = jnp.stack([jnp.where(side == 0, total, other), jnp.where(side == 0, other, total)])
        joined = joined.reshape(2, 3, half, D).astype(F32)
        s_gate, s_up, s_down = [joined[:, k].reshape(2 * half, D) for k in range(3)]

    with jax.named_scope("sums_attention"):
        packed = reduce_rows(jnp.concatenate(d_weights, axis=1))
        first = place * packed.shape[0]
        w_all = jnp.concatenate(
            [lax.dynamic_slice_in_dim(w, first, packed.shape[0]) for w in (w_query, w_key, w_value)], axis=1
        )
        s_attn = jnp.sum(packed * w_all.astype(F32), axis=1)
        s_attn = s_attn / lax.dynamic_slice_in_dim(attn_gain, first, packed.shape[0])
        wide = KV * HEAD
        s_query, s_key, s_value = packed[:, :D], packed[:, D : D + wide], packed[:, D + wide :]

    return (
        output,
        d_tokens,
        s_attn,
        s_query,
        s_key,
        s_value,
        s_out,
        s_ffn,
        s_router,
        s_gate.T[None],
        s_up.T[None],
        s_down[None],
    )


def solution(mesh):
    rows, whole, slices = P(("rep", "ep"), None), P(), P("ep", None)
    expert = P("ep", None, None)
    return jax.shard_map(
        local,
        mesh=mesh,
        in_specs=(rows,) * 3 + (whole,) * 7 + (expert,) * 3 + (rows,),
        out_specs=(rows, rows, P("ep")) + (slices,) * 4 + (P("ep"), slices) + (expert,) * 3,
        check_vma=False,
    )
```

```python
import functools
import math

import jax
import jax.numpy as jnp
import numpy as np
from jax import lax
from jax.experimental import pallas as pl
from jax.experimental.pallas import tpu as pltpu
from jax.sharding import PartitionSpec as P

D = 1536
HEADS = 24
KV = 8
HEAD = 64
LEN = 1024
PIECE = 256
QUERIES = HEADS // KV
WIDE = 256
TILE = 256
GROUP = 4
PARTS = 4

eps = 1e-06
theta_base = 10000.0
masked_score = -1e30
score_scale = HEAD ** (-0.5)
two_scale = score_scale * math.log2(math.e)

F32 = jnp.float32
BF16 = jnp.bfloat16
NN = (((1,), (0,)), ((), ()))
NT = (((1,), (1,)), ((), ()))
TN = (((0,), (0,)), ((), ()))
ANY = pl.BlockSpec(memory_space=pl.ANY)
SMEM = pl.BlockSpec(memory_space=pltpu.SMEM)


def dot(left, right, dims):
    return lax.dot_general(left, right, dims, preferred_element_type=F32)


def shaped(shape, dtype):
    return jax.ShapeDtypeStruct(shape, dtype)


def estimate(micros):
    return pl.CostEstimate(flops=int(micros * 1e7), bytes_accessed=int(micros * 1e4), transcendentals=0)


def rms_scale(values):
    return lax.rsqrt(jnp.mean(values * values, axis=-1, keepdims=True) + eps)


def rotary_tables():
    half_head = HEAD // 2
    frequency = theta_base ** (-(np.arange(half_head, dtype=np.float64) * 2.0) / HEAD)
    angles = frequency[:, None] * np.arange(LEN, dtype=np.float64)[None, :]
    return np.cos(angles).astype(np.float32), np.sin(angles).astype(np.float32)


def turn(values, cosine, sine):
    first, second = values[: HEAD // 2], values[HEAD // 2 :]
    return jnp.concatenate([first * cosine - second * sine, second * cosine + first * sine], axis=0)


def turn_back(grads, cosine, sine):
    first, second = grads[: HEAD // 2], grads[HEAD // 2 :]
    return jnp.concatenate([first * cosine + second * sine, second * cosine - first * sine], axis=0)


def fill_bias(pieces, bias):
    for block in range(LEN // WIDE):
        first = block * WIDE
        shape = bias.shape[1:]
        key = lax.broadcasted_iota(jnp.int32, shape, 0) + first
        query = lax.broadcasted_iota(jnp.int32, shape, 1) + first
        allowed = key <= query
        for piece in range(pieces.shape[1]):
            start = pieces[0, piece]
            low, high = jnp.minimum(key, query), jnp.maximum(key, query)
            allowed = allowed | ((low >= start) & (high < start + PIECE))
        bias[block] = jnp.where(allowed, 0.0, masked_score)


def key_span(block):
    return block * WIDE, min((block + 2) * WIDE, LEN)


def masked_scores(keys, queries, bias, block):
    first, last = key_span(block)
    scores = dot(keys[:last], queries, NN)
    masked = scores[first:] + bias[block, : last - first]
    return masked if first == 0 else jnp.concatenate([scores[:first], masked], axis=0)


def rows_at(place):
    return pl.BlockSpec((HEAD, LEN), lambda *grid: (place(*grid), 0))


def packed_row(head, kind):
    per = KV // PARTS
    part, inner = head // per, head % per
    row = {3: QUERIES * per + inner, 4: (QUERIES + 1) * per + inner}.get(kind, QUERIES * inner + kind)
    return part * (QUERIES + 2) * per + row


def table_spec():
    return pl.BlockSpec((HEAD // 2, LEN), lambda *grid: (0, 0))


def attend_kernel(pieces, q0, q1, q2, k_in, v_in, cosine, sine, attn, q_out, k_out, v_out, lse, bias):
    @pl.when(pl.program_id(0) == 0)
    def _():
        fill_bias(pieces, bias)

    cos, sin = cosine[...], sine[...]
    k_rot = turn(k_in[...], cos, sin)
    k_out[...] = k_rot.astype(BF16)
    keys = k_rot.T.astype(BF16)
    values = v_in[...].astype(BF16)
    v_out[...] = values
    for head, q_in in enumerate((q0, q1, q2)):
        rows = pl.ds(head * HEAD, HEAD)
        q_rot = turn(q_in[...], cos, sin).astype(BF16)
        q_out[rows, :] = q_rot
        for block in range(LEN // WIDE):
            columns = pl.ds(block * WIDE, WIDE)
            last = key_span(block)[1]
            scores = masked_scores(keys, q_rot[:, block * WIDE : (block + 1) * WIDE], bias, block)
            highest = jnp.max(scores, axis=0, keepdims=True) * two_scale
            weights = jnp.exp2(scores * two_scale - highest)
            total = jnp.sum(weights, axis=0, keepdims=True)
            mixed = dot(values[:, :last], weights.astype(BF16), NN) / total
            attn[rows, columns] = mixed.astype(BF16)
            lse[head : head + 1, columns] = highest + jnp.log2(total)


def attend_call(pieces, packed, cosine, sine):
    rows = lambda count: pl.BlockSpec((count, LEN), lambda i: (i, 0))
    width = QUERIES * HEAD
    return pl.pallas_call(
        attend_kernel,
        grid=(KV,),
        in_specs=[SMEM]
        + [rows_at(functools.partial(packed_row, kind=kind)) for kind in range(5)]
        + [table_spec(), table_spec()],
        out_specs=[rows(width), rows(width), rows(HEAD), rows(HEAD), rows(8)],
        out_shape=[
            shaped((D, LEN), BF16),
            shaped((D, LEN), BF16),
            shaped((KV * HEAD, LEN), BF16),
            shaped((KV * HEAD, LEN), BF16),
            shaped((KV * 8, LEN), F32),
        ],
        scratch_shapes=[pltpu.VMEM((LEN // WIDE, 2 * WIDE, WIDE), F32)],
        compiler_params=pltpu.CompilerParams(vmem_limit_bytes=48 << 20),
        cost_estimate=estimate(25),
        name="attend",
    )(pieces, *[packed] * 5, cosine, sine)


def attend_back_kernel(
    pieces, q_in, k_in, v_in, do_in, lse, cosine, sine, out, bias, keys_kept, values_kept, dk_sum, dv_sum
):
    kind = pl.program_id(1)

    @pl.when((pl.program_id(0) == 0) & (kind == 0))
    def _():
        fill_bias(pieces, bias)

    cos, sin = cosine[...], sine[...]

    @pl.when(kind == 0)
    def _():
        keys_kept[...] = k_in[...].astype(F32).T.astype(BF16)
        values_kept[...] = v_in[...].astype(F32).T.astype(BF16)
        dk_sum[...] = jnp.zeros_like(dk_sum)
        dv_sum[...] = jnp.zeros_like(dv_sum)

    @pl.when(kind < QUERIES)
    def _():
        k_cols, keys, values = k_in[...], keys_kept[...], values_kept[...]
        q_cols, do_cols = q_in[...], do_in[...]
        q_rows = q_cols.astype(F32).T.astype(BF16)
        do_rows = do_cols.astype(F32).T.astype(BF16)
        row_lse = lse[pl.ds(kind, 1), :]
        for block in range(LEN // WIDE):
            part = slice(block * WIDE, (block + 1) * WIDE)
            last = key_span(block)[1]
            scores = masked_scores(keys, q_cols[:, part], bias, block)
            probs = jnp.exp2(scores * two_scale - row_lse[:, part])
            d_probs = dot(values[:last], do_cols[:, part], NN)
            product = probs * d_probs
            delta = jnp.sum(product, axis=0, keepdims=True)
            d_scores = (product - probs * delta).astype(BF16)
            dv_sum[:last] += dot(probs.astype(BF16), do_rows[part], NN)
            dk_sum[:last] += dot(d_scores, q_rows[part], NN)
            d_query = dot(k_cols[:, :last], d_scores, NN) * score_scale
            out[:, part] = turn_back(d_query, cos[:, part], sin[:, part]).astype(BF16)

    @pl.when(kind == QUERIES)
    def _():
        out[...] = turn_back(dk_sum[...].T * score_scale, cos, sin).astype(BF16)

    @pl.when(kind == QUERIES + 1)
    def _():
        out[...] = dv_sum[...].T.astype(BF16)


def attend_back_call(part, pieces, q_in, k_in, v_in, do_in, lse, cosine, sine):
    per = KV // PARTS
    first = part * per
    query = rows_at(lambda i, j: (first + i) * QUERIES + jnp.minimum(j, QUERIES - 1))
    key = rows_at(lambda i, j: first + i)

    def place(i, j):
        tail = jnp.where(j == QUERIES, QUERIES * per + i, (QUERIES + 1) * per + i)
        return jnp.where(j < QUERIES, QUERIES * i + j, tail)

    return pl.pallas_call(
        attend_back_kernel,
        grid=(per, QUERIES + 2),
        in_specs=[SMEM, query, key, key, query, pl.BlockSpec((8, LEN), lambda i, j: (first + i, 0))]
        + [table_spec(), table_spec()],
        out_specs=rows_at(place),
        out_shape=shaped(((QUERIES + 2) * per * HEAD, LEN), BF16),
        scratch_shapes=[
            pltpu.VMEM((LEN // WIDE, 2 * WIDE, WIDE), F32),
            pltpu.VMEM((LEN, HEAD), BF16),
            pltpu.VMEM((LEN, HEAD), BF16),
            pltpu.VMEM((LEN, HEAD), F32),
            pltpu.VMEM((LEN, HEAD), F32),
        ],
        compiler_params=pltpu.CompilerParams(vmem_limit_bytes=48 << 20),
        cost_estimate=estimate(15),
        name="attend_back",
    )(pieces, q_in, k_in, v_in, do_in, lse, cosine, sine)


def expert_kernel(count, fresh, first, last_tokens, steps, ids, *rest):
    rest = list(rest)

    def take(number):
        taken = rest[:number]
        del rest[:number]
        return taken

    n2, up, gate = take(2), take(2), take(2)
    w_in = [take(2) for _ in range(count)]
    sums_in = [[] if new else take(2) for new in fresh]
    carry_in = [] if first else take(3)
    outs = take(6) if last_tokens else take(3)
    sums_out = [take(2) for _ in range(count)]
    weights, sums = take(1)[0], take(1)[0]
    low = None if all(fresh) else take(1)[0]
    sem = rest[0]
    half = weights.shape[1] // 6
    width = 2 * half
    step = pl.program_id(0)
    ahead = step < steps // 2

    def pieces_of(parts, whole):
        return [
            (ref.at[pl.ds(kind * half, half)], whole.at[pl.ds((2 * kind + part) * half, half)])
            for kind in range(3)
            for part, ref in enumerate(parts)
        ]

    def copies_of(pairs, lane):
        return [pltpu.make_async_copy(a, b, sem.at[lane, n]) for n, (a, b) in enumerate(pairs)]

    loads = [copies_of(pieces_of(w_in[e], weights.at[e]), e) for e in range(count)]
    sum_loads = [copies_of(pieces_of(sums_in[e], sums.at[e]), count + e) for e in range(count) if not fresh[e]]

    @pl.when(step == 0)
    def _():
        for copy in sum(loads + sum_loads, []):
            copy.start()
        for e in range(count):
            if fresh[e]:
                sums[e] = jnp.zeros(sums.shape[1:], F32)
        for copy in sum(loads + sum_loads, []):
            copy.wait()

    rows = jnp.where(ahead, n2[0][...], n2[1][...])
    grads = jnp.where(ahead, up[0][...], up[1][...])
    gates = jnp.where(ahead, gate[0][...], gate[1][...])
    lanes = lax.broadcasted_iota(jnp.int32, gates.shape, 1)
    mixed = d_rows = d_shares = None
    add = lambda total, value: value if total is None else total + value
    for e in range(count):
        w_both, w_down = weights.at[e, : 2 * width], weights.at[e, 2 * width :]
        hit = lanes == ids[e]
        share = jnp.sum(jnp.where(hit, gates, 0.0), axis=1, keepdims=True)
        acts = dot(rows, w_both[...], NT)
        gate_act, up_act = acts[:, :width], acts[:, width:]
        d_plain = dot(grads, w_down[...], NT)
        sigmoid = 1.0 / (1.0 + jnp.exp(-gate_act))
        silu = gate_act * sigmoid
        hidden = silu * up_act
        shared = (share * hidden).astype(BF16)
        d_share = jnp.sum(hidden * d_plain, axis=1, keepdims=True)
        d_hidden = share * d_plain
        d_gate = (d_hidden * up_act * (sigmoid + silu * (1.0 - sigmoid))).astype(BF16)
        d_up = (d_hidden * silu).astype(BF16)
        d_both = jnp.concatenate([d_gate, d_up], axis=1)
        mixed = add(mixed, dot(shared, w_down[...], NN))
        d_rows = add(d_rows, dot(d_both, w_both[...], NN))
        d_shares = add(d_shares, jnp.where(hit, d_share, 0.0))
        sums[e, : 2 * width] += dot(d_both, rows, TN)
        sums[e, 2 * width :] += dot(shared, grads, TN)
    results = [mixed, d_rows, d_shares]
    if not first:
        results = [result + ref[...] for result, ref in zip(results, carry_in)]
    if last_tokens:

        @pl.when(ahead)
        def _():
            for ref, result in zip(outs[:3], results):
                ref[...] = result

        @pl.when(jnp.logical_not(ahead))
        def _():
            for ref, result in zip(outs[3:], results):
                ref[...] = result.astype(ref.dtype)
    else:
        for ref, result in zip(outs, results):
            ref[...] = result

    @pl.when(step == steps - 1)
    def _():
        stores = []
        for e in range(count):
            pairs = [(b, a) for a, b in pieces_of(sums_out[e], sums.at[e])]
            if not fresh[e]:
                for kind in range(3):
                    low[e, pl.ds(kind * half, half)] = sums[e, pl.ds((2 * kind + 1) * half, half)].astype(BF16)
                pairs = pairs[::2] + [(low.at[e], sums_out[e][1])]
            stores += copies_of(pairs, e)
        for copy in stores:
            copy.start()
        for copy in stores:
            copy.wait()


def expert_call(ids, n2, up, gate, weights, sums, carry, last_tokens):
    tokens, experts, height, count = 2 * n2[0].shape[0], gate[0].shape[1], weights[0][0].shape[0], len(weights)
    steps = tokens // TILE
    rows = lambda cols: pl.BlockSpec((TILE, cols), lambda i: (i, 0))
    near = lambda cols: pl.BlockSpec((TILE, cols), lambda i: (jnp.minimum(i, steps // 2 - 1), 0))
    far = lambda cols: pl.BlockSpec((TILE, cols), lambda i: (jnp.maximum(i - steps // 2, 0), 0))
    ins = [ids, *n2, *up, *gate] + [w for pair in weights for w in pair]
    specs = [SMEM, near(D), far(D), near(D), far(D), near(experts), far(experts)] + [ANY] * (2 * count)
    fresh, first = [pair is None for pair in sums], carry is None
    columns = (D, D, experts)
    if last_tokens:
        outs = [shaped((tokens // 2, c), F32) for c in columns]
        outs += [shaped((tokens // 2, c), t) for c, t in zip(columns, (BF16, BF16, F32))]
        out_specs = [near(c) for c in columns] + [far(c) for c in columns]
    else:
        outs = [shaped((tokens, c), F32) for c in columns]
        out_specs = [rows(c) for c in columns]
    aliases = {}
    for pair in sums:
        if pair is not None:
            ins += pair
            specs += [ANY, ANY]
    if not first:
        if not last_tokens:
            aliases.update({len(ins) + k: k for k in range(3)})
        ins += carry
        specs += [rows(c) for c in columns]
    tokens_out = len(outs)
    for new in fresh:
        outs += [shaped((height, D), F32), shaped((height, D), F32 if new else BF16)]
        out_specs += [ANY, ANY]
    scratch = [pltpu.VMEM((count, 2 * height, D), BF16), pltpu.VMEM((count, 2 * height, D), F32)]
    if not all(fresh):
        scratch.append(pltpu.VMEM((count, height, D), BF16))
    scratch.append(pltpu.SemaphoreType.DMA((2 * count, 6)))
    done = pl.pallas_call(
        functools.partial(expert_kernel, count, fresh, first, last_tokens, steps),
        grid=(steps,),
        in_specs=specs,
        out_specs=out_specs,
        out_shape=outs,
        scratch_shapes=scratch,
        input_output_aliases=aliases,
        compiler_params=pltpu.CompilerParams(vmem_limit_bytes=60 << 20),
        cost_estimate=estimate(15 * count),
        name="expert",
    )(*ins)
    return list(done[:tokens_out]), [tuple(done[tokens_out + 2 * e : tokens_out + 2 * e + 2]) for e in range(count)]


def join_kernel(side, held, landed, gate, up, down):
    here = pl.program_id(0) == 0
    rows = jnp.where(here, held[...], landed[...]).astype(F32)
    half = down.shape[0]
    gate[...] = rows[:half].T
    up[...] = rows[half : 2 * half].T
    down[...] = rows[2 * half :]


def join_call(side, held, landed):
    half = held.shape[0] // 3
    whole = pl.BlockSpec(held.shape, lambda i, side: (0, 0))
    columns = pl.BlockSpec((D, half), lambda i, side: (0, lax.rem(side[0] + i, 2)))
    return pl.pallas_call(
        join_kernel,
        grid_spec=pltpu.PrefetchScalarGridSpec(
            num_scalar_prefetch=1,
            grid=(2,),
            in_specs=[whole, whole],
            out_specs=[columns, columns, pl.BlockSpec((half, D), lambda i, side: (lax.rem(side[0] + i, 2), 0))],
        ),
        out_shape=[shaped((D, 2 * half), F32), shaped((D, 2 * half), F32), shaped((2 * half, D), F32)],
        compiler_params=pltpu.CompilerParams(vmem_limit_bytes=48 << 20),
        cost_estimate=estimate(5),
        name="join",
    )(side, held, landed)


def after(values, *others):
    return lax.optimization_barrier((values, *others))[0]


class Task:
    def __init__(self, steps):
        self.steps, self.result, self.over = steps, None, False

    def step(self):
        if self.over:
            return []
        try:
            return [next(self.steps)]
        except StopIteration as stop:
            self.result, self.over = stop.value, True
            return [self.result]

    def finish(self):
        while not self.over:
            self.step()
        return self.result


def local(
    tokens,
    routes,
    pieces,
    attn_gain,
    w_query,
    w_key,
    w_value,
    w_out,
    ffn_gain,
    w_router,
    expert_gate,
    expert_up,
    expert_down,
    cotangent,
):
    shards, reps = lax.axis_size("ep"), lax.axis_size("rep")
    experts = w_router.shape[1]
    slots = shards // GROUP
    place = lax.axis_index("ep")
    side = lax.axis_index("rep") % 2

    def swap(values, bits):
        return lax.ppermute(values, "ep", [(i, i ^ bits) for i in range(shards)])

    def swap_rep(values, bits=1):
        return lax.ppermute(values, "rep", [(i, i ^ bits) for i in range(reps)])


    def reduce_reps(values, bits=1):
        while bits < reps:
            values = values.astype(BF16)
            landed = swap_rep(values, bits)
            yield values
            values = values.astype(F32) + landed.astype(F32)
            bits *= 2
        return values

    def reduce_rows(values):
        values = values.reshape(shards, -1, values.shape[1])
        bits = 1
        while bits < shards:
            values = values.reshape(values.shape[0] // 2, 2, *values.shape[1:])
            bit = (place // bits) % 2
            kept, sent = [
                lax.dynamic_index_in_dim(values, index, axis=1, keepdims=False) for index in (bit, 1 - bit)
            ]
            landed = swap(sent, bits)
            yield sent
            values = (kept.astype(F32) + landed.astype(F32)).astype(BF16)
            bits *= 2
        return (yield from reduce_reps(values[0]))

    def reduce_small(values):
        bits = 1
        while bits < shards:
            landed = swap(values, bits)
            yield values
            values = values + landed
            bits *= 2
        bits = 1
        while bits < reps:
            landed = swap_rep(values, bits)
            yield values
            values = values + landed
            bits *= 2
        return values

    def home_steps(keep, send, bits):
        landed = swap(send, bits)
        yield send
        return keep + landed.astype(F32)

    def sum_steps(slot, own, other):
        landed = swap_rep(other)
        yield other
        own = own + landed.astype(F32)
        if slot == 0:
            return own
        own = own.astype(BF16)
        landed = swap(own, slot * GROUP)
        yield own
        return landed

    with jax.named_scope("weights_out"):
        half = expert_gate.shape[2] // 2
        whole = [expert_gate[0].T, expert_up[0].T, expert_down[0]]
        halves = [jnp.concatenate([w[k * half : (k + 1) * half] for w in whole]) for k in range(2)]
        mine = jnp.where(side == 0, halves[0], halves[1])
        theirs = jnp.where(side == 0, halves[1], halves[0])
        tokens, mine, theirs = lax.optimization_barrier((tokens, mine, theirs))
        landed = [mine, swap(mine, GROUP)]

    with jax.named_scope("cotangent_out"):
        grads_next = swap(cotangent, 2)
        grads_in = [(cotangent, swap(cotangent, 1)), None]

    with jax.named_scope("attention"):
        inputs = tokens.astype(F32)
        scale_one = rms_scale(inputs)
        norm_one = inputs * scale_one
        normed_one = (norm_one * attn_gain).astype(BF16)
        per = KV // PARTS * HEAD
        w_all = jnp.concatenate(
            [
                w[:, part * wide * per : (part + 1) * wide * per]
                for part in range(PARTS)
                for w, wide in ((w_query, QUERIES), (w_key, 1), (w_value, 1))
            ],
            axis=1,
        )
        packed = dot(w_all, normed_one, (((0,), (1,)), ((), ())))
        landed.append(swap(after(mine, packed), 2 * GROUP))
        cosine, sine = [jnp.asarray(table) for table in rotary_tables()]
        attn, query_rot, key_rot, value_low, lse = attend_call(pieces, packed, cosine, sine)
        attn, lse = lax.optimization_barrier((attn, lse, landed[1], grads_next, grads_in[0][1]))[:2]

    with jax.named_scope("weights_out"):
        weights = [(mine, theirs), (landed[1], swap_rep(landed[1]))]
        late = after(mine, attn)
        landed += [swap(late, slot * GROUP) for slot in range(3, slots)]
        ids = [((place // GROUP) ^ slot) * GROUP + place % GROUP for slot in range(slots)]
        ids = [expert.astype(jnp.int32) for expert in ids]

    with jax.named_scope("cotangent_out"):
        grads_in[1] = (grads_next, swap(grads_next, 1))

    with jax.named_scope("routing"):
        residual = inputs + dot(attn, w_out, TN)
        scale_two = rms_scale(residual)
        norm_two = residual * scale_two
        normed_two = (norm_two * ffn_gain).astype(BF16)
        logits = jnp.dot(normed_two, w_router, preferred_element_type=F32)
        chosen = jnp.any(routes[:, :, None] == jnp.arange(experts, dtype=jnp.int32), axis=1)
        gate_share = jax.nn.softmax(jnp.where(chosen, logits, masked_score), axis=-1)
        rows_next, gates_next = swap(normed_two, 2), swap(gate_share, 2)
        rows_in = [(normed_two, swap(normed_two, 1)), None]
        gates_in = [(gate_share, swap(gate_share, 1)), None]

    carry, sums, clock = [None, None], [None] * slots, None
    tasks = [None] * slots

    def run(chip, group, last=False):
        nonlocal clock
        called = jnp.stack([ids[slot] for slot in group])
        if clock is not None:
            called = after(called, clock)
        carry[chip], done = expert_call(
            called,
            rows_in[chip],
            grads_in[chip],
            gates_in[chip],
            [weights[slot] for slot in group],
            [sums[slot] for slot in group],
            carry[chip],
            last,
        )
        clock = carry[chip][2]
        for slot, pair in zip(group, done):
            if sums[slot] is not None:
                tasks[slot] = Task(sum_steps(slot, *pair))
                tasks[slot].step()
            sums[slot] = pair

    def tick(*arrays):
        nonlocal clock
        clock = after(clock, *arrays)

    with jax.named_scope("experts"):
        run(0, [0])
        tick(*landed[2:3])
        weights += [(landed[2], swap_rep(landed[2]))]
        run(0, [1])
        tick(rows_next, gates_next)
        rows_in[1] = (rows_next, swap(rows_next, 1))
        gates_in[1] = (gates_next, swap(gates_next, 1))
        run(1, [0])
        tick(*landed[3:])
        weights += [(held, swap_rep(held)) for held in landed[3:]]
        for slot in range(1, slots - 1, 2):
            run(1, [slot, slot + 1])
        tick(*tasks[0].step())
        run(1, [slots - 1], True)
        home = [Task(home_steps(carry[1][k], carry[1][3 + k], 1)) for k in range(3)]
        [task.step() for task in home[1:]]
        there = [task.finish() for task in home[1:]]
        tick(*there)
        there_low = there[0].astype(BF16)
        rows_home, shares_home = swap(there_low, 2), swap(there[1], 2)
        tick(there_low, *tasks[1].step())
        for slot in range(2, slots):
            run(0, [slot], slot == slots - 1)
            tick(*[array for task in tasks[1 : slot - 1] for array in task.step()])

    with jax.named_scope("routing_back"):
        here = [carry[0][k] + swap(carry[0][3 + k], 1).astype(F32) for k in (1, 2)]
        d_rows = here[0] + rows_home.astype(F32)
        d_share = here[1] + shares_home
        upstream = cotangent.astype(F32)
        d_chosen = gate_share * (d_share - jnp.sum(gate_share * d_share, axis=-1, keepdims=True))
        d_logits = d_chosen.astype(BF16)
        d_router = dot(d_logits, normed_two, TN)
        d_normed_two = dot(d_logits, w_router, NT) + d_rows
        d_ffn_gain = jnp.sum(d_normed_two * norm_two, axis=0, keepdims=True)
        scaled_two = d_normed_two * ffn_gain
        d_residual = upstream + scale_two * (
            scaled_two - norm_two * jnp.mean(scaled_two * norm_two, axis=-1, keepdims=True)
        )
        d_mixed = d_residual.astype(BF16)
        d_out = dot(attn, d_mixed, NN).astype(BF16)
        d_attn = dot(w_out, d_mixed, NT).astype(BF16)

    with jax.named_scope("combine"):
        mix_send = after(carry[1][3], d_rows)
        mix_there = (carry[1][0] + swap(mix_send, 1).astype(F32)).astype(BF16)
        mix_home = swap(mix_there, 2)
        mix_here = carry[0][0] + swap(after(carry[0][3], d_rows), 1).astype(F32)

    with jax.named_scope("attention_back"):
        out_task, small_task = Task(reduce_rows(d_out)), Task(reduce_small(jnp.concatenate([d_router, d_ffn_gain])))
        running = [out_task, small_task]
        in_dims = (((0,), (1,)), ((), ()))
        pins = [array for task in running for array in task.step()]
        pins += [array for task in tasks[2 : slots - 1] for array in task.step()] + [mix_there]
        d_attn = after(d_attn, *pins)
        d_packed, w_tasks = [], []
        for part in range(PARTS):
            d_packed.append(
                attend_back_call(part, pieces, query_rot, key_rot, value_low, d_attn, lse, cosine, sine)
            )
            pins = [array for task in running for array in task.step()]
            if part == 0:
                pins += tasks[slots - 1].step()
            w_tasks.append(Task(reduce_rows(dot(normed_one, d_packed[-1], in_dims).astype(BF16))))
            pins += w_tasks[-1].step()
            if part < PARTS - 1:
                d_attn = after(d_attn, d_packed[-1], *pins)
            running.append(w_tasks[-1])
        span = w_all.shape[1] // PARTS
        d_normed_one = sum(
            dot(g, w_all[:, part * span : (part + 1) * span], in_dims) for part, g in enumerate(d_packed)
        )
        scaled_one = d_normed_one * attn_gain
        d_tokens = d_residual + scale_one * (
            scaled_one - norm_one * jnp.mean(scaled_one * norm_one, axis=-1, keepdims=True)
        )

    with jax.named_scope("combine"):
        output = (residual + mix_here + mix_home.astype(F32)).astype(BF16)

    with jax.named_scope("sums_experts"):
        total = tasks[0].finish()
        for task in tasks[1:]:
            total = total + task.finish().astype(F32)
        total = Task(reduce_reps(total, 2)).finish().astype(BF16)
        s_gate, s_up, s_down = join_call(side.astype(jnp.int32).reshape(1), total, swap_rep(total))

    with jax.named_scope("sums_rest"):
        s_out = out_task.finish()
        count = s_out.shape[0]
        first = place * count
        small = lax.dynamic_slice_in_dim(small_task.finish(), first, count, axis=1)
        s_router, s_ffn = small[:experts].T, small[experts]
        s_parts = [task.finish() for task in w_tasks]
        w_rows = lax.dynamic_slice_in_dim(w_all, first, count)
        s_attn = jnp.sum(jnp.concatenate(s_parts, axis=1) * w_rows.astype(F32), axis=1)
        s_attn = s_attn / lax.dynamic_slice_in_dim(attn_gain, first, count)
        cuts = [QUERIES * per, (QUERIES + 1) * per]
        s_query, s_key, s_value = [
            jnp.concatenate(group, axis=1) for group in zip(*[jnp.split(part, cuts, axis=1) for part in s_parts])
        ]

    return (
        output,
        d_tokens,
        s_attn,
        s_query,
        s_key,
        s_value,
        s_out.astype(F32),
        s_ffn,
        s_router,
        s_gate[None],
        s_up[None],
        s_down[None],
    )


def solution(mesh):
    rows, whole, slices = P(("rep", "ep"), None), P(), P("ep", None)
    expert = P("ep", None, None)
    return jax.shard_map(
        local,
        mesh=mesh,
        in_specs=(rows,) * 3 + (whole,) * 7 + (expert,) * 3 + (rows,),
        out_specs=(rows, rows, P("ep")) + (slices,) * 4 + (P("ep"), slices) + (expert,) * 3,
        check_vma=False,
    )
```

```python
import functools
import math

import jax
import jax.numpy as jnp
import numpy as np
from jax import lax
from jax.experimental import pallas as pl
from jax.experimental.pallas import tpu as pltpu
from jax.sharding import PartitionSpec as P

D = 1536
HEADS = 24
KV = 8
HEAD = 64
LEN = 1024
PIECE = 256
QUERIES = HEADS // KV
WIDE = 256
TILE = 256
GROUP = 4
PARTS = (4, 2, 2)
LANES = 128
WIDTH = D + LANES

eps = 1e-06
theta_base = 10000.0
masked_score = -1e30
score_scale = HEAD ** (-0.5)
two_scale = score_scale * math.log2(math.e)

F32 = jnp.float32
BF16 = jnp.bfloat16
NN = (((1,), (0,)), ((), ()))
NT = (((1,), (1,)), ((), ()))
TN = (((0,), (0,)), ((), ()))
ANY = pl.BlockSpec(memory_space=pl.ANY)
SMEM = pl.BlockSpec(memory_space=pltpu.SMEM)


def dot(left, right, dims):
    return lax.dot_general(left, right, dims, preferred_element_type=F32)


def shaped(shape, dtype):
    return jax.ShapeDtypeStruct(shape, dtype)


def estimate(micros):
    return pl.CostEstimate(flops=int(micros * 1e7), bytes_accessed=int(micros * 1e4), transcendentals=0)


def rms_scale(values):
    return lax.rsqrt(jnp.mean(values * values, axis=-1, keepdims=True) + eps)


def rotary_tables():
    half_head = HEAD // 2
    frequency = theta_base ** (-(np.arange(half_head, dtype=np.float64) * 2.0) / HEAD)
    angles = frequency[:, None] * np.arange(LEN, dtype=np.float64)[None, :]
    return np.cos(angles).astype(np.float32), np.sin(angles).astype(np.float32)


def turn(values, cosine, sine):
    first, second = values[: HEAD // 2], values[HEAD // 2 :]
    return jnp.concatenate([first * cosine - second * sine, second * cosine + first * sine], axis=0)


def turn_back(grads, cosine, sine):
    first, second = grads[: HEAD // 2], grads[HEAD // 2 :]
    return jnp.concatenate([first * cosine + second * sine, second * cosine - first * sine], axis=0)


def fill_bias(pieces, bias):
    for block in range(LEN // WIDE):
        first = block * WIDE
        shape = bias.shape[1:]
        key = lax.broadcasted_iota(jnp.int32, shape, 0) + first
        query = lax.broadcasted_iota(jnp.int32, shape, 1) + first
        allowed = key <= query
        for piece in range(pieces.shape[1]):
            start = pieces[0, piece]
            low, high = jnp.minimum(key, query), jnp.maximum(key, query)
            allowed = allowed | ((low >= start) & (high < start + PIECE))
        bias[block] = jnp.where(allowed, 0.0, masked_score)


def key_span(block):
    return block * WIDE, min((block + 2) * WIDE, LEN)


def masked_scores(keys, queries, bias, block):
    first, last = key_span(block)
    scores = dot(keys[:last], queries, NN)
    masked = scores[first:] + bias[block, : last - first]
    return masked if first == 0 else jnp.concatenate([scores[:first], masked], axis=0)


def rows_at(place):
    return pl.BlockSpec((HEAD, LEN), lambda *grid: (place(*grid), 0))


def packed_row(head, kind):
    row = 0
    for part, per in enumerate(PARTS):
        first = sum(PARTS[:part])
        inner = head - first
        here = {3: QUERIES * per + inner, 4: (QUERIES + 1) * per + inner}.get(kind, QUERIES * inner + kind)
        row = jnp.where(inner >= 0, (QUERIES + 2) * first + here, row)
    return row


def table_spec():
    return pl.BlockSpec((HEAD // 2, LEN), lambda *grid: (0, 0))


def attend_kernel(pieces, q0, q1, q2, k_in, v_in, cosine, sine, attn, q_out, k_out, v_out, lse, bias):
    @pl.when(pl.program_id(0) == 0)
    def _():
        fill_bias(pieces, bias)

    cos, sin = cosine[...], sine[...]
    k_rot = turn(k_in[...], cos, sin)
    k_out[...] = k_rot.astype(BF16)
    keys = k_rot.T.astype(BF16)
    values = v_in[...].astype(BF16)
    v_out[...] = values
    for head, q_in in enumerate((q0, q1, q2)):
        rows = pl.ds(head * HEAD, HEAD)
        q_rot = turn(q_in[...], cos, sin).astype(BF16)
        q_out[rows, :] = q_rot
        for block in range(LEN // WIDE):
            columns = pl.ds(block * WIDE, WIDE)
            last = key_span(block)[1]
            scores = masked_scores(keys, q_rot[:, block * WIDE : (block + 1) * WIDE], bias, block)
            highest = jnp.max(scores, axis=0, keepdims=True) * two_scale
            weights = jnp.exp2(scores * two_scale - highest)
            total = jnp.sum(weights, axis=0, keepdims=True)
            mixed = dot(values[:, :last], weights.astype(BF16), NN) / total
            attn[rows, columns] = mixed.astype(BF16)
            lse[head : head + 1, columns] = highest + jnp.log2(total)


def attend_call(pieces, packed, cosine, sine):
    rows = lambda count: pl.BlockSpec((count, LEN), lambda i: (i, 0))
    width = QUERIES * HEAD
    return pl.pallas_call(
        attend_kernel,
        grid=(KV,),
        in_specs=[SMEM]
        + [rows_at(functools.partial(packed_row, kind=kind)) for kind in range(5)]
        + [table_spec(), table_spec()],
        out_specs=[rows(width), rows(width), rows(HEAD), rows(HEAD), rows(8)],
        out_shape=[
            shaped((D, LEN), BF16),
            shaped((D, LEN), BF16),
            shaped((KV * HEAD, LEN), BF16),
            shaped((KV * HEAD, LEN), BF16),
            shaped((KV * 8, LEN), F32),
        ],
        scratch_shapes=[pltpu.VMEM((LEN // WIDE, 2 * WIDE, WIDE), F32)],
        compiler_params=pltpu.CompilerParams(vmem_limit_bytes=48 << 20),
        cost_estimate=estimate(25),
        name="attend",
    )(pieces, *[packed] * 5, cosine, sine)


def attend_back_kernel(
    pieces, q_in, k_in, v_in, do_in, lse, cosine, sine, out, bias, keys_kept, values_kept, dk_sum, dv_sum
):
    kind = pl.program_id(1)

    @pl.when((pl.program_id(0) == 0) & (kind == 0))
    def _():
        fill_bias(pieces, bias)

    cos, sin = cosine[...], sine[...]

    @pl.when(kind == 0)
    def _():
        keys_kept[...] = k_in[...].astype(F32).T.astype(BF16)
        values_kept[...] = v_in[...].astype(F32).T.astype(BF16)
        dk_sum[...] = jnp.zeros_like(dk_sum)
        dv_sum[...] = jnp.zeros_like(dv_sum)

    @pl.when(kind < QUERIES)
    def _():
        k_cols, keys, values = k_in[...], keys_kept[...], values_kept[...]
        q_cols, do_cols = q_in[...], do_in[...]
        q_rows = q_cols.astype(F32).T.astype(BF16)
        do_rows = do_cols.astype(F32).T.astype(BF16)
        row_lse = lse[pl.ds(kind, 1), :]
        for block in range(LEN // WIDE):
            part = slice(block * WIDE, (block + 1) * WIDE)
            last = key_span(block)[1]
            scores = masked_scores(keys, q_cols[:, part], bias, block)
            probs = jnp.exp2(scores * two_scale - row_lse[:, part])
            d_probs = dot(values[:last], do_cols[:, part], NN)
            product = probs * d_probs
            delta = jnp.sum(product, axis=0, keepdims=True)
            d_scores = (product - probs * delta).astype(BF16)
            dv_sum[:last] += dot(probs.astype(BF16), do_rows[part], NN)
            dk_sum[:last] += dot(d_scores, q_rows[part], NN)
            d_query = dot(k_cols[:, :last], d_scores, NN) * score_scale
            out[:, part] = turn_back(d_query, cos[:, part], sin[:, part]).astype(BF16)

    @pl.when(kind == QUERIES)
    def _():
        out[...] = turn_back(dk_sum[...].T * score_scale, cos, sin).astype(BF16)

    @pl.when(kind == QUERIES + 1)
    def _():
        out[...] = dv_sum[...].T.astype(BF16)


def attend_back_call(part, pieces, q_in, k_in, v_in, do_in, lse, cosine, sine):
    per, first = PARTS[part], sum(PARTS[:part])
    query = rows_at(lambda i, j: (first + i) * QUERIES + jnp.minimum(j, QUERIES - 1))
    key = rows_at(lambda i, j: first + i)

    def place(i, j):
        tail = jnp.where(j == QUERIES, QUERIES * per + i, (QUERIES + 1) * per + i)
        return jnp.where(j < QUERIES, QUERIES * i + j, tail)

    return pl.pallas_call(
        attend_back_kernel,
        grid=(per, QUERIES + 2),
        in_specs=[SMEM, query, key, key, query, pl.BlockSpec((8, LEN), lambda i, j: (first + i, 0))]
        + [table_spec(), table_spec()],
        out_specs=rows_at(place),
        out_shape=shaped(((QUERIES + 2) * per * HEAD, LEN), BF16),
        scratch_shapes=[
            pltpu.VMEM((LEN // WIDE, 2 * WIDE, WIDE), F32),
            pltpu.VMEM((LEN, HEAD), BF16),
            pltpu.VMEM((LEN, HEAD), BF16),
            pltpu.VMEM((LEN, HEAD), F32),
            pltpu.VMEM((LEN, HEAD), F32),
        ],
        compiler_params=pltpu.CompilerParams(vmem_limit_bytes=48 << 20),
        cost_estimate=estimate(15),
        name="attend_back",
    )(pieces, q_in, k_in, v_in, do_in, lse, cosine, sine)


def split_lanes(values, experts):
    lanes = lax.broadcasted_iota(jnp.int32, values.shape, 1)
    high = values.astype(BF16).astype(F32)
    return jnp.where(lanes < experts, high, jnp.where(lanes < 2 * experts, values - high, 0.0)).astype(BF16)


def join_lanes(parts, experts):
    return parts + pltpu.roll(parts, LANES - experts, 1)


def route_kernel(experts, tokens, attn, w_out, gain, w_router, routes, residual, rows, gate):
    values = tokens[...].astype(F32) + dot(attn[...], w_out[...], TN)
    residual[...] = values
    normed = (values * rms_scale(values) * gain[...]).astype(BF16)
    logits = dot(normed, w_router[...], NN)
    lanes = lax.broadcasted_iota(jnp.int32, logits.shape, 1)
    expert = lax.rem(lanes, experts)
    chosen = lanes < 0
    for k in range(routes.shape[1]):
        chosen = chosen | (routes[:, k : k + 1] == expert)
    chosen = chosen & (lanes < 2 * experts)
    logits = jnp.where(chosen, logits, masked_score)
    weights = jnp.exp(logits - jnp.max(logits, axis=1, keepdims=True))
    share = weights / (0.5 * jnp.sum(weights, axis=1, keepdims=True))
    gate[...] = share
    rows[:, :D] = normed
    rows[:, D:] = split_lanes(share, experts)


def route_call(experts, tokens, attn, w_out, gain, w_router, routes):
    rows = lambda cols: pl.BlockSpec((TILE, cols), lambda i: (i, 0))
    whole = lambda *shape: pl.BlockSpec(shape, lambda i: (0, 0), pipeline_mode=pl.Buffered(1))
    return pl.pallas_call(
        functools.partial(route_kernel, experts),
        grid=(LEN // TILE,),
        in_specs=[rows(D), pl.BlockSpec((D, TILE), lambda i: (0, i)), whole(D, D), whole(1, D), whole(D, LANES)]
        + [rows(routes.shape[1])],
        out_specs=[rows(D), rows(WIDTH), rows(LANES)],
        out_shape=[shaped((LEN, D), F32), shaped((LEN, WIDTH), BF16), shaped((LEN, LANES), F32)],
        compiler_params=pltpu.CompilerParams(vmem_limit_bytes=40 << 20),
        cost_estimate=estimate(5),
        name="route",
    )(tokens, attn, w_out, gain, w_router, routes)


def merge_kernel(experts, kept, kept_share, landed, out):
    out[:, :D] = (kept[...] + landed[:, :D].astype(F32)).astype(BF16)
    if kept_share is not None:
        share = kept_share[...] + join_lanes(landed[:, D:].astype(F32), experts)
        share = jnp.where(lax.broadcasted_iota(jnp.int32, share.shape, 1) < experts, share, 0.0)
        out[:, D:] = split_lanes(share + pltpu.roll(share, experts, 1), experts)


def merge_call(experts, kept, kept_share, landed):
    rows = lambda cols: pl.BlockSpec((TILE, cols), lambda i: (i, 0))
    width = landed.shape[1]
    kernel = functools.partial(merge_kernel, experts)
    if kept_share is None:
        kernel = lambda kept, landed, out: merge_kernel(experts, kept, None, landed, out)
    return pl.pallas_call(
        kernel,
        grid=(LEN // TILE,),
        in_specs=[rows(D)] + ([] if kept_share is None else [rows(LANES)]) + [rows(width)],
        out_specs=rows(width),
        out_shape=shaped((LEN, width), BF16),
        compiler_params=pltpu.CompilerParams(vmem_limit_bytes=32 << 20),
        cost_estimate=estimate(3),
        name="merge",
    )(*[ref for ref in (kept, kept_share, landed) if ref is not None])


def back_kernel(
    experts, kept, kept_share, core, chip, residual, cotangent, gate, gain, w_router, w_out, d_res, d_mix, d_attn, d_gain, d_router
):
    @pl.when(pl.program_id(0) == 0)
    def _():
        d_gain[...] = jnp.zeros_like(d_gain)
        d_router[...] = jnp.zeros_like(d_router)

    landed = core[:, D:].astype(F32) + chip[:, D:].astype(F32)
    share = kept_share[...] + join_lanes(landed, experts)
    first = lax.broadcasted_iota(jnp.int32, share.shape, 1) < experts
    gates = jnp.where(first, gate[...], 0.0)
    inner = jnp.sum(gates * share, axis=1, keepdims=True)
    d_logits = jnp.where(first, gates * (share - inner), 0.0).astype(BF16)
    d_normed = kept[...] + core[:, :D].astype(F32) + chip[:, :D].astype(F32) + dot(d_logits, w_router[...], NT)
    values, gains = residual[...], gain[...]
    scale = rms_scale(values)
    norm = values * scale
    d_gain[0:1] += jnp.sum(d_normed * norm, axis=0, keepdims=True)
    scaled = d_normed * gains
    d_values = cotangent[...].astype(F32) + scale * (scaled - norm * jnp.mean(scaled * norm, axis=1, keepdims=True))
    d_res[...] = d_values
    mixed = d_values.astype(BF16)
    d_mix[...] = mixed
    d_attn[...] = dot(w_out[...], mixed, NT).astype(BF16)
    d_router[...] += dot(d_logits, (norm * gains).astype(BF16), TN)


def back_call(experts, kept, kept_share, core, chip, residual, cotangent, gate, gain, w_router, w_out):
    rows = lambda cols: pl.BlockSpec((TILE, cols), lambda i: (i, 0))
    whole = lambda *shape: pl.BlockSpec(shape, lambda i: (0, 0), pipeline_mode=pl.Buffered(1))
    return pl.pallas_call(
        functools.partial(back_kernel, experts),
        grid=(LEN // TILE,),
        in_specs=[rows(D), rows(LANES), rows(WIDTH), rows(WIDTH), rows(D), rows(D), rows(LANES)]
        + [whole(1, D), whole(D, LANES), whole(D, D)],
        out_specs=[rows(D), rows(D), pl.BlockSpec((D, TILE), lambda i: (0, i)), whole(8, D), whole(LANES, D)],
        out_shape=[
            shaped((LEN, D), F32),
            shaped((LEN, D), BF16),
            shaped((D, LEN), BF16),
            shaped((8, D), F32),
            shaped((LANES, D), F32),
        ],
        compiler_params=pltpu.CompilerParams(vmem_limit_bytes=48 << 20),
        cost_estimate=estimate(8),
        name="back",
    )(kept, kept_share, core, chip, residual, cotangent, gate, gain, w_router, w_out)


def expert_kernel(count, experts, fresh, first, last_tokens, steps, ids, *rest):
    rest = list(rest)

    def take(number):
        taken = rest[:number]
        del rest[:number]
        return taken

    n2, up = take(2), take(2)
    w_in = [take(2) for _ in range(count)]
    sums_in = [[] if new else take(2) for new in fresh]
    carry_in = [] if first else take(3)
    outs = take(5) if last_tokens else take(3)
    sums_out = [take(2) for _ in range(count)]
    weights, sums = take(1)[0], take(1)[0]
    low = None if all(fresh) else take(1)[0]
    sem = rest[0]
    half = weights.shape[1] // 6
    width = 2 * half
    step = pl.program_id(0)
    ahead = step < steps // 2

    def pieces_of(parts, whole):
        return [
            (ref.at[pl.ds(kind * half, half)], whole.at[pl.ds((2 * kind + part) * half, half)])
            for kind in range(3)
            for part, ref in enumerate(parts)
        ]

    def copies_of(pairs, lane):
        return [pltpu.make_async_copy(a, b, sem.at[lane, n]) for n, (a, b) in enumerate(pairs)]

    loads = [copies_of(pieces_of(w_in[e], weights.at[e]), e) for e in range(count)]
    sum_loads = [copies_of(pieces_of(sums_in[e], sums.at[e]), count + e) for e in range(count) if not fresh[e]]

    @pl.when(step == 0)
    def _():
        for copy in sum(loads + sum_loads, []):
            copy.start()
        for e in range(count):
            if fresh[e]:
                sums[e] = jnp.zeros(sums.shape[1:], F32)
        for copy in sum(loads + sum_loads, []):
            copy.wait()

    rows = jnp.where(ahead, n2[0][...], n2[1][...])
    grads = jnp.where(ahead, up[0][...], up[1][...])
    rows, gates = rows[:, :D], rows[:, D:].astype(F32)
    lanes = lax.broadcasted_iota(jnp.int32, gates.shape, 1)
    mixed = d_rows = d_shares = None
    add = lambda total, value: value if total is None else total + value
    for e in range(count):
        w_both, w_down = weights.at[e, : 2 * width], weights.at[e, 2 * width :]
        hit = (lanes == ids[e]) | (lanes == ids[e] + experts)
        share = jnp.sum(jnp.where(hit, gates, 0.0), axis=1, keepdims=True)
        acts = dot(rows, w_both[...], NT)
        gate_act, up_act = acts[:, :width], acts[:, width:]
        d_plain = dot(grads, w_down[...], NT)
        sigmoid = 1.0 / (1.0 + jnp.exp(-gate_act))
        silu = gate_act * sigmoid
        hidden = silu * up_act
        shared = (share * hidden).astype(BF16)
        d_share = jnp.sum(hidden * d_plain, axis=1, keepdims=True)
        d_hidden = share * d_plain
        d_gate = (d_hidden * up_act * (sigmoid + silu * (1.0 - sigmoid))).astype(BF16)
        d_up = (d_hidden * silu).astype(BF16)
        d_both = jnp.concatenate([d_gate, d_up], axis=1)
        mixed = add(mixed, dot(shared, w_down[...], NN))
        d_rows = add(d_rows, dot(d_both, w_both[...], NN))
        d_shares = add(d_shares, jnp.where(hit, d_share, 0.0))
        sums[e, : 2 * width] += dot(d_both, rows, TN)
        sums[e, 2 * width :] += dot(shared, grads, TN)
    results = [mixed, d_rows, d_shares]
    if not first:
        results = [result + ref[...] for result, ref in zip(results, carry_in)]
    if last_tokens:

        @pl.when(ahead)
        def _():
            for ref, result in zip(outs[:3], results):
                ref[...] = result

        @pl.when(jnp.logical_not(ahead))
        def _():
            outs[3][...] = results[0].astype(BF16)
            outs[4][:, :D] = results[1].astype(BF16)
            outs[4][:, D:] = split_lanes(results[2], experts)
    else:
        for ref, result in zip(outs, results):
            ref[...] = result

    @pl.when(step == steps - 1)
    def _():
        stores = []
        for e in range(count):
            pairs = [(b, a) for a, b in pieces_of(sums_out[e], sums.at[e])]
            if not fresh[e]:
                for kind in range(3):
                    low[e, pl.ds(kind * half, half)] = sums[e, pl.ds((2 * kind + 1) * half, half)].astype(BF16)
                pairs = pairs[::2] + [(low.at[e], sums_out[e][1])]
            stores += copies_of(pairs, e)
        for copy in stores:
            copy.start()
        for copy in stores:
            copy.wait()


def expert_call(ids, experts, n2, up, weights, sums, carry, last_tokens):
    tokens, height, count = 2 * n2[0].shape[0], weights[0][0].shape[0], len(weights)
    steps = tokens // TILE
    rows = lambda cols: pl.BlockSpec((TILE, cols), lambda i: (i, 0))
    near = lambda cols: pl.BlockSpec((TILE, cols), lambda i: (jnp.minimum(i, steps // 2 - 1), 0))
    far = lambda cols: pl.BlockSpec((TILE, cols), lambda i: (jnp.maximum(i - steps // 2, 0), 0))
    ins = [ids, *n2, *up] + [w for pair in weights for w in pair]
    specs = [SMEM, near(WIDTH), far(WIDTH), near(D), far(D)] + [ANY] * (2 * count)
    fresh, first = [pair is None for pair in sums], carry is None
    columns = (D, D, LANES)
    if last_tokens:
        outs = [shaped((tokens // 2, c), F32) for c in columns]
        outs += [shaped((tokens // 2, c), BF16) for c in (D, WIDTH)]
        out_specs = [near(c) for c in columns] + [far(D), far(WIDTH)]
    else:
        outs = [shaped((tokens, c), F32) for c in columns]
        out_specs = [rows(c) for c in columns]
    aliases = {}
    for pair in sums:
        if pair is not None:
            ins += pair
            specs += [ANY, ANY]
    if not first:
        if not last_tokens:
            aliases.update({len(ins) + k: k for k in range(3)})
        ins += carry
        specs += [rows(c) for c in columns]
    tokens_out = len(outs)
    for new in fresh:
        outs += [shaped((height, D), F32), shaped((height, D), F32 if new else BF16)]
        out_specs += [ANY, ANY]
    scratch = [pltpu.VMEM((count, 2 * height, D), BF16), pltpu.VMEM((count, 2 * height, D), F32)]
    if not all(fresh):
        scratch.append(pltpu.VMEM((count, height, D), BF16))
    scratch.append(pltpu.SemaphoreType.DMA((2 * count, 6)))
    done = pl.pallas_call(
        functools.partial(expert_kernel, count, experts, fresh, first, last_tokens, steps),
        grid=(steps,),
        in_specs=specs,
        out_specs=out_specs,
        out_shape=outs,
        scratch_shapes=scratch,
        input_output_aliases=aliases,
        compiler_params=pltpu.CompilerParams(vmem_limit_bytes=60 << 20),
        cost_estimate=estimate(15 * count),
        name="expert",
    )(*ins)
    return list(done[:tokens_out]), [tuple(done[tokens_out + 2 * e : tokens_out + 2 * e + 2]) for e in range(count)]


def join_kernel(side, held, landed, gate, up, down):
    here = pl.program_id(0) == 0
    rows = jnp.where(here, held[...], landed[...]).astype(F32)
    half = down.shape[0]
    gate[...] = rows[:half].T
    up[...] = rows[half : 2 * half].T
    down[...] = rows[2 * half :]


def join_call(side, held, landed):
    half = held.shape[0] // 3
    whole = pl.BlockSpec(held.shape, lambda i, side: (0, 0))
    columns = pl.BlockSpec((D, half), lambda i, side: (0, lax.rem(side[0] + i, 2)))
    return pl.pallas_call(
        join_kernel,
        grid_spec=pltpu.PrefetchScalarGridSpec(
            num_scalar_prefetch=1,
            grid=(2,),
            in_specs=[whole, whole],
            out_specs=[columns, columns, pl.BlockSpec((half, D), lambda i, side: (lax.rem(side[0] + i, 2), 0))],
        ),
        out_shape=[shaped((D, 2 * half), F32), shaped((D, 2 * half), F32), shaped((2 * half, D), F32)],
        compiler_params=pltpu.CompilerParams(vmem_limit_bytes=48 << 20),
        cost_estimate=estimate(5),
        name="join",
    )(side, held, landed)


def after(values, *others):
    return lax.optimization_barrier((values, *others))[0]


class Task:
    def __init__(self, steps):
        self.steps, self.result, self.over = steps, None, False

    def step(self):
        if self.over:
            return []
        try:
            return [next(self.steps)]
        except StopIteration as stop:
            self.result, self.over = stop.value, True
            return [self.result]

    def finish(self):
        while not self.over:
            self.step()
        return self.result


def local(
    tokens,
    routes,
    pieces,
    attn_gain,
    w_query,
    w_key,
    w_value,
    w_out,
    ffn_gain,
    w_router,
    expert_gate,
    expert_up,
    expert_down,
    cotangent,
):
    shards, reps = lax.axis_size("ep"), lax.axis_size("rep")
    experts = w_router.shape[1]
    slots = shards // GROUP
    place = lax.axis_index("ep")
    side = lax.axis_index("rep") % 2

    def swap(values, bits):
        return lax.ppermute(values, "ep", [(i, i ^ bits) for i in range(shards)])

    def swap_rep(values, bits=1):
        return lax.ppermute(values, "rep", [(i, i ^ bits) for i in range(reps)])


    def reduce_reps(values, bits=1):
        while bits < reps:
            values = values.astype(BF16)
            landed = swap_rep(values, bits)
            yield values
            values = values.astype(F32) + landed.astype(F32)
            bits *= 2
        return values

    def reduce_rows(values):
        values = values.reshape(shards, -1, values.shape[1])
        bits = 1
        while bits < shards:
            values = values.reshape(values.shape[0] // 2, 2, *values.shape[1:])
            bit = (place // bits) % 2
            kept, sent = [
                lax.dynamic_index_in_dim(values, index, axis=1, keepdims=False) for index in (bit, 1 - bit)
            ]
            landed = swap(sent, bits)
            yield sent
            values = (kept.astype(F32) + landed.astype(F32)).astype(BF16)
            bits *= 2
        return (yield from reduce_reps(values[0]))

    def sum_steps(slot, own, other):
        landed = swap_rep(other)
        yield other
        own = own + landed.astype(F32)
        if slot == 0:
            return own
        own = own.astype(BF16)
        landed = swap(own, slot * GROUP)
        yield own
        return landed

    with jax.named_scope("weights_out"):
        half = expert_gate.shape[2] // 2
        whole = [expert_gate[0].T, expert_up[0].T, expert_down[0]]
        halves = [jnp.concatenate([w[k * half : (k + 1) * half] for w in whole]) for k in range(2)]
        mine = jnp.where(side == 0, halves[0], halves[1])
        theirs = jnp.where(side == 0, halves[1], halves[0])
        tokens, mine, theirs = lax.optimization_barrier((tokens, mine, theirs))
        landed = {slot: swap(mine, slot * GROUP) for slot in range(2, min(3, slots))}

    with jax.named_scope("cotangent_out"):
        grads_next = swap(cotangent, 2)
        grads_in = [(cotangent, swap(cotangent, 1)), None]

    with jax.named_scope("attention"):
        inputs = tokens.astype(F32)
        scale_one = rms_scale(inputs)
        norm_one = inputs * scale_one
        normed_one = (norm_one * attn_gain).astype(BF16)
        cuts, first = [], 0
        for per in PARTS:
            for w, wide in ((w_query, QUERIES), (w_key, 1), (w_value, 1)):
                cuts.append(w[:, first * wide * HEAD : (first + per) * wide * HEAD])
            first += per
        w_all = jnp.concatenate(cuts, axis=1)
        packed = dot(w_all, normed_one, (((0,), (1,)), ((), ())))
        cosine, sine = [jnp.asarray(table) for table in rotary_tables()]
        attn, query_rot, key_rot, value_low, lse = attend_call(pieces, packed, cosine, sine)
        attn = after(attn, grads_next, grads_in[0][1])

    with jax.named_scope("cotangent_out"):
        grads_in[1] = (grads_next, swap(grads_next, 1))

    with jax.named_scope("routing"):
        pad = jnp.zeros((D, LANES - 2 * experts), BF16)
        router_twice = jnp.concatenate([w_router, w_router, pad], axis=1)
        gain_two = ffn_gain.reshape(1, D)
        residual, rows, gate = route_call(experts, tokens, attn, w_out, gain_two, router_twice, routes)
        rows = after(rows, grads_in[1][1], *landed.values())
        rows_next = swap(rows, 2)
        rows_in = [(rows, swap(rows, 1)), None]

    with jax.named_scope("weights_out"):
        weights = {0: (mine, theirs)}
        weights.update({slot: (held, swap_rep(held)) for slot, held in landed.items()})
        late = after(mine, rows)
        coming = [slot for slot in [*range(3, slots), 1] if slot < slots]
        landed = {slot: swap(late, slot * GROUP) for slot in coming}
        ids = [((place // GROUP) ^ slot) * GROUP + place % GROUP for slot in range(slots)]
        ids = [expert.astype(jnp.int32) for expert in ids]

    carry, sums, clock = [None, None], [None] * slots, None
    tasks = [None] * slots

    def run(chip, group, last=False):
        nonlocal clock
        called = jnp.stack([ids[slot] for slot in group])
        if clock is not None:
            called = after(called, clock)
        carry[chip], done = expert_call(
            called,
            experts,
            rows_in[chip],
            grads_in[chip],
            [weights[slot] for slot in group],
            [sums[slot] for slot in group],
            carry[chip],
            last,
        )
        clock = carry[chip][2]
        for slot, pair in zip(group, done):
            if sums[slot] is not None:
                tasks[slot] = Task(sum_steps(slot, *pair))
            sums[slot] = pair

    def tick(*arrays):
        nonlocal clock
        clock = after(clock, *arrays)

    def arrive(slot):
        tick(landed[slot])
        weights[slot] = (landed[slot], swap_rep(landed[slot]))

    with jax.named_scope("experts"):
        run(0, [0])
        tick(rows_next)
        rows_in[1] = (rows_next, swap(rows_next, 1))
        run(1, [0])
        if slots > 3:
            arrive(3)
        run(1, [2])
        for slot in [*range(4, slots), 1]:
            arrive(slot)
        run(0, [2])
        tasks[2].step()
        pairs = [[slot, slot + 1] for slot in range(3, slots - 1, 2)] + [[slots - 1, 1]]
        for pair in pairs:
            last = pair == pairs[-1]
            run(1, pair, last)
            if last:
                there = merge_call(experts, carry[1][1], carry[1][2], swap(carry[1][4], 1))
                d_next = swap(there, 2)
                tick(there, *tasks[2].step())
                tasks[0].step()
                mix_landed = swap(after(carry[1][3], there), 1)
            run(0, pair[:1])
            tasks[pair[0]].step()
            if last:
                mix_there = merge_call(experts, carry[1][0], None, mix_landed)
                tick(mix_there, *tasks[0].step())
            run(0, pair[1:], last)
            tasks[pair[1]].step()

    with jax.named_scope("routing_back"):
        d_core = swap(carry[0][4], 1)
        d_residual, d_mixed, d_attn, d_ffn_gain, d_router = back_call(
            experts, carry[0][1], carry[0][2], d_core, d_next, residual, cotangent, gate, gain_two, router_twice, w_out
        )

    with jax.named_scope("combine"):
        mix_home = swap(after(mix_there, d_attn), 2)
        mix_core = swap(after(carry[0][3], d_attn), 1)

    with jax.named_scope("sums_out"):
        d_out = dot(attn, d_mixed, NN).astype(BF16)
        small = jnp.concatenate([d_router[:experts], d_ffn_gain[:1]]).T
        sum_out, sum_small = [lax.psum_scatter(v, "ep", scatter_dimension=0, tiled=True) for v in (d_out, small)]

    with jax.named_scope("attention_back"):
        in_dims = (((0,), (1,)), ((), ()))
        d_attn = after(d_attn, d_out, *[array for task in tasks[2:] for array in task.step()])
        d_packed, w_tasks = [], []
        for part in range(len(PARTS)):
            d_packed.append(
                attend_back_call(part, pieces, query_rot, key_rot, value_low, d_attn, lse, cosine, sine)
            )
            pins = [array for task in w_tasks for array in task.step()]
            if part == 0:
                pins += tasks[1].step() + [mix_home, mix_core]
            w_tasks.append(Task(reduce_rows(dot(normed_one, d_packed[-1], in_dims).astype(BF16))))
            pins += w_tasks[-1].step()
            if part < len(PARTS) - 1:
                d_attn = after(d_attn, d_packed[-1], *pins)
        out_tasks = [Task(reduce_reps(sum_out)), Task(reduce_reps(sum_small))]
        d_normed_one, first = None, 0
        for part, grads in enumerate(d_packed):
            span = grads.shape[0]
            term = dot(grads, w_all[:, first : first + span], in_dims)
            d_normed_one = term if part == 0 else d_normed_one + term
            first += span
            pins = [array for task in w_tasks + (out_tasks if part == 1 else []) for array in task.step()]
            d_normed_one = after(d_normed_one, *pins)
        scaled_one = d_normed_one * attn_gain
        d_tokens = d_residual + scale_one * (
            scaled_one - norm_one * jnp.mean(scaled_one * norm_one, axis=-1, keepdims=True)
        )

    with jax.named_scope("combine"):
        output = (residual + carry[0][0] + mix_core.astype(F32) + mix_home.astype(F32)).astype(BF16)

    with jax.named_scope("sums_experts"):
        total = tasks[0].finish()
        for task in tasks[1:]:
            total = total + task.finish().astype(F32)
        total = Task(reduce_reps(total, 2)).finish().astype(BF16)
        s_gate, s_up, s_down = join_call(side.astype(jnp.int32).reshape(1), total, swap_rep(total))

    with jax.named_scope("sums_rest"):
        s_out, s_small = [task.finish() for task in out_tasks]
        count = s_out.shape[0]
        first = place * count
        s_parts = [task.finish() for task in w_tasks]
        w_rows = lax.dynamic_slice_in_dim(w_all, first, count)
        s_attn = jnp.sum(jnp.concatenate(s_parts, axis=1) * w_rows.astype(F32), axis=1)
        s_attn = s_attn / lax.dynamic_slice_in_dim(attn_gain, first, count)
        columns = [[], [], []]
        for per, part in zip(PARTS, s_parts):
            for group, column in zip(columns, jnp.split(part, [QUERIES * per * HEAD, (QUERIES + 1) * per * HEAD], axis=1)):
                group.append(column)
        s_query, s_key, s_value = [jnp.concatenate(group, axis=1) for group in columns]

    return (
        output,
        d_tokens,
        s_attn,
        s_query,
        s_key,
        s_value,
        s_out.astype(F32),
        s_small[:, experts].astype(F32),
        s_small[:, :experts].astype(F32),
        s_gate[None],
        s_up[None],
        s_down[None],
    )


def solution(mesh):
    rows, whole, slices = P(("rep", "ep"), None), P(), P("ep", None)
    expert = P("ep", None, None)
    return jax.shard_map(
        local,
        mesh=mesh,
        in_specs=(rows,) * 3 + (whole,) * 7 + (expert,) * 3 + (rows,),
        out_specs=(rows, rows, P("ep")) + (slices,) * 4 + (P("ep"), slices) + (expert,) * 3,
        check_vma=False,
    )
```

```python
import functools
import math

import jax
import jax.numpy as jnp
import numpy as np
from jax import lax
from jax.experimental import pallas as pl
from jax.experimental.pallas import tpu as pltpu
from jax.sharding import PartitionSpec as P

D = 1536
HEADS = 24
KV = 8
HEAD = 64
LEN = 1024
PIECE = 256
QUERIES = HEADS // KV
WIDE = 256
TILE = 256
GROUP = 4
PARTS = (2, 4, 2)
LANES = 128
WIDTH = D + LANES

eps = 1e-06
theta_base = 10000.0
masked_score = -1e30
score_scale = HEAD ** (-0.5)
two_scale = score_scale * math.log2(math.e)

F32 = jnp.float32
BF16 = jnp.bfloat16
NN = (((1,), (0,)), ((), ()))
NT = (((1,), (1,)), ((), ()))
TN = (((0,), (0,)), ((), ()))
ANY = pl.BlockSpec(memory_space=pl.ANY)
SMEM = pl.BlockSpec(memory_space=pltpu.SMEM)


def dot(left, right, dims):
    return lax.dot_general(left, right, dims, preferred_element_type=F32)


def shaped(shape, dtype):
    return jax.ShapeDtypeStruct(shape, dtype)


def estimate(micros):
    return pl.CostEstimate(flops=int(micros * 1e10), bytes_accessed=int(micros * 1e6), transcendentals=0)


def rms_scale(values):
    return lax.rsqrt(jnp.mean(values * values, axis=-1, keepdims=True) + eps)


def rotary_tables():
    half_head = HEAD // 2
    frequency = theta_base ** (-(np.arange(half_head, dtype=np.float64) * 2.0) / HEAD)
    angles = frequency[:, None] * np.arange(LEN, dtype=np.float64)[None, :]
    return np.cos(angles).astype(np.float32), np.sin(angles).astype(np.float32)


def turn(values, cosine, sine):
    first, second = values[: HEAD // 2], values[HEAD // 2 :]
    return jnp.concatenate([first * cosine - second * sine, second * cosine + first * sine], axis=0)


def turn_back(grads, cosine, sine):
    first, second = grads[: HEAD // 2], grads[HEAD // 2 :]
    return jnp.concatenate([first * cosine + second * sine, second * cosine - first * sine], axis=0)


def fill_bias(pieces, bias):
    for block in range(LEN // WIDE):
        first = block * WIDE
        shape = bias.shape[1:]
        key = lax.broadcasted_iota(jnp.int32, shape, 0) + first
        query = lax.broadcasted_iota(jnp.int32, shape, 1) + first
        allowed = key <= query
        for piece in range(pieces.shape[1]):
            start = pieces[0, piece]
            low, high = jnp.minimum(key, query), jnp.maximum(key, query)
            allowed = allowed | ((low >= start) & (high < start + PIECE))
        bias[block] = jnp.where(allowed, 0.0, masked_score)


def key_span(block):
    return block * WIDE, min((block + 2) * WIDE, LEN)


def masked_scores(keys, queries, bias, block):
    first, last = key_span(block)
    scores = dot(keys[:last], queries, NN)
    masked = scores[first:] + bias[block, : last - first]
    return masked if first == 0 else jnp.concatenate([scores[:first], masked], axis=0)


def rows_at(place):
    return pl.BlockSpec((HEAD, LEN), lambda *grid: (place(*grid), 0))


def packed_row(head, kind):
    row = 0
    for part, per in enumerate(PARTS):
        first = sum(PARTS[:part])
        inner = head - first
        here = {3: QUERIES * per + inner, 4: (QUERIES + 1) * per + inner}.get(kind, QUERIES * inner + kind)
        row = jnp.where(inner >= 0, (QUERIES + 2) * first + here, row)
    return row


def table_spec():
    return pl.BlockSpec((HEAD // 2, LEN), lambda *grid: (0, 0))


def attend_kernel(pieces, q0, q1, q2, k_in, v_in, cosine, sine, attn, q_out, k_out, v_out, lse, bias):
    @pl.when(pl.program_id(0) == 0)
    def _():
        fill_bias(pieces, bias)

    cos, sin = cosine[...], sine[...]
    k_rot = turn(k_in[...], cos, sin)
    k_out[...] = k_rot.astype(BF16)
    keys = k_rot.T.astype(BF16)
    values = v_in[...].astype(BF16)
    v_out[...] = values
    for head, q_in in enumerate((q0, q1, q2)):
        rows = pl.ds(head * HEAD, HEAD)
        q_rot = turn(q_in[...], cos, sin).astype(BF16)
        q_out[rows, :] = q_rot
        for block in range(LEN // WIDE):
            columns = pl.ds(block * WIDE, WIDE)
            last = key_span(block)[1]
            scores = masked_scores(keys, q_rot[:, block * WIDE : (block + 1) * WIDE], bias, block)
            highest = jnp.max(scores, axis=0, keepdims=True) * two_scale
            weights = jnp.exp2(scores * two_scale - highest)
            total = jnp.sum(weights, axis=0, keepdims=True)
            mixed = dot(values[:, :last], weights.astype(BF16), NN) / total
            attn[rows, columns] = mixed.astype(BF16)
            lse[head : head + 1, columns] = highest + jnp.log2(total)


def attend_call(pieces, packed, cosine, sine):
    rows = lambda count: pl.BlockSpec((count, LEN), lambda i: (i, 0))
    width = QUERIES * HEAD
    return pl.pallas_call(
        attend_kernel,
        grid=(KV,),
        in_specs=[SMEM]
        + [rows_at(functools.partial(packed_row, kind=kind)) for kind in range(5)]
        + [table_spec(), table_spec()],
        out_specs=[rows(width), rows(width), rows(HEAD), rows(HEAD), rows(8)],
        out_shape=[
            shaped((D, LEN), BF16),
            shaped((D, LEN), BF16),
            shaped((KV * HEAD, LEN), BF16),
            shaped((KV * HEAD, LEN), BF16),
            shaped((KV * 8, LEN), F32),
        ],
        scratch_shapes=[pltpu.VMEM((LEN // WIDE, 2 * WIDE, WIDE), F32)],
        compiler_params=pltpu.CompilerParams(vmem_limit_bytes=48 << 20),
        cost_estimate=estimate(25),
        name="attend",
    )(pieces, *[packed] * 5, cosine, sine)


def attend_back_kernel(
    mark, pieces, q_in, k_in, v_in, do_in, lse, cosine, sine, out, bias, keys_kept, values_kept, dk_sum, dv_sum
):
    kind = pl.program_id(1)

    @pl.when((pl.program_id(0) == 0) & (kind == 0))
    def _():
        fill_bias(pieces, bias)

    cos, sin = cosine[...], sine[...]

    @pl.when(kind == 0)
    def _():
        keys_kept[...] = k_in[...].astype(F32).T.astype(BF16)
        values_kept[...] = v_in[...].astype(F32).T.astype(BF16)
        dk_sum[...] = jnp.zeros_like(dk_sum)
        dv_sum[...] = jnp.zeros_like(dv_sum)

    @pl.when(kind < QUERIES)
    def _():
        k_cols, keys, values = k_in[...], keys_kept[...], values_kept[...]
        q_cols, do_cols = q_in[...], do_in[...]
        q_rows = q_cols.astype(F32).T.astype(BF16)
        do_rows = do_cols.astype(F32).T.astype(BF16)
        row_lse = lse[pl.ds(kind, 1), :]
        for block in range(LEN // WIDE):
            part = slice(block * WIDE, (block + 1) * WIDE)
            last = key_span(block)[1]
            scores = masked_scores(keys, q_cols[:, part], bias, block)
            probs = jnp.exp2(scores * two_scale - row_lse[:, part])
            d_probs = dot(values[:last], do_cols[:, part], NN)
            product = probs * d_probs
            delta = jnp.sum(product, axis=0, keepdims=True)
            d_scores = (product - probs * delta).astype(BF16)
            dv_sum[:last] += dot(probs.astype(BF16), do_rows[part], NN)
            dk_sum[:last] += dot(d_scores, q_rows[part], NN)
            d_query = dot(k_cols[:, :last], d_scores, NN) * score_scale
            out[:, part] = turn_back(d_query, cos[:, part], sin[:, part]).astype(BF16)

    @pl.when(kind == QUERIES)
    def _():
        out[...] = turn_back(dk_sum[...].T * score_scale, cos, sin).astype(BF16)

    @pl.when(kind == QUERIES + 1)
    def _():
        out[...] = dv_sum[...].T.astype(BF16)


def attend_back_call(part, mark, pieces, q_in, k_in, v_in, do_in, lse, cosine, sine):
    per, first = PARTS[part], sum(PARTS[:part])
    query = rows_at(lambda i, j: (first + i) * QUERIES + jnp.minimum(j, QUERIES - 1))
    key = rows_at(lambda i, j: first + i)

    def place(i, j):
        tail = jnp.where(j == QUERIES, QUERIES * per + i, (QUERIES + 1) * per + i)
        return jnp.where(j < QUERIES, QUERIES * i + j, tail)

    return pl.pallas_call(
        attend_back_kernel,
        grid=(per, QUERIES + 2),
        in_specs=[ANY, SMEM, query, key, key, query, pl.BlockSpec((8, LEN), lambda i, j: (first + i, 0))]
        + [table_spec(), table_spec()],
        out_specs=rows_at(place),
        out_shape=shaped(((QUERIES + 2) * per * HEAD, LEN), BF16),
        scratch_shapes=[
            pltpu.VMEM((LEN // WIDE, 2 * WIDE, WIDE), F32),
            pltpu.VMEM((LEN, HEAD), BF16),
            pltpu.VMEM((LEN, HEAD), BF16),
            pltpu.VMEM((LEN, HEAD), F32),
            pltpu.VMEM((LEN, HEAD), F32),
        ],
        compiler_params=pltpu.CompilerParams(vmem_limit_bytes=48 << 20),
        cost_estimate=estimate(15),
        name="attend_back",
    )(mark, pieces, q_in, k_in, v_in, do_in, lse, cosine, sine)


def split_lanes(values, experts):
    lanes = lax.broadcasted_iota(jnp.int32, values.shape, 1)
    high = values.astype(BF16).astype(F32)
    return jnp.where(lanes < experts, high, jnp.where(lanes < 2 * experts, values - high, 0.0)).astype(BF16)


def join_lanes(parts, experts):
    return parts + pltpu.roll(parts, LANES - experts, 1)


def route_kernel(experts, tokens, attn, w_out, gain, w_router, routes, residual, rows, gate):
    values = tokens[...].astype(F32) + dot(attn[...], w_out[...], TN)
    residual[...] = values
    normed = (values * rms_scale(values) * gain[...]).astype(BF16)
    logits = dot(normed, w_router[...], NN)
    lanes = lax.broadcasted_iota(jnp.int32, logits.shape, 1)
    expert = lax.rem(lanes, experts)
    chosen = lanes < 0
    for k in range(routes.shape[1]):
        chosen = chosen | (routes[:, k : k + 1] == expert)
    chosen = chosen & (lanes < 2 * experts)
    logits = jnp.where(chosen, logits, masked_score)
    weights = jnp.exp(logits - jnp.max(logits, axis=1, keepdims=True))
    share = weights / (0.5 * jnp.sum(weights, axis=1, keepdims=True))
    gate[...] = share
    rows[:, :D] = normed
    rows[:, D:] = split_lanes(share, experts)


def route_call(experts, tokens, attn, w_out, gain, w_router, routes):
    rows = lambda cols: pl.BlockSpec((TILE, cols), lambda i: (i, 0))
    whole = lambda *shape: pl.BlockSpec(shape, lambda i: (0, 0), pipeline_mode=pl.Buffered(1))
    return pl.pallas_call(
        functools.partial(route_kernel, experts),
        grid=(LEN // TILE,),
        in_specs=[rows(D), pl.BlockSpec((D, TILE), lambda i: (0, i)), whole(D, D), whole(1, D), whole(D, LANES)]
        + [rows(routes.shape[1])],
        out_specs=[rows(D), rows(WIDTH), rows(LANES)],
        out_shape=[shaped((LEN, D), F32), shaped((LEN, WIDTH), BF16), shaped((LEN, LANES), F32)],
        compiler_params=pltpu.CompilerParams(vmem_limit_bytes=40 << 20),
        cost_estimate=estimate(5),
        name="route",
    )(tokens, attn, w_out, gain, w_router, routes)


def merge_kernel(experts, mark, kept, kept_share, landed, out):
    out[:, :D] = (kept[...] + landed[:, :D].astype(F32)).astype(BF16)
    if kept_share is not None:
        share = kept_share[...] + join_lanes(landed[:, D:].astype(F32), experts)
        share = jnp.where(lax.broadcasted_iota(jnp.int32, share.shape, 1) < experts, share, 0.0)
        out[:, D:] = split_lanes(share + pltpu.roll(share, experts, 1), experts)


def merge_call(experts, mark, kept, kept_share, landed):
    rows = lambda cols: pl.BlockSpec((TILE, cols), lambda i: (i, 0))
    width = landed.shape[1]
    kernel = functools.partial(merge_kernel, experts)
    if kept_share is None:
        kernel = lambda mark, kept, landed, out: merge_kernel(experts, mark, kept, None, landed, out)
    return pl.pallas_call(
        kernel,
        grid=(LEN // TILE,),
        in_specs=[ANY, rows(D)] + ([] if kept_share is None else [rows(LANES)]) + [rows(width)],
        out_specs=rows(width),
        out_shape=shaped((LEN, width), BF16),
        compiler_params=pltpu.CompilerParams(vmem_limit_bytes=32 << 20),
        cost_estimate=estimate(3),
        name="merge",
    )(*[ref for ref in (mark, kept, kept_share, landed) if ref is not None])


def back_kernel(
    experts, mark, kept, kept_share, core, chip, residual, cotangent, gate, gain, w_router, w_out, d_res, d_mix, d_attn, d_router
):
    @pl.when(pl.program_id(0) == 0)
    def _():
        d_router[...] = jnp.zeros_like(d_router)

    landed = core[:, D:].astype(F32) + chip[:, D:].astype(F32)
    share = kept_share[...] + join_lanes(landed, experts)
    first = lax.broadcasted_iota(jnp.int32, share.shape, 1) < experts
    gates = jnp.where(first, gate[...], 0.0)
    inner = jnp.sum(gates * share, axis=1, keepdims=True)
    d_logits = jnp.where(first, gates * (share - inner), 0.0).astype(BF16)
    d_normed = kept[...] + core[:, :D].astype(F32) + chip[:, :D].astype(F32) + dot(d_logits, w_router[...], NT)
    values, gains = residual[...], gain[...]
    scale = rms_scale(values)
    norm = values * scale
    d_gain = jnp.sum(d_normed * norm, axis=0, keepdims=True)
    scaled = d_normed * gains
    d_values = cotangent[...].astype(F32) + scale * (scaled - norm * jnp.mean(scaled * norm, axis=1, keepdims=True))
    d_res[...] = d_values
    mixed = d_values.astype(BF16)
    d_mix[...] = mixed
    d_attn[...] = dot(w_out[...], mixed, NT).astype(BF16)
    d_router[...] += dot(d_logits, (norm * gains).astype(BF16), TN)
    d_router[experts : experts + 1] += d_gain


def back_call(experts, mark, kept, kept_share, core, chip, residual, cotangent, gate, gain, w_router, w_out):
    rows = lambda cols: pl.BlockSpec((TILE, cols), lambda i: (i, 0))
    whole = lambda *shape: pl.BlockSpec(shape, lambda i: (0, 0), pipeline_mode=pl.Buffered(1))
    return pl.pallas_call(
        functools.partial(back_kernel, experts),
        grid=(LEN // TILE,),
        in_specs=[ANY, rows(D), rows(LANES), rows(WIDTH), rows(WIDTH), rows(D), rows(D), rows(LANES)]
        + [whole(1, D), whole(D, LANES), whole(D, D)],
        out_specs=[rows(D), rows(D), pl.BlockSpec((D, TILE), lambda i: (0, i)), whole(LANES, D)],
        out_shape=[
            shaped((LEN, D), F32),
            shaped((LEN, D), BF16),
            shaped((D, LEN), BF16),
            shaped((LANES, D), F32),
        ],
        compiler_params=pltpu.CompilerParams(vmem_limit_bytes=48 << 20),
        cost_estimate=estimate(8),
        name="back",
    )(mark, kept, kept_share, core, chip, residual, cotangent, gate, gain, w_router, w_out)


def out_kernel(mark, attn, mixed, small, out):
    out[:, :D] = dot(attn[...], mixed[...], NN).astype(BF16)
    out[:, D:] = small[...].T.astype(BF16)


def out_call(mark, attn, mixed, small):
    return pl.pallas_call(
        out_kernel,
        grid=(D // TILE,),
        in_specs=[
            ANY,
            pl.BlockSpec((TILE, LEN), lambda i: (i, 0)),
            pl.BlockSpec((LEN, D), lambda i: (0, 0), pipeline_mode=pl.Buffered(1)),
            pl.BlockSpec((LANES, TILE), lambda i: (0, i)),
        ],
        out_specs=pl.BlockSpec((TILE, WIDTH), lambda i: (i, 0)),
        out_shape=shaped((D, WIDTH), BF16),
        compiler_params=pltpu.CompilerParams(vmem_limit_bytes=32 << 20),
        cost_estimate=estimate(5),
        name="out_grad",
    )(mark, attn, mixed, small)


def pause_kernel(mark, out):
    out[...] = mark[...]


def pause_call(mark):
    return pl.pallas_call(
        pause_kernel, out_shape=shaped(mark.shape, mark.dtype), cost_estimate=estimate(10), name="pause"
    )(mark)


def expert_kernel(count, experts, fresh, first, last_tokens, steps, ids, mark, *rest):
    rest = list(rest)

    def take(number):
        taken = rest[:number]
        del rest[:number]
        return taken

    n2, up = take(2), take(2)
    w_in = [take(2) for _ in range(count)]
    sums_in = [[] if new else take(2) for new in fresh]
    carry_in = [] if first else take(3)
    outs = take(5) if last_tokens else take(3)
    sums_out = [take(2) for _ in range(count)]
    weights, sums = take(1)[0], take(1)[0]
    low = None if all(fresh) else take(1)[0]
    sem = rest[0]
    half = weights.shape[1] // 6
    width = 2 * half
    step = pl.program_id(0)
    ahead = step < steps // 2

    def pieces_of(parts, whole):
        return [
            (ref.at[pl.ds(kind * half, half)], whole.at[pl.ds((2 * kind + part) * half, half)])
            for kind in range(3)
            for part, ref in enumerate(parts)
        ]

    def copies_of(pairs, lane):
        return [pltpu.make_async_copy(a, b, sem.at[lane, n]) for n, (a, b) in enumerate(pairs)]

    loads = [copies_of(pieces_of(w_in[e], weights.at[e]), e) for e in range(count)]
    sum_loads = [copies_of(pieces_of(sums_in[e], sums.at[e]), count + e) for e in range(count) if not fresh[e]]

    @pl.when(step == 0)
    def _():
        for copy in sum(loads + sum_loads, []):
            copy.start()
        for e in range(count):
            if fresh[e]:
                sums[e] = jnp.zeros(sums.shape[1:], F32)
        for copy in sum(loads + sum_loads, []):
            copy.wait()

    rows = jnp.where(ahead, n2[0][...], n2[1][...])
    grads = jnp.where(ahead, up[0][...], up[1][...])
    rows, gates = rows[:, :D], rows[:, D:].astype(F32)
    lanes = lax.broadcasted_iota(jnp.int32, gates.shape, 1)
    mixed = d_rows = d_shares = None
    add = lambda total, value: value if total is None else total + value
    for e in range(count):
        w_both, w_down = weights.at[e, : 2 * width], weights.at[e, 2 * width :]
        hit = (lanes == ids[e]) | (lanes == ids[e] + experts)
        share = jnp.sum(jnp.where(hit, gates, 0.0), axis=1, keepdims=True)
        acts = dot(rows, w_both[...], NT)
        gate_act, up_act = acts[:, :width], acts[:, width:]
        d_plain = dot(grads, w_down[...], NT)
        sigmoid = 1.0 / (1.0 + jnp.exp(-gate_act))
        silu = gate_act * sigmoid
        hidden = silu * up_act
        shared = (share * hidden).astype(BF16)
        d_share = jnp.sum(hidden * d_plain, axis=1, keepdims=True)
        d_hidden = share * d_plain
        d_gate = (d_hidden * up_act * (sigmoid + silu * (1.0 - sigmoid))).astype(BF16)
        d_up = (d_hidden * silu).astype(BF16)
        d_both = jnp.concatenate([d_gate, d_up], axis=1)
        mixed = add(mixed, dot(shared, w_down[...], NN))
        d_rows = add(d_rows, dot(d_both, w_both[...], NN))
        d_shares = add(d_shares, jnp.where(hit, d_share, 0.0))
        sums[e, : 2 * width] += dot(d_both, rows, TN)
        sums[e, 2 * width :] += dot(shared, grads, TN)
    results = [mixed, d_rows, d_shares]
    if not first:
        results = [result + ref[...] for result, ref in zip(results, carry_in)]
    if last_tokens:

        @pl.when(ahead)
        def _():
            for ref, result in zip(outs[:3], results):
                ref[...] = result

        @pl.when(jnp.logical_not(ahead))
        def _():
            outs[3][...] = results[0].astype(BF16)
            outs[4][:, :D] = results[1].astype(BF16)
            outs[4][:, D:] = split_lanes(results[2], experts)
    else:
        for ref, result in zip(outs, results):
            ref[...] = result

    @pl.when(step == steps - 1)
    def _():
        stores = []
        for e in range(count):
            pairs = [(b, a) for a, b in pieces_of(sums_out[e], sums.at[e])]
            if not fresh[e]:
                for kind in range(3):
                    low[e, pl.ds(kind * half, half)] = sums[e, pl.ds((2 * kind + 1) * half, half)].astype(BF16)
                pairs = pairs[::2] + [(low.at[e], sums_out[e][1])]
            stores += copies_of(pairs, e)
        for copy in stores:
            copy.start()
        for copy in stores:
            copy.wait()


def expert_call(ids, mark, experts, n2, up, weights, sums, carry, last_tokens):
    tokens, height, count = 2 * n2[0].shape[0], weights[0][0].shape[0], len(weights)
    steps = tokens // TILE
    rows = lambda cols: pl.BlockSpec((TILE, cols), lambda i: (i, 0))
    near = lambda cols: pl.BlockSpec((TILE, cols), lambda i: (jnp.minimum(i, steps // 2 - 1), 0))
    far = lambda cols: pl.BlockSpec((TILE, cols), lambda i: (jnp.maximum(i - steps // 2, 0), 0))
    ins = [ids, mark, *n2, *up] + [w for pair in weights for w in pair]
    specs = [SMEM, ANY, near(WIDTH), far(WIDTH), near(D), far(D)] + [ANY] * (2 * count)
    fresh, first = [pair is None for pair in sums], carry is None
    columns = (D, D, LANES)
    if last_tokens:
        outs = [shaped((tokens // 2, c), F32) for c in columns]
        outs += [shaped((tokens // 2, c), BF16) for c in (D, WIDTH)]
        out_specs = [near(c) for c in columns] + [far(D), far(WIDTH)]
    else:
        outs = [shaped((tokens, c), F32) for c in columns]
        out_specs = [rows(c) for c in columns]
    aliases = {}
    for pair in sums:
        if pair is not None:
            ins += pair
            specs += [ANY, ANY]
    if not first:
        if not last_tokens:
            aliases.update({len(ins) + k: k for k in range(3)})
        ins += carry
        specs += [rows(c) for c in columns]
    tokens_out = len(outs)
    for new in fresh:
        outs += [shaped((height, D), F32), shaped((height, D), F32 if new else BF16)]
        out_specs += [ANY, ANY]
    scratch = [pltpu.VMEM((count, 2 * height, D), BF16), pltpu.VMEM((count, 2 * height, D), F32)]
    if not all(fresh):
        scratch.append(pltpu.VMEM((count, height, D), BF16))
    scratch.append(pltpu.SemaphoreType.DMA((2 * count, 6)))
    done = pl.pallas_call(
        functools.partial(expert_kernel, count, experts, fresh, first, last_tokens, steps),
        grid=(steps,),
        in_specs=specs,
        out_specs=out_specs,
        out_shape=outs,
        scratch_shapes=scratch,
        input_output_aliases=aliases,
        compiler_params=pltpu.CompilerParams(vmem_limit_bytes=60 << 20),
        cost_estimate=estimate(15 * count),
        name="expert",
    )(*ins)
    return list(done[:tokens_out]), [tuple(done[tokens_out + 2 * e : tokens_out + 2 * e + 2]) for e in range(count)]


def join_kernel(side, held, landed, gate, up, down):
    here = pl.program_id(0) == 0
    rows = jnp.where(here, held[...], landed[...]).astype(F32)
    half = down.shape[0]
    gate[...] = rows[:half].T
    up[...] = rows[half : 2 * half].T
    down[...] = rows[2 * half :]


def join_call(side, held, landed):
    half = held.shape[0] // 3
    whole = pl.BlockSpec(held.shape, lambda i, side: (0, 0))
    columns = pl.BlockSpec((D, half), lambda i, side: (0, lax.rem(side[0] + i, 2)))
    return pl.pallas_call(
        join_kernel,
        grid_spec=pltpu.PrefetchScalarGridSpec(
            num_scalar_prefetch=1,
            grid=(2,),
            in_specs=[whole, whole],
            out_specs=[columns, columns, pl.BlockSpec((half, D), lambda i, side: (lax.rem(side[0] + i, 2), 0))],
        ),
        out_shape=[shaped((D, 2 * half), F32), shaped((D, 2 * half), F32), shaped((2 * half, D), F32)],
        compiler_params=pltpu.CompilerParams(vmem_limit_bytes=48 << 20),
        cost_estimate=estimate(5),
        name="join",
    )(side, held, landed)


def after(values, *others):
    return lax.optimization_barrier((values, *others))[0]


class Task:
    def __init__(self, steps):
        self.steps, self.result, self.over = steps, None, False

    def step(self):
        if self.over:
            return []
        try:
            return [next(self.steps)]
        except StopIteration as stop:
            self.result, self.over = stop.value, True
            return [self.result]

    def finish(self):
        while not self.over:
            self.step()
        return self.result


def local(
    tokens,
    routes,
    pieces,
    attn_gain,
    w_query,
    w_key,
    w_value,
    w_out,
    ffn_gain,
    w_router,
    expert_gate,
    expert_up,
    expert_down,
    cotangent,
):
    shards, reps = lax.axis_size("ep"), lax.axis_size("rep")
    experts = w_router.shape[1]
    slots = shards // GROUP
    place = lax.axis_index("ep")
    side = lax.axis_index("rep") % 2

    def swap(values, bits):
        return lax.ppermute(values, "ep", [(i, i ^ bits) for i in range(shards)])

    def swap_rep(values, bits=1):
        return lax.ppermute(values, "rep", [(i, i ^ bits) for i in range(reps)])


    def reduce_reps(values, bits=1):
        while bits < reps:
            values = values.astype(BF16)
            landed = swap_rep(values, bits)
            yield values
            values = values.astype(F32) + hold(landed).astype(F32)
            bits *= 2
        return values

    def reduce_rows(values):
        values = values.reshape(shards, -1, values.shape[1])
        bits = 1
        while bits < shards:
            values = values.reshape(values.shape[0] // 2, 2, *values.shape[1:])
            bit = (place // bits) % 2
            kept, sent = [
                lax.dynamic_index_in_dim(values, index, axis=1, keepdims=False) for index in (bit, 1 - bit)
            ]
            landed = swap(sent, bits)
            yield sent
            values = (kept.astype(F32) + hold(landed).astype(F32)).astype(BF16)
            bits *= 2
        return (yield from reduce_reps(values[0]))

    def sum_steps(slot, own, other):
        other = hold(other)
        landed = swap_rep(other)
        yield other
        own = own + hold(landed).astype(F32)
        if slot == 0:
            return own
        own = own.astype(BF16)
        landed = swap(own, slot * GROUP)
        yield own
        return hold(landed)

    with jax.named_scope("weights_out"):
        half = expert_gate.shape[2] // 2
        whole = [expert_gate[0].T, expert_up[0].T, expert_down[0]]
        halves = [jnp.concatenate([w[k * half : (k + 1) * half] for w in whole]) for k in range(2)]
        mine = jnp.where(side == 0, halves[0], halves[1])
        theirs = jnp.where(side == 0, halves[1], halves[0])
        tokens, mine, theirs = lax.optimization_barrier((tokens, mine, theirs))
        landed = {slot: swap(mine, slot * GROUP) for slot in range(2, min(3, slots))}

    with jax.named_scope("cotangent_out"):
        grads_next = swap(cotangent, 2)
        grads_in = [(cotangent, swap(cotangent, 1)), None]

    with jax.named_scope("attention"):
        inputs = tokens.astype(F32)
        scale_one = rms_scale(inputs)
        norm_one = inputs * scale_one
        normed_one = (norm_one * attn_gain).astype(BF16)
        cuts, first = [], 0
        for per in PARTS:
            for w, wide in ((w_query, QUERIES), (w_key, 1), (w_value, 1)):
                cuts.append(w[:, first * wide * HEAD : (first + per) * wide * HEAD])
            first += per
        w_all = jnp.concatenate(cuts, axis=1)
        packed = dot(w_all, normed_one, (((0,), (1,)), ((), ())))
        cosine, sine = [jnp.asarray(table) for table in rotary_tables()]
        attn, query_rot, key_rot, value_low, lse = attend_call(pieces, packed, cosine, sine)
        attn = after(attn, grads_next, grads_in[0][1])

    with jax.named_scope("cotangent_out"):
        grads_in[1] = (grads_next, swap(after(grads_next, attn), 1))

    with jax.named_scope("routing"):
        pad = jnp.zeros((D, LANES - 2 * experts), BF16)
        router_twice = jnp.concatenate([w_router, w_router, pad], axis=1)
        gain_two = ffn_gain.reshape(1, D)
        residual, rows, gate = route_call(experts, tokens, attn, w_out, gain_two, router_twice, routes)
        rows, held = lax.optimization_barrier((rows, grads_in[1][1], landed.get(2, mine)))[::2]
        rows_next = swap(rows, 2)
        rows_in = [(rows, swap(rows, 1)), None]

    with jax.named_scope("weights_out"):
        weights = {0: (mine, theirs), 2: (held, swap_rep(held))}
        late = after(mine, rows)
        coming = [slot for slot in [*range(3, slots), 1] if slot < slots]
        landed = {slot: swap(late, slot * GROUP) for slot in coming}
        ids = [((place // GROUP) ^ slot) * GROUP + place % GROUP for slot in range(slots)]
        ids = [expert.astype(jnp.int32) for expert in ids]

    carry, sums, tasks = [None, None], [None] * slots, [None] * slots
    mark, point = after(jnp.zeros((8, LANES), F32), rows), rows

    def tick(*arrays):
        nonlocal mark
        mark = after(mark, *arrays)

    def hold(values):
        return after(values, point)

    def pause():
        nonlocal mark
        mark = pause_call(mark)

    def pulse():
        return swap(mark, 1)

    def passed(value, beat=None):
        nonlocal mark, point
        if beat is not None:
            mark = mark + beat
        mark, point = after(mark, value), value

    def run(chip, group, last=False, beats=True):
        beat = pulse() if beats else None
        carry[chip], done = expert_call(
            jnp.stack([ids[slot] for slot in group]),
            mark,
            experts,
            rows_in[chip],
            grads_in[chip],
            [weights[slot] for slot in group],
            [sums[slot] for slot in group],
            carry[chip],
            last,
        )
        passed(carry[chip][2], beat)
        for slot, pair in zip(group, done):
            if sums[slot] is not None:
                tasks[slot] = Task(sum_steps(slot, *pair))
            sums[slot] = pair

    def arrive(slot):
        tick(landed[slot])
        held = hold(landed[slot])
        weights[slot] = (held, swap_rep(held))

    with jax.named_scope("experts"):
        run(0, [0], beats=False)
        tick(rows_next)
        rows_in[1] = (rows_next, swap(hold(rows_next), 1))
        pause()
        tick(rows_in[1][1])
        run(1, [0])
        tick(weights[2][1])
        if slots > 3:
            arrive(3)
        run(1, [2])
        for slot in [*range(4, slots), 1]:
            arrive(slot)
        run(0, [2])
        tick(*[weights[slot][1] for slot in [*range(3, slots), 1]])
        tasks[2].step()
        pairs = [[slot, slot + 1] for slot in range(3, slots - 1, 2)] + [[slots - 1, 1]]
        for pair in pairs:
            last = pair == pairs[-1]
            run(1, pair, last)
            if last:
                there_landed = swap(hold(carry[1][4]), 1)
                pause()
                there = merge_call(experts, mark, carry[1][1], carry[1][2], there_landed)
                d_next = swap(there, 2)
                tick(there, *tasks[2].step())
                tasks[0].step()
                mix_landed = swap(hold(carry[1][3]), 1)
            run(0, pair[:1])
            if last:
                mix_there = merge_call(experts, mark, carry[1][0], None, mix_landed)
                tick(mix_there, *tasks[0].step())
            tasks[pair[0]].step()
            run(0, pair[1:], last)

    with jax.named_scope("routing_back"):
        d_core = swap(hold(carry[0][4]), 1)
        tasks[1].step()
        pause()
        tick(d_core, d_next, *[array for task in tasks[2:] for array in task.step()])
        point = mark
        mix_home = swap(hold(mix_there), 2)
        mix_core = swap(hold(carry[0][3]), 1)
        d_residual, d_mixed, d_attn, d_small = back_call(
            experts, mark, carry[0][1], carry[0][2], d_core, d_next, residual, cotangent, gate, gain_two, router_twice, w_out
        )
        passed(d_small)
        tick(mix_core)
        d_out = out_call(mark, attn, d_mixed, d_small)
        passed(d_out)

    with jax.named_scope("attention_back"):
        in_dims = (((0,), (1,)), ((), ()))
        out_task, w_tasks, d_packed = Task(reduce_rows(d_out)), [], []
        tick(*out_task.step())
        for part in range(len(PARTS)):
            d_packed.append(
                attend_back_call(part, mark, pieces, query_rot, key_rot, value_low, d_attn, lse, cosine, sine)
            )
            passed(d_packed[-1])
            tick(*[array for task in [out_task] + w_tasks for array in task.step()])
            if part == 0:
                tick(*tasks[1].step())
            if part == 1:
                tick(mix_home)
            w_tasks.append(Task(reduce_rows(dot(normed_one, d_packed[-1], in_dims).astype(BF16))))
            tick(*w_tasks[-1].step())
        turns = [[w_tasks[2], w_tasks[0]], [w_tasks[1], out_task], [w_tasks[2], w_tasks[0]]]
        d_normed_one, first = None, 0
        for part, grads in enumerate(d_packed):
            span = grads.shape[0]
            if part > 0:
                grads = after(grads, d_normed_one)
            term = dot(grads, w_all[:, first : first + span], in_dims)
            d_normed_one = point = term if part == 0 else d_normed_one + term
            first += span
            d_normed_one = after(d_normed_one, *[array for task in turns[part] for array in task.step()])
        scaled_one = d_normed_one * attn_gain
        d_tokens = d_residual + scale_one * (
            scaled_one - norm_one * jnp.mean(scaled_one * norm_one, axis=-1, keepdims=True)
        )

    with jax.named_scope("combine"):
        output = (residual + carry[0][0] + mix_core.astype(F32) + mix_home.astype(F32)).astype(BF16)

    with jax.named_scope("sums_experts"):
        total = tasks[0].finish()
        for task in tasks[1:]:
            total = total + task.finish().astype(F32)
        total = Task(reduce_reps(total, 2)).finish().astype(BF16)
        s_gate, s_up, s_down = join_call(side.astype(jnp.int32).reshape(1), total, swap_rep(total))

    with jax.named_scope("sums_rest"):
        s_mixed = out_task.finish()
        s_out, s_small = s_mixed[:, :D], s_mixed[:, D:]
        count = s_out.shape[0]
        first = place * count
        s_parts = [task.finish() for task in w_tasks]
        w_rows = lax.dynamic_slice_in_dim(w_all, first, count)
        s_attn = jnp.sum(jnp.concatenate(s_parts, axis=1) * w_rows.astype(F32), axis=1)
        s_attn = s_attn / lax.dynamic_slice_in_dim(attn_gain, first, count)
        columns = [[], [], []]
        for per, part in zip(PARTS, s_parts):
            for group, column in zip(columns, jnp.split(part, [QUERIES * per * HEAD, (QUERIES + 1) * per * HEAD], axis=1)):
                group.append(column)
        s_query, s_key, s_value = [jnp.concatenate(group, axis=1) for group in columns]

    return (
        output,
        d_tokens,
        s_attn,
        s_query,
        s_key,
        s_value,
        s_out,
        s_small[:, experts],
        s_small[:, :experts],
        s_gate[None],
        s_up[None],
        s_down[None],
    )


def solution(mesh):
    rows, whole, slices = P(("rep", "ep"), None), P(), P("ep", None)
    expert = P("ep", None, None)
    return jax.shard_map(
        local,
        mesh=mesh,
        in_specs=(rows,) * 3 + (whole,) * 7 + (expert,) * 3 + (rows,),
        out_specs=(rows, rows, P("ep")) + (slices,) * 4 + (P("ep"), slices) + (expert,) * 3,
        check_vma=False,
    )
```

```python
import functools
import math

import jax
import jax.numpy as jnp
import numpy as np
from jax import lax
from jax.experimental import pallas as pl
from jax.experimental.pallas import tpu as pltpu
from jax.sharding import PartitionSpec as P

D = 1536
HEADS = 24
KV = 8
HEAD = 64
LEN = 1024
PIECE = 256
QUERIES = HEADS // KV
WIDE = 256
TILE = 256
GROUP = 4
PARTS = (2, 4, 2)
LANES = 128
WIDTH = D + LANES

eps = 1e-06
theta_base = 10000.0
masked_score = -1e30
score_scale = HEAD ** (-0.5)
two_scale = score_scale * math.log2(math.e)

F32 = jnp.float32
BF16 = jnp.bfloat16
NN = (((1,), (0,)), ((), ()))
NT = (((1,), (1,)), ((), ()))
TN = (((0,), (0,)), ((), ()))
ANY = pl.BlockSpec(memory_space=pl.ANY)
SMEM = pl.BlockSpec(memory_space=pltpu.SMEM)


def dot(left, right, dims):
    return lax.dot_general(left, right, dims, preferred_element_type=F32)


def shaped(shape, dtype):
    return jax.ShapeDtypeStruct(shape, dtype)


def estimate(micros):
    return pl.CostEstimate(flops=int(micros * 1e10), bytes_accessed=int(micros * 1e6), transcendentals=0)


def rms_scale(values):
    return lax.rsqrt(jnp.mean(values * values, axis=-1, keepdims=True) + eps)


def rotary_tables():
    half_head = HEAD // 2
    frequency = theta_base ** (-(np.arange(half_head, dtype=np.float64) * 2.0) / HEAD)
    angles = frequency[:, None] * np.arange(LEN, dtype=np.float64)[None, :]
    return np.cos(angles).astype(np.float32), np.sin(angles).astype(np.float32)


def turn(values, cosine, sine):
    first, second = values[: HEAD // 2], values[HEAD // 2 :]
    return jnp.concatenate([first * cosine - second * sine, second * cosine + first * sine], axis=0)


def turn_back(grads, cosine, sine):
    first, second = grads[: HEAD // 2], grads[HEAD // 2 :]
    return jnp.concatenate([first * cosine + second * sine, second * cosine - first * sine], axis=0)


def fill_bias(pieces, bias):
    for block in range(LEN // WIDE):
        first = block * WIDE
        shape = bias.shape[1:]
        key = lax.broadcasted_iota(jnp.int32, shape, 0) + first
        query = lax.broadcasted_iota(jnp.int32, shape, 1) + first
        allowed = key <= query
        for piece in range(pieces.shape[1]):
            start = pieces[0, piece]
            low, high = jnp.minimum(key, query), jnp.maximum(key, query)
            allowed = allowed | ((low >= start) & (high < start + PIECE))
        bias[block] = jnp.where(allowed, 0.0, masked_score)


def key_span(block):
    return block * WIDE, min((block + 2) * WIDE, LEN)


def masked_scores(keys, queries, bias, block):
    first, last = key_span(block)
    scores = dot(keys[:last], queries, NN)
    masked = scores[first:] + bias[block, : last - first]
    return masked if first == 0 else jnp.concatenate([scores[:first], masked], axis=0)


def rows_at(place):
    return pl.BlockSpec((HEAD, LEN), lambda *grid: (place(*grid), 0))


def packed_row(head, kind):
    row = 0
    for part, per in enumerate(PARTS):
        first = sum(PARTS[:part])
        inner = head - first
        here = {3: QUERIES * per + inner, 4: (QUERIES + 1) * per + inner}.get(kind, QUERIES * inner + kind)
        row = jnp.where(inner >= 0, (QUERIES + 2) * first + here, row)
    return row


def table_spec():
    return pl.BlockSpec((HEAD // 2, LEN), lambda *grid: (0, 0))


def attend_kernel(pieces, q0, q1, q2, k_in, v_in, cosine, sine, attn, q_out, k_out, v_out, lse, bias):
    @pl.when(pl.program_id(0) == 0)
    def _():
        fill_bias(pieces, bias)

    cos, sin = cosine[...], sine[...]
    k_rot = turn(k_in[...], cos, sin)
    k_out[...] = k_rot.astype(BF16)
    keys = k_rot.T.astype(BF16)
    values = v_in[...].astype(BF16)
    v_out[...] = values
    for head, q_in in enumerate((q0, q1, q2)):
        rows = pl.ds(head * HEAD, HEAD)
        q_rot = turn(q_in[...], cos, sin).astype(BF16)
        q_out[rows, :] = q_rot
        for block in range(LEN // WIDE):
            columns = pl.ds(block * WIDE, WIDE)
            last = key_span(block)[1]
            scores = masked_scores(keys, q_rot[:, block * WIDE : (block + 1) * WIDE], bias, block)
            highest = jnp.max(scores, axis=0, keepdims=True) * two_scale
            weights = jnp.exp2(scores * two_scale - highest)
            total = jnp.sum(weights, axis=0, keepdims=True)
            mixed = dot(values[:, :last], weights.astype(BF16), NN) / total
            attn[rows, columns] = mixed.astype(BF16)
            lse[head : head + 1, columns] = highest + jnp.log2(total)


def attend_call(pieces, packed, cosine, sine):
    rows = lambda count: pl.BlockSpec((count, LEN), lambda i: (i, 0))
    width = QUERIES * HEAD
    return pl.pallas_call(
        attend_kernel,
        grid=(KV,),
        in_specs=[SMEM]
        + [rows_at(functools.partial(packed_row, kind=kind)) for kind in range(5)]
        + [table_spec(), table_spec()],
        out_specs=[rows(width), rows(width), rows(HEAD), rows(HEAD), rows(8)],
        out_shape=[
            shaped((D, LEN), BF16),
            shaped((D, LEN), BF16),
            shaped((KV * HEAD, LEN), BF16),
            shaped((KV * HEAD, LEN), BF16),
            shaped((KV * 8, LEN), F32),
        ],
        scratch_shapes=[pltpu.VMEM((LEN // WIDE, 2 * WIDE, WIDE), F32)],
        compiler_params=pltpu.CompilerParams(vmem_limit_bytes=60 << 20),
        cost_estimate=estimate(25),
        name="attend",
    )(pieces, *[packed] * 5, cosine, sine)


def attend_back_kernel(
    mark, pieces, q_in, k_in, v_in, do_in, lse, cosine, sine, out, bias, keys_kept, values_kept, dk_sum, dv_sum
):
    kind = pl.program_id(1)

    @pl.when((pl.program_id(0) == 0) & (kind == 0))
    def _():
        fill_bias(pieces, bias)

    cos, sin = cosine[...], sine[...]

    @pl.when(kind == 0)
    def _():
        keys_kept[...] = k_in[...].astype(F32).T.astype(BF16)
        values_kept[...] = v_in[...].astype(F32).T.astype(BF16)
        dk_sum[...] = jnp.zeros_like(dk_sum)
        dv_sum[...] = jnp.zeros_like(dv_sum)

    @pl.when(kind < QUERIES)
    def _():
        k_cols, keys, values = k_in[...], keys_kept[...], values_kept[...]
        q_cols, do_cols = q_in[...], do_in[...]
        q_rows = q_cols.astype(F32).T.astype(BF16)
        do_rows = do_cols.astype(F32).T.astype(BF16)
        row_lse = lse[pl.ds(kind, 1), :]
        for block in range(LEN // WIDE):
            part = slice(block * WIDE, (block + 1) * WIDE)
            last = key_span(block)[1]
            scores = masked_scores(keys, q_cols[:, part], bias, block)
            probs = jnp.exp2(scores * two_scale - row_lse[:, part])
            d_probs = dot(values[:last], do_cols[:, part], NN)
            product = probs * d_probs
            delta = jnp.sum(product, axis=0, keepdims=True)
            d_scores = (product - probs * delta).astype(BF16)
            dv_sum[:last] += dot(probs.astype(BF16), do_rows[part], NN)
            dk_sum[:last] += dot(d_scores, q_rows[part], NN)
            d_query = dot(k_cols[:, :last], d_scores, NN) * score_scale
            out[:, part] = turn_back(d_query, cos[:, part], sin[:, part]).astype(BF16)

    @pl.when(kind == QUERIES)
    def _():
        out[...] = turn_back(dk_sum[...].T * score_scale, cos, sin).astype(BF16)

    @pl.when(kind == QUERIES + 1)
    def _():
        out[...] = dv_sum[...].T.astype(BF16)


def attend_back_call(part, mark, pieces, q_in, k_in, v_in, do_in, lse, cosine, sine):
    per, first = PARTS[part], sum(PARTS[:part])
    query = rows_at(lambda i, j: (first + i) * QUERIES + jnp.minimum(j, QUERIES - 1))
    key = rows_at(lambda i, j: first + i)

    def place(i, j):
        tail = jnp.where(j == QUERIES, QUERIES * per + i, (QUERIES + 1) * per + i)
        return jnp.where(j < QUERIES, QUERIES * i + j, tail)

    return pl.pallas_call(
        attend_back_kernel,
        grid=(per, QUERIES + 2),
        in_specs=[ANY, SMEM, query, key, key, query, pl.BlockSpec((8, LEN), lambda i, j: (first + i, 0))]
        + [table_spec(), table_spec()],
        out_specs=rows_at(place),
        out_shape=shaped(((QUERIES + 2) * per * HEAD, LEN), BF16),
        scratch_shapes=[
            pltpu.VMEM((LEN // WIDE, 2 * WIDE, WIDE), F32),
            pltpu.VMEM((LEN, HEAD), BF16),
            pltpu.VMEM((LEN, HEAD), BF16),
            pltpu.VMEM((LEN, HEAD), F32),
            pltpu.VMEM((LEN, HEAD), F32),
        ],
        compiler_params=pltpu.CompilerParams(vmem_limit_bytes=60 << 20),
        cost_estimate=estimate(15),
        name="attend_back",
    )(mark, pieces, q_in, k_in, v_in, do_in, lse, cosine, sine)


def split_lanes(values, experts):
    lanes = lax.broadcasted_iota(jnp.int32, values.shape, 1)
    high = values.astype(BF16).astype(F32)
    return jnp.where(lanes < experts, high, jnp.where(lanes < 2 * experts, values - high, 0.0)).astype(BF16)


def join_lanes(parts, experts):
    return parts + pltpu.roll(parts, LANES - experts, 1)


def route_kernel(experts, tokens, attn, w_out, gain, w_router, routes, residual, rows, gate):
    values = tokens[...].astype(F32) + dot(attn[...], w_out[...], TN)
    residual[...] = values
    normed = (values * rms_scale(values) * gain[...]).astype(BF16)
    logits = dot(normed, w_router[...], NN)
    lanes = lax.broadcasted_iota(jnp.int32, logits.shape, 1)
    expert = lax.rem(lanes, experts)
    chosen = lanes < 0
    for k in range(routes.shape[1]):
        chosen = chosen | (routes[:, k : k + 1] == expert)
    chosen = chosen & (lanes < 2 * experts)
    logits = jnp.where(chosen, logits, masked_score)
    weights = jnp.exp(logits - jnp.max(logits, axis=1, keepdims=True))
    share = weights / (0.5 * jnp.sum(weights, axis=1, keepdims=True))
    gate[...] = share
    rows[:, :D] = normed
    rows[:, D:] = split_lanes(share, experts)


def route_call(experts, tokens, attn, w_out, gain, w_router, routes):
    rows = lambda cols: pl.BlockSpec((TILE, cols), lambda i: (i, 0))
    whole = lambda *shape: pl.BlockSpec(shape, lambda i: (0, 0), pipeline_mode=pl.Buffered(1))
    return pl.pallas_call(
        functools.partial(route_kernel, experts),
        grid=(LEN // TILE,),
        in_specs=[rows(D), pl.BlockSpec((D, TILE), lambda i: (0, i)), whole(D, D), whole(1, D), whole(D, LANES)]
        + [rows(routes.shape[1])],
        out_specs=[rows(D), rows(WIDTH), rows(LANES)],
        out_shape=[shaped((LEN, D), F32), shaped((LEN, WIDTH), BF16), shaped((LEN, LANES), F32)],
        compiler_params=pltpu.CompilerParams(vmem_limit_bytes=60 << 20),
        cost_estimate=estimate(5),
        name="route",
    )(tokens, attn, w_out, gain, w_router, routes)


def merge_kernel(experts, mark, kept, kept_share, landed, out):
    out[:, :D] = (kept[...] + landed[:, :D].astype(F32)).astype(BF16)
    if kept_share is not None:
        share = kept_share[...] + join_lanes(landed[:, D:].astype(F32), experts)
        share = jnp.where(lax.broadcasted_iota(jnp.int32, share.shape, 1) < experts, share, 0.0)
        out[:, D:] = split_lanes(share + pltpu.roll(share, experts, 1), experts)


def merge_call(experts, mark, kept, kept_share, landed):
    rows = lambda cols: pl.BlockSpec((TILE, cols), lambda i: (i, 0))
    width = landed.shape[1]
    kernel = functools.partial(merge_kernel, experts)
    if kept_share is None:
        kernel = lambda mark, kept, landed, out: merge_kernel(experts, mark, kept, None, landed, out)
    return pl.pallas_call(
        kernel,
        grid=(LEN // TILE,),
        in_specs=[ANY, rows(D)] + ([] if kept_share is None else [rows(LANES)]) + [rows(width)],
        out_specs=rows(width),
        out_shape=shaped((LEN, width), BF16),
        compiler_params=pltpu.CompilerParams(vmem_limit_bytes=60 << 20),
        cost_estimate=estimate(3),
        name="merge",
    )(*[ref for ref in (mark, kept, kept_share, landed) if ref is not None])


def back_kernel(
    experts, mark, kept, kept_share, core, chip, residual, cotangent, gate, gain, w_router, w_out, d_res, d_mix, d_attn, d_router
):
    @pl.when(pl.program_id(0) == 0)
    def _():
        d_router[...] = jnp.zeros_like(d_router)

    landed = core[:, D:].astype(F32) + chip[:, D:].astype(F32)
    share = kept_share[...] + join_lanes(landed, experts)
    first = lax.broadcasted_iota(jnp.int32, share.shape, 1) < experts
    gates = jnp.where(first, gate[...], 0.0)
    inner = jnp.sum(gates * share, axis=1, keepdims=True)
    d_logits = jnp.where(first, gates * (share - inner), 0.0).astype(BF16)
    d_normed = kept[...] + core[:, :D].astype(F32) + chip[:, :D].astype(F32) + dot(d_logits, w_router[...], NT)
    values, gains = residual[...], gain[...]
    scale = rms_scale(values)
    norm = values * scale
    d_gain = jnp.sum(d_normed * norm, axis=0, keepdims=True)
    scaled = d_normed * gains
    d_values = cotangent[...].astype(F32) + scale * (scaled - norm * jnp.mean(scaled * norm, axis=1, keepdims=True))
    d_res[...] = d_values
    mixed = d_values.astype(BF16)
    d_mix[...] = mixed
    d_attn[...] = dot(w_out[...], mixed, NT).astype(BF16)
    d_router[...] += dot(d_logits, (norm * gains).astype(BF16), TN)
    d_router[experts : experts + 1] += d_gain


def back_call(experts, mark, kept, kept_share, core, chip, residual, cotangent, gate, gain, w_router, w_out):
    rows = lambda cols: pl.BlockSpec((TILE, cols), lambda i: (i, 0))
    whole = lambda *shape: pl.BlockSpec(shape, lambda i: (0, 0), pipeline_mode=pl.Buffered(1))
    return pl.pallas_call(
        functools.partial(back_kernel, experts),
        grid=(LEN // TILE,),
        in_specs=[ANY, rows(D), rows(LANES), rows(WIDTH), rows(WIDTH), rows(D), rows(D), rows(LANES)]
        + [whole(1, D), whole(D, LANES), whole(D, D)],
        out_specs=[rows(D), rows(D), pl.BlockSpec((D, TILE), lambda i: (0, i)), whole(LANES, D)],
        out_shape=[
            shaped((LEN, D), F32),
            shaped((LEN, D), BF16),
            shaped((D, LEN), BF16),
            shaped((LANES, D), F32),
        ],
        compiler_params=pltpu.CompilerParams(vmem_limit_bytes=60 << 20),
        cost_estimate=estimate(8),
        name="back",
    )(mark, kept, kept_share, core, chip, residual, cotangent, gate, gain, w_router, w_out)


def out_kernel(mark, attn, mixed, small, out):
    out[:, :D] = dot(attn[...], mixed[...], NN).astype(BF16)
    out[:, D:] = small[...].T.astype(BF16)


def out_call(mark, attn, mixed, small):
    return pl.pallas_call(
        out_kernel,
        grid=(D // TILE,),
        in_specs=[
            ANY,
            pl.BlockSpec((TILE, LEN), lambda i: (i, 0)),
            pl.BlockSpec((LEN, D), lambda i: (0, 0), pipeline_mode=pl.Buffered(1)),
            pl.BlockSpec((LANES, TILE), lambda i: (0, i)),
        ],
        out_specs=pl.BlockSpec((TILE, WIDTH), lambda i: (i, 0)),
        out_shape=shaped((D, WIDTH), BF16),
        compiler_params=pltpu.CompilerParams(vmem_limit_bytes=60 << 20),
        cost_estimate=estimate(5),
        name="out_grad",
    )(mark, attn, mixed, small)


def pause_kernel(mark, out):
    out[...] = mark[...]


def pause_call(mark):
    return pl.pallas_call(
        pause_kernel, out_shape=shaped(mark.shape, mark.dtype), cost_estimate=estimate(10), name="pause"
    )(mark)


def expert_kernel(count, experts, fresh, first, last_tokens, steps, ids, mark, *rest):
    rest = list(rest)

    def take(number):
        taken = rest[:number]
        del rest[:number]
        return taken

    n2, up = take(2), take(2)
    w_in = [take(2) for _ in range(count)]
    sums_in = [[] if new else take(2) for new in fresh]
    carry_in = [] if first else take(3)
    outs = take(5) if last_tokens else take(3)
    sums_out = [take(2) for _ in range(count)]
    weights, sums = take(1)[0], take(1)[0]
    low = None if all(fresh) else take(1)[0]
    sem = rest[0]
    half = weights.shape[1] // 6
    width = 2 * half
    step = pl.program_id(0)
    ahead = step < steps // 2

    def pieces_of(parts, whole):
        return [
            (ref.at[pl.ds(kind * half, half)], whole.at[pl.ds((2 * kind + part) * half, half)])
            for kind in range(3)
            for part, ref in enumerate(parts)
        ]

    def copies_of(pairs, lane):
        return [pltpu.make_async_copy(a, b, sem.at[lane, n]) for n, (a, b) in enumerate(pairs)]

    loads = [copies_of(pieces_of(w_in[e], weights.at[e]), e) for e in range(count)]
    sum_loads = [copies_of(pieces_of(sums_in[e], sums.at[e]), count + e) for e in range(count) if not fresh[e]]

    @pl.when(step == 0)
    def _():
        for copy in sum(loads + sum_loads, []):
            copy.start()
        for e in range(count):
            if fresh[e]:
                sums[e] = jnp.zeros(sums.shape[1:], F32)
        for copy in sum(loads + sum_loads, []):
            copy.wait()

    rows = jnp.where(ahead, n2[0][...], n2[1][...])
    grads = jnp.where(ahead, up[0][...], up[1][...])
    rows, gates = rows[:, :D], rows[:, D:].astype(F32)
    lanes = lax.broadcasted_iota(jnp.int32, gates.shape, 1)
    mixed = d_rows = d_shares = None
    add = lambda total, value: value if total is None else total + value
    for e in range(count):
        w_both, w_down = weights.at[e, : 2 * width], weights.at[e, 2 * width :]
        hit = (lanes == ids[e]) | (lanes == ids[e] + experts)
        share = jnp.sum(jnp.where(hit, gates, 0.0), axis=1, keepdims=True)
        acts = dot(rows, w_both[...], NT)
        gate_act, up_act = acts[:, :width], acts[:, width:]
        d_plain = dot(grads, w_down[...], NT)
        sigmoid = 1.0 / (1.0 + jnp.exp(-gate_act))
        silu = gate_act * sigmoid
        hidden = silu * up_act
        shared = (share * hidden).astype(BF16)
        d_share = jnp.sum(hidden * d_plain, axis=1, keepdims=True)
        d_hidden = share * d_plain
        d_gate = (d_hidden * up_act * (sigmoid + silu * (1.0 - sigmoid))).astype(BF16)
        d_up = (d_hidden * silu).astype(BF16)
        d_both = jnp.concatenate([d_gate, d_up], axis=1)
        mixed = add(mixed, dot(shared, w_down[...], NN))
        d_rows = add(d_rows, dot(d_both, w_both[...], NN))
        d_shares = add(d_shares, jnp.where(hit, d_share, 0.0))
        sums[e, : 2 * width] += dot(d_both, rows, TN)
        sums[e, 2 * width :] += dot(shared, grads, TN)
    results = [mixed, d_rows, d_shares]
    if not first:
        results = [result + ref[...] for result, ref in zip(results, carry_in)]
    if last_tokens:

        @pl.when(ahead)
        def _():
            for ref, result in zip(outs[:3], results):
                ref[...] = result

        @pl.when(jnp.logical_not(ahead))
        def _():
            outs[3][...] = results[0].astype(BF16)
            outs[4][:, :D] = results[1].astype(BF16)
            outs[4][:, D:] = split_lanes(results[2], experts)
    else:
        for ref, result in zip(outs, results):
            ref[...] = result

    @pl.when(step == steps - 1)
    def _():
        stores = []
        for e in range(count):
            pairs = [(b, a) for a, b in pieces_of(sums_out[e], sums.at[e])]
            if not fresh[e]:
                for kind in range(3):
                    low[e, pl.ds(kind * half, half)] = sums[e, pl.ds((2 * kind + 1) * half, half)].astype(BF16)
                pairs = pairs[::2] + [(low.at[e], sums_out[e][1])]
            stores += copies_of(pairs, e)
        for copy in stores:
            copy.start()
        for copy in stores:
            copy.wait()


def expert_call(ids, mark, experts, n2, up, weights, sums, carry, last_tokens):
    tokens, height, count = 2 * n2[0].shape[0], weights[0][0].shape[0], len(weights)
    steps = tokens // TILE
    rows = lambda cols: pl.BlockSpec((TILE, cols), lambda i: (i, 0))
    near = lambda cols: pl.BlockSpec((TILE, cols), lambda i: (jnp.minimum(i, steps // 2 - 1), 0))
    far = lambda cols: pl.BlockSpec((TILE, cols), lambda i: (jnp.maximum(i - steps // 2, 0), 0))
    ins = [ids, mark, *n2, *up] + [w for pair in weights for w in pair]
    specs = [SMEM, ANY, near(WIDTH), far(WIDTH), near(D), far(D)] + [ANY] * (2 * count)
    fresh, first = [pair is None for pair in sums], carry is None
    columns = (D, D, LANES)
    if last_tokens:
        outs = [shaped((tokens // 2, c), F32) for c in columns]
        outs += [shaped((tokens // 2, c), BF16) for c in (D, WIDTH)]
        out_specs = [near(c) for c in columns] + [far(D), far(WIDTH)]
    else:
        outs = [shaped((tokens, c), F32) for c in columns]
        out_specs = [rows(c) for c in columns]
    aliases = {}
    for pair in sums:
        if pair is not None:
            ins += pair
            specs += [ANY, ANY]
    if not first:
        if not last_tokens:
            aliases.update({len(ins) + k: k for k in range(3)})
        ins += carry
        specs += [rows(c) for c in columns]
    tokens_out = len(outs)
    for new in fresh:
        outs += [shaped((height, D), F32), shaped((height, D), F32 if new else BF16)]
        out_specs += [ANY, ANY]
    scratch = [pltpu.VMEM((count, 2 * height, D), BF16), pltpu.VMEM((count, 2 * height, D), F32)]
    if not all(fresh):
        scratch.append(pltpu.VMEM((count, height, D), BF16))
    scratch.append(pltpu.SemaphoreType.DMA((2 * count, 6)))
    done = pl.pallas_call(
        functools.partial(expert_kernel, count, experts, fresh, first, last_tokens, steps),
        grid=(steps,),
        in_specs=specs,
        out_specs=out_specs,
        out_shape=outs,
        scratch_shapes=scratch,
        input_output_aliases=aliases,
        compiler_params=pltpu.CompilerParams(vmem_limit_bytes=60 << 20),
        cost_estimate=estimate(15 * count),
        name="expert",
    )(*ins)
    return list(done[:tokens_out]), [tuple(done[tokens_out + 2 * e : tokens_out + 2 * e + 2]) for e in range(count)]


def join_kernel(side, held, landed, gate, up, down):
    here = pl.program_id(0) == 0
    rows = jnp.where(here, held[...], landed[...]).astype(F32)
    half = down.shape[0]
    gate[...] = rows[:half].T
    up[...] = rows[half : 2 * half].T
    down[...] = rows[2 * half :]


def join_call(side, held, landed):
    half = held.shape[0] // 3
    whole = pl.BlockSpec(held.shape, lambda i, side: (0, 0))
    columns = pl.BlockSpec((D, half), lambda i, side: (0, lax.rem(side[0] + i, 2)))
    return pl.pallas_call(
        join_kernel,
        grid_spec=pltpu.PrefetchScalarGridSpec(
            num_scalar_prefetch=1,
            grid=(2,),
            in_specs=[whole, whole],
            out_specs=[columns, columns, pl.BlockSpec((half, D), lambda i, side: (lax.rem(side[0] + i, 2), 0))],
        ),
        out_shape=[shaped((D, 2 * half), F32), shaped((D, 2 * half), F32), shaped((2 * half, D), F32)],
        compiler_params=pltpu.CompilerParams(vmem_limit_bytes=60 << 20),
        cost_estimate=estimate(5),
        name="join",
    )(side, held, landed)


def after(values, *others):
    return lax.optimization_barrier((values, *others))[0]


class Task:
    def __init__(self, steps):
        self.steps, self.result, self.over = steps, None, False

    def step(self):
        if self.over:
            return []
        try:
            return [next(self.steps)]
        except StopIteration as stop:
            self.result, self.over = stop.value, True
            return [self.result]

    def finish(self):
        while not self.over:
            self.step()
        return self.result


def local(
    tokens,
    routes,
    pieces,
    attn_gain,
    w_query,
    w_key,
    w_value,
    w_out,
    ffn_gain,
    w_router,
    expert_gate,
    expert_up,
    expert_down,
    cotangent,
):
    shards, reps = lax.axis_size("ep"), lax.axis_size("rep")
    experts = w_router.shape[1]
    slots = shards // GROUP
    place = lax.axis_index("ep")
    side = lax.axis_index("rep") % 2

    def swap(values, bits):
        return lax.ppermute(values, "ep", [(i, i ^ bits) for i in range(shards)])

    def swap_rep(values, bits=1):
        return lax.ppermute(values, "rep", [(i, i ^ bits) for i in range(reps)])


    def reduce_reps(values, bits=1):
        while bits < reps:
            values = values.astype(BF16)
            landed = swap_rep(values, bits)
            yield values
            values = values.astype(F32) + hold(landed).astype(F32)
            bits *= 2
        return values

    def reduce_rows(values):
        values = values.reshape(shards, -1, values.shape[1])
        bits = 1
        while bits < shards:
            values = values.reshape(values.shape[0] // 2, 2, *values.shape[1:])
            bit = (place // bits) % 2
            kept, sent = [
                lax.dynamic_index_in_dim(values, index, axis=1, keepdims=False) for index in (bit, 1 - bit)
            ]
            landed = swap(sent, bits)
            yield sent
            values = (kept.astype(F32) + hold(landed).astype(F32)).astype(BF16)
            bits *= 2
        return (yield from reduce_reps(values[0]))

    def sum_steps(slot, own, other):
        other = hold(other)
        landed = swap_rep(other)
        yield other
        own = own + hold(landed).astype(F32)
        if slot == 0:
            return own
        own = own.astype(BF16)
        landed = swap(own, slot * GROUP)
        yield own
        return hold(landed)

    with jax.named_scope("weights_out"):
        half = expert_gate.shape[2] // 2
        whole = [expert_gate[0].T, expert_up[0].T, expert_down[0]]
        halves = [jnp.concatenate([w[k * half : (k + 1) * half] for w in whole]) for k in range(2)]
        mine = jnp.where(side == 0, halves[0], halves[1])
        theirs = jnp.where(side == 0, halves[1], halves[0])
        tokens, mine, theirs = lax.optimization_barrier((tokens, mine, theirs))
        landed = {slot: swap(mine, slot * GROUP) for slot in (2, 1)}

    with jax.named_scope("cotangent_out"):
        grads_next = swap(cotangent, 2)
        grads_in = [(cotangent, swap(cotangent, 1)), None]

    with jax.named_scope("attention"):
        inputs = tokens.astype(F32)
        scale_one = rms_scale(inputs)
        norm_one = inputs * scale_one
        normed_one = (norm_one * attn_gain).astype(BF16)
        cuts, first = [], 0
        for per in PARTS:
            for w, wide in ((w_query, QUERIES), (w_key, 1), (w_value, 1)):
                cuts.append(w[:, first * wide * HEAD : (first + per) * wide * HEAD])
            first += per
        w_all = jnp.concatenate(cuts, axis=1)
        packed = dot(w_all, normed_one, (((0,), (1,)), ((), ())))
        cosine, sine = [jnp.asarray(table) for table in rotary_tables()]
        attn, query_rot, key_rot, value_low, lse = attend_call(pieces, packed, cosine, sine)
        attn = after(attn, grads_next, grads_in[0][1])

    with jax.named_scope("cotangent_out"):
        grads_in[1] = (grads_next, swap(after(grads_next, attn), 1))

    with jax.named_scope("routing"):
        pad = jnp.zeros((D, LANES - 2 * experts), BF16)
        router_twice = jnp.concatenate([w_router, w_router, pad], axis=1)
        gain_two = ffn_gain.reshape(1, D)
        residual, rows, gate = route_call(experts, tokens, attn, w_out, gain_two, router_twice, routes)
        rows, _, held, near = lax.optimization_barrier((rows, grads_in[1][1], landed[2], landed[1]))
        rows_next = swap(rows, 2)
        rows_in = [(rows, swap(rows, 1)), None]

    with jax.named_scope("weights_out"):
        weights = {0: (mine, theirs), 2: (held, swap_rep(held))}
        late = after(mine, rows)
        landed = {slot: swap(late, slot * GROUP) for slot in range(3, slots)}
        ids = [((place // GROUP) ^ slot) * GROUP + place % GROUP for slot in range(slots)]
        ids = [expert.astype(jnp.int32) for expert in ids]

    carry, sums, tasks = [None, None], [None] * slots, [None] * slots
    mark, point = after(jnp.zeros((8, LANES), F32), rows), rows

    def tick(*arrays):
        nonlocal mark
        mark = after(mark, *arrays)

    def hold(values):
        return after(values, point)

    def pause():
        nonlocal mark
        mark = pause_call(mark)

    def pulse():
        return swap(mark, 1)

    def passed(value, beat=None):
        nonlocal mark, point
        if beat is not None:
            mark = mark + beat
        mark, point = after(mark, value), value

    def run(chip, group, last=False, beats=True):
        beat = pulse() if beats else None
        carry[chip], done = expert_call(
            jnp.stack([ids[slot] for slot in group]),
            mark,
            experts,
            rows_in[chip],
            grads_in[chip],
            [weights[slot] for slot in group],
            [sums[slot] for slot in group],
            carry[chip],
            last,
        )
        passed(carry[chip][2], beat)
        for slot, pair in zip(group, done):
            if sums[slot] is not None:
                tasks[slot] = Task(sum_steps(slot, *pair))
            sums[slot] = pair

    def arrive(slot):
        tick(landed[slot])
        held = hold(landed[slot])
        weights[slot] = (held, swap_rep(held))

    with jax.named_scope("experts"):
        run(0, [0], beats=False)
        tick(weights[2][1])
        near = hold(near)
        weights[1] = (near, swap_rep(near))
        run(0, [2])
        tick(rows_next, weights[1][1])
        for slot in range(3, slots):
            arrive(slot)
        rows_in[1] = (rows_next, swap(hold(rows_next), 1))
        pause()
        tick(rows_in[1][1])
        run(1, [0, 2])
        tick(*[weights[slot][1] for slot in range(3, slots)])
        tasks[2].step()
        pairs = [[slot, slot + 1] for slot in range(3, slots - 1, 2)] + [[slots - 1, 1]]
        for pair in pairs:
            last = pair == pairs[-1]
            run(1, pair, last)
            if last:
                there_landed = swap(hold(carry[1][4]), 1)
                pause()
                there = merge_call(experts, mark, carry[1][1], carry[1][2], there_landed)
                d_next = swap(there, 2)
                tick(there, *tasks[2].step())
                tasks[0].step()
                mix_landed = swap(hold(carry[1][3]), 1)
            run(0, pair[:1])
            if last:
                mix_there = merge_call(experts, mark, carry[1][0], None, mix_landed)
                tick(mix_there, *tasks[0].step())
            tasks[pair[0]].step()
            run(0, pair[1:], last)

    with jax.named_scope("routing_back"):
        d_core = swap(hold(carry[0][4]), 1)
        tasks[1].step()
        pause()
        tick(d_core, d_next, *[array for task in tasks[2:] for array in task.step()])
        point = mark
        mix_home = swap(hold(mix_there), 2)
        mix_core = swap(hold(carry[0][3]), 1)
        d_residual, d_mixed, d_attn, d_small = back_call(
            experts, mark, carry[0][1], carry[0][2], d_core, d_next, residual, cotangent, gate, gain_two, router_twice, w_out
        )
        passed(d_small)
        tick(mix_core)
        d_out = out_call(mark, attn, d_mixed, d_small)
        passed(d_out)

    with jax.named_scope("attention_back"):
        in_dims = (((0,), (1,)), ((), ()))
        out_task, w_tasks, d_packed = Task(reduce_rows(d_out)), [], []
        tick(*out_task.step())
        for part in range(len(PARTS)):
            d_packed.append(
                attend_back_call(part, mark, pieces, query_rot, key_rot, value_low, d_attn, lse, cosine, sine)
            )
            passed(d_packed[-1])
            tick(*[array for task in w_tasks + [out_task] * (part < 2) for array in task.step()])
            if part == 0:
                tick(*tasks[1].step())
            w_tasks.append(Task(reduce_rows(dot(normed_one, d_packed[-1], in_dims).astype(BF16))))
            if part < len(PARTS) - 1:
                tick(*w_tasks[-1].step())

    with jax.named_scope("sums_experts"):
        total = tasks[0].finish()
        for task in tasks[1:]:
            total = total + task.finish().astype(F32)
        total = Task(reduce_reps(total, 2)).finish().astype(BF16)
        total_landed = swap_rep(total)

    with jax.named_scope("tail"):
        mark = after(mark, total)
        d_normed_one, first = None, 0
        turns = [[w_tasks[2], out_task], [w_tasks[1], w_tasks[0]], [out_task]]
        stepped = w_tasks[2].step()
        for part, grads in enumerate(d_packed):
            span = grads.shape[0]
            grads = after(grads, mark, *stepped)
            term = dot(grads, w_all[:, first : first + span], in_dims)
            d_normed_one = point = term if part == 0 else d_normed_one + term
            first += span
            stepped = [array for task in turns[part] for array in task.step()]
        mix_home = after(mix_home, point, *stepped)
        output = (residual + carry[0][0] + mix_core.astype(F32) + mix_home.astype(F32)).astype(BF16)
        point = output
        stepped = [array for task in (w_tasks[2], w_tasks[1], w_tasks[0]) for array in task.step()]
        d_normed_one = after(d_normed_one, output, *stepped)
        scaled_one = d_normed_one * attn_gain
        d_tokens = point = d_residual + scale_one * (
            scaled_one - norm_one * jnp.mean(scaled_one * norm_one, axis=-1, keepdims=True)
        )
        stepped = [array for task in (w_tasks[2], w_tasks[1], out_task) for array in task.step()]
        total, total_landed = lax.optimization_barrier((total, total_landed, point, *stepped))[:2]
        s_gate, s_up, s_down = join_call(side.astype(jnp.int32).reshape(1), total, total_landed)
        point = s_down

    with jax.named_scope("sums_rest"):
        s_mixed = out_task.finish()
        s_out, s_small = s_mixed[:, :D], s_mixed[:, D:]
        count = s_out.shape[0]
        first = place * count
        s_parts = [task.finish() for task in w_tasks]
        w_rows = lax.dynamic_slice_in_dim(w_all, first, count)
        s_attn = jnp.sum(jnp.concatenate(s_parts, axis=1) * w_rows.astype(F32), axis=1)
        s_attn = s_attn / lax.dynamic_slice_in_dim(attn_gain, first, count)
        columns = [[], [], []]
        for per, part in zip(PARTS, s_parts):
            for group, column in zip(columns, jnp.split(part, [QUERIES * per * HEAD, (QUERIES + 1) * per * HEAD], axis=1)):
                group.append(column)
        s_query, s_key, s_value = [jnp.concatenate(group, axis=1) for group in columns]

    return (
        output,
        d_tokens,
        s_attn,
        s_query,
        s_key,
        s_value,
        s_out,
        s_small[:, experts],
        s_small[:, :experts],
        s_gate[None],
        s_up[None],
        s_down[None],
    )


def solution(mesh):
    rows, whole, slices = P(("rep", "ep"), None), P(), P("ep", None)
    expert = P("ep", None, None)
    return jax.shard_map(
        local,
        mesh=mesh,
        in_specs=(rows,) * 3 + (whole,) * 7 + (expert,) * 3 + (rows,),
        out_specs=(rows, rows, P("ep")) + (slices,) * 4 + (P("ep"), slices) + (expert,) * 3,
        check_vma=False,
    )
```

```python
import functools
import math

import jax
import jax.numpy as jnp
import numpy as np
from jax import lax
from jax.experimental import pallas as pl
from jax.experimental.pallas import tpu as pltpu
from jax.sharding import PartitionSpec as P

D = 1536
HEADS = 24
KV = 8
HEAD = 64
LEN = 1024
PIECE = 256
QUERIES = HEADS // KV
WIDE = 256
TILE = 256
GROUP = 4
PARTS = (2, 4, 2)
LANES = 128
WIDTH = D + LANES

eps = 1e-06
theta_base = 10000.0
masked_score = -1e30
score_scale = HEAD ** (-0.5)
two_scale = score_scale * math.log2(math.e)

F32 = jnp.float32
BF16 = jnp.bfloat16
NN = (((1,), (0,)), ((), ()))
NT = (((1,), (1,)), ((), ()))
TN = (((0,), (0,)), ((), ()))
ANY = pl.BlockSpec(memory_space=pl.ANY)
SMEM = pl.BlockSpec(memory_space=pltpu.SMEM)


def dot(left, right, dims):
    return lax.dot_general(left, right, dims, preferred_element_type=F32)


def shaped(shape, dtype):
    return jax.ShapeDtypeStruct(shape, dtype)


def estimate(micros):
    return pl.CostEstimate(flops=int(micros * 1e10), bytes_accessed=int(micros * 1e6), transcendentals=0)


def rms_scale(values):
    return lax.rsqrt(jnp.mean(values * values, axis=-1, keepdims=True) + eps)


def rotary_tables():
    half_head = HEAD // 2
    frequency = theta_base ** (-(np.arange(half_head, dtype=np.float64) * 2.0) / HEAD)
    angles = frequency[:, None] * np.arange(LEN, dtype=np.float64)[None, :]
    return np.cos(angles).astype(np.float32), np.sin(angles).astype(np.float32)


def turn(values, cosine, sine):
    first, second = values[: HEAD // 2], values[HEAD // 2 :]
    return jnp.concatenate([first * cosine - second * sine, second * cosine + first * sine], axis=0)


def turn_back(grads, cosine, sine):
    first, second = grads[: HEAD // 2], grads[HEAD // 2 :]
    return jnp.concatenate([first * cosine + second * sine, second * cosine - first * sine], axis=0)


def fill_bias(pieces, bias):
    for block in range(LEN // WIDE):
        first = block * WIDE
        shape = bias.shape[1:]
        key = lax.broadcasted_iota(jnp.int32, shape, 0) + first
        query = lax.broadcasted_iota(jnp.int32, shape, 1) + first
        allowed = key <= query
        for piece in range(pieces.shape[1]):
            start = pieces[0, piece]
            low, high = jnp.minimum(key, query), jnp.maximum(key, query)
            allowed = allowed | ((low >= start) & (high < start + PIECE))
        bias[block] = jnp.where(allowed, 0.0, masked_score)


def key_span(block):
    return block * WIDE, min((block + 2) * WIDE, LEN)


def rows_at(place):
    return pl.BlockSpec((HEAD, LEN), lambda *grid: (place(*grid), 0))


def packed_row(head, kind):
    row = 0
    for part, per in enumerate(PARTS):
        first = sum(PARTS[:part])
        inner = head - first
        here = {3: QUERIES * per + inner, 4: (QUERIES + 1) * per + inner}.get(kind, QUERIES * inner + kind)
        row = jnp.where(inner >= 0, (QUERIES + 2) * first + here, row)
    return row


def table_spec():
    return pl.BlockSpec((HEAD // 2, LEN), lambda *grid: (0, 0))


def attend_kernel(pieces, q0, q1, q2, k_in, v_in, cosine, sine, attn, q_out, k_out, v_out, lse, bias):
    @pl.when(pl.program_id(0) == 0)
    def _():
        fill_bias(pieces, bias)

    cos, sin = cosine[...], sine[...]
    k_rot = turn(k_in[...], cos, sin) * two_scale
    k_out[...] = k_rot.astype(BF16)
    keys = k_rot.T.astype(BF16)
    values = v_in[...].astype(BF16)
    v_out[...] = values
    for head, q_in in enumerate((q0, q1, q2)):
        rows = pl.ds(head * HEAD, HEAD)
        q_rot = turn(q_in[...], cos, sin).astype(BF16)
        q_out[rows, :] = q_rot
        for block in range(LEN // WIDE):
            columns = pl.ds(block * WIDE, WIDE)
            first, last = key_span(block)
            queries = q_rot[:, block * WIDE : (block + 1) * WIDE]
            spans = [(first, last)] + ([(0, first)] if first > 0 else [])
            scores = [dot(keys[a:b], queries, NN) for a, b in spans]
            scores[0] = scores[0] + bias[block, : last - first]
            highest = functools.reduce(jnp.maximum, [jnp.max(s, axis=0, keepdims=True) for s in scores])
            weights = [jnp.exp2(s - highest) for s in scores]
            total = sum(jnp.sum(w, axis=0, keepdims=True) for w in weights)
            mixed = sum(dot(values[:, a:b], w.astype(BF16), NN) for (a, b), w in zip(spans, weights)) / total
            attn[rows, columns] = mixed.astype(BF16)
            lse[head : head + 1, columns] = highest + jnp.log2(total)


def attend_call(pieces, packed, cosine, sine):
    rows = lambda count: pl.BlockSpec((count, LEN), lambda i: (i, 0))
    width = QUERIES * HEAD
    return pl.pallas_call(
        attend_kernel,
        grid=(KV,),
        in_specs=[SMEM]
        + [rows_at(functools.partial(packed_row, kind=kind)) for kind in range(5)]
        + [table_spec(), table_spec()],
        out_specs=[rows(width), rows(width), rows(HEAD), rows(HEAD), rows(8)],
        out_shape=[
            shaped((D, LEN), BF16),
            shaped((D, LEN), BF16),
            shaped((KV * HEAD, LEN), BF16),
            shaped((KV * HEAD, LEN), BF16),
            shaped((KV * 8, LEN), F32),
        ],
        scratch_shapes=[pltpu.VMEM((LEN // WIDE, 2 * WIDE, WIDE), F32)],
        compiler_params=pltpu.CompilerParams(vmem_limit_bytes=48 << 20),
        cost_estimate=estimate(25),
        name="attend",
    )(pieces, *[packed] * 5, cosine, sine)


def with_parts(columns, row):
    rank = lax.broadcasted_iota(jnp.int32, columns.shape, 0)
    high = row.astype(BF16).astype(F32)
    middle = (row - high).astype(BF16).astype(F32)
    parts = jnp.where(rank == 0, high, jnp.where(rank == 1, middle, jnp.where(rank == 2, row - high - middle, 0.0)))
    return jnp.concatenate([columns, parts.astype(BF16)], axis=0)


def attend_back_kernel(
    mark, pieces, q_in, k_in, v_in, do_in, attn, lse, cosine, sine, out, bias, keys_kept, values_kept, dk_sum, dv_sum
):
    kind = pl.program_id(1)

    @pl.when((pl.program_id(0) == 0) & (kind == 0))
    def _():
        fill_bias(pieces, bias)

    cos, sin = cosine[...], sine[...]

    @pl.when(kind == 0)
    def _():
        tail = jnp.where(lax.broadcasted_iota(jnp.int32, (LEN, HEAD), 1) < 3, -1.0, 0.0)
        for kept, ref in ((keys_kept, k_in), (values_kept, v_in)):
            kept[...] = jnp.concatenate([ref[...].astype(F32).T, tail], axis=1).astype(BF16)
        dk_sum[...] = jnp.zeros_like(dk_sum)
        dv_sum[...] = jnp.zeros_like(dv_sum)

    @pl.when(kind < QUERIES)
    def _():
        k_cols, keys, values = k_in[...], keys_kept[...], values_kept[...]
        q_cols, do_cols = q_in[...], do_in[...]
        q_rows = q_cols.astype(F32).T.astype(BF16)
        do_rows = do_cols.astype(F32).T.astype(BF16)
        delta = jnp.sum(do_cols.astype(F32) * attn[...].astype(F32), axis=0, keepdims=True)
        q_wide = with_parts(q_cols, lse[pl.ds(kind, 1), :])
        do_wide = with_parts(do_cols, delta)
        for block in range(LEN // WIDE):
            part = slice(block * WIDE, (block + 1) * WIDE)
            first, last = key_span(block)
            d_query = 0.0
            for a, b in [(first, last)] + ([(0, first)] if first > 0 else []):
                scores = dot(keys[a:b], q_wide[:, part], NN)
                if a == first:
                    scores = scores + bias[block, : b - a]
                probs = jnp.exp2(scores)
                d_scores = (probs * dot(values[a:b], do_wide[:, part], NN)).astype(BF16)
                dv_sum[a:b] += dot(probs.astype(BF16), do_rows[part], NN)
                dk_sum[a:b] += dot(d_scores, q_rows[part], NN)
                d_query = d_query + dot(k_cols[:, a:b], d_scores, NN)
            out[:, part] = turn_back(d_query * math.log(2.0), cos[:, part], sin[:, part]).astype(BF16)

    @pl.when(kind == QUERIES)
    def _():
        out[...] = turn_back(dk_sum[...].T * score_scale, cos, sin).astype(BF16)

    @pl.when(kind == QUERIES + 1)
    def _():
        out[...] = dv_sum[...].T.astype(BF16)


def attend_back_call(part, mark, pieces, q_in, k_in, v_in, do_in, attn, lse, cosine, sine):
    per, first = PARTS[part], sum(PARTS[:part])
    query = rows_at(lambda i, j: (first + i) * QUERIES + jnp.minimum(j, QUERIES - 1))
    key = rows_at(lambda i, j: first + i)

    def place(i, j):
        tail = jnp.where(j == QUERIES, QUERIES * per + i, (QUERIES + 1) * per + i)
        return jnp.where(j < QUERIES, QUERIES * i + j, tail)

    return pl.pallas_call(
        attend_back_kernel,
        grid=(per, QUERIES + 2),
        in_specs=[ANY, SMEM, query, key, key, query, query, pl.BlockSpec((8, LEN), lambda i, j: (first + i, 0))]
        + [table_spec(), table_spec()],
        out_specs=rows_at(place),
        out_shape=shaped(((QUERIES + 2) * per * HEAD, LEN), BF16),
        scratch_shapes=[
            pltpu.VMEM((LEN // WIDE, 2 * WIDE, WIDE), F32),
            pltpu.VMEM((LEN, 2 * HEAD), BF16),
            pltpu.VMEM((LEN, 2 * HEAD), BF16),
            pltpu.VMEM((LEN, HEAD), F32),
            pltpu.VMEM((LEN, HEAD), F32),
        ],
        compiler_params=pltpu.CompilerParams(vmem_limit_bytes=48 << 20),
        cost_estimate=estimate(15),
        name="attend_back",
    )(mark, pieces, q_in, k_in, v_in, do_in, attn, lse, cosine, sine)


def split_lanes(values, experts):
    lanes = lax.broadcasted_iota(jnp.int32, values.shape, 1)
    high = values.astype(BF16).astype(F32)
    return jnp.where(lanes < experts, high, jnp.where(lanes < 2 * experts, values - high, 0.0)).astype(BF16)


def join_lanes(parts, experts):
    return parts + pltpu.roll(parts, LANES - experts, 1)


def route_kernel(experts, tokens, attn, w_out, gain, w_router, routes, residual, rows, gate):
    values = tokens[...].astype(F32) + dot(attn[...], w_out[...], TN)
    residual[...] = values
    normed = (values * rms_scale(values) * gain[...]).astype(BF16)
    logits = dot(normed, w_router[...], NN)
    lanes = lax.broadcasted_iota(jnp.int32, logits.shape, 1)
    expert = lax.rem(lanes, experts)
    chosen = lanes < 0
    for k in range(routes.shape[1]):
        chosen = chosen | (routes[:, k : k + 1] == expert)
    chosen = chosen & (lanes < 2 * experts)
    logits = jnp.where(chosen, logits, masked_score)
    weights = jnp.exp(logits - jnp.max(logits, axis=1, keepdims=True))
    share = weights / (0.5 * jnp.sum(weights, axis=1, keepdims=True))
    gate[...] = share
    rows[:, :D] = normed
    rows[:, D:] = split_lanes(share, experts)


def route_call(experts, tokens, attn, w_out, gain, w_router, routes):
    rows = lambda cols: pl.BlockSpec((TILE, cols), lambda i: (i, 0))
    whole = lambda *shape: pl.BlockSpec(shape, lambda i: (0, 0), pipeline_mode=pl.Buffered(1))
    return pl.pallas_call(
        functools.partial(route_kernel, experts),
        grid=(LEN // TILE,),
        in_specs=[rows(D), pl.BlockSpec((D, TILE), lambda i: (0, i)), whole(D, D), whole(1, D), whole(D, LANES)]
        + [rows(routes.shape[1])],
        out_specs=[rows(D), rows(WIDTH), rows(LANES)],
        out_shape=[shaped((LEN, D), F32), shaped((LEN, WIDTH), BF16), shaped((LEN, LANES), F32)],
        compiler_params=pltpu.CompilerParams(vmem_limit_bytes=60 << 20),
        cost_estimate=estimate(5),
        name="route",
    )(tokens, attn, w_out, gain, w_router, routes)


def merge_kernel(experts, mark, kept, kept_share, landed, out):
    out[:, :D] = (kept[...].astype(F32) + landed[:, :D].astype(F32)).astype(BF16)
    if kept_share is not None:
        share = kept_share[...] + join_lanes(landed[:, D:].astype(F32), experts)
        share = jnp.where(lax.broadcasted_iota(jnp.int32, share.shape, 1) < experts, share, 0.0)
        out[:, D:] = split_lanes(share + pltpu.roll(share, experts, 1), experts)


def merge_call(experts, mark, kept, kept_share, landed):
    rows = lambda cols: pl.BlockSpec((TILE, cols), lambda i: (i, 0))
    width = landed.shape[1]
    kernel = functools.partial(merge_kernel, experts)
    if kept_share is None:
        kernel = lambda mark, kept, landed, out: merge_kernel(experts, mark, kept, None, landed, out)
    return pl.pallas_call(
        kernel,
        grid=(LEN // TILE,),
        in_specs=[ANY, rows(D)] + ([] if kept_share is None else [rows(LANES)]) + [rows(width)],
        out_specs=rows(width),
        out_shape=shaped((LEN, width), BF16),
        compiler_params=pltpu.CompilerParams(vmem_limit_bytes=32 << 20),
        cost_estimate=estimate(3),
        name="merge",
    )(*[ref for ref in (mark, kept, kept_share, landed) if ref is not None])


def back_kernel(
    experts, mark, kept, kept_share, core, chip, residual, cotangent, gate, gain, w_router, w_out, d_res, d_mix, d_attn, d_router
):
    @pl.when(pl.program_id(0) == 0)
    def _():
        d_router[...] = jnp.zeros_like(d_router)

    landed = core[:, D:].astype(F32) + chip[:, D:].astype(F32)
    share = kept_share[...] + join_lanes(landed, experts)
    first = lax.broadcasted_iota(jnp.int32, share.shape, 1) < experts
    gates = jnp.where(first, gate[...], 0.0)
    inner = jnp.sum(gates * share, axis=1, keepdims=True)
    d_logits = jnp.where(first, gates * (share - inner), 0.0).astype(BF16)
    d_normed = kept[...].astype(F32) + core[:, :D].astype(F32) + chip[:, :D].astype(F32) + dot(d_logits, w_router[...], NT)
    values, gains = residual[...], gain[...]
    scale = rms_scale(values)
    norm = values * scale
    d_gain = jnp.sum(d_normed * norm, axis=0, keepdims=True)
    scaled = d_normed * gains
    d_values = cotangent[...].astype(F32) + scale * (scaled - norm * jnp.mean(scaled * norm, axis=1, keepdims=True))
    d_res[...] = d_values
    mixed = d_values.astype(BF16)
    d_mix[...] = mixed
    d_attn[...] = dot(w_out[...], mixed, NT).astype(BF16)
    d_router[...] += dot(d_logits, (norm * gains).astype(BF16), TN)
    d_router[experts : experts + 1] += d_gain


def back_call(experts, mark, kept, kept_share, core, chip, residual, cotangent, gate, gain, w_router, w_out):
    rows = lambda cols: pl.BlockSpec((TILE, cols), lambda i: (i, 0))
    whole = lambda *shape: pl.BlockSpec(shape, lambda i: (0, 0), pipeline_mode=pl.Buffered(1))
    return pl.pallas_call(
        functools.partial(back_kernel, experts),
        grid=(LEN // TILE,),
        in_specs=[ANY, rows(D), rows(LANES), rows(WIDTH), rows(WIDTH), rows(D), rows(D), rows(LANES)]
        + [whole(1, D), whole(D, LANES), whole(D, D)],
        out_specs=[rows(D), rows(D), pl.BlockSpec((D, TILE), lambda i: (0, i)), whole(LANES, D)],
        out_shape=[
            shaped((LEN, D), F32),
            shaped((LEN, D), BF16),
            shaped((D, LEN), BF16),
            shaped((LANES, D), F32),
        ],
        compiler_params=pltpu.CompilerParams(vmem_limit_bytes=48 << 20),
        cost_estimate=estimate(8),
        name="back",
    )(mark, kept, kept_share, core, chip, residual, cotangent, gate, gain, w_router, w_out)


def out_kernel(mark, attn, mixed, small, out):
    out[:, :D] = dot(attn[...], mixed[...], NN).astype(BF16)
    out[:, D:] = small[...].T.astype(BF16)


def out_call(mark, attn, mixed, small):
    return pl.pallas_call(
        out_kernel,
        grid=(D // TILE,),
        in_specs=[
            ANY,
            pl.BlockSpec((TILE, LEN), lambda i: (i, 0)),
            pl.BlockSpec((LEN, D), lambda i: (0, 0), pipeline_mode=pl.Buffered(1)),
            pl.BlockSpec((LANES, TILE), lambda i: (0, i)),
        ],
        out_specs=pl.BlockSpec((TILE, WIDTH), lambda i: (i, 0)),
        out_shape=shaped((D, WIDTH), BF16),
        compiler_params=pltpu.CompilerParams(vmem_limit_bytes=32 << 20),
        cost_estimate=estimate(5),
        name="out_grad",
    )(mark, attn, mixed, small)


def pause_kernel(mark, out):
    out[...] = mark[...]


def pause_call(mark):
    return pl.pallas_call(
        pause_kernel, out_shape=shaped(mark.shape, mark.dtype), cost_estimate=estimate(10), name="pause"
    )(mark)


def expert_kernel(count, experts, fresh, first, last_tokens, steps, ids, mark, *rest):
    rest = list(rest)

    def take(number):
        taken = rest[:number]
        del rest[:number]
        return taken

    n2, up = take(2), take(2)
    w_in = [take(2) for _ in range(count)]
    sums_in = [[] if new else take(2) for new in fresh]
    carry_in = [] if first else take(3)
    outs = take(5) if last_tokens else take(3)
    sums_out = [take(2) for _ in range(count)]
    weights, sums = take(1)[0], take(1)[0]
    low, sem = rest
    half = weights.shape[1] // 6
    width = 2 * half
    step = pl.program_id(0)
    ahead = step < steps // 2

    def pieces_of(parts, whole):
        return [
            (ref.at[pl.ds(kind * half, half)], whole.at[pl.ds((2 * kind + part) * half, half)])
            for kind in range(3)
            for part, ref in enumerate(parts)
        ]

    def copies_of(pairs, lane):
        return [pltpu.make_async_copy(a, b, sem.at[lane, n]) for n, (a, b) in enumerate(pairs)]

    loads = [copies_of(pieces_of(w_in[e], weights.at[e]), e) for e in range(count)]
    prior = [[] if fresh[e] else copies_of(pieces_of(sums_in[e], low.at[e]), count + e) for e in range(count)]
    stores = [copies_of([(b, a) for a, b in pieces_of(sums_out[e], low.at[e])], e) for e in range(count)]

    @pl.when(step == 0)
    def _():
        for copy in sum(loads + prior, []):
            copy.start()
        for copy in sum(loads, []):
            copy.wait()

    rows = jnp.where(ahead, n2[0][...], n2[1][...])
    grads = jnp.where(ahead, up[0][...], up[1][...])
    rows, gates = rows[:, :D], rows[:, D:].astype(F32)
    lanes = lax.broadcasted_iota(jnp.int32, gates.shape, 1)
    mixed = d_rows = d_shares = None
    add = lambda total, value: value if total is None else total + value
    for e in range(count):
        w_both, w_down = weights.at[e, : 2 * width], weights.at[e, 2 * width :]
        hit = (lanes == ids[e]) | (lanes == ids[e] + experts)
        share = jnp.sum(jnp.where(hit, gates, 0.0), axis=1, keepdims=True)
        acts = dot(rows, w_both[...], NT)
        gate_act, up_act = acts[:, :width], acts[:, width:]
        d_plain = dot(grads, w_down[...], NT)
        sigmoid = 1.0 / (1.0 + jnp.exp(-gate_act))
        silu = gate_act * sigmoid
        hidden = silu * up_act
        shared = (share * hidden).astype(BF16)
        d_share = jnp.sum(hidden * d_plain, axis=1, keepdims=True)
        d_hidden = share * d_plain
        d_gate = (d_hidden * up_act * (sigmoid + silu * (1.0 - sigmoid))).astype(BF16)
        d_up = (d_hidden * silu).astype(BF16)
        d_both = jnp.concatenate([d_gate, d_up], axis=1)
        mixed = add(mixed, dot(shared, w_down[...], NN))
        d_rows = add(d_rows, dot(d_both, w_both[...], NN))
        d_shares = add(d_shares, jnp.where(hit, d_share, 0.0))
        before = jnp.where(step == 0, 0.0, sums[e, : 2 * width])
        sums[e, : 2 * width] = before + dot(d_both, rows, TN)
        before = jnp.where(step == 0, 0.0, sums[e, 2 * width :])
        sums[e, 2 * width :] = before + dot(shared, grads, TN)

        @pl.when(step == steps - 1)
        def _(e=e):
            for copy in prior[e]:
                copy.wait()
            low[e] = (sums[e] if fresh[e] else sums[e] + low[e].astype(F32)).astype(BF16)
            for copy in stores[e]:
                copy.start()

    results = [mixed, d_rows, d_shares]
    if not first:
        results = [result + ref[...].astype(F32) for result, ref in zip(results, carry_in)]
    if last_tokens:

        @pl.when(ahead)
        def _():
            for ref, result in zip(outs[:3], results):
                ref[...] = result.astype(ref.dtype)

        @pl.when(jnp.logical_not(ahead))
        def _():
            outs[3][...] = results[0].astype(BF16)
            outs[4][:, :D] = results[1].astype(BF16)
            outs[4][:, D:] = split_lanes(results[2], experts)
    else:
        for ref, result in zip(outs, results):
            ref[...] = result.astype(ref.dtype)

    @pl.when(step == steps - 1)
    def _():
        for copy in sum(stores, []):
            copy.wait()


def expert_call(ids, mark, experts, n2, up, weights, sums, carry, last_tokens):
    tokens, height, count = 2 * n2[0].shape[0], weights[0][0].shape[0], len(weights)
    steps = tokens // TILE
    rows = lambda cols: pl.BlockSpec((TILE, cols), lambda i: (i, 0))
    near = lambda cols: pl.BlockSpec((TILE, cols), lambda i: (jnp.minimum(i, steps // 2 - 1), 0))
    far = lambda cols: pl.BlockSpec((TILE, cols), lambda i: (jnp.maximum(i - steps // 2, 0), 0))
    ins = [ids, mark, *n2, *up] + [w for pair in weights for w in pair]
    specs = [SMEM, ANY, near(WIDTH), far(WIDTH), near(D), far(D)] + [ANY] * (2 * count)
    fresh, first = [pair is None for pair in sums], carry is None
    columns = (D, D, LANES)
    if last_tokens:
        outs = [shaped((tokens // 2, c), t) for c, t in zip(columns, (BF16, BF16, F32))]
        outs += [shaped((tokens // 2, c), BF16) for c in (D, WIDTH)]
        out_specs = [near(c) for c in columns] + [far(D), far(WIDTH)]
    else:
        outs = [shaped((tokens, c), t) for c, t in zip(columns, (BF16, F32, F32))]
        out_specs = [rows(c) for c in columns]
    aliases = {}
    for pair in sums:
        if pair is not None:
            ins += pair
            specs += [ANY, ANY]
    if not first:
        if not last_tokens:
            aliases.update({len(ins) + k: k for k in range(3)})
        ins += carry
        specs += [rows(c) for c in columns]
    tokens_out = len(outs)
    for _ in range(count):
        outs += [shaped((height, D), BF16)] * 2
        out_specs += [ANY, ANY]
    scratch = [pltpu.VMEM((count, 2 * height, D), BF16), pltpu.VMEM((count, 2 * height, D), F32)]
    scratch.append(pltpu.VMEM((count, 2 * height, D), BF16))
    scratch.append(pltpu.SemaphoreType.DMA((2 * count, 6)))
    done = pl.pallas_call(
        functools.partial(expert_kernel, count, experts, fresh, first, last_tokens, steps),
        grid=(steps,),
        in_specs=specs,
        out_specs=out_specs,
        out_shape=outs,
        scratch_shapes=scratch,
        input_output_aliases=aliases,
        compiler_params=pltpu.CompilerParams(vmem_limit_bytes=63 << 20),
        cost_estimate=estimate(15 * count),
        name="expert",
    )(*ins)
    return list(done[:tokens_out]), [tuple(done[tokens_out + 2 * e : tokens_out + 2 * e + 2]) for e in range(count)]


def join_kernel(side, held, landed, gate, up, down):
    here = pl.program_id(0) == 0
    rows = jnp.where(here, held[...], landed[...]).astype(F32)
    half = down.shape[0]
    gate[...] = rows[:half].T
    up[...] = rows[half : 2 * half].T
    down[...] = rows[2 * half :]


def join_call(side, held, landed):
    half = held.shape[0] // 3
    whole = pl.BlockSpec(held.shape, lambda i, side: (0, 0))
    columns = pl.BlockSpec((D, half), lambda i, side: (0, lax.rem(side[0] + i, 2)))
    return pl.pallas_call(
        join_kernel,
        grid_spec=pltpu.PrefetchScalarGridSpec(
            num_scalar_prefetch=1,
            grid=(2,),
            in_specs=[whole, whole],
            out_specs=[columns, columns, pl.BlockSpec((half, D), lambda i, side: (lax.rem(side[0] + i, 2), 0))],
        ),
        out_shape=[shaped((D, 2 * half), F32), shaped((D, 2 * half), F32), shaped((2 * half, D), F32)],
        compiler_params=pltpu.CompilerParams(vmem_limit_bytes=48 << 20),
        cost_estimate=estimate(5),
        name="join",
    )(side, held, landed)


def after(values, *others):
    return lax.optimization_barrier((values, *others))[0]


class Task:
    def __init__(self, steps):
        self.steps, self.result, self.over = steps, None, False

    def step(self):
        if self.over:
            return []
        try:
            return [next(self.steps)]
        except StopIteration as stop:
            self.result, self.over = stop.value, True
            return [self.result]

    def finish(self):
        while not self.over:
            self.step()
        return self.result


def local(
    tokens,
    routes,
    pieces,
    attn_gain,
    w_query,
    w_key,
    w_value,
    w_out,
    ffn_gain,
    w_router,
    expert_gate,
    expert_up,
    expert_down,
    cotangent,
):
    shards, reps = lax.axis_size("ep"), lax.axis_size("rep")
    experts = w_router.shape[1]
    slots = shards // GROUP
    place = lax.axis_index("ep")
    side = lax.axis_index("rep") % 2

    def swap(values, bits):
        return lax.ppermute(values, "ep", [(i, i ^ bits) for i in range(shards)])

    def swap_rep(values, bits=1):
        return lax.ppermute(values, "rep", [(i, i ^ bits) for i in range(reps)])


    def reduce_reps(values, bits=1):
        while bits < reps:
            values = values.astype(BF16)
            landed = swap_rep(values, bits)
            yield values
            values = values.astype(F32) + hold(landed).astype(F32)
            bits *= 2
        return values

    def reduce_rows(values):
        values = values.reshape(shards, -1, values.shape[1])
        bits = 1
        while bits < shards:
            values = values.reshape(values.shape[0] // 2, 2, *values.shape[1:])
            bit = (place // bits) % 2
            kept, sent = [
                lax.dynamic_index_in_dim(values, index, axis=1, keepdims=False) for index in (bit, 1 - bit)
            ]
            landed = swap(sent, bits)
            yield sent
            values = (kept.astype(F32) + hold(landed).astype(F32)).astype(BF16)
            bits *= 2
        return (yield from reduce_reps(values[0]))

    def sum_steps(slot, own, other):
        other = hold(other)
        landed = swap_rep(other)
        yield other
        own = own.astype(F32) + hold(landed).astype(F32)
        if slot == 0:
            return own
        own = own.astype(BF16)
        landed = swap(own, slot * GROUP)
        yield own
        return hold(landed)

    with jax.named_scope("weights_out"):
        half = expert_gate.shape[2] // 2
        whole = [expert_gate[0].T, expert_up[0].T, expert_down[0]]
        halves = [jnp.concatenate([w[k * half : (k + 1) * half] for w in whole]) for k in range(2)]
        mine = jnp.where(side == 0, halves[0], halves[1])
        theirs = jnp.where(side == 0, halves[1], halves[0])
        tokens, mine, theirs = lax.optimization_barrier((tokens, mine, theirs))
        landed = {slot: swap(mine, slot * GROUP) for slot in (2, 1)}

    with jax.named_scope("cotangent_out"):
        grads_next = swap(cotangent, 2)
        grads_in = [(cotangent, swap(cotangent, 1)), None]

    with jax.named_scope("attention"):
        inputs = tokens.astype(F32)
        scale_one = rms_scale(inputs)
        norm_one = inputs * scale_one
        normed_one = (norm_one * attn_gain).astype(BF16)
        cuts, first = [], 0
        for per in PARTS:
            for w, wide in ((w_query, QUERIES), (w_key, 1), (w_value, 1)):
                cuts.append(w[:, first * wide * HEAD : (first + per) * wide * HEAD])
            first += per
        w_all = jnp.concatenate(cuts, axis=1)
        packed = dot(w_all, normed_one, (((0,), (1,)), ((), ())))
        cosine, sine = [jnp.asarray(table) for table in rotary_tables()]
        attn, query_rot, key_rot, value_low, lse = attend_call(pieces, packed, cosine, sine)
        attn = after(attn, grads_next, grads_in[0][1])

    with jax.named_scope("cotangent_out"):
        grads_in[1] = (grads_next, swap(after(grads_next, attn), 1))

    with jax.named_scope("routing"):
        pad = jnp.zeros((D, LANES - 2 * experts), BF16)
        router_twice = jnp.concatenate([w_router, w_router, pad], axis=1)
        gain_two = ffn_gain.reshape(1, D)
        residual, rows, gate = route_call(experts, tokens, attn, w_out, gain_two, router_twice, routes)
        rows, _, held, near = lax.optimization_barrier((rows, grads_in[1][1], landed[2], landed[1]))
        rows_next = swap(rows, 2)
        rows_in = [(rows, swap(rows, 1)), None]

    with jax.named_scope("weights_out"):
        weights = {0: (mine, theirs), 2: (held, swap_rep(held))}
        late = after(mine, rows)
        landed = {slot: swap(late, slot * GROUP) for slot in range(3, slots)}
        ids = [((place // GROUP) ^ slot) * GROUP + place % GROUP for slot in range(slots)]
        ids = [expert.astype(jnp.int32) for expert in ids]

    carry, sums, tasks = [None, None], [None] * slots, [None] * slots
    mark, point = after(jnp.zeros((8, LANES), F32), rows), rows

    def tick(*arrays):
        nonlocal mark
        mark = after(mark, *arrays)

    def hold(values):
        return after(values, point)

    def pause():
        nonlocal mark
        mark = pause_call(mark)

    def pulse():
        return swap(mark, 1)

    def passed(value, beat=None):
        nonlocal mark, point
        if beat is not None:
            mark = mark + beat
        mark, point = after(mark, value), value

    def run(chip, group, last=False, beats=True):
        beat = pulse() if beats else None
        carry[chip], done = expert_call(
            jnp.stack([ids[slot] for slot in group]),
            mark,
            experts,
            rows_in[chip],
            grads_in[chip],
            [weights[slot] for slot in group],
            [sums[slot] for slot in group],
            carry[chip],
            last,
        )
        passed(carry[chip][2], beat)
        for slot, pair in zip(group, done):
            if sums[slot] is not None:
                tasks[slot] = Task(sum_steps(slot, *pair))
            sums[slot] = pair

    def arrive(slot):
        tick(landed[slot])
        held = hold(landed[slot])
        weights[slot] = (held, swap_rep(held))

    with jax.named_scope("experts"):
        run(0, [0], beats=False)
        tick(weights[2][1])
        near = hold(near)
        weights[1] = (near, swap_rep(near))
        run(0, [2])
        tick(rows_next, weights[1][1])
        for slot in range(3, slots):
            arrive(slot)
        rows_in[1] = (rows_next, swap(hold(rows_next), 1))
        pause()
        tick(rows_in[1][1])
        run(1, [0, 2])
        tick(*[weights[slot][1] for slot in range(3, slots)])
        tasks[2].step()
        pairs = [[slot, slot + 1] for slot in range(3, slots - 1, 2)] + [[slots - 1, 1]]
        for pair in pairs:
            last = pair == pairs[-1]
            run(1, pair, last)
            if last:
                there_landed = swap(hold(carry[1][4]), 1)
                pause()
                there = merge_call(experts, mark, carry[1][1], carry[1][2], there_landed)
                d_next = swap(there, 2)
                tick(there, *tasks[2].step())
                tasks[0].step()
                mix_landed = swap(hold(carry[1][3]), 1)
            run(0, pair[:1])
            if last:
                mix_there = merge_call(experts, mark, carry[1][0], None, mix_landed)
                tick(mix_there, *tasks[0].step())
            tasks[pair[0]].step()
            run(0, pair[1:], last)

    with jax.named_scope("routing_back"):
        d_core = swap(hold(carry[0][4]), 1)
        tasks[1].step()
        pause()
        tick(d_core, d_next, *[array for task in tasks[2:] for array in task.step()])
        point = mark
        mix_home = swap(hold(mix_there), 2)
        mix_core = swap(hold(carry[0][3]), 1)
        d_residual, d_mixed, d_attn, d_small = back_call(
            experts, mark, carry[0][1], carry[0][2], d_core, d_next, residual, cotangent, gate, gain_two, router_twice, w_out
        )
        passed(d_small)
        tick(mix_core)
        d_out = out_call(mark, attn, d_mixed, d_small)
        passed(d_out)

    with jax.named_scope("attention_back"):
        in_dims = (((0,), (1,)), ((), ()))
        out_task, w_tasks, d_packed = Task(reduce_rows(d_out)), [], []
        tick(*out_task.step())
        for part in range(len(PARTS)):
            d_packed.append(
                attend_back_call(part, mark, pieces, query_rot, key_rot, value_low, d_attn, attn, lse, cosine, sine)
            )
            passed(d_packed[-1])
            tick(*[array for task in w_tasks + [out_task] * (part < 2) for array in task.step()])
            if part == 0:
                tick(*tasks[1].step())
            w_tasks.append(Task(reduce_rows(dot(normed_one, d_packed[-1], in_dims).astype(BF16))))
            if part < len(PARTS) - 1:
                tick(*w_tasks[-1].step())

    with jax.named_scope("sums_experts"):
        total = tasks[0].finish()
        for task in tasks[1:]:
            total = total + task.finish().astype(F32)
        total = Task(reduce_reps(total, 2)).finish().astype(BF16)
        total_landed = swap_rep(total)

    with jax.named_scope("tail"):
        mark = after(mark, total)
        d_normed_one, first = None, 0
        turns = [[w_tasks[2], out_task], [w_tasks[1], w_tasks[0]], [out_task]]
        stepped = w_tasks[2].step()
        for part, grads in enumerate(d_packed):
            span = grads.shape[0]
            grads = after(grads, mark, *stepped)
            term = dot(grads, w_all[:, first : first + span], in_dims)
            d_normed_one = point = term if part == 0 else d_normed_one + term
            first += span
            stepped = [array for task in turns[part] for array in task.step()]
        mix_home = after(mix_home, point, *stepped)
        output = (residual + carry[0][0].astype(F32) + mix_core.astype(F32) + mix_home.astype(F32)).astype(BF16)
        point = output
        stepped = [array for task in (w_tasks[2], w_tasks[1], w_tasks[0]) for array in task.step()]
        d_normed_one = after(d_normed_one, output, *stepped)
        scaled_one = d_normed_one * attn_gain
        d_tokens = point = d_residual + scale_one * (
            scaled_one - norm_one * jnp.mean(scaled_one * norm_one, axis=-1, keepdims=True)
        )
        stepped = [array for task in (w_tasks[2], w_tasks[1], out_task) for array in task.step()]
        total, total_landed = lax.optimization_barrier((total, total_landed, point, *stepped))[:2]
        s_gate, s_up, s_down = join_call(side.astype(jnp.int32).reshape(1), total, total_landed)
        point = s_down

    with jax.named_scope("sums_rest"):
        s_mixed = out_task.finish()
        s_out, s_small = s_mixed[:, :D], s_mixed[:, D:]
        count = s_out.shape[0]
        first = place * count
        s_parts = [task.finish() for task in w_tasks]
        w_rows = lax.dynamic_slice_in_dim(w_all, first, count)
        s_attn = jnp.sum(jnp.concatenate(s_parts, axis=1) * w_rows.astype(F32), axis=1)
        s_attn = s_attn / lax.dynamic_slice_in_dim(attn_gain, first, count)
        columns = [[], [], []]
        for per, part in zip(PARTS, s_parts):
            for group, column in zip(columns, jnp.split(part, [QUERIES * per * HEAD, (QUERIES + 1) * per * HEAD], axis=1)):
                group.append(column)
        s_query, s_key, s_value = [jnp.concatenate(group, axis=1) for group in columns]

    return (
        output,
        d_tokens,
        s_attn,
        s_query,
        s_key,
        s_value,
        s_out,
        s_small[:, experts],
        s_small[:, :experts],
        s_gate[None],
        s_up[None],
        s_down[None],
    )


def solution(mesh):
    rows, whole, slices = P(("rep", "ep"), None), P(), P("ep", None)
    expert = P("ep", None, None)
    return jax.shard_map(
        local,
        mesh=mesh,
        in_specs=(rows,) * 3 + (whole,) * 7 + (expert,) * 3 + (rows,),
        out_specs=(rows, rows, P("ep")) + (slices,) * 4 + (P("ep"), slices) + (expert,) * 3,
        check_vma=False,
    )
```

```python
import functools
import math

import jax
import jax.numpy as jnp
import numpy as np
from jax import lax
from jax.experimental import pallas as pl
from jax.experimental.pallas import tpu as pltpu
from jax.sharding import PartitionSpec as P

D = 1536
HEADS = 24
KV = 8
HEAD = 64
LEN = 1024
PIECE = 256
QUERIES = HEADS // KV
WIDE = 256
TILE = 256
GROUP = 4
PARTS = 2
TURNS = 2
LANES = 128
WIDTH = D + LANES

eps = 1e-06
theta_base = 10000.0
masked_score = -1e30
score_scale = HEAD ** (-0.5)
two_scale = score_scale * math.log2(math.e)

F32 = jnp.float32
BF16 = jnp.bfloat16
NN = (((1,), (0,)), ((), ()))
NT = (((1,), (1,)), ((), ()))
TN = (((0,), (0,)), ((), ()))
ANY = pl.BlockSpec(memory_space=pl.ANY)
SMEM = pl.BlockSpec(memory_space=pltpu.SMEM)


def dot(left, right, dims):
    return lax.dot_general(left, right, dims, preferred_element_type=F32)


def shaped(shape, dtype):
    return jax.ShapeDtypeStruct(shape, dtype)


def estimate(micros):
    return pl.CostEstimate(flops=int(micros * 1e10), bytes_accessed=int(micros * 1e6), transcendentals=0)


def rms_scale(values):
    return lax.rsqrt(jnp.mean(values * values, axis=-1, keepdims=True) + eps)


def rotary_tables():
    half_head = HEAD // 2
    frequency = theta_base ** (-(np.arange(half_head, dtype=np.float64) * 2.0) / HEAD)
    angles = frequency[:, None] * np.arange(LEN, dtype=np.float64)[None, :]
    return np.cos(angles).astype(np.float32), np.sin(angles).astype(np.float32)


def turn(values, cosine, sine):
    first, second = values[: HEAD // 2], values[HEAD // 2 :]
    return jnp.concatenate([first * cosine - second * sine, second * cosine + first * sine], axis=0)


def turn_back(grads, cosine, sine):
    first, second = grads[: HEAD // 2], grads[HEAD // 2 :]
    return jnp.concatenate([first * cosine + second * sine, second * cosine - first * sine], axis=0)


def fill_bias(pieces, bias):
    for block in range(LEN // WIDE):
        first = block * WIDE
        shape = bias.shape[1:]
        key = lax.broadcasted_iota(jnp.int32, shape, 0) + first
        query = lax.broadcasted_iota(jnp.int32, shape, 1) + first
        allowed = key <= query
        for piece in range(pieces.shape[1]):
            start = pieces[0, piece]
            low, high = jnp.minimum(key, query), jnp.maximum(key, query)
            allowed = allowed | ((low >= start) & (high < start + PIECE))
        bias[block] = jnp.where(allowed, 0.0, masked_score)


def key_span(block):
    return block * WIDE, min((block + 2) * WIDE, LEN)


def rows_at(place):
    return pl.BlockSpec((HEAD, LEN), lambda *grid: (place(*grid), 0))


def table_spec():
    return pl.BlockSpec((HEAD // 2, LEN), lambda *grid: (0, 0))


def attend_kernel(pieces, q0, q1, q2, k_in, v_in, cosine, sine, attn, q_out, k_out, v_out, lse, bias):
    @pl.when(pl.program_id(0) == 0)
    def _():
        fill_bias(pieces, bias)

    cos, sin = cosine[...], sine[...]
    k_rot = turn(k_in[...], cos, sin) * two_scale
    k_out[...] = k_rot.astype(BF16)
    keys = k_rot.T.astype(BF16)
    values = v_in[...].astype(BF16)
    v_out[...] = values
    for head, q_in in enumerate((q0, q1, q2)):
        rows = pl.ds(head * HEAD, HEAD)
        q_rot = turn(q_in[...], cos, sin).astype(BF16)
        q_out[rows, :] = q_rot
        for block in range(LEN // WIDE):
            columns = pl.ds(block * WIDE, WIDE)
            first, last = key_span(block)
            queries = q_rot[:, block * WIDE : (block + 1) * WIDE]
            spans = [(first, last)] + ([(0, first)] if first > 0 else [])
            scores = [dot(keys[a:b], queries, NN) for a, b in spans]
            scores[0] = scores[0] + bias[block, : last - first]
            highest = functools.reduce(jnp.maximum, [jnp.max(s, axis=0, keepdims=True) for s in scores])
            weights = [jnp.exp2(s - highest) for s in scores]
            total = sum(jnp.sum(w, axis=0, keepdims=True) for w in weights)
            mixed = sum(dot(values[:, a:b], w.astype(BF16), NN) for (a, b), w in zip(spans, weights)) / total
            attn[rows, columns] = mixed.astype(BF16)
            lse[head : head + 1, columns] = highest + jnp.log2(total)


def attend_call(pieces, query, key, value, cosine, sine):
    rows = lambda count: pl.BlockSpec((count, LEN), lambda i: (i, 0))
    width = QUERIES * HEAD
    return pl.pallas_call(
        attend_kernel,
        grid=(KV,),
        in_specs=[SMEM]
        + [rows_at(lambda i, head=head: QUERIES * i + head) for head in range(QUERIES)]
        + [rows_at(lambda i: i), rows_at(lambda i: i)]
        + [table_spec(), table_spec()],
        out_specs=[rows(width), rows(width), rows(HEAD), rows(HEAD), rows(8)],
        out_shape=[
            shaped((D, LEN), BF16),
            shaped((D, LEN), BF16),
            shaped((KV * HEAD, LEN), BF16),
            shaped((KV * HEAD, LEN), BF16),
            shaped((KV * 8, LEN), F32),
        ],
        scratch_shapes=[pltpu.VMEM((LEN // WIDE, 2 * WIDE, WIDE), F32)],
        compiler_params=pltpu.CompilerParams(vmem_limit_bytes=48 << 20),
        cost_estimate=estimate(25),
        name="attend",
    )(pieces, *[query] * QUERIES, key, value, cosine, sine)


def with_parts(columns, row):
    rank = lax.broadcasted_iota(jnp.int32, columns.shape, 0)
    high = row.astype(BF16).astype(F32)
    middle = (row - high).astype(BF16).astype(F32)
    parts = jnp.where(rank == 0, high, jnp.where(rank == 1, middle, jnp.where(rank == 2, row - high - middle, 0.0)))
    return jnp.concatenate([columns, parts.astype(BF16)], axis=0)


def attend_back_kernel(
    mark, pieces, q_in, k_in, v_in, do_in, attn, lse, cosine, sine, *rest
):
    out, bias, keys_kept, values_kept, dk_sum, dv_sum = rest[-6:]
    kind = pl.program_id(1)

    @pl.when((pl.program_id(0) == 0) & (kind == 0))
    def _():
        fill_bias(pieces, bias)

    cos, sin = cosine[...], sine[...]

    @pl.when(kind == 0)
    def _():
        tail = jnp.where(lax.broadcasted_iota(jnp.int32, (LEN, HEAD), 1) < 3, -1.0, 0.0)
        for kept, ref in ((keys_kept, k_in), (values_kept, v_in)):
            kept[...] = jnp.concatenate([ref[...].astype(F32).T, tail], axis=1).astype(BF16)
        dk_sum[...] = jnp.zeros_like(dk_sum)
        dv_sum[...] = jnp.zeros_like(dv_sum)

    @pl.when(kind < QUERIES)
    def _():
        k_cols, keys, values = k_in[...], keys_kept[...], values_kept[...]
        q_cols, do_cols = q_in[...], do_in[...]
        q_rows = q_cols.astype(F32).T.astype(BF16)
        do_rows = do_cols.astype(F32).T.astype(BF16)
        delta = jnp.sum(do_cols.astype(F32) * attn[...].astype(F32), axis=0, keepdims=True)
        q_wide = with_parts(q_cols, lse[pl.ds(kind, 1), :])
        do_wide = with_parts(do_cols, delta)
        for block in range(LEN // WIDE):
            part = slice(block * WIDE, (block + 1) * WIDE)
            first, last = key_span(block)
            d_query = 0.0
            for a, b in [(first, last)] + ([(0, first)] if first > 0 else []):
                scores = dot(keys[a:b], q_wide[:, part], NN)
                if a == first:
                    scores = scores + bias[block, : b - a]
                probs = jnp.exp2(scores)
                d_scores = (probs * dot(values[a:b], do_wide[:, part], NN)).astype(BF16)
                dv_sum[a:b] += dot(probs.astype(BF16), do_rows[part], NN)
                dk_sum[a:b] += dot(d_scores, q_rows[part], NN)
                d_query = d_query + dot(k_cols[:, a:b], d_scores, NN)
            out[:, part] = turn_back(d_query * math.log(2.0), cos[:, part], sin[:, part]).astype(BF16)

    @pl.when(kind == QUERIES)
    def _():
        out[...] = turn_back(dk_sum[...].T * score_scale, cos, sin).astype(BF16)

    @pl.when(kind == QUERIES + 1)
    def _():
        out[...] = dv_sum[...].T.astype(BF16)


def attend_back_call(part, turn, mark, pieces, q_in, k_in, v_in, do_in, attn, lse, cosine, sine, before):
    group = KV // PARTS
    per = group // TURNS
    first = part * group + turn * per
    query = rows_at(lambda i, j: (first + i) * QUERIES + jnp.minimum(j, QUERIES - 1))
    key = rows_at(lambda i, j: first + i)

    def place(i, j):
        inner = turn * per + i
        tail = jnp.where(j == QUERIES, QUERIES * group + inner, (QUERIES + 1) * group + inner)
        return jnp.where(j < QUERIES, QUERIES * inner + j, tail)

    ins = [mark, pieces, q_in, k_in, v_in, do_in, attn, lse, cosine, sine] + ([] if before is None else [before])
    return pl.pallas_call(
        attend_back_kernel,
        grid=(per, QUERIES + 2),
        in_specs=[ANY, SMEM, query, key, key, query, query, pl.BlockSpec((8, LEN), lambda i, j: (first + i, 0))]
        + [table_spec(), table_spec()]
        + ([] if before is None else [ANY]),
        out_specs=rows_at(place),
        out_shape=shaped(((QUERIES + 2) * group * HEAD, LEN), BF16),
        input_output_aliases={} if before is None else {len(ins) - 1: 0},
        scratch_shapes=[
            pltpu.VMEM((LEN // WIDE, 2 * WIDE, WIDE), F32),
            pltpu.VMEM((LEN, 2 * HEAD), BF16),
            pltpu.VMEM((LEN, 2 * HEAD), BF16),
            pltpu.VMEM((LEN, HEAD), F32),
            pltpu.VMEM((LEN, HEAD), F32),
        ],
        compiler_params=pltpu.CompilerParams(vmem_limit_bytes=48 << 20),
        cost_estimate=estimate(15),
        name="attend_back",
    )(*ins)


def halve_kernel(side, gate, up, down, mine, theirs):
    half = down.shape[0]

    def write(out):
        out[:half] = gate[...].T
        out[half : 2 * half] = up[...].T
        out[2 * half :] = down[...]

    pl.when(pl.program_id(0) == 0)(lambda: write(mine))
    pl.when(pl.program_id(0) == 1)(lambda: write(theirs))


def halve_call(side, gate, up, down):
    half = down.shape[0] // 2
    columns = pl.BlockSpec((D, half), lambda i, side: (0, lax.rem(side[0] + i, 2)))
    whole = pl.BlockSpec((3 * half, D), lambda i, side: (0, 0))
    return pl.pallas_call(
        halve_kernel,
        grid_spec=pltpu.PrefetchScalarGridSpec(
            num_scalar_prefetch=1,
            grid=(2,),
            in_specs=[columns, columns, pl.BlockSpec((half, D), lambda i, side: (lax.rem(side[0] + i, 2), 0))],
            out_specs=[whole, whole],
        ),
        out_shape=[shaped((3 * half, D), BF16)] * 2,
        compiler_params=pltpu.CompilerParams(vmem_limit_bytes=60 << 20),
        cost_estimate=estimate(5),
        name="halve",
    )(side, gate, up, down)


def finish_kernel(parts, tokens, residual, w_query, w_key, w_value, gain, *rest):
    grads, out = rest[:-1], rest[-1]
    total = 0.0
    for part, ref in enumerate(grads):
        columns = ref[...].T
        first = 0
        for weight in (w_query, w_key, w_value):
            wide = weight.shape[1] // parts
            total = total + dot(columns[:, first : first + wide], weight[:, part * wide : (part + 1) * wide], NT)
            first += wide
    values = tokens[...].astype(F32)
    scale = rms_scale(values)
    norm = values * scale
    scaled = total * gain[...]
    out[...] = residual[...] + scale * (scaled - norm * jnp.mean(scaled * norm, axis=1, keepdims=True))


def finish_call(tokens, residual, weights, gain, grads):
    rows = pl.BlockSpec((TILE, D), lambda i: (i, 0))
    whole = lambda array: pl.BlockSpec(array.shape, lambda i: (0, 0), pipeline_mode=pl.Buffered(1))
    return pl.pallas_call(
        functools.partial(finish_kernel, len(grads)),
        grid=(LEN // TILE,),
        in_specs=[rows, rows, *[whole(w) for w in weights], whole(gain)]
        + [pl.BlockSpec((g.shape[0], TILE), lambda i: (0, i)) for g in grads],
        out_specs=rows,
        out_shape=shaped((LEN, D), F32),
        compiler_params=pltpu.CompilerParams(vmem_limit_bytes=48 << 20),
        cost_estimate=estimate(5),
        name="finish",
    )(tokens, residual, *weights, gain, *grads)


def split_lanes(values, experts):
    lanes = lax.broadcasted_iota(jnp.int32, values.shape, 1)
    high = values.astype(BF16).astype(F32)
    return jnp.where(lanes < experts, high, jnp.where(lanes < 2 * experts, values - high, 0.0)).astype(BF16)


def join_lanes(parts, experts):
    return parts + pltpu.roll(parts, LANES - experts, 1)


def route_kernel(experts, tokens, attn, w_out, gain, w_router, routes, residual, rows, gate):
    values = tokens[...].astype(F32) + dot(attn[...], w_out[...], TN)
    residual[...] = values
    normed = (values * rms_scale(values) * gain[...]).astype(BF16)
    logits = dot(normed, w_router[...], NN)
    lanes = lax.broadcasted_iota(jnp.int32, logits.shape, 1)
    expert = lax.rem(lanes, experts)
    chosen = lanes < 0
    for k in range(routes.shape[1]):
        chosen = chosen | (routes[:, k : k + 1] == expert)
    chosen = chosen & (lanes < 2 * experts)
    logits = jnp.where(chosen, logits, masked_score)
    weights = jnp.exp(logits - jnp.max(logits, axis=1, keepdims=True))
    share = weights / (0.5 * jnp.sum(weights, axis=1, keepdims=True))
    gate[...] = share
    rows[:, :D] = normed
    rows[:, D:] = split_lanes(share, experts)


def route_call(experts, tokens, attn, w_out, gain, w_router, routes):
    rows = lambda cols: pl.BlockSpec((TILE, cols), lambda i: (i, 0))
    whole = lambda *shape: pl.BlockSpec(shape, lambda i: (0, 0), pipeline_mode=pl.Buffered(1))
    return pl.pallas_call(
        functools.partial(route_kernel, experts),
        grid=(LEN // TILE,),
        in_specs=[rows(D), pl.BlockSpec((D, TILE), lambda i: (0, i)), whole(D, D), whole(1, D), whole(D, LANES)]
        + [rows(routes.shape[1])],
        out_specs=[rows(D), rows(WIDTH), rows(LANES)],
        out_shape=[shaped((LEN, D), F32), shaped((LEN, WIDTH), BF16), shaped((LEN, LANES), F32)],
        compiler_params=pltpu.CompilerParams(vmem_limit_bytes=60 << 20),
        cost_estimate=estimate(5),
        name="route",
    )(tokens, attn, w_out, gain, w_router, routes)


def merge_kernel(experts, mark, kept, kept_share, landed, out):
    out[:, :D] = (kept[...].astype(F32) + landed[:, :D].astype(F32)).astype(BF16)
    if kept_share is not None:
        share = kept_share[...] + join_lanes(landed[:, D:].astype(F32), experts)
        share = jnp.where(lax.broadcasted_iota(jnp.int32, share.shape, 1) < experts, share, 0.0)
        out[:, D:] = split_lanes(share + pltpu.roll(share, experts, 1), experts)


def merge_call(experts, mark, kept, kept_share, landed):
    rows = lambda cols: pl.BlockSpec((TILE, cols), lambda i: (i, 0))
    width = landed.shape[1]
    kernel = functools.partial(merge_kernel, experts)
    if kept_share is None:
        kernel = lambda mark, kept, landed, out: merge_kernel(experts, mark, kept, None, landed, out)
    return pl.pallas_call(
        kernel,
        grid=(LEN // TILE,),
        in_specs=[ANY, rows(D)] + ([] if kept_share is None else [rows(LANES)]) + [rows(width)],
        out_specs=rows(width),
        out_shape=shaped((LEN, width), BF16),
        compiler_params=pltpu.CompilerParams(vmem_limit_bytes=32 << 20),
        cost_estimate=estimate(3),
        name="merge",
    )(*[ref for ref in (mark, kept, kept_share, landed) if ref is not None])


def back_kernel(
    experts, mark, kept, kept_share, core, chip, residual, cotangent, gate, gain, w_router, w_out, d_res, d_mix, d_attn, d_router
):
    @pl.when(pl.program_id(0) == 0)
    def _():
        d_router[...] = jnp.zeros_like(d_router)

    landed = core[:, D:].astype(F32) + chip[:, D:].astype(F32)
    share = kept_share[...] + join_lanes(landed, experts)
    first = lax.broadcasted_iota(jnp.int32, share.shape, 1) < experts
    gates = jnp.where(first, gate[...], 0.0)
    inner = jnp.sum(gates * share, axis=1, keepdims=True)
    d_logits = jnp.where(first, gates * (share - inner), 0.0).astype(BF16)
    d_normed = kept[...].astype(F32) + core[:, :D].astype(F32) + chip[:, :D].astype(F32) + dot(d_logits, w_router[...], NT)
    values, gains = residual[...], gain[...]
    scale = rms_scale(values)
    norm = values * scale
    d_gain = jnp.sum(d_normed * norm, axis=0, keepdims=True)
    scaled = d_normed * gains
    d_values = cotangent[...].astype(F32) + scale * (scaled - norm * jnp.mean(scaled * norm, axis=1, keepdims=True))
    d_res[...] = d_values
    mixed = d_values.astype(BF16)
    d_mix[...] = mixed
    d_attn[...] = dot(w_out[...], mixed, NT).astype(BF16)
    d_router[...] += dot(d_logits, (norm * gains).astype(BF16), TN)
    d_router[experts : experts + 1] += d_gain


def back_call(experts, mark, kept, kept_share, core, chip, residual, cotangent, gate, gain, w_router, w_out):
    rows = lambda cols: pl.BlockSpec((TILE, cols), lambda i: (i, 0))
    whole = lambda *shape: pl.BlockSpec(shape, lambda i: (0, 0), pipeline_mode=pl.Buffered(1))
    return pl.pallas_call(
        functools.partial(back_kernel, experts),
        grid=(LEN // TILE,),
        in_specs=[ANY, rows(D), rows(LANES), rows(WIDTH), rows(WIDTH), rows(D), rows(D), rows(LANES)]
        + [whole(1, D), whole(D, LANES), whole(D, D)],
        out_specs=[rows(D), rows(D), pl.BlockSpec((D, TILE), lambda i: (0, i)), whole(LANES, D)],
        out_shape=[
            shaped((LEN, D), F32),
            shaped((LEN, D), BF16),
            shaped((D, LEN), BF16),
            shaped((LANES, D), F32),
        ],
        compiler_params=pltpu.CompilerParams(vmem_limit_bytes=48 << 20),
        cost_estimate=estimate(8),
        name="back",
    )(mark, kept, kept_share, core, chip, residual, cotangent, gate, gain, w_router, w_out)


def out_kernel(mark, attn, mixed, small, out):
    out[:, :D] = dot(attn[...], mixed[...], NN).astype(BF16)
    out[:, D:] = small[...].T.astype(BF16)


def out_call(mark, attn, mixed, small):
    return pl.pallas_call(
        out_kernel,
        grid=(D // TILE,),
        in_specs=[
            ANY,
            pl.BlockSpec((TILE, LEN), lambda i: (i, 0)),
            pl.BlockSpec((LEN, D), lambda i: (0, 0), pipeline_mode=pl.Buffered(1)),
            pl.BlockSpec((LANES, TILE), lambda i: (0, i)),
        ],
        out_specs=pl.BlockSpec((TILE, WIDTH), lambda i: (i, 0)),
        out_shape=shaped((D, WIDTH), BF16),
        compiler_params=pltpu.CompilerParams(vmem_limit_bytes=32 << 20),
        cost_estimate=estimate(5),
        name="out_grad",
    )(mark, attn, mixed, small)


def pause_kernel(mark, out):
    out[...] = mark[...]


def pause_call(mark):
    return pl.pallas_call(
        pause_kernel, out_shape=shaped(mark.shape, mark.dtype), cost_estimate=estimate(10), name="pause"
    )(mark)


def expert_kernel(count, experts, fresh, first, last_tokens, steps, ids, mark, *rest):
    rest = list(rest)

    def take(number):
        taken = rest[:number]
        del rest[:number]
        return taken

    n2, up = take(2), take(2)
    w_in = [take(2) for _ in range(count)]
    sums_in = [[] if new else take(2) for new in fresh]
    carry_in = [] if first else take(3)
    outs = take(5) if last_tokens else take(3)
    sums_out = [take(2) for _ in range(count)]
    weights, sums = take(1)[0], take(1)[0]
    low, sem = rest
    half = weights.shape[1] // 6
    width = 2 * half
    step = pl.program_id(0)
    ahead = step < steps // 2

    def pieces_of(parts, whole):
        return [
            (ref.at[pl.ds(kind * half, half)], whole.at[pl.ds((2 * kind + part) * half, half)])
            for kind in range(3)
            for part, ref in enumerate(parts)
        ]

    def copies_of(pairs, lane):
        return [pltpu.make_async_copy(a, b, sem.at[lane, n]) for n, (a, b) in enumerate(pairs)]

    loads = [copies_of(pieces_of(w_in[e], weights.at[e]), e) for e in range(count)]
    prior = [[] if fresh[e] else copies_of(pieces_of(sums_in[e], low.at[e]), count + e) for e in range(count)]
    stores = [copies_of([(b, a) for a, b in pieces_of(sums_out[e], low.at[e])], e) for e in range(count)]

    @pl.when(step == 0)
    def _():
        for copy in sum(loads + prior, []):
            copy.start()
        sums[...] = jnp.zeros_like(sums)
        for copy in sum(loads, []):
            copy.wait()

    rows = jnp.where(ahead, n2[0][...], n2[1][...])
    grads = jnp.where(ahead, up[0][...], up[1][...])
    rows, gates = rows[:, :D], rows[:, D:].astype(F32)
    lanes = lax.broadcasted_iota(jnp.int32, gates.shape, 1)
    mixed = d_rows = d_shares = None
    add = lambda total, value: value if total is None else total + value
    for e in range(count):
        w_both, w_down = weights.at[e, : 2 * width], weights.at[e, 2 * width :]
        hit = (lanes == ids[e]) | (lanes == ids[e] + experts)
        share = jnp.sum(jnp.where(hit, gates, 0.0), axis=1, keepdims=True)
        acts = dot(rows, w_both[...], NT)
        gate_act, up_act = acts[:, :width], acts[:, width:]
        d_plain = dot(grads, w_down[...], NT)
        sigmoid = 1.0 / (1.0 + jnp.exp(-gate_act))
        silu = gate_act * sigmoid
        hidden = silu * up_act
        shared = (share * hidden).astype(BF16)
        d_share = jnp.sum(hidden * d_plain, axis=1, keepdims=True)
        d_hidden = share * d_plain
        d_gate = (d_hidden * up_act * (sigmoid + silu * (1.0 - sigmoid))).astype(BF16)
        d_up = (d_hidden * silu).astype(BF16)
        d_both = jnp.concatenate([d_gate, d_up], axis=1)
        mixed = add(mixed, dot(shared, w_down[...], NN))
        d_rows = add(d_rows, dot(d_both, w_both[...], NN))
        d_shares = add(d_shares, jnp.where(hit, d_share, 0.0))
        sums[e, : 2 * width] += dot(d_both, rows, TN)
        sums[e, 2 * width :] += dot(shared, grads, TN)

        @pl.when(step == steps - 1)
        def _(e=e):
            for copy in prior[e]:
                copy.wait()
            low[e] = (sums[e] if fresh[e] else sums[e] + low[e].astype(F32)).astype(BF16)
            for copy in stores[e]:
                copy.start()

    results = [mixed, d_rows, d_shares]
    if not first:
        results = [result + ref[...].astype(F32) for result, ref in zip(results, carry_in)]
    if last_tokens:

        @pl.when(ahead)
        def _():
            for ref, result in zip(outs[:3], results):
                ref[...] = result.astype(ref.dtype)

        @pl.when(jnp.logical_not(ahead))
        def _():
            outs[3][...] = results[0].astype(BF16)
            outs[4][:, :D] = results[1].astype(BF16)
            outs[4][:, D:] = split_lanes(results[2], experts)
    else:
        for ref, result in zip(outs, results):
            ref[...] = result.astype(ref.dtype)

    @pl.when(step == steps - 1)
    def _():
        for copy in sum(stores, []):
            copy.wait()


def expert_call(ids, mark, experts, n2, up, weights, sums, carry, last_tokens):
    tokens, height, count = 2 * n2[0].shape[0], weights[0][0].shape[0], len(weights)
    steps = tokens // TILE
    rows = lambda cols: pl.BlockSpec((TILE, cols), lambda i: (i, 0))
    near = lambda cols: pl.BlockSpec((TILE, cols), lambda i: (jnp.minimum(i, steps // 2 - 1), 0))
    far = lambda cols: pl.BlockSpec((TILE, cols), lambda i: (jnp.maximum(i - steps // 2, 0), 0))
    ins = [ids, mark, *n2, *up] + [w for pair in weights for w in pair]
    specs = [SMEM, ANY, near(WIDTH), far(WIDTH), near(D), far(D)] + [ANY] * (2 * count)
    fresh, first = [pair is None for pair in sums], carry is None
    columns = (D, D, LANES)
    if last_tokens:
        outs = [shaped((tokens // 2, c), t) for c, t in zip(columns, (BF16, BF16, F32))]
        outs += [shaped((tokens // 2, c), BF16) for c in (D, WIDTH)]
        out_specs = [near(c) for c in columns] + [far(D), far(WIDTH)]
    else:
        outs = [shaped((tokens, c), t) for c, t in zip(columns, (BF16, F32, F32))]
        out_specs = [rows(c) for c in columns]
    aliases = {}
    for pair in sums:
        if pair is not None:
            ins += pair
            specs += [ANY, ANY]
    if not first:
        if not last_tokens:
            aliases.update({len(ins) + k: k for k in range(3)})
        ins += carry
        specs += [rows(c) for c in columns]
    tokens_out = len(outs)
    for _ in range(count):
        outs += [shaped((height, D), BF16)] * 2
        out_specs += [ANY, ANY]
    scratch = [pltpu.VMEM((count, 2 * height, D), BF16), pltpu.VMEM((count, 2 * height, D), F32)]
    scratch.append(pltpu.VMEM((count, 2 * height, D), BF16))
    scratch.append(pltpu.SemaphoreType.DMA((2 * count, 6)))
    done = pl.pallas_call(
        functools.partial(expert_kernel, count, experts, fresh, first, last_tokens, steps),
        grid=(steps,),
        in_specs=specs,
        out_specs=out_specs,
        out_shape=outs,
        scratch_shapes=scratch,
        input_output_aliases=aliases,
        compiler_params=pltpu.CompilerParams(vmem_limit_bytes=63 << 20),
        cost_estimate=estimate(15 * count),
        name="expert",
    )(*ins)
    return list(done[:tokens_out]), [tuple(done[tokens_out + 2 * e : tokens_out + 2 * e + 2]) for e in range(count)]


def join_kernel(side, held, landed, gate, up, down):
    here = pl.program_id(0) == 0
    rows = jnp.where(here, held[...], landed[...]).astype(F32)
    half = down.shape[0]
    gate[...] = rows[:half].T
    up[...] = rows[half : 2 * half].T
    down[...] = rows[2 * half :]


def join_call(side, held, landed):
    half = held.shape[0] // 3
    whole = pl.BlockSpec(held.shape, lambda i, side: (0, 0))
    columns = pl.BlockSpec((D, half), lambda i, side: (0, lax.rem(side[0] + i, 2)))
    return pl.pallas_call(
        join_kernel,
        grid_spec=pltpu.PrefetchScalarGridSpec(
            num_scalar_prefetch=1,
            grid=(2,),
            in_specs=[whole, whole],
            out_specs=[columns, columns, pl.BlockSpec((half, D), lambda i, side: (lax.rem(side[0] + i, 2), 0))],
        ),
        out_shape=[shaped((D, 2 * half), F32), shaped((D, 2 * half), F32), shaped((2 * half, D), F32)],
        compiler_params=pltpu.CompilerParams(vmem_limit_bytes=48 << 20),
        cost_estimate=estimate(5),
        name="join",
    )(side, held, landed)


def after(values, *others):
    return lax.optimization_barrier((values, *others))[0]


class Task:
    def __init__(self, steps):
        self.steps, self.result, self.over = steps, None, False

    def step(self):
        if self.over:
            return []
        try:
            return [next(self.steps)]
        except StopIteration as stop:
            self.result, self.over = stop.value, True
            return [self.result]

    def finish(self):
        while not self.over:
            self.step()
        return self.result


def local(
    tokens,
    routes,
    pieces,
    attn_gain,
    w_query,
    w_key,
    w_value,
    w_out,
    ffn_gain,
    w_router,
    expert_gate,
    expert_up,
    expert_down,
    cotangent,
):
    shards, reps = lax.axis_size("ep"), lax.axis_size("rep")
    experts = w_router.shape[1]
    slots = shards // GROUP
    place = lax.axis_index("ep")
    side = lax.axis_index("rep") % 2

    def swap(values, bits):
        return lax.ppermute(values, "ep", [(i, i ^ bits) for i in range(shards)])

    def swap_rep(values, bits=1):
        return lax.ppermute(values, "rep", [(i, i ^ bits) for i in range(reps)])


    def reduce_reps(values, bits=1):
        while bits < reps:
            values = values.astype(BF16)
            landed = swap_rep(values, bits)
            yield values
            values = values.astype(F32) + hold(landed).astype(F32)
            bits *= 2
        return values

    def reduce_rows(values):
        values = values.reshape(shards, -1, values.shape[1])
        bits = 1
        while bits < shards:
            values = values.reshape(values.shape[0] // 2, 2, *values.shape[1:])
            bit = (place // bits) % 2
            kept, sent = [
                lax.dynamic_index_in_dim(values, index, axis=1, keepdims=False) for index in (bit, 1 - bit)
            ]
            landed = swap(sent, bits)
            yield sent
            values = (kept.astype(F32) + hold(landed).astype(F32)).astype(BF16)
            bits *= 2
        return (yield from reduce_reps(values[0]))

    def sum_steps(slot, own, other):
        other = hold(other)
        landed = swap_rep(other)
        yield other
        own = own.astype(F32) + hold(landed).astype(F32)
        if slot == 0:
            return own
        own = own.astype(BF16)
        landed = swap(own, slot * GROUP)
        yield own
        return hold(landed)

    with jax.named_scope("weights_out"):
        turned = side.astype(jnp.int32).reshape(1)
        mine, theirs = halve_call(turned, expert_gate[0], expert_up[0], expert_down[0])
        tokens, mine, theirs = lax.optimization_barrier((tokens, mine, theirs))
        landed = {slot: swap(mine, slot * GROUP) for slot in (2, 1)}

    with jax.named_scope("cotangent_out"):
        grads_next = swap(cotangent, 2)
        grads_in = [(cotangent, swap(cotangent, 1)), None]

    with jax.named_scope("attention"):
        inputs = tokens.astype(F32)
        scale_one = rms_scale(inputs)
        norm_one = inputs * scale_one
        normed_one = (norm_one * attn_gain).astype(BF16)
        w_dims = (((0,), (1,)), ((), ()))
        projections = (w_query, w_key, w_value)
        query, key, value = [dot(w, normed_one, w_dims) for w in projections]
        cosine, sine = [jnp.asarray(table) for table in rotary_tables()]
        attn, query_rot, key_rot, value_low, lse = attend_call(pieces, query, key, value, cosine, sine)
        attn = after(attn, grads_next, grads_in[0][1])

    with jax.named_scope("cotangent_out"):
        grads_in[1] = (grads_next, swap(after(grads_next, attn), 1))

    with jax.named_scope("routing"):
        pad = jnp.zeros((D, LANES - 2 * experts), BF16)
        router_twice = jnp.concatenate([w_router, w_router, pad], axis=1)
        gain_two = ffn_gain.reshape(1, D)
        residual, rows, gate = route_call(experts, tokens, attn, w_out, gain_two, router_twice, routes)
        rows, _, held, near = lax.optimization_barrier((rows, grads_in[1][1], landed[2], landed[1]))
        rows_next = swap(rows, 2)
        rows_in = [(rows, swap(rows, 1)), None]

    with jax.named_scope("weights_out"):
        weights = {0: (mine, theirs), 2: (held, swap_rep(held))}
        late = after(mine, rows)
        landed = {slot: swap(late, slot * GROUP) for slot in range(3, slots)}
        ids = [((place // GROUP) ^ slot) * GROUP + place % GROUP for slot in range(slots)]
        ids = [expert.astype(jnp.int32) for expert in ids]

    carry, sums, tasks = [None, None], [None] * slots, [None] * slots
    mark, point = after(jnp.zeros((8, LANES), F32), rows), rows

    def tick(*arrays):
        nonlocal mark
        mark = after(mark, *arrays)

    def hold(values):
        return after(values, point)

    def pause():
        nonlocal mark
        mark = pause_call(mark)

    def pulse():
        return swap(mark, 1)

    def passed(value, beat=None):
        nonlocal mark, point
        if beat is not None:
            mark = mark + beat
        mark, point = after(mark, value), value

    def run(chip, group, last=False, beats=True):
        beat = pulse() if beats else None
        carry[chip], done = expert_call(
            jnp.stack([ids[slot] for slot in group]),
            mark,
            experts,
            rows_in[chip],
            grads_in[chip],
            [weights[slot] for slot in group],
            [sums[slot] for slot in group],
            carry[chip],
            last,
        )
        passed(carry[chip][2], beat)
        for slot, pair in zip(group, done):
            if sums[slot] is not None:
                tasks[slot] = Task(sum_steps(slot, *pair))
            sums[slot] = pair

    def arrive(slot):
        tick(landed[slot])
        held = hold(landed[slot])
        weights[slot] = (held, swap_rep(held))

    with jax.named_scope("experts"):
        run(0, [0], beats=False)
        tick(weights[2][1])
        near = hold(near)
        weights[1] = (near, swap_rep(near))
        run(0, [2])
        tick(rows_next, weights[1][1])
        for slot in range(3, slots):
            arrive(slot)
        rows_in[1] = (rows_next, swap(hold(rows_next), 1))
        pause()
        tick(rows_in[1][1])
        run(1, [0, 2])
        tick(*[weights[slot][1] for slot in range(3, slots)])
        tasks[2].step()
        pairs = [[slot, slot + 1] for slot in range(3, slots - 1, 2)] + [[slots - 1, 1]]
        for pair in pairs:
            last = pair == pairs[-1]
            run(1, pair, last)
            if last:
                there_landed = swap(hold(carry[1][4]), 1)
                pause()
                there = merge_call(experts, mark, carry[1][1], carry[1][2], there_landed)
                d_next = swap(there, 2)
                tick(there, *tasks[2].step())
                tasks[0].step()
                mix_landed = swap(hold(carry[1][3]), 1)
            run(0, pair[:1])
            if last:
                mix_there = merge_call(experts, mark, carry[1][0], None, mix_landed)
                tick(mix_there, *tasks[0].step())
            tasks[pair[0]].step()
            run(0, pair[1:], last)

    with jax.named_scope("routing_back"):
        d_core = swap(hold(carry[0][4]), 1)
        tasks[1].step()
        pause()
        tick(d_core, d_next, *[array for task in tasks[2:] for array in task.step()])
        point = mark
        mix_home = swap(hold(mix_there), 2)
        mix_core = swap(hold(carry[0][3]), 1)
        beat = pulse()
        d_residual, d_mixed, d_attn, d_small = back_call(
            experts, mark, carry[0][1], carry[0][2], d_core, d_next, residual, cotangent, gate, gain_two, router_twice, w_out
        )
        passed(d_small, beat)
        tick(mix_core)
        d_out = out_call(mark, attn, d_mixed, d_small)
        passed(d_out)

    with jax.named_scope("attention_back"):
        in_dims = (((0,), (1,)), ((), ()))
        out_task, w_tasks, d_packed = Task(reduce_rows(d_out)), [], []
        tick(*out_task.step())
        for part in range(PARTS):
            packed = None
            for turn in range(TURNS):
                beat = pulse() if (part, turn) == (0, 1) else None
                packed = attend_back_call(
                    part, turn, mark, pieces, query_rot, key_rot, value_low, d_attn, attn, lse, cosine, sine, packed
                )
                passed(packed, beat)
                if (part, turn) == (0, 0):
                    tick(*tasks[1].step())
                if (part, turn) == (0, 1):
                    tick(mix_home)
                if part == turn:
                    tick(*out_task.step())
                tick(*[array for task in w_tasks for array in task.step()])
            d_packed.append(packed)
            w_tasks.append(Task(reduce_rows(dot(normed_one, packed, in_dims).astype(BF16))))
            if part < PARTS - 1:
                tick(*w_tasks[-1].step())

    with jax.named_scope("sums_experts"):
        total = tasks[0].finish()
        for task in tasks[1:]:
            total = total + task.finish().astype(F32)
        total = Task(reduce_reps(total, 2)).finish().astype(BF16)
        total_landed = swap_rep(total)

    with jax.named_scope("tail"):
        last, other = w_tasks[1], w_tasks[0]
        mix_home = after(mix_home, packed, total, *last.step())
        output = point = (residual + carry[0][0].astype(F32) + mix_core.astype(F32) + mix_home.astype(F32)).astype(BF16)
        stepped = last.step() + other.step() + out_task.step()
        gain_one = after(attn_gain.reshape(1, D), output, *stepped)
        d_tokens = point = finish_call(tokens, d_residual, projections, gain_one, d_packed)
        stepped = other.step() + out_task.step() + last.step()
        total, total_landed = lax.optimization_barrier((total, total_landed, point, *stepped))[:2]
        s_gate, s_up, s_down = join_call(turned, total, total_landed)

    with jax.named_scope("sums_rest"):
        s_mixed = out_task.finish()
        s_out, s_small = s_mixed[:, :D], s_mixed[:, D:]
        count = s_out.shape[0]
        first = place * count
        s_parts = [task.finish() for task in w_tasks]
        s_attn, groups = 0.0, []
        for k, w in enumerate(projections):
            wide = w.shape[1] // PARTS
            cut = sum(v.shape[1] // PARTS for v in projections[:k])
            groups.append(jnp.concatenate([part[:, cut : cut + wide] for part in s_parts], axis=1))
            s_attn += jnp.sum(groups[-1] * lax.dynamic_slice_in_dim(w, first, count).astype(F32), axis=1)
        s_query, s_key, s_value = groups
        s_attn = s_attn / lax.dynamic_slice_in_dim(attn_gain, first, count)

    return (
        output,
        d_tokens,
        s_attn,
        s_query,
        s_key,
        s_value,
        s_out,
        s_small[:, experts],
        s_small[:, :experts],
        s_gate[None],
        s_up[None],
        s_down[None],
    )


def solution(mesh):
    rows, whole, slices = P(("rep", "ep"), None), P(), P("ep", None)
    expert = P("ep", None, None)
    return jax.shard_map(
        local,
        mesh=mesh,
        in_specs=(rows,) * 3 + (whole,) * 7 + (expert,) * 3 + (rows,),
        out_specs=(rows, rows, P("ep")) + (slices,) * 4 + (P("ep"), slices) + (expert,) * 3,
        check_vma=False,
    )
```

```python
import functools
import math

import jax
import jax.numpy as jnp
import numpy as np
from jax import lax
from jax.experimental import pallas as pl
from jax.experimental.pallas import tpu as pltpu
from jax.sharding import PartitionSpec as P

D = 1536
HEADS = 24
KV = 8
HEAD = 64
LEN = 1024
PIECE = 256
QUERIES = HEADS // KV
WIDE = 256
TILE = 256
GROUP = 4
PARTS = 2
TURNS = 2
LANES = 128
WIDTH = D + LANES

eps = 1e-06
theta_base = 10000.0
masked_score = -1e30
score_scale = HEAD ** (-0.5)
two_scale = score_scale * math.log2(math.e)

F32 = jnp.float32
BF16 = jnp.bfloat16
NN = (((1,), (0,)), ((), ()))
NT = (((1,), (1,)), ((), ()))
TN = (((0,), (0,)), ((), ()))
ANY = pl.BlockSpec(memory_space=pl.ANY)
SMEM = pl.BlockSpec(memory_space=pltpu.SMEM)


def dot(left, right, dims):
    return lax.dot_general(left, right, dims, preferred_element_type=F32)


def shaped(shape, dtype):
    return jax.ShapeDtypeStruct(shape, dtype)


def estimate(micros):
    return pl.CostEstimate(flops=int(micros * 1e10), bytes_accessed=int(micros * 1e6), transcendentals=0)


def rms_scale(values):
    return lax.rsqrt(jnp.mean(values * values, axis=-1, keepdims=True) + eps)


def rotary_tables():
    half_head = HEAD // 2
    frequency = theta_base ** (-(np.arange(half_head, dtype=np.float64) * 2.0) / HEAD)
    angles = frequency[:, None] * np.arange(LEN, dtype=np.float64)[None, :]
    return np.cos(angles).astype(np.float32), np.sin(angles).astype(np.float32)


def turn(values, cosine, sine):
    first, second = values[: HEAD // 2], values[HEAD // 2 :]
    return jnp.concatenate([first * cosine - second * sine, second * cosine + first * sine], axis=0)


def turn_back(grads, cosine, sine):
    first, second = grads[: HEAD // 2], grads[HEAD // 2 :]
    return jnp.concatenate([first * cosine + second * sine, second * cosine - first * sine], axis=0)


def fill_bias(pieces, bias):
    for block in range(LEN // WIDE):
        first = block * WIDE
        shape = bias.shape[1:]
        key = lax.broadcasted_iota(jnp.int32, shape, 0) + first
        query = lax.broadcasted_iota(jnp.int32, shape, 1) + first
        allowed = key <= query
        for piece in range(pieces.shape[1]):
            start = pieces[0, piece]
            low, high = jnp.minimum(key, query), jnp.maximum(key, query)
            allowed = allowed | ((low >= start) & (high < start + PIECE))
        bias[block] = jnp.where(allowed, 0.0, masked_score)


def key_span(block):
    return block * WIDE, min((block + 2) * WIDE, LEN)


def rows_at(place):
    return pl.BlockSpec((HEAD, LEN), lambda *grid: (place(*grid), 0))


def table_spec():
    return pl.BlockSpec((HEAD // 2, LEN), lambda *grid: (0, 0))


def attend_kernel(pieces, q0, q1, q2, k_in, v_in, cosine, sine, attn, q_out, k_out, v_out, lse, bias):
    @pl.when(pl.program_id(0) == 0)
    def _():
        fill_bias(pieces, bias)

    cos, sin = cosine[...], sine[...]
    k_rot = turn(k_in[...], cos, sin) * two_scale
    k_out[...] = k_rot.astype(BF16)
    keys = k_rot.T.astype(BF16)
    values = v_in[...].astype(BF16)
    v_out[...] = values
    for head, q_in in enumerate((q0, q1, q2)):
        rows = pl.ds(head * HEAD, HEAD)
        q_rot = turn(q_in[...], cos, sin).astype(BF16)
        q_out[rows, :] = q_rot
        for block in range(LEN // WIDE):
            columns = pl.ds(block * WIDE, WIDE)
            first, last = key_span(block)
            queries = q_rot[:, block * WIDE : (block + 1) * WIDE]
            spans = [(first, last)] + ([(0, first)] if first > 0 else [])
            scores = [dot(keys[a:b], queries, NN) for a, b in spans]
            scores[0] = scores[0] + bias[block, : last - first]
            highest = functools.reduce(jnp.maximum, [jnp.max(s, axis=0, keepdims=True) for s in scores])
            weights = [jnp.exp2(s - highest) for s in scores]
            total = sum(jnp.sum(w, axis=0, keepdims=True) for w in weights)
            mixed = sum(dot(values[:, a:b], w.astype(BF16), NN) for (a, b), w in zip(spans, weights)) / total
            attn[rows, columns] = mixed.astype(BF16)
            lse[head : head + 1, columns] = highest + jnp.log2(total)


def attend_call(pieces, query, key, value, cosine, sine):
    rows = lambda count: pl.BlockSpec((count, LEN), lambda i: (i, 0))
    width = QUERIES * HEAD
    return pl.pallas_call(
        attend_kernel,
        grid=(KV,),
        in_specs=[SMEM]
        + [rows_at(lambda i, head=head: QUERIES * i + head) for head in range(QUERIES)]
        + [rows_at(lambda i: i), rows_at(lambda i: i)]
        + [table_spec(), table_spec()],
        out_specs=[rows(width), rows(width), rows(HEAD), rows(HEAD), rows(8)],
        out_shape=[
            shaped((D, LEN), BF16),
            shaped((D, LEN), BF16),
            shaped((KV * HEAD, LEN), BF16),
            shaped((KV * HEAD, LEN), BF16),
            shaped((KV * 8, LEN), F32),
        ],
        scratch_shapes=[pltpu.VMEM((LEN // WIDE, 2 * WIDE, WIDE), F32)],
        compiler_params=pltpu.CompilerParams(vmem_limit_bytes=48 << 20),
        cost_estimate=estimate(25),
        name="attend",
    )(pieces, *[query] * QUERIES, key, value, cosine, sine)


def with_parts(columns, row):
    rank = lax.broadcasted_iota(jnp.int32, columns.shape, 0)
    high = row.astype(BF16).astype(F32)
    middle = (row - high).astype(BF16).astype(F32)
    parts = jnp.where(rank == 0, high, jnp.where(rank == 1, middle, jnp.where(rank == 2, row - high - middle, 0.0)))
    return jnp.concatenate([columns, parts.astype(BF16)], axis=0)


def attend_back_kernel(
    mark, pieces, q_in, k_in, v_in, do_in, attn, lse, cosine, sine, *rest
):
    out, bias, keys_kept, values_kept, dk_sum, dv_sum = rest[-6:]
    kind = pl.program_id(1)

    @pl.when((pl.program_id(0) == 0) & (kind == 0))
    def _():
        fill_bias(pieces, bias)

    cos, sin = cosine[...], sine[...]

    @pl.when(kind == 0)
    def _():
        tail = jnp.where(lax.broadcasted_iota(jnp.int32, (LEN, HEAD), 1) < 3, -1.0, 0.0)
        for kept, ref in ((keys_kept, k_in), (values_kept, v_in)):
            kept[...] = jnp.concatenate([ref[...].astype(F32).T, tail], axis=1).astype(BF16)
        dk_sum[...] = jnp.zeros_like(dk_sum)
        dv_sum[...] = jnp.zeros_like(dv_sum)

    @pl.when(kind < QUERIES)
    def _():
        k_cols, keys, values = k_in[...], keys_kept[...], values_kept[...]
        q_cols, do_cols = q_in[...], do_in[...]
        q_rows = q_cols.astype(F32).T.astype(BF16)
        do_rows = do_cols.astype(F32).T.astype(BF16)
        delta = jnp.sum(do_cols.astype(F32) * attn[...].astype(F32), axis=0, keepdims=True)
        q_wide = with_parts(q_cols, lse[pl.ds(kind, 1), :])
        do_wide = with_parts(do_cols, delta)
        for block in range(LEN // WIDE):
            part = slice(block * WIDE, (block + 1) * WIDE)
            first, last = key_span(block)
            d_query = 0.0
            for a, b in [(first, last)] + ([(0, first)] if first > 0 else []):
                scores = dot(keys[a:b], q_wide[:, part], NN)
                if a == first:
                    scores = scores + bias[block, : b - a]
                probs = jnp.exp2(scores)
                d_scores = (probs * dot(values[a:b], do_wide[:, part], NN)).astype(BF16)
                dv_sum[a:b] += dot(probs.astype(BF16), do_rows[part], NN)
                dk_sum[a:b] += dot(d_scores, q_rows[part], NN)
                d_query = d_query + dot(k_cols[:, a:b], d_scores, NN)
            out[:, part] = turn_back(d_query * math.log(2.0), cos[:, part], sin[:, part]).astype(BF16)

    @pl.when(kind == QUERIES)
    def _():
        out[...] = turn_back(dk_sum[...].T * score_scale, cos, sin).astype(BF16)

    @pl.when(kind == QUERIES + 1)
    def _():
        out[...] = dv_sum[...].T.astype(BF16)


def attend_back_call(part, turn, mark, pieces, q_in, k_in, v_in, do_in, attn, lse, cosine, sine, before):
    group = KV // PARTS
    per = group // TURNS
    first = part * group + turn * per
    query = rows_at(lambda i, j: (first + i) * QUERIES + jnp.minimum(j, QUERIES - 1))
    key = rows_at(lambda i, j: first + i)

    def place(i, j):
        inner = turn * per + i
        tail = jnp.where(j == QUERIES, QUERIES * group + inner, (QUERIES + 1) * group + inner)
        return jnp.where(j < QUERIES, QUERIES * inner + j, tail)

    ins = [mark, pieces, q_in, k_in, v_in, do_in, attn, lse, cosine, sine] + ([] if before is None else [before])
    return pl.pallas_call(
        attend_back_kernel,
        grid=(per, QUERIES + 2),
        in_specs=[ANY, SMEM, query, key, key, query, query, pl.BlockSpec((8, LEN), lambda i, j: (first + i, 0))]
        + [table_spec(), table_spec()]
        + ([] if before is None else [ANY]),
        out_specs=rows_at(place),
        out_shape=shaped(((QUERIES + 2) * group * HEAD, LEN), BF16),
        input_output_aliases={} if before is None else {len(ins) - 1: 0},
        scratch_shapes=[
            pltpu.VMEM((LEN // WIDE, 2 * WIDE, WIDE), F32),
            pltpu.VMEM((LEN, 2 * HEAD), BF16),
            pltpu.VMEM((LEN, 2 * HEAD), BF16),
            pltpu.VMEM((LEN, HEAD), F32),
            pltpu.VMEM((LEN, HEAD), F32),
        ],
        compiler_params=pltpu.CompilerParams(vmem_limit_bytes=48 << 20),
        cost_estimate=estimate(15),
        name="attend_back",
    )(*ins)


def halve_kernel(side, gate, up, down, mine, theirs):
    half = down.shape[0]

    def write(out):
        out[:half] = gate[...].T
        out[half : 2 * half] = up[...].T
        out[2 * half :] = down[...]

    pl.when(pl.program_id(0) == 0)(lambda: write(mine))
    pl.when(pl.program_id(0) == 1)(lambda: write(theirs))


def halve_call(side, gate, up, down):
    half = down.shape[0] // 2
    columns = pl.BlockSpec((D, half), lambda i, side: (0, lax.rem(side[0] + i, 2)))
    whole = pl.BlockSpec((3 * half, D), lambda i, side: (0, 0))
    return pl.pallas_call(
        halve_kernel,
        grid_spec=pltpu.PrefetchScalarGridSpec(
            num_scalar_prefetch=1,
            grid=(2,),
            in_specs=[columns, columns, pl.BlockSpec((half, D), lambda i, side: (lax.rem(side[0] + i, 2), 0))],
            out_specs=[whole, whole],
        ),
        out_shape=[shaped((3 * half, D), BF16)] * 2,
        compiler_params=pltpu.CompilerParams(vmem_limit_bytes=60 << 20),
        cost_estimate=estimate(5),
        name="halve",
    )(side, gate, up, down)


def finish_kernel(parts, tokens, residual, w_query, w_key, w_value, gain, *rest):
    grads, out = rest[:-1], rest[-1]
    total = 0.0
    for part, ref in enumerate(grads):
        columns = ref[...].T
        first = 0
        for weight in (w_query, w_key, w_value):
            wide = weight.shape[1] // parts
            total = total + dot(columns[:, first : first + wide], weight[:, part * wide : (part + 1) * wide], NT)
            first += wide
    values = tokens[...].astype(F32)
    scale = rms_scale(values)
    norm = values * scale
    scaled = total * gain[...]
    out[...] = residual[...] + scale * (scaled - norm * jnp.mean(scaled * norm, axis=1, keepdims=True))


def finish_call(tokens, residual, weights, gain, grads):
    rows = pl.BlockSpec((TILE, D), lambda i: (i, 0))
    whole = lambda array: pl.BlockSpec(array.shape, lambda i: (0, 0), pipeline_mode=pl.Buffered(1))
    return pl.pallas_call(
        functools.partial(finish_kernel, len(grads)),
        grid=(LEN // TILE,),
        in_specs=[rows, rows, *[whole(w) for w in weights], whole(gain)]
        + [pl.BlockSpec((g.shape[0], TILE), lambda i: (0, i)) for g in grads],
        out_specs=rows,
        out_shape=shaped((LEN, D), F32),
        compiler_params=pltpu.CompilerParams(vmem_limit_bytes=48 << 20),
        cost_estimate=estimate(5),
        name="finish",
    )(tokens, residual, *weights, gain, *grads)


def split_lanes(values, experts):
    lanes = lax.broadcasted_iota(jnp.int32, values.shape, 1)
    high = values.astype(BF16).astype(F32)
    return jnp.where(lanes < experts, high, jnp.where(lanes < 2 * experts, values - high, 0.0)).astype(BF16)


def join_lanes(parts, experts):
    return parts + pltpu.roll(parts, LANES - experts, 1)


def route_kernel(experts, tokens, attn, w_out, gain, w_router, routes, residual, rows, gate):
    values = tokens[...].astype(F32) + dot(attn[...], w_out[...], TN)
    residual[...] = values
    normed = (values * rms_scale(values) * gain[...]).astype(BF16)
    logits = dot(normed, w_router[...], NN)
    lanes = lax.broadcasted_iota(jnp.int32, logits.shape, 1)
    expert = lax.rem(lanes, experts)
    chosen = lanes < 0
    for k in range(routes.shape[1]):
        chosen = chosen | (routes[:, k : k + 1] == expert)
    chosen = chosen & (lanes < 2 * experts)
    logits = jnp.where(chosen, logits, masked_score)
    weights = jnp.exp(logits - jnp.max(logits, axis=1, keepdims=True))
    share = weights / (0.5 * jnp.sum(weights, axis=1, keepdims=True))
    gate[...] = share
    rows[:, :D] = normed
    rows[:, D:] = split_lanes(share, experts)


def route_call(experts, tokens, attn, w_out, gain, w_router, routes):
    rows = lambda cols: pl.BlockSpec((TILE, cols), lambda i: (i, 0))
    whole = lambda *shape: pl.BlockSpec(shape, lambda i: (0, 0), pipeline_mode=pl.Buffered(1))
    return pl.pallas_call(
        functools.partial(route_kernel, experts),
        grid=(LEN // TILE,),
        in_specs=[rows(D), pl.BlockSpec((D, TILE), lambda i: (0, i)), whole(D, D), whole(1, D), whole(D, LANES)]
        + [rows(routes.shape[1])],
        out_specs=[rows(D), rows(WIDTH), rows(LANES)],
        out_shape=[shaped((LEN, D), F32), shaped((LEN, WIDTH), BF16), shaped((LEN, LANES), F32)],
        compiler_params=pltpu.CompilerParams(vmem_limit_bytes=60 << 20),
        cost_estimate=estimate(5),
        name="route",
    )(tokens, attn, w_out, gain, w_router, routes)


def merge_kernel(experts, mark, kept, kept_share, landed, out):
    out[:, :D] = (kept[...].astype(F32) + landed[:, :D].astype(F32)).astype(BF16)
    if kept_share is not None:
        share = kept_share[...] + join_lanes(landed[:, D:].astype(F32), experts)
        share = jnp.where(lax.broadcasted_iota(jnp.int32, share.shape, 1) < experts, share, 0.0)
        out[:, D:] = split_lanes(share + pltpu.roll(share, experts, 1), experts)


def merge_call(experts, mark, kept, kept_share, landed):
    rows = lambda cols: pl.BlockSpec((TILE, cols), lambda i: (i, 0))
    width = landed.shape[1]
    kernel = functools.partial(merge_kernel, experts)
    if kept_share is None:
        kernel = lambda mark, kept, landed, out: merge_kernel(experts, mark, kept, None, landed, out)
    return pl.pallas_call(
        kernel,
        grid=(LEN // TILE,),
        in_specs=[ANY, rows(D)] + ([] if kept_share is None else [rows(LANES)]) + [rows(width)],
        out_specs=rows(width),
        out_shape=shaped((LEN, width), BF16),
        compiler_params=pltpu.CompilerParams(vmem_limit_bytes=32 << 20),
        cost_estimate=estimate(3),
        name="merge",
    )(*[ref for ref in (mark, kept, kept_share, landed) if ref is not None])


def back_kernel(
    experts, mark, kept, kept_share, core, chip, residual, cotangent, gate, gain, w_router, w_out, d_res, d_mix, d_attn, d_router
):
    @pl.when(pl.program_id(0) == 0)
    def _():
        d_router[...] = jnp.zeros_like(d_router)

    landed = core[:, D:].astype(F32) + chip[:, D:].astype(F32)
    share = kept_share[...] + join_lanes(landed, experts)
    first = lax.broadcasted_iota(jnp.int32, share.shape, 1) < experts
    gates = jnp.where(first, gate[...], 0.0)
    inner = jnp.sum(gates * share, axis=1, keepdims=True)
    d_logits = jnp.where(first, gates * (share - inner), 0.0).astype(BF16)
    d_normed = kept[...].astype(F32) + core[:, :D].astype(F32) + chip[:, :D].astype(F32) + dot(d_logits, w_router[...], NT)
    values, gains = residual[...], gain[...]
    scale = rms_scale(values)
    norm = values * scale
    d_gain = jnp.sum(d_normed * norm, axis=0, keepdims=True)
    scaled = d_normed * gains
    d_values = cotangent[...].astype(F32) + scale * (scaled - norm * jnp.mean(scaled * norm, axis=1, keepdims=True))
    d_res[...] = d_values
    mixed = d_values.astype(BF16)
    d_mix[...] = mixed
    d_attn[...] = dot(w_out[...], mixed, NT).astype(BF16)
    d_router[...] += dot(d_logits, (norm * gains).astype(BF16), TN)
    d_router[experts : experts + 1] += d_gain


def back_call(experts, mark, kept, kept_share, core, chip, residual, cotangent, gate, gain, w_router, w_out):
    rows = lambda cols: pl.BlockSpec((TILE, cols), lambda i: (i, 0))
    whole = lambda *shape: pl.BlockSpec(shape, lambda i: (0, 0), pipeline_mode=pl.Buffered(1))
    return pl.pallas_call(
        functools.partial(back_kernel, experts),
        grid=(LEN // TILE,),
        in_specs=[ANY, rows(D), rows(LANES), rows(WIDTH), rows(WIDTH), rows(D), rows(D), rows(LANES)]
        + [whole(1, D), whole(D, LANES), whole(D, D)],
        out_specs=[rows(D), rows(D), pl.BlockSpec((D, TILE), lambda i: (0, i)), whole(LANES, D)],
        out_shape=[
            shaped((LEN, D), F32),
            shaped((LEN, D), BF16),
            shaped((D, LEN), BF16),
            shaped((LANES, D), F32),
        ],
        compiler_params=pltpu.CompilerParams(vmem_limit_bytes=48 << 20),
        cost_estimate=estimate(8),
        name="back",
    )(mark, kept, kept_share, core, chip, residual, cotangent, gate, gain, w_router, w_out)


def out_kernel(mark, attn, mixed, small, out):
    out[:, :D] = dot(attn[...], mixed[...], NN).astype(BF16)
    out[:, D:] = small[...].T.astype(BF16)


def out_call(mark, attn, mixed, small):
    return pl.pallas_call(
        out_kernel,
        grid=(D // TILE,),
        in_specs=[
            ANY,
            pl.BlockSpec((TILE, LEN), lambda i: (i, 0)),
            pl.BlockSpec((LEN, D), lambda i: (0, 0), pipeline_mode=pl.Buffered(1)),
            pl.BlockSpec((LANES, TILE), lambda i: (0, i)),
        ],
        out_specs=pl.BlockSpec((TILE, WIDTH), lambda i: (i, 0)),
        out_shape=shaped((D, WIDTH), BF16),
        compiler_params=pltpu.CompilerParams(vmem_limit_bytes=32 << 20),
        cost_estimate=estimate(5),
        name="out_grad",
    )(mark, attn, mixed, small)


def pause_kernel(mark, out):
    out[...] = mark[...]


def pause_call(mark):
    return pl.pallas_call(
        pause_kernel, out_shape=shaped(mark.shape, mark.dtype), cost_estimate=estimate(10), name="pause"
    )(mark)


def expert_kernel(count, experts, fresh, first, last_tokens, steps, ids, mark, *rest):
    rest = list(rest)

    def take(number):
        taken = rest[:number]
        del rest[:number]
        return taken

    n2, up = take(2), take(2)
    w_in = [take(2) for _ in range(count)]
    sums_in = [[] if new else take(2) for new in fresh]
    carry_in = [] if first else take(3)
    outs = take(5) if last_tokens else take(3)
    sums_out = [take(2) for _ in range(count)]
    weights, sums = take(1)[0], take(1)[0]
    low, sem = rest
    half = weights.shape[1] // 6
    width = 2 * half
    step = pl.program_id(0)
    ahead = step < steps // 2

    def pieces_of(parts, whole):
        return [
            (ref.at[pl.ds(kind * half, half)], whole.at[pl.ds((2 * kind + part) * half, half)])
            for kind in range(3)
            for part, ref in enumerate(parts)
        ]

    def copies_of(pairs, lane):
        return [pltpu.make_async_copy(a, b, sem.at[lane, n]) for n, (a, b) in enumerate(pairs)]

    loads = [copies_of(pieces_of(w_in[e], weights.at[e]), e) for e in range(count)]
    prior = [[] if fresh[e] else copies_of(pieces_of(sums_in[e], low.at[e]), count + e) for e in range(count)]
    stores = [copies_of([(b, a) for a, b in pieces_of(sums_out[e], low.at[e])], e) for e in range(count)]

    @pl.when(step == 0)
    def _():
        for copy in sum(loads + prior, []):
            copy.start()
        sums[...] = jnp.zeros_like(sums)
        for copy in sum(loads, []):
            copy.wait()

    rows = jnp.where(ahead, n2[0][...], n2[1][...])
    grads = jnp.where(ahead, up[0][...], up[1][...])
    rows, gates = rows[:, :D], rows[:, D:].astype(F32)
    lanes = lax.broadcasted_iota(jnp.int32, gates.shape, 1)
    mixed = d_rows = d_shares = None
    add = lambda total, value: value if total is None else total + value
    for e in range(count):
        w_both, w_down = weights.at[e, : 2 * width], weights.at[e, 2 * width :]
        hit = (lanes == ids[e]) | (lanes == ids[e] + experts)
        share = jnp.sum(jnp.where(hit, gates, 0.0), axis=1, keepdims=True)
        acts = dot(rows, w_both[...], NT)
        gate_act, up_act = acts[:, :width], acts[:, width:]
        d_plain = dot(grads, w_down[...], NT)
        sigmoid = 1.0 / (1.0 + jnp.exp(-gate_act))
        silu = gate_act * sigmoid
        hidden = silu * up_act
        shared = (share * hidden).astype(BF16)
        d_share = jnp.sum(hidden * d_plain, axis=1, keepdims=True)
        d_hidden = share * d_plain
        d_gate = (d_hidden * up_act * (sigmoid + silu * (1.0 - sigmoid))).astype(BF16)
        d_up = (d_hidden * silu).astype(BF16)
        d_both = jnp.concatenate([d_gate, d_up], axis=1)
        mixed = add(mixed, dot(shared, w_down[...], NN))
        d_rows = add(d_rows, dot(d_both, w_both[...], NN))
        d_shares = add(d_shares, jnp.where(hit, d_share, 0.0))
        sums[e, : 2 * width] += dot(d_both, rows, TN)
        sums[e, 2 * width :] += dot(shared, grads, TN)

        @pl.when(step == steps - 1)
        def _(e=e):
            for copy in prior[e]:
                copy.wait()
            low[e] = (sums[e] if fresh[e] else sums[e] + low[e].astype(F32)).astype(BF16)
            for copy in stores[e]:
                copy.start()

    results = [mixed, d_rows, d_shares]
    if not first:
        results = [result + ref[...].astype(F32) for result, ref in zip(results, carry_in)]
    if last_tokens:

        @pl.when(ahead)
        def _():
            for ref, result in zip(outs[:3], results):
                ref[...] = result.astype(ref.dtype)

        @pl.when(jnp.logical_not(ahead))
        def _():
            outs[3][...] = results[0].astype(BF16)
            outs[4][:, :D] = results[1].astype(BF16)
            outs[4][:, D:] = split_lanes(results[2], experts)
    else:
        for ref, result in zip(outs, results):
            ref[...] = result.astype(ref.dtype)

    @pl.when(step == steps - 1)
    def _():
        for copy in sum(stores, []):
            copy.wait()


def expert_call(ids, mark, experts, n2, up, weights, sums, carry, last_tokens):
    tokens, height, count = 2 * n2[0].shape[0], weights[0][0].shape[0], len(weights)
    steps = tokens // TILE
    rows = lambda cols: pl.BlockSpec((TILE, cols), lambda i: (i, 0))
    near = lambda cols: pl.BlockSpec((TILE, cols), lambda i: (jnp.minimum(i, steps // 2 - 1), 0))
    far = lambda cols: pl.BlockSpec((TILE, cols), lambda i: (jnp.maximum(i - steps // 2, 0), 0))
    ins = [ids, mark, *n2, *up] + [w for pair in weights for w in pair]
    specs = [SMEM, ANY, near(WIDTH), far(WIDTH), near(D), far(D)] + [ANY] * (2 * count)
    fresh, first = [pair is None for pair in sums], carry is None
    columns = (D, D, LANES)
    if last_tokens:
        outs = [shaped((tokens // 2, c), t) for c, t in zip(columns, (BF16, BF16, F32))]
        outs += [shaped((tokens // 2, c), BF16) for c in (D, WIDTH)]
        out_specs = [near(c) for c in columns] + [far(D), far(WIDTH)]
    else:
        outs = [shaped((tokens, c), t) for c, t in zip(columns, (BF16, F32, F32))]
        out_specs = [rows(c) for c in columns]
    aliases = {}
    for pair in sums:
        if pair is not None:
            ins += pair
            specs += [ANY, ANY]
    if not first:
        if not last_tokens:
            aliases.update({len(ins) + k: k for k in range(3)})
        ins += carry
        specs += [rows(c) for c in columns]
    tokens_out = len(outs)
    for _ in range(count):
        outs += [shaped((height, D), BF16)] * 2
        out_specs += [ANY, ANY]
    scratch = [pltpu.VMEM((count, 2 * height, D), BF16), pltpu.VMEM((count, 2 * height, D), F32)]
    scratch.append(pltpu.VMEM((count, 2 * height, D), BF16))
    scratch.append(pltpu.SemaphoreType.DMA((2 * count, 6)))
    done = pl.pallas_call(
        functools.partial(expert_kernel, count, experts, fresh, first, last_tokens, steps),
        grid=(steps,),
        in_specs=specs,
        out_specs=out_specs,
        out_shape=outs,
        scratch_shapes=scratch,
        input_output_aliases=aliases,
        compiler_params=pltpu.CompilerParams(vmem_limit_bytes=63 << 20),
        cost_estimate=estimate(15 * count),
        name="expert",
    )(*ins)
    return list(done[:tokens_out]), [tuple(done[tokens_out + 2 * e : tokens_out + 2 * e + 2]) for e in range(count)]


def join_kernel(side, held, landed, gate, up, down):
    here = pl.program_id(0) == 0
    rows = jnp.where(here, held[...], landed[...]).astype(F32)
    half = down.shape[0]
    gate[...] = rows[:half].T
    up[...] = rows[half : 2 * half].T
    down[...] = rows[2 * half :]


def join_call(side, held, landed):
    half = held.shape[0] // 3
    whole = pl.BlockSpec(held.shape, lambda i, side: (0, 0))
    columns = pl.BlockSpec((D, half), lambda i, side: (0, lax.rem(side[0] + i, 2)))
    return pl.pallas_call(
        join_kernel,
        grid_spec=pltpu.PrefetchScalarGridSpec(
            num_scalar_prefetch=1,
            grid=(2,),
            in_specs=[whole, whole],
            out_specs=[columns, columns, pl.BlockSpec((half, D), lambda i, side: (lax.rem(side[0] + i, 2), 0))],
        ),
        out_shape=[shaped((D, 2 * half), F32), shaped((D, 2 * half), F32), shaped((2 * half, D), F32)],
        compiler_params=pltpu.CompilerParams(vmem_limit_bytes=48 << 20),
        cost_estimate=estimate(5),
        name="join",
    )(side, held, landed)


def after(values, *others):
    return lax.optimization_barrier((values, *others))[0]


class Task:
    def __init__(self, steps):
        self.steps, self.result, self.over = steps, None, False

    def step(self):
        if self.over:
            return []
        try:
            return [next(self.steps)]
        except StopIteration as stop:
            self.result, self.over = stop.value, True
            return [self.result]

    def finish(self):
        while not self.over:
            self.step()
        return self.result


def local(
    tokens,
    routes,
    pieces,
    attn_gain,
    w_query,
    w_key,
    w_value,
    w_out,
    ffn_gain,
    w_router,
    expert_gate,
    expert_up,
    expert_down,
    cotangent,
):
    shards, reps = lax.axis_size("ep"), lax.axis_size("rep")
    experts = w_router.shape[1]
    slots = shards // GROUP
    place = lax.axis_index("ep")
    side = lax.axis_index("rep") % 2

    def swap(values, bits):
        return lax.ppermute(values, "ep", [(i, i ^ bits) for i in range(shards)])

    def swap_rep(values, bits=1):
        return lax.ppermute(values, "rep", [(i, i ^ bits) for i in range(reps)])


    def reduce_reps(values, bits=1):
        while bits < reps:
            values = values.astype(BF16)
            landed = swap_rep(values, bits)
            yield values
            values = values.astype(F32) + hold(landed).astype(F32)
            bits *= 2
        return values

    def reduce_rows(values):
        values = values.reshape(shards, -1, values.shape[1])
        bits = 1
        while bits < shards:
            values = values.reshape(values.shape[0] // 2, 2, *values.shape[1:])
            bit = (place // bits) % 2
            kept, sent = [
                lax.dynamic_index_in_dim(values, index, axis=1, keepdims=False) for index in (bit, 1 - bit)
            ]
            landed = swap(sent, bits)
            yield sent
            values = (kept.astype(F32) + hold(landed).astype(F32)).astype(BF16)
            bits *= 2
        return (yield from reduce_reps(values[0]))

    def sum_steps(slot, own, other):
        other = hold(other)
        landed = swap_rep(other)
        yield other
        own = own.astype(F32) + hold(landed).astype(F32)
        if slot == 0:
            return own
        if slot == 2 and slots > 3:
            own = own + tasks[3].finish().astype(F32)
        own = own.astype(BF16)
        landed = swap(own, GROUP if slot == 3 else slot * GROUP)
        yield own
        return hold(landed)

    with jax.named_scope("weights_out"):
        turned = side.astype(jnp.int32).reshape(1)
        mine, theirs = halve_call(turned, expert_gate[0], expert_up[0], expert_down[0])
        tokens, mine, theirs = lax.optimization_barrier((tokens, mine, theirs))
        near = swap(mine, GROUP)

    with jax.named_scope("cotangent_out"):
        grads_next = swap(cotangent, 2)
        grads_in = [(cotangent, swap(cotangent, 1)), None]

    with jax.named_scope("attention"):
        inputs = tokens.astype(F32)
        scale_one = rms_scale(inputs)
        norm_one = inputs * scale_one
        normed_one = (norm_one * attn_gain).astype(BF16)
        w_dims = (((0,), (1,)), ((), ()))
        projections = (w_query, w_key, w_value)
        query, key, value = [dot(w, normed_one, w_dims) for w in projections]
        far = swap(after(mine, key, value, query), 2 * GROUP)
        cosine, sine = [jnp.asarray(table) for table in rotary_tables()]
        attn, query_rot, key_rot, value_low, lse = attend_call(pieces, query, key, value, cosine, sine)
        attn = after(attn, grads_next, grads_in[0][1])

    with jax.named_scope("cotangent_out"):
        grads_in[1] = (grads_next, swap(after(grads_next, attn), 1))

    with jax.named_scope("routing"):
        pad = jnp.zeros((D, LANES - 2 * experts), BF16)
        router_twice = jnp.concatenate([w_router, w_router, pad], axis=1)
        gain_two = ffn_gain.reshape(1, D)
        residual, rows, gate = route_call(experts, tokens, attn, w_out, gain_two, router_twice, routes)
        rows, _, near = lax.optimization_barrier((rows, grads_in[1][1], near))
        rows_next = swap(rows, 2)
        rows_in = [(rows, swap(rows, 1)), None]

    with jax.named_scope("weights_out"):
        weights = {0: (mine, theirs), 1: (near, swap_rep(near))}
        ids = [((place // GROUP) ^ slot) * GROUP + place % GROUP for slot in range(slots)]
        ids = [expert.astype(jnp.int32) for expert in ids]

    carry, sums, tasks = [None, None], [None] * slots, [None] * slots
    mark, point = after(jnp.zeros((8, LANES), F32), rows), rows

    def tick(*arrays):
        nonlocal mark
        mark = after(mark, *arrays)

    def hold(values):
        return after(values, point)

    def pause():
        nonlocal mark
        mark = pause_call(mark)

    def pulse():
        return swap(mark, 1)

    def passed(value, beat=None):
        nonlocal mark, point
        if beat is not None:
            mark = mark + beat
        mark, point = after(mark, value), value

    def run(chip, group, last=False, beats=True):
        beat = pulse() if beats else None
        carry[chip], done = expert_call(
            jnp.stack([ids[slot] for slot in group]),
            mark,
            experts,
            rows_in[chip],
            grads_in[chip],
            [weights[slot] for slot in group],
            [sums[slot] for slot in group],
            carry[chip],
            last,
        )
        passed(carry[chip][2], beat)
        for slot, pair in zip(group, done):
            if sums[slot] is not None:
                tasks[slot] = Task(sum_steps(slot, *pair))
            sums[slot] = pair

    with jax.named_scope("experts"):
        pause()
        run(0, [0], beats=False)
        tick(weights[1][1], far)
        far = hold(far)
        weights[2] = (far, swap_rep(far))
        landed = {slot: swap(far, GROUP) if slot == 3 else swap(hold(mine), slot * GROUP) for slot in range(3, slots)}
        run(0, [1])
        tick(rows_next, weights[2][1], *landed.values())
        for slot, held in landed.items():
            held = hold(held)
            weights[slot] = (held, swap_rep(held))
        rows_in[1] = (rows_next, swap(hold(rows_next), 1))
        pause()
        tick(rows_in[1][1])
        run(1, [0, 1])
        tick(*[weights[slot][1] for slot in landed])
        tasks[1].step()
        for slot in range(4, slots, 2):
            run(1, [slot, slot + 1])
            run(0, [slot])
            run(0, [slot + 1])
        run(1, [2, 3], True)
        there_landed = swap(hold(carry[1][4]), 1)
        pause()
        there = merge_call(experts, mark, carry[1][1], carry[1][2], there_landed)
        d_next = swap(there, 2)
        tick(there, *tasks[1].step())
        tasks[0].step()
        mix_landed = swap(hold(carry[1][3]), 1)
        run(0, [3])
        mix_there = merge_call(experts, mark, carry[1][0], None, mix_landed)
        tick(mix_there, *tasks[0].step())
        tasks[3].step()
        run(0, [2], True)

    with jax.named_scope("routing_back"):
        d_core = swap(hold(carry[0][4]), 1)
        tasks[2].step()
        pause()
        tick(d_core, d_next, *[array for task in tasks[3:] for array in task.step()])
        point = mark
        mix_home = swap(hold(mix_there), 2)
        mix_core = swap(hold(carry[0][3]), 1)
        beat = pulse()
        d_residual, d_mixed, d_attn, d_small = back_call(
            experts, mark, carry[0][1], carry[0][2], d_core, d_next, residual, cotangent, gate, gain_two, router_twice, w_out
        )
        passed(d_small, beat)
        tick(mix_core)
        d_out = out_call(mark, attn, d_mixed, d_small)
        passed(d_out)

    with jax.named_scope("attention_back"):
        in_dims = (((0,), (1,)), ((), ()))
        out_task, w_tasks, d_packed = Task(reduce_rows(d_out)), [], []
        tick(*out_task.step())
        for part in range(PARTS):
            packed = None
            for turn in range(TURNS):
                beat = pulse() if (part, turn) == (0, 1) else None
                packed = attend_back_call(
                    part, turn, mark, pieces, query_rot, key_rot, value_low, d_attn, attn, lse, cosine, sine, packed
                )
                passed(packed, beat)
                if (part, turn) == (0, 0):
                    tick(*tasks[2].step())
                if (part, turn) == (1, 0):
                    tick(mix_home)
                stepped = [array for task in w_tasks for array in task.step()]
                stepped += out_task.step() if part == turn else []
                tick(*stepped)
            d_packed.append(packed)
            w_tasks.append(Task(reduce_rows(dot(normed_one, packed, in_dims).astype(BF16))))
            if part < PARTS - 1:
                tick(*w_tasks[-1].step())

    with jax.named_scope("tail"):
        last, other = w_tasks[1], w_tasks[0]
        mix_home = after(mix_home, packed, *stepped, *last.step())
        output = point = (residual + carry[0][0].astype(F32) + mix_core.astype(F32) + mix_home.astype(F32)).astype(BF16)
        stepped = last.step() + other.step() + out_task.step()
        gain_one = after(attn_gain.reshape(1, D), output, *stepped)
        d_tokens = point = finish_call(tokens, d_residual, projections, gain_one, d_packed)

    with jax.named_scope("sums_experts"):
        total = tasks[0].finish()
        for task in tasks[1:3] + tasks[4:]:
            total = total + task.finish().astype(F32)
        total = Task(reduce_reps(total, 2)).finish().astype(BF16)
        total_landed = swap_rep(total)
        stepped = last.step() + other.step() + out_task.step()
        total, total_landed = lax.optimization_barrier((total, total_landed, *stepped))[:2]
        s_gate, s_up, s_down = join_call(turned, total, total_landed)

    with jax.named_scope("sums_rest"):
        s_mixed = out_task.finish()
        s_out, s_small = s_mixed[:, :D], s_mixed[:, D:]
        count = s_out.shape[0]
        first = place * count
        s_parts = [task.finish() for task in w_tasks]
        s_attn, groups = 0.0, []
        for k, w in enumerate(projections):
            wide = w.shape[1] // PARTS
            cut = sum(v.shape[1] // PARTS for v in projections[:k])
            groups.append(jnp.concatenate([part[:, cut : cut + wide] for part in s_parts], axis=1))
            s_attn += jnp.sum(groups[-1] * lax.dynamic_slice_in_dim(w, first, count).astype(F32), axis=1)
        s_query, s_key, s_value = groups
        s_attn = s_attn / lax.dynamic_slice_in_dim(attn_gain, first, count)

    return (
        output,
        d_tokens,
        s_attn,
        s_query,
        s_key,
        s_value,
        s_out,
        s_small[:, experts],
        s_small[:, :experts],
        s_gate[None],
        s_up[None],
        s_down[None],
    )


def solution(mesh):
    rows, whole, slices = P(("rep", "ep"), None), P(), P("ep", None)
    expert = P("ep", None, None)
    return jax.shard_map(
        local,
        mesh=mesh,
        in_specs=(rows,) * 3 + (whole,) * 7 + (expert,) * 3 + (rows,),
        out_specs=(rows, rows, P("ep")) + (slices,) * 4 + (P("ep"), slices) + (expert,) * 3,
        check_vma=False,
    )
```

```python
import functools
import math

import jax
import jax.numpy as jnp
import numpy as np
from jax import lax
from jax.experimental import pallas as pl
from jax.experimental.pallas import tpu as pltpu
from jax.sharding import PartitionSpec as P

D = 1536
HEADS = 24
KV = 8
HEAD = 64
LEN = 1024
PIECE = 256
QUERIES = HEADS // KV
WIDE = 256
TILE = 256
GROUP = 4
PARTS = 2
TURNS = 2
LANES = 128
WIDTH = D + LANES

eps = 1e-06
theta_base = 10000.0
masked_score = -1e30
score_scale = HEAD ** (-0.5)
two_scale = score_scale * math.log2(math.e)

F32 = jnp.float32
BF16 = jnp.bfloat16
NN = (((1,), (0,)), ((), ()))
NT = (((1,), (1,)), ((), ()))
TN = (((0,), (0,)), ((), ()))
ANY = pl.BlockSpec(memory_space=pl.ANY)
SMEM = pl.BlockSpec(memory_space=pltpu.SMEM)


def dot(left, right, dims):
    return lax.dot_general(left, right, dims, preferred_element_type=F32)


def shaped(shape, dtype):
    return jax.ShapeDtypeStruct(shape, dtype)


def estimate(micros):
    return pl.CostEstimate(flops=int(micros * 1e10), bytes_accessed=int(micros * 1e6), transcendentals=0)


def rms_scale(values):
    return lax.rsqrt(jnp.mean(values * values, axis=-1, keepdims=True) + eps)


def rotary_tables():
    half_head = HEAD // 2
    frequency = theta_base ** (-(np.arange(half_head, dtype=np.float64) * 2.0) / HEAD)
    angles = frequency[:, None] * np.arange(LEN, dtype=np.float64)[None, :]
    return np.cos(angles).astype(np.float32), np.sin(angles).astype(np.float32)


def turn(values, cosine, sine):
    first, second = values[: HEAD // 2], values[HEAD // 2 :]
    return jnp.concatenate([first * cosine - second * sine, second * cosine + first * sine], axis=0)


def turn_back(grads, cosine, sine):
    first, second = grads[: HEAD // 2], grads[HEAD // 2 :]
    return jnp.concatenate([first * cosine + second * sine, second * cosine - first * sine], axis=0)


def fill_bias(pieces, bias):
    for block in range(LEN // WIDE):
        first = block * WIDE
        shape = bias.shape[1:]
        key = lax.broadcasted_iota(jnp.int32, shape, 0) + first
        query = lax.broadcasted_iota(jnp.int32, shape, 1) + first
        allowed = key <= query
        for piece in range(pieces.shape[1]):
            start = pieces[0, piece]
            low, high = jnp.minimum(key, query), jnp.maximum(key, query)
            allowed = allowed | ((low >= start) & (high < start + PIECE))
        bias[block] = jnp.where(allowed, 0.0, masked_score)


def key_span(block):
    return block * WIDE, min((block + 2) * WIDE, LEN)


def rows_at(place):
    return pl.BlockSpec((HEAD, LEN), lambda *grid: (place(*grid), 0))


def table_spec():
    return pl.BlockSpec((HEAD // 2, LEN), lambda *grid: (0, 0))


def attend_kernel(pieces, q0, q1, q2, k_in, v_in, cosine, sine, attn, q_out, k_out, v_out, lse, bias):
    @pl.when(pl.program_id(0) == 0)
    def _():
        fill_bias(pieces, bias)

    cos, sin = cosine[...], sine[...]
    k_rot = turn(k_in[...], cos, sin) * two_scale
    k_out[...] = k_rot.astype(BF16)
    keys = k_rot.T.astype(BF16)
    values = v_in[...].astype(BF16)
    v_out[...] = values
    for head, q_in in enumerate((q0, q1, q2)):
        rows = pl.ds(head * HEAD, HEAD)
        q_rot = turn(q_in[...], cos, sin).astype(BF16)
        q_out[rows, :] = q_rot
        for block in range(LEN // WIDE):
            columns = pl.ds(block * WIDE, WIDE)
            first, last = key_span(block)
            queries = q_rot[:, block * WIDE : (block + 1) * WIDE]
            spans = [(first, last)] + ([(0, first)] if first > 0 else [])
            scores = [dot(keys[a:b], queries, NN) for a, b in spans]
            scores[0] = scores[0] + bias[block, : last - first]
            highest = functools.reduce(jnp.maximum, [jnp.max(s, axis=0, keepdims=True) for s in scores])
            weights = [jnp.exp2(s - highest) for s in scores]
            total = sum(jnp.sum(w, axis=0, keepdims=True) for w in weights)
            mixed = sum(dot(values[:, a:b], w.astype(BF16), NN) for (a, b), w in zip(spans, weights)) / total
            attn[rows, columns] = mixed.astype(BF16)
            lse[head : head + 1, columns] = highest + jnp.log2(total)


def attend_call(pieces, query, key, value, cosine, sine):
    rows = lambda count: pl.BlockSpec((count, LEN), lambda i: (i, 0))
    width = QUERIES * HEAD
    return pl.pallas_call(
        attend_kernel,
        grid=(KV,),
        in_specs=[SMEM]
        + [rows_at(lambda i, head=head: QUERIES * i + head) for head in range(QUERIES)]
        + [rows_at(lambda i: i), rows_at(lambda i: i)]
        + [table_spec(), table_spec()],
        out_specs=[rows(width), rows(width), rows(HEAD), rows(HEAD), rows(8)],
        out_shape=[
            shaped((D, LEN), BF16),
            shaped((D, LEN), BF16),
            shaped((KV * HEAD, LEN), BF16),
            shaped((KV * HEAD, LEN), BF16),
            shaped((KV * 8, LEN), F32),
        ],
        scratch_shapes=[pltpu.VMEM((LEN // WIDE, 2 * WIDE, WIDE), F32)],
        compiler_params=pltpu.CompilerParams(vmem_limit_bytes=48 << 20),
        cost_estimate=estimate(25),
        name="attend",
    )(pieces, *[query] * QUERIES, key, value, cosine, sine)


def with_parts(columns, row):
    rank = lax.broadcasted_iota(jnp.int32, columns.shape, 0)
    high = row.astype(BF16).astype(F32)
    middle = (row - high).astype(BF16).astype(F32)
    parts = jnp.where(rank == 0, high, jnp.where(rank == 1, middle, jnp.where(rank == 2, row - high - middle, 0.0)))
    return jnp.concatenate([columns, parts.astype(BF16)], axis=0)


def attend_back_kernel(
    mark, pieces, q_in, k_in, v_in, do_in, attn, lse, cosine, sine, *rest
):
    out, bias, keys_kept, values_kept, dk_sum, dv_sum = rest[-6:]
    kind = pl.program_id(1)

    @pl.when((pl.program_id(0) == 0) & (kind == 0))
    def _():
        fill_bias(pieces, bias)

    cos, sin = cosine[...], sine[...]

    @pl.when(kind == 0)
    def _():
        tail = jnp.where(lax.broadcasted_iota(jnp.int32, (LEN, HEAD), 1) < 3, -1.0, 0.0)
        for kept, ref in ((keys_kept, k_in), (values_kept, v_in)):
            kept[...] = jnp.concatenate([ref[...].astype(F32).T, tail], axis=1).astype(BF16)
        dk_sum[...] = jnp.zeros_like(dk_sum)
        dv_sum[...] = jnp.zeros_like(dv_sum)

    @pl.when(kind < QUERIES)
    def _():
        k_cols, keys, values = k_in[...], keys_kept[...], values_kept[...]
        q_cols, do_cols = q_in[...], do_in[...]
        q_rows = q_cols.astype(F32).T.astype(BF16)
        do_rows = do_cols.astype(F32).T.astype(BF16)
        delta = jnp.sum(do_cols.astype(F32) * attn[...].astype(F32), axis=0, keepdims=True)
        q_wide = with_parts(q_cols, lse[pl.ds(kind, 1), :])
        do_wide = with_parts(do_cols, delta)
        for block in range(LEN // WIDE):
            part = slice(block * WIDE, (block + 1) * WIDE)
            first, last = key_span(block)
            d_query = 0.0
            for a, b in [(first, last)] + ([(0, first)] if first > 0 else []):
                scores = dot(keys[a:b], q_wide[:, part], NN)
                if a == first:
                    scores = scores + bias[block, : b - a]
                probs = jnp.exp2(scores)
                d_scores = (probs * dot(values[a:b], do_wide[:, part], NN)).astype(BF16)
                dv_sum[a:b] += dot(probs.astype(BF16), do_rows[part], NN)
                dk_sum[a:b] += dot(d_scores, q_rows[part], NN)
                d_query = d_query + dot(k_cols[:, a:b], d_scores, NN)
            out[:, part] = turn_back(d_query * math.log(2.0), cos[:, part], sin[:, part]).astype(BF16)

    @pl.when(kind == QUERIES)
    def _():
        out[...] = turn_back(dk_sum[...].T * score_scale, cos, sin).astype(BF16)

    @pl.when(kind == QUERIES + 1)
    def _():
        out[...] = dv_sum[...].T.astype(BF16)


def attend_back_call(part, turn, mark, pieces, q_in, k_in, v_in, do_in, attn, lse, cosine, sine, before):
    group = KV // PARTS
    per = group // TURNS
    first = part * group + turn * per
    query = rows_at(lambda i, j: (first + i) * QUERIES + jnp.minimum(j, QUERIES - 1))
    key = rows_at(lambda i, j: first + i)

    def place(i, j):
        inner = turn * per + i
        tail = jnp.where(j == QUERIES, QUERIES * group + inner, (QUERIES + 1) * group + inner)
        return jnp.where(j < QUERIES, QUERIES * inner + j, tail)

    ins = [mark, pieces, q_in, k_in, v_in, do_in, attn, lse, cosine, sine] + ([] if before is None else [before])
    return pl.pallas_call(
        attend_back_kernel,
        grid=(per, QUERIES + 2),
        in_specs=[ANY, SMEM, query, key, key, query, query, pl.BlockSpec((8, LEN), lambda i, j: (first + i, 0))]
        + [table_spec(), table_spec()]
        + ([] if before is None else [ANY]),
        out_specs=rows_at(place),
        out_shape=shaped(((QUERIES + 2) * group * HEAD, LEN), BF16),
        input_output_aliases={} if before is None else {len(ins) - 1: 0},
        scratch_shapes=[
            pltpu.VMEM((LEN // WIDE, 2 * WIDE, WIDE), F32),
            pltpu.VMEM((LEN, 2 * HEAD), BF16),
            pltpu.VMEM((LEN, 2 * HEAD), BF16),
            pltpu.VMEM((LEN, HEAD), F32),
            pltpu.VMEM((LEN, HEAD), F32),
        ],
        compiler_params=pltpu.CompilerParams(vmem_limit_bytes=48 << 20),
        cost_estimate=estimate(15),
        name="attend_back",
    )(*ins)


def halve_kernel(side, gate, up, down, mine, theirs):
    half = down.shape[0]

    def write(out):
        out[:half] = gate[...].T
        out[half : 2 * half] = up[...].T
        out[2 * half :] = down[...]

    pl.when(pl.program_id(0) == 0)(lambda: write(mine))
    pl.when(pl.program_id(0) == 1)(lambda: write(theirs))


def halve_call(side, gate, up, down):
    half = down.shape[0] // 2
    columns = pl.BlockSpec((D, half), lambda i, side: (0, lax.rem(side[0] + i, 2)))
    whole = pl.BlockSpec((3 * half, D), lambda i, side: (0, 0))
    return pl.pallas_call(
        halve_kernel,
        grid_spec=pltpu.PrefetchScalarGridSpec(
            num_scalar_prefetch=1,
            grid=(2,),
            in_specs=[columns, columns, pl.BlockSpec((half, D), lambda i, side: (lax.rem(side[0] + i, 2), 0))],
            out_specs=[whole, whole],
        ),
        out_shape=[shaped((3 * half, D), BF16)] * 2,
        compiler_params=pltpu.CompilerParams(vmem_limit_bytes=60 << 20),
        cost_estimate=estimate(5),
        name="halve",
    )(side, gate, up, down)


def finish_kernel(parts, tokens, residual, w_query, w_key, w_value, gain, *rest):
    grads, out = rest[:-1], rest[-1]
    total = 0.0
    for part, ref in enumerate(grads):
        columns = ref[...].T
        first = 0
        for weight in (w_query, w_key, w_value):
            wide = weight.shape[1] // parts
            total = total + dot(columns[:, first : first + wide], weight[:, part * wide : (part + 1) * wide], NT)
            first += wide
    values = tokens[...].astype(F32)
    scale = rms_scale(values)
    norm = values * scale
    scaled = total * gain[...]
    out[...] = residual[...] + scale * (scaled - norm * jnp.mean(scaled * norm, axis=1, keepdims=True))


def finish_call(tokens, residual, weights, gain, grads):
    rows = pl.BlockSpec((TILE, D), lambda i: (i, 0))
    whole = lambda array: pl.BlockSpec(array.shape, lambda i: (0, 0), pipeline_mode=pl.Buffered(1))
    return pl.pallas_call(
        functools.partial(finish_kernel, len(grads)),
        grid=(LEN // TILE,),
        in_specs=[rows, rows, *[whole(w) for w in weights], whole(gain)]
        + [pl.BlockSpec((g.shape[0], TILE), lambda i: (0, i)) for g in grads],
        out_specs=rows,
        out_shape=shaped((LEN, D), F32),
        compiler_params=pltpu.CompilerParams(vmem_limit_bytes=48 << 20),
        cost_estimate=estimate(5),
        name="finish",
    )(tokens, residual, *weights, gain, *grads)


def split_lanes(values, experts):
    lanes = lax.broadcasted_iota(jnp.int32, values.shape, 1)
    high = values.astype(BF16).astype(F32)
    return jnp.where(lanes < experts, high, jnp.where(lanes < 2 * experts, values - high, 0.0)).astype(BF16)


def join_lanes(parts, experts):
    return parts + pltpu.roll(parts, LANES - experts, 1)


def route_kernel(experts, tokens, attn, w_out, gain, w_router, routes, residual, rows, gate):
    values = tokens[...].astype(F32) + dot(attn[...], w_out[...], TN)
    residual[...] = values
    normed = (values * rms_scale(values) * gain[...]).astype(BF16)
    logits = dot(normed, w_router[...], NN)
    lanes = lax.broadcasted_iota(jnp.int32, logits.shape, 1)
    expert = lax.rem(lanes, experts)
    chosen = lanes < 0
    for k in range(routes.shape[1]):
        chosen = chosen | (routes[:, k : k + 1] == expert)
    chosen = chosen & (lanes < 2 * experts)
    logits = jnp.where(chosen, logits, masked_score)
    weights = jnp.exp(logits - jnp.max(logits, axis=1, keepdims=True))
    share = weights / (0.5 * jnp.sum(weights, axis=1, keepdims=True))
    gate[...] = share
    rows[:, :D] = normed
    rows[:, D:] = split_lanes(share, experts)


def route_call(experts, tokens, attn, w_out, gain, w_router, routes):
    rows = lambda cols: pl.BlockSpec((TILE, cols), lambda i: (i, 0))
    whole = lambda *shape: pl.BlockSpec(shape, lambda i: (0, 0), pipeline_mode=pl.Buffered(1))
    return pl.pallas_call(
        functools.partial(route_kernel, experts),
        grid=(LEN // TILE,),
        in_specs=[rows(D), pl.BlockSpec((D, TILE), lambda i: (0, i)), whole(D, D), whole(1, D), whole(D, LANES)]
        + [rows(routes.shape[1])],
        out_specs=[rows(D), rows(WIDTH), rows(LANES)],
        out_shape=[shaped((LEN, D), F32), shaped((LEN, WIDTH), BF16), shaped((LEN, LANES), F32)],
        compiler_params=pltpu.CompilerParams(vmem_limit_bytes=60 << 20),
        cost_estimate=estimate(5),
        name="route",
    )(tokens, attn, w_out, gain, w_router, routes)


def merge_kernel(experts, mark, kept, kept_share, landed, out):
    out[:, :D] = (kept[...].astype(F32) + landed[:, :D].astype(F32)).astype(BF16)
    if kept_share is not None:
        share = kept_share[...] + join_lanes(landed[:, D:].astype(F32), experts)
        share = jnp.where(lax.broadcasted_iota(jnp.int32, share.shape, 1) < experts, share, 0.0)
        out[:, D:] = split_lanes(share + pltpu.roll(share, experts, 1), experts)


def merge_call(experts, mark, kept, kept_share, landed):
    rows = lambda cols: pl.BlockSpec((TILE, cols), lambda i: (i, 0))
    width = landed.shape[1]
    kernel = functools.partial(merge_kernel, experts)
    if kept_share is None:
        kernel = lambda mark, kept, landed, out: merge_kernel(experts, mark, kept, None, landed, out)
    return pl.pallas_call(
        kernel,
        grid=(LEN // TILE,),
        in_specs=[ANY, rows(D)] + ([] if kept_share is None else [rows(LANES)]) + [rows(width)],
        out_specs=rows(width),
        out_shape=shaped((LEN, width), BF16),
        compiler_params=pltpu.CompilerParams(vmem_limit_bytes=32 << 20),
        cost_estimate=estimate(3),
        name="merge",
    )(*[ref for ref in (mark, kept, kept_share, landed) if ref is not None])


def back_kernel(
    experts, mark, kept, kept_share, core, chip, residual, cotangent, gate, gain, w_router, w_out, d_res, d_mix, d_attn, d_router
):
    @pl.when(pl.program_id(0) == 0)
    def _():
        d_router[...] = jnp.zeros_like(d_router)

    landed = core[:, D:].astype(F32) + chip[:, D:].astype(F32)
    share = kept_share[...] + join_lanes(landed, experts)
    first = lax.broadcasted_iota(jnp.int32, share.shape, 1) < experts
    gates = jnp.where(first, gate[...], 0.0)
    inner = jnp.sum(gates * share, axis=1, keepdims=True)
    d_logits = jnp.where(first, gates * (share - inner), 0.0).astype(BF16)
    d_normed = kept[...].astype(F32) + core[:, :D].astype(F32) + chip[:, :D].astype(F32) + dot(d_logits, w_router[...], NT)
    values, gains = residual[...], gain[...]
    scale = rms_scale(values)
    norm = values * scale
    d_gain = jnp.sum(d_normed * norm, axis=0, keepdims=True)
    scaled = d_normed * gains
    d_values = cotangent[...].astype(F32) + scale * (scaled - norm * jnp.mean(scaled * norm, axis=1, keepdims=True))
    d_res[...] = d_values
    mixed = d_values.astype(BF16)
    d_mix[...] = mixed
    d_attn[...] = dot(w_out[...], mixed, NT).astype(BF16)
    d_router[...] += dot(d_logits, (norm * gains).astype(BF16), TN)
    d_router[experts : experts + 1] += d_gain


def back_call(experts, mark, kept, kept_share, core, chip, residual, cotangent, gate, gain, w_router, w_out):
    rows = lambda cols: pl.BlockSpec((TILE, cols), lambda i: (i, 0))
    whole = lambda *shape: pl.BlockSpec(shape, lambda i: (0, 0), pipeline_mode=pl.Buffered(1))
    return pl.pallas_call(
        functools.partial(back_kernel, experts),
        grid=(LEN // TILE,),
        in_specs=[ANY, rows(D), rows(LANES), rows(WIDTH), rows(WIDTH), rows(D), rows(D), rows(LANES)]
        + [whole(1, D), whole(D, LANES), whole(D, D)],
        out_specs=[rows(D), rows(D), pl.BlockSpec((D, TILE), lambda i: (0, i)), whole(LANES, D)],
        out_shape=[
            shaped((LEN, D), F32),
            shaped((LEN, D), BF16),
            shaped((D, LEN), BF16),
            shaped((LANES, D), F32),
        ],
        compiler_params=pltpu.CompilerParams(vmem_limit_bytes=48 << 20),
        cost_estimate=estimate(8),
        name="back",
    )(mark, kept, kept_share, core, chip, residual, cotangent, gate, gain, w_router, w_out)


def out_kernel(mark, attn, mixed, small, out):
    out[:, :D] = dot(attn[...], mixed[...], NN).astype(BF16)
    out[:, D:] = small[...].T.astype(BF16)


def out_call(mark, attn, mixed, small):
    return pl.pallas_call(
        out_kernel,
        grid=(D // TILE,),
        in_specs=[
            ANY,
            pl.BlockSpec((TILE, LEN), lambda i: (i, 0)),
            pl.BlockSpec((LEN, D), lambda i: (0, 0), pipeline_mode=pl.Buffered(1)),
            pl.BlockSpec((LANES, TILE), lambda i: (0, i)),
        ],
        out_specs=pl.BlockSpec((TILE, WIDTH), lambda i: (i, 0)),
        out_shape=shaped((D, WIDTH), BF16),
        compiler_params=pltpu.CompilerParams(vmem_limit_bytes=32 << 20),
        cost_estimate=estimate(5),
        name="out_grad",
    )(mark, attn, mixed, small)


def pause_kernel(mark, out):
    out[...] = mark[...]


def pause_call(mark):
    return pl.pallas_call(
        pause_kernel, out_shape=shaped(mark.shape, mark.dtype), cost_estimate=estimate(10), name="pause"
    )(mark)


def expert_kernel(count, experts, fresh, first, last_tokens, steps, ids, mark, *rest):
    rest = list(rest)

    def take(number):
        taken = rest[:number]
        del rest[:number]
        return taken

    n2, up = take(2), take(2)
    w_in = [take(2) for _ in range(count)]
    sums_in = [[] if new else take(2) for new in fresh]
    carry_in = [] if first else take(3)
    outs = take(5) if last_tokens else take(3)
    sums_out = [take(2) for _ in range(count)]
    weights, sums = take(1)[0], take(1)[0]
    low, sem = rest
    half = weights.shape[1] // 6
    width = 2 * half
    step = pl.program_id(0)
    ahead = step < steps // 2

    def pieces_of(parts, whole):
        return [
            (ref.at[pl.ds(kind * half, half)], whole.at[pl.ds((2 * kind + part) * half, half)])
            for kind in range(3)
            for part, ref in enumerate(parts)
        ]

    def copies_of(pairs, lane):
        return [pltpu.make_async_copy(a, b, sem.at[lane, n]) for n, (a, b) in enumerate(pairs)]

    loads = [copies_of(pieces_of(w_in[e], weights.at[e]), e) for e in range(count)]
    prior = [[] if fresh[e] else copies_of(pieces_of(sums_in[e], low.at[e]), count + e) for e in range(count)]
    stores = [copies_of([(b, a) for a, b in pieces_of(sums_out[e], low.at[e])], e) for e in range(count)]

    @pl.when(step == 0)
    def _():
        for copy in sum(loads + prior, []):
            copy.start()
        sums[...] = jnp.zeros_like(sums)
        for copy in sum(loads, []):
            copy.wait()

    rows = jnp.where(ahead, n2[0][...], n2[1][...])
    grads = jnp.where(ahead, up[0][...], up[1][...])
    rows, gates = rows[:, :D], rows[:, D:].astype(F32)
    lanes = lax.broadcasted_iota(jnp.int32, gates.shape, 1)
    mixed = d_rows = d_shares = None
    add = lambda total, value: value if total is None else total + value
    for e in range(count):
        w_both, w_down = weights.at[e, : 2 * width], weights.at[e, 2 * width :]
        hit = (lanes == ids[e]) | (lanes == ids[e] + experts)
        share = jnp.sum(jnp.where(hit, gates, 0.0), axis=1, keepdims=True)
        acts = dot(rows, w_both[...], NT)
        gate_act, up_act = acts[:, :width], acts[:, width:]
        d_plain = dot(grads, w_down[...], NT)
        sigmoid = 1.0 / (1.0 + jnp.exp(-gate_act))
        silu = gate_act * sigmoid
        hidden = silu * up_act
        shared = (share * hidden).astype(BF16)
        d_share = jnp.sum(hidden * d_plain, axis=1, keepdims=True)
        d_hidden = share * d_plain
        d_gate = (d_hidden * up_act * (sigmoid + silu * (1.0 - sigmoid))).astype(BF16)
        d_up = (d_hidden * silu).astype(BF16)
        d_both = jnp.concatenate([d_gate, d_up], axis=1)
        mixed = add(mixed, dot(shared, w_down[...], NN))
        d_rows = add(d_rows, dot(d_both, w_both[...], NN))
        d_shares = add(d_shares, jnp.where(hit, d_share, 0.0))
        sums[e, : 2 * width] += dot(d_both, rows, TN)
        sums[e, 2 * width :] += dot(shared, grads, TN)

        @pl.when(step == steps - 1)
        def _(e=e):
            for copy in prior[e]:
                copy.wait()
            low[e] = (sums[e] if fresh[e] else sums[e] + low[e].astype(F32)).astype(BF16)
            for copy in stores[e]:
                copy.start()

    results = [mixed, d_rows, d_shares]
    if not first:
        results = [result + ref[...].astype(F32) for result, ref in zip(results, carry_in)]
    if last_tokens:

        @pl.when(ahead)
        def _():
            for ref, result in zip(outs[:3], results):
                ref[...] = result.astype(ref.dtype)

        @pl.when(jnp.logical_not(ahead))
        def _():
            outs[3][...] = results[0].astype(BF16)
            outs[4][:, :D] = results[1].astype(BF16)
            outs[4][:, D:] = split_lanes(results[2], experts)
    else:
        for ref, result in zip(outs, results):
            ref[...] = result.astype(ref.dtype)

    @pl.when(step == steps - 1)
    def _():
        for copy in sum(stores, []):
            copy.wait()


def expert_call(ids, mark, experts, n2, up, weights, sums, carry, last_tokens):
    tokens, height, count = 2 * n2[0].shape[0], weights[0][0].shape[0], len(weights)
    steps = tokens // TILE
    rows = lambda cols: pl.BlockSpec((TILE, cols), lambda i: (i, 0))
    near = lambda cols: pl.BlockSpec((TILE, cols), lambda i: (jnp.minimum(i, steps // 2 - 1), 0))
    far = lambda cols: pl.BlockSpec((TILE, cols), lambda i: (jnp.maximum(i - steps // 2, 0), 0))
    ins = [ids, mark, *n2, *up] + [w for pair in weights for w in pair]
    specs = [SMEM, ANY, near(WIDTH), far(WIDTH), near(D), far(D)] + [ANY] * (2 * count)
    fresh, first = [pair is None for pair in sums], carry is None
    columns = (D, D, LANES)
    if last_tokens:
        outs = [shaped((tokens // 2, c), t) for c, t in zip(columns, (BF16, BF16, F32))]
        outs += [shaped((tokens // 2, c), BF16) for c in (D, WIDTH)]
        out_specs = [near(c) for c in columns] + [far(D), far(WIDTH)]
    else:
        outs = [shaped((tokens, c), t) for c, t in zip(columns, (BF16, F32, F32))]
        out_specs = [rows(c) for c in columns]
    aliases = {}
    for pair in sums:
        if pair is not None:
            ins += pair
            specs += [ANY, ANY]
    if not first:
        if not last_tokens:
            aliases.update({len(ins) + k: k for k in range(3)})
        ins += carry
        specs += [rows(c) for c in columns]
    tokens_out = len(outs)
    for _ in range(count):
        outs += [shaped((height, D), BF16)] * 2
        out_specs += [ANY, ANY]
    scratch = [pltpu.VMEM((count, 2 * height, D), BF16), pltpu.VMEM((count, 2 * height, D), F32)]
    scratch.append(pltpu.VMEM((count, 2 * height, D), BF16))
    scratch.append(pltpu.SemaphoreType.DMA((2 * count, 6)))
    done = pl.pallas_call(
        functools.partial(expert_kernel, count, experts, fresh, first, last_tokens, steps),
        grid=(steps,),
        in_specs=specs,
        out_specs=out_specs,
        out_shape=outs,
        scratch_shapes=scratch,
        input_output_aliases=aliases,
        compiler_params=pltpu.CompilerParams(vmem_limit_bytes=63 << 20),
        cost_estimate=estimate(15 * count),
        name="expert",
    )(*ins)
    return list(done[:tokens_out]), [tuple(done[tokens_out + 2 * e : tokens_out + 2 * e + 2]) for e in range(count)]


def join_kernel(side, held, landed, gate, up, down):
    here = pl.program_id(0) == 0
    rows = jnp.where(here, held[...], landed[...]).astype(F32)
    half = down.shape[0]
    gate[...] = rows[:half].T
    up[...] = rows[half : 2 * half].T
    down[...] = rows[2 * half :]


def join_call(side, held, landed):
    half = held.shape[0] // 3
    whole = pl.BlockSpec(held.shape, lambda i, side: (0, 0))
    columns = pl.BlockSpec((D, half), lambda i, side: (0, lax.rem(side[0] + i, 2)))
    return pl.pallas_call(
        join_kernel,
        grid_spec=pltpu.PrefetchScalarGridSpec(
            num_scalar_prefetch=1,
            grid=(2,),
            in_specs=[whole, whole],
            out_specs=[columns, columns, pl.BlockSpec((half, D), lambda i, side: (lax.rem(side[0] + i, 2), 0))],
        ),
        out_shape=[shaped((D, 2 * half), F32), shaped((D, 2 * half), F32), shaped((2 * half, D), F32)],
        compiler_params=pltpu.CompilerParams(vmem_limit_bytes=48 << 20),
        cost_estimate=estimate(5),
        name="join",
    )(side, held, landed)


def after(values, *others):
    return lax.optimization_barrier((values, *others))[0]


class Task:
    def __init__(self, steps):
        self.steps, self.result, self.over = steps, None, False

    def step(self):
        if self.over:
            return []
        try:
            return [next(self.steps)]
        except StopIteration as stop:
            self.result, self.over = stop.value, True
            return [self.result]

    def finish(self):
        while not self.over:
            self.step()
        return self.result


def local(
    tokens,
    routes,
    pieces,
    attn_gain,
    w_query,
    w_key,
    w_value,
    w_out,
    ffn_gain,
    w_router,
    expert_gate,
    expert_up,
    expert_down,
    cotangent,
):
    shards, reps = lax.axis_size("ep"), lax.axis_size("rep")
    experts = w_router.shape[1]
    slots = shards // GROUP
    place = lax.axis_index("ep")
    side = lax.axis_index("rep") % 2

    def swap(values, bits):
        return lax.ppermute(values, "ep", [(i, i ^ bits) for i in range(shards)])

    def swap_rep(values, bits=1):
        return lax.ppermute(values, "rep", [(i, i ^ bits) for i in range(reps)])


    def reduce_reps(values, bits=1):
        while bits < reps:
            values = values.astype(BF16)
            landed = swap_rep(values, bits)
            yield values
            values = values.astype(F32) + hold(landed).astype(F32)
            bits *= 2
        return values

    def reduce_rows(values):
        values = values.reshape(shards, -1, values.shape[1])
        bits = 1
        while bits < shards:
            values = values.reshape(values.shape[0] // 2, 2, *values.shape[1:])
            bit = (place // bits) % 2
            kept, sent = [
                lax.dynamic_index_in_dim(values, index, axis=1, keepdims=False) for index in (bit, 1 - bit)
            ]
            landed = swap(sent, bits)
            yield sent
            values = (kept.astype(F32) + hold(landed).astype(F32)).astype(BF16)
            bits *= 2
        return (yield from reduce_reps(values[0]))

    def sum_steps(slot, own, other):
        other = hold(other)
        landed = swap_rep(other)
        yield other
        own = own.astype(F32) + hold(landed).astype(F32)
        if slot == 0:
            return own
        if slot == 2 and slots > 3:
            own = own + tasks[3].finish().astype(F32)
        own = own.astype(BF16)
        landed = swap(own, GROUP if slot == 3 else slot * GROUP)
        yield own
        return hold(landed)

    with jax.named_scope("weights_out"):
        turned = side.astype(jnp.int32).reshape(1)
        mine, theirs = halve_call(turned, expert_gate[0], expert_up[0], expert_down[0])
        tokens, mine, theirs = lax.optimization_barrier((tokens, mine, theirs))
        near = swap(mine, GROUP)

    with jax.named_scope("cotangent_out"):
        grads_next = swap(cotangent, 2)
        grads_in = [(cotangent, swap(cotangent, 1)), None]

    with jax.named_scope("attention"):
        inputs = tokens.astype(F32)
        scale_one = rms_scale(inputs)
        norm_one = inputs * scale_one
        normed_one = (norm_one * attn_gain).astype(BF16)
        w_dims = (((0,), (1,)), ((), ()))
        projections = (w_query, w_key, w_value)
        query, key, value = [dot(w, normed_one, w_dims) for w in projections]
        far = swap(after(mine, key, value, query), 2 * GROUP)
        cosine, sine = [jnp.asarray(table) for table in rotary_tables()]
        attn, query_rot, key_rot, value_low, lse = attend_call(pieces, query, key, value, cosine, sine)
        attn = after(attn, grads_next, grads_in[0][1])

    with jax.named_scope("cotangent_out"):
        grads_in[1] = (grads_next, swap(after(grads_next, attn), 1))

    with jax.named_scope("routing"):
        pad = jnp.zeros((D, LANES - 2 * experts), BF16)
        router_twice = jnp.concatenate([w_router, w_router, pad], axis=1)
        gain_two = ffn_gain.reshape(1, D)
        residual, rows, gate = route_call(experts, tokens, attn, w_out, gain_two, router_twice, routes)
        rows, _, near = lax.optimization_barrier((rows, grads_in[1][1], near))
        rows_next = swap(rows, 2)
        rows_in = [(rows, swap(rows, 1)), None]

    with jax.named_scope("weights_out"):
        weights = {0: (mine, theirs), 1: (near, swap_rep(near))}
        ids = [((place // GROUP) ^ slot) * GROUP + place % GROUP for slot in range(slots)]
        ids = [expert.astype(jnp.int32) for expert in ids]

    carry, sums, tasks = [None, None], [None] * slots, [None] * slots
    mark, point = after(jnp.zeros((8, LANES), F32), rows), rows

    def tick(*arrays):
        nonlocal mark
        mark = after(mark, *arrays)

    def hold(values):
        return after(values, point)

    def pause():
        nonlocal mark
        mark = pause_call(mark)

    def pulse():
        return swap(mark, 1)

    def passed(value, beat=None):
        nonlocal mark, point
        if beat is not None:
            mark = mark + beat
        mark, point = after(mark, value), value

    def run(chip, group, last=False, beats=True):
        beat = pulse() if beats else None
        carry[chip], done = expert_call(
            jnp.stack([ids[slot] for slot in group]),
            mark,
            experts,
            rows_in[chip],
            grads_in[chip],
            [weights[slot] for slot in group],
            [sums[slot] for slot in group],
            carry[chip],
            last,
        )
        passed(carry[chip][2], beat)
        for slot, pair in zip(group, done):
            if sums[slot] is not None:
                tasks[slot] = Task(sum_steps(slot, *pair))
            sums[slot] = pair

    with jax.named_scope("experts"):
        pause()
        run(0, [0], beats=False)
        tick(weights[1][1], far)
        far = hold(far)
        weights[2] = (far, swap_rep(far))
        landed = {slot: swap(far, GROUP) if slot == 3 else swap(hold(mine), slot * GROUP) for slot in range(3, slots)}
        run(0, [1])
        tick(rows_next, weights[2][1], *landed.values())
        for slot, held in landed.items():
            held = hold(held)
            weights[slot] = (held, swap_rep(held))
        rows_in[1] = (rows_next, swap(hold(rows_next), 1))
        pause()
        tick(rows_in[1][1])
        run(1, [0, 1])
        tick(*[weights[slot][1] for slot in landed])
        tasks[1].step()
        for slot in range(4, slots, 2):
            run(1, [slot, slot + 1])
            run(0, [slot])
            run(0, [slot + 1])
        run(1, [2, 3], True)
        there_landed = swap(hold(carry[1][4]), 1)
        pause()
        there = merge_call(experts, mark, carry[1][1], carry[1][2], there_landed)
        d_next = swap(there, 2)
        tick(there, *tasks[1].step())
        tasks[0].step()
        mix_landed = swap(hold(carry[1][3]), 1)
        run(0, [3])
        mix_there = merge_call(experts, mark, carry[1][0], None, mix_landed)
        tick(mix_there, *tasks[0].step())
        tasks[3].step()
        run(0, [2], True)

    with jax.named_scope("routing_back"):
        d_core = swap(hold(carry[0][4]), 1)
        tasks[2].step()
        pause()
        tick(d_core, d_next, *[array for task in tasks[3:] for array in task.step()])
        point = mark
        mix_home = swap(hold(mix_there), 2)
        mix_core = swap(hold(carry[0][3]), 1)
        beat = pulse()
        d_residual, d_mixed, d_attn, d_small = back_call(
            experts, mark, carry[0][1], carry[0][2], d_core, d_next, residual, cotangent, gate, gain_two, router_twice, w_out
        )
        passed(d_small, beat)
        tick(mix_core)
        d_out = out_call(mark, attn, d_mixed, d_small)
        passed(d_out)

    with jax.named_scope("attention_back"):
        in_dims = (((0,), (1,)), ((), ()))
        out_task, w_tasks, d_packed = Task(reduce_rows(d_out)), [], []
        tick(*out_task.step())
        for part in range(PARTS):
            packed = None
            for turn in range(TURNS):
                beat = pulse() if (part, turn) == (0, 1) else None
                packed = attend_back_call(
                    part, turn, mark, pieces, query_rot, key_rot, value_low, d_attn, attn, lse, cosine, sine, packed
                )
                passed(packed, beat)
                if (part, turn) == (0, 0):
                    tick(*tasks[2].step())
                if (part, turn) == (1, 0):
                    tick(mix_home)
                stepped = [array for task in w_tasks for array in task.step()]
                stepped += out_task.step() if part == turn else []
                tick(*stepped)
            d_packed.append(packed)
            w_tasks.append(Task(reduce_rows(dot(normed_one, packed, in_dims).astype(BF16))))
            if part < PARTS - 1:
                tick(*w_tasks[-1].step())

    with jax.named_scope("tail"):
        last, other = w_tasks[1], w_tasks[0]
        mix_home = after(mix_home, packed, *stepped, *last.step())
        output = point = (residual + carry[0][0].astype(F32) + mix_core.astype(F32) + mix_home.astype(F32)).astype(BF16)
        total = tasks[0].finish()
        for task in tasks[1:3] + tasks[4:]:
            total = total + task.finish().astype(F32)
        total = Task(reduce_reps(total, 2)).finish().astype(BF16)
        total_landed = swap_rep(total)
        gain_one = after(attn_gain.reshape(1, D), output, total, *last.step())
        d_tokens = point = finish_call(tokens, d_residual, projections, gain_one, d_packed)
        point = after(d_tokens, *other.step(), *out_task.step(), *last.step())
        d_tokens = point
        for task in (last, other, out_task, last):
            stepped = task.step()
            point = stepped[0]
        total, total_landed = lax.optimization_barrier((total, total_landed, point))[:2]
        s_gate, s_up, s_down = join_call(turned, total, total_landed)
        point = s_down

    with jax.named_scope("sums_rest"):
        s_mixed = out_task.finish()
        s_out, s_small = s_mixed[:, :D], s_mixed[:, D:]
        count = s_out.shape[0]
        first = place * count
        s_parts = [task.finish() for task in w_tasks]
        s_attn, groups = 0.0, []
        for k, w in enumerate(projections):
            wide = w.shape[1] // PARTS
            cut = sum(v.shape[1] // PARTS for v in projections[:k])
            groups.append(jnp.concatenate([part[:, cut : cut + wide] for part in s_parts], axis=1))
            s_attn += jnp.sum(groups[-1] * lax.dynamic_slice_in_dim(w, first, count).astype(F32), axis=1)
        s_query, s_key, s_value = groups
        s_attn = s_attn / lax.dynamic_slice_in_dim(attn_gain, first, count)

    return (
        output,
        d_tokens,
        s_attn,
        s_query,
        s_key,
        s_value,
        s_out,
        s_small[:, experts],
        s_small[:, :experts],
        s_gate[None],
        s_up[None],
        s_down[None],
    )


def solution(mesh):
    rows, whole, slices = P(("rep", "ep"), None), P(), P("ep", None)
    expert = P("ep", None, None)
    return jax.shard_map(
        local,
        mesh=mesh,
        in_specs=(rows,) * 3 + (whole,) * 7 + (expert,) * 3 + (rows,),
        out_specs=(rows, rows, P("ep")) + (slices,) * 4 + (P("ep"), slices) + (expert,) * 3,
        check_vma=False,
    )
```

```python
import functools
import math

import jax
import jax.numpy as jnp
import numpy as np
from jax import lax
from jax.experimental import pallas as pl
from jax.experimental.pallas import tpu as pltpu
from jax.sharding import PartitionSpec as P

D = 1536
HEADS = 24
KV = 8
HEAD = 64
LEN = 1024
PIECE = 256
QUERIES = HEADS // KV
WIDE = 256
TILE = 256
GROUP = 4
PARTS = 2
TURNS = 2
LANES = 128
WIDTH = D + LANES

eps = 1e-06
theta_base = 10000.0
masked_score = -1e30
score_scale = HEAD ** (-0.5)
two_scale = score_scale * math.log2(math.e)

F32 = jnp.float32
BF16 = jnp.bfloat16
NN = (((1,), (0,)), ((), ()))
NT = (((1,), (1,)), ((), ()))
TN = (((0,), (0,)), ((), ()))
ANY = pl.BlockSpec(memory_space=pl.ANY)
SMEM = pl.BlockSpec(memory_space=pltpu.SMEM)


def dot(left, right, dims):
    return lax.dot_general(left, right, dims, preferred_element_type=F32)


def shaped(shape, dtype):
    return jax.ShapeDtypeStruct(shape, dtype)


def estimate(micros):
    return pl.CostEstimate(flops=int(micros * 1e10), bytes_accessed=int(micros * 1e6), transcendentals=0)


def rms_scale(values):
    return lax.rsqrt(jnp.mean(values * values, axis=-1, keepdims=True) + eps)


def rotary_tables():
    half_head = HEAD // 2
    frequency = theta_base ** (-(np.arange(half_head, dtype=np.float64) * 2.0) / HEAD)
    angles = frequency[:, None] * np.arange(LEN, dtype=np.float64)[None, :]
    return np.cos(angles).astype(np.float32), np.sin(angles).astype(np.float32)


def turn(values, cosine, sine):
    first, second = values[: HEAD // 2], values[HEAD // 2 :]
    return jnp.concatenate([first * cosine - second * sine, second * cosine + first * sine], axis=0)


def turn_back(grads, cosine, sine):
    first, second = grads[: HEAD // 2], grads[HEAD // 2 :]
    return jnp.concatenate([first * cosine + second * sine, second * cosine - first * sine], axis=0)


def fill_bias(pieces, bias):
    for block in range(LEN // WIDE):
        first = block * WIDE
        shape = bias.shape[1:]
        key = lax.broadcasted_iota(jnp.int32, shape, 0) + first
        query = lax.broadcasted_iota(jnp.int32, shape, 1) + first
        allowed = key <= query
        for piece in range(pieces.shape[1]):
            start = pieces[0, piece]
            low, high = jnp.minimum(key, query), jnp.maximum(key, query)
            allowed = allowed | ((low >= start) & (high < start + PIECE))
        bias[block] = jnp.where(allowed, 0.0, masked_score)


def key_span(block):
    return block * WIDE, min((block + 2) * WIDE, LEN)


def rows_at(place):
    return pl.BlockSpec((HEAD, LEN), lambda *grid: (place(*grid), 0))


def table_spec():
    return pl.BlockSpec((HEAD // 2, LEN), lambda *grid: (0, 0))


def attend_kernel(pieces, q0, q1, q2, k_in, v_in, cosine, sine, attn, q_out, k_out, v_out, lse, bias):
    @pl.when(pl.program_id(0) == 0)
    def _():
        fill_bias(pieces, bias)

    cos, sin = cosine[...], sine[...]
    k_rot = turn(k_in[...], cos, sin) * two_scale
    k_out[...] = k_rot.astype(BF16)
    keys = k_rot.T.astype(BF16)
    values = v_in[...].astype(BF16)
    v_out[...] = values
    for head, q_in in enumerate((q0, q1, q2)):
        rows = pl.ds(head * HEAD, HEAD)
        q_rot = turn(q_in[...], cos, sin).astype(BF16)
        q_out[rows, :] = q_rot
        for block in range(LEN // WIDE):
            columns = pl.ds(block * WIDE, WIDE)
            first, last = key_span(block)
            queries = q_rot[:, block * WIDE : (block + 1) * WIDE]
            spans = [(first, last)] + ([(0, first)] if first > 0 else [])
            scores = [dot(keys[a:b], queries, NN) for a, b in spans]
            scores[0] = scores[0] + bias[block, : last - first]
            highest = functools.reduce(jnp.maximum, [jnp.max(s, axis=0, keepdims=True) for s in scores])
            weights = [jnp.exp2(s - highest) for s in scores]
            total = sum(jnp.sum(w, axis=0, keepdims=True) for w in weights)
            mixed = sum(dot(values[:, a:b], w.astype(BF16), NN) for (a, b), w in zip(spans, weights)) / total
            attn[rows, columns] = mixed.astype(BF16)
            lse[head : head + 1, columns] = highest + jnp.log2(total)


def attend_call(pieces, query, key, value, cosine, sine):
    rows = lambda count: pl.BlockSpec((count, LEN), lambda i: (i, 0))
    width = QUERIES * HEAD
    return pl.pallas_call(
        attend_kernel,
        grid=(KV,),
        in_specs=[SMEM]
        + [rows_at(lambda i, head=head: QUERIES * i + head) for head in range(QUERIES)]
        + [rows_at(lambda i: i), rows_at(lambda i: i)]
        + [table_spec(), table_spec()],
        out_specs=[rows(width), rows(width), rows(HEAD), rows(HEAD), rows(8)],
        out_shape=[
            shaped((D, LEN), BF16),
            shaped((D, LEN), BF16),
            shaped((KV * HEAD, LEN), BF16),
            shaped((KV * HEAD, LEN), BF16),
            shaped((KV * 8, LEN), F32),
        ],
        scratch_shapes=[pltpu.VMEM((LEN // WIDE, 2 * WIDE, WIDE), F32)],
        compiler_params=pltpu.CompilerParams(vmem_limit_bytes=48 << 20),
        cost_estimate=estimate(25),
        name="attend",
    )(pieces, *[query] * QUERIES, key, value, cosine, sine)


def with_parts(columns, row):
    rank = lax.broadcasted_iota(jnp.int32, columns.shape, 0)
    high = row.astype(BF16).astype(F32)
    middle = (row - high).astype(BF16).astype(F32)
    parts = jnp.where(rank == 0, high, jnp.where(rank == 1, middle, jnp.where(rank == 2, row - high - middle, 0.0)))
    return jnp.concatenate([columns, parts.astype(BF16)], axis=0)


def attend_back_kernel(
    mark, beat, pieces, q_in, k_in, v_in, do_in, attn, lse, cosine, sine, *rest
):
    out, bias, keys_kept, values_kept, dk_sum, dv_sum = rest[-6:]
    kind = pl.program_id(1)

    @pl.when((pl.program_id(0) == 0) & (kind == 0))
    def _():
        fill_bias(pieces, bias)

    cos, sin = cosine[...], sine[...]

    @pl.when(kind == 0)
    def _():
        tail = jnp.where(lax.broadcasted_iota(jnp.int32, (LEN, HEAD), 1) < 3, -1.0, 0.0)
        for kept, ref in ((keys_kept, k_in), (values_kept, v_in)):
            kept[...] = jnp.concatenate([ref[...].astype(F32).T, tail], axis=1).astype(BF16)
        dk_sum[...] = jnp.zeros_like(dk_sum)
        dv_sum[...] = jnp.zeros_like(dv_sum)

    @pl.when(kind < QUERIES)
    def _():
        k_cols, keys, values = k_in[...], keys_kept[...], values_kept[...]
        q_cols, do_cols = q_in[...], do_in[...]
        q_rows = q_cols.astype(F32).T.astype(BF16)
        do_rows = do_cols.astype(F32).T.astype(BF16)
        delta = jnp.sum(do_cols.astype(F32) * attn[...].astype(F32), axis=0, keepdims=True)
        q_wide = with_parts(q_cols, lse[pl.ds(kind, 1), :])
        do_wide = with_parts(do_cols, delta)
        for block in range(LEN // WIDE):
            part = slice(block * WIDE, (block + 1) * WIDE)
            first, last = key_span(block)
            d_query = 0.0
            for a, b in [(first, last)] + ([(0, first)] if first > 0 else []):
                scores = dot(keys[a:b], q_wide[:, part], NN)
                if a == first:
                    scores = scores + bias[block, : b - a]
                probs = jnp.exp2(scores)
                d_scores = (probs * dot(values[a:b], do_wide[:, part], NN)).astype(BF16)
                dv_sum[a:b] += dot(probs.astype(BF16), do_rows[part], NN)
                dk_sum[a:b] += dot(d_scores, q_rows[part], NN)
                d_query = d_query + dot(k_cols[:, a:b], d_scores, NN)
            out[:, part] = turn_back(d_query * math.log(2.0), cos[:, part], sin[:, part]).astype(BF16)

    @pl.when(kind == QUERIES)
    def _():
        out[...] = turn_back(dk_sum[...].T * score_scale, cos, sin).astype(BF16)

    @pl.when(kind == QUERIES + 1)
    def _():
        out[...] = dv_sum[...].T.astype(BF16)


def attend_back_call(part, turn, marks, pieces, q_in, k_in, v_in, do_in, attn, lse, cosine, sine, before):
    group = KV // PARTS
    per = group // TURNS
    first = part * group + turn * per
    query = rows_at(lambda i, j: (first + i) * QUERIES + jnp.minimum(j, QUERIES - 1))
    key = rows_at(lambda i, j: first + i)

    def place(i, j):
        inner = turn * per + i
        tail = jnp.where(j == QUERIES, QUERIES * group + inner, (QUERIES + 1) * group + inner)
        return jnp.where(j < QUERIES, QUERIES * inner + j, tail)

    ins = [*marks, pieces, q_in, k_in, v_in, do_in, attn, lse, cosine, sine] + ([] if before is None else [before])
    return pl.pallas_call(
        attend_back_kernel,
        grid=(per, QUERIES + 2),
        in_specs=[ANY, ANY, SMEM, query, key, key, query, query, pl.BlockSpec((8, LEN), lambda i, j: (first + i, 0))]
        + [table_spec(), table_spec()]
        + ([] if before is None else [ANY]),
        out_specs=rows_at(place),
        out_shape=shaped(((QUERIES + 2) * group * HEAD, LEN), BF16),
        input_output_aliases={} if before is None else {len(ins) - 1: 0},
        scratch_shapes=[
            pltpu.VMEM((LEN // WIDE, 2 * WIDE, WIDE), F32),
            pltpu.VMEM((LEN, 2 * HEAD), BF16),
            pltpu.VMEM((LEN, 2 * HEAD), BF16),
            pltpu.VMEM((LEN, HEAD), F32),
            pltpu.VMEM((LEN, HEAD), F32),
        ],
        compiler_params=pltpu.CompilerParams(vmem_limit_bytes=48 << 20),
        cost_estimate=estimate(15),
        name="attend_back",
    )(*ins)


def halve_kernel(side, gate, up, down, mine, theirs):
    half = down.shape[0]

    def write(out):
        out[:half] = gate[...].T
        out[half : 2 * half] = up[...].T
        out[2 * half :] = down[...]

    pl.when(pl.program_id(0) == 0)(lambda: write(mine))
    pl.when(pl.program_id(0) == 1)(lambda: write(theirs))


def halve_call(side, gate, up, down):
    half = down.shape[0] // 2
    columns = pl.BlockSpec((D, half), lambda i, side: (0, lax.rem(side[0] + i, 2)))
    whole = pl.BlockSpec((3 * half, D), lambda i, side: (0, 0))
    return pl.pallas_call(
        halve_kernel,
        grid_spec=pltpu.PrefetchScalarGridSpec(
            num_scalar_prefetch=1,
            grid=(2,),
            in_specs=[columns, columns, pl.BlockSpec((half, D), lambda i, side: (lax.rem(side[0] + i, 2), 0))],
            out_specs=[whole, whole],
        ),
        out_shape=[shaped((3 * half, D), BF16)] * 2,
        compiler_params=pltpu.CompilerParams(vmem_limit_bytes=60 << 20),
        cost_estimate=estimate(5),
        name="halve",
    )(side, gate, up, down)


def finish_kernel(parts, tokens, residual, w_query, w_key, w_value, gain, *rest):
    grads, out = rest[:-1], rest[-1]
    total = 0.0
    for part, ref in enumerate(grads):
        columns = ref[...].T
        first = 0
        for weight in (w_query, w_key, w_value):
            wide = weight.shape[1] // parts
            total = total + dot(columns[:, first : first + wide], weight[:, part * wide : (part + 1) * wide], NT)
            first += wide
    values = tokens[...].astype(F32)
    scale = rms_scale(values)
    norm = values * scale
    scaled = total * gain[...]
    out[...] = residual[...] + scale * (scaled - norm * jnp.mean(scaled * norm, axis=1, keepdims=True))


def finish_call(tokens, residual, weights, gain, grads):
    rows = pl.BlockSpec((TILE, D), lambda i: (i, 0))
    whole = lambda array: pl.BlockSpec(array.shape, lambda i: (0, 0), pipeline_mode=pl.Buffered(1))
    return pl.pallas_call(
        functools.partial(finish_kernel, len(grads)),
        grid=(LEN // TILE,),
        in_specs=[rows, rows, *[whole(w) for w in weights], whole(gain)]
        + [pl.BlockSpec((g.shape[0], TILE), lambda i: (0, i)) for g in grads],
        out_specs=rows,
        out_shape=shaped((LEN, D), F32),
        compiler_params=pltpu.CompilerParams(vmem_limit_bytes=48 << 20),
        cost_estimate=estimate(5),
        name="finish",
    )(tokens, residual, *weights, gain, *grads)


def split_lanes(values, experts):
    lanes = lax.broadcasted_iota(jnp.int32, values.shape, 1)
    high = values.astype(BF16).astype(F32)
    return jnp.where(lanes < experts, high, jnp.where(lanes < 2 * experts, values - high, 0.0)).astype(BF16)


def join_lanes(parts, experts):
    return parts + pltpu.roll(parts, LANES - experts, 1)


def route_kernel(experts, tokens, attn, w_out, gain, w_router, routes, residual, rows, gate):
    values = tokens[...].astype(F32) + dot(attn[...], w_out[...], TN)
    residual[...] = values
    normed = (values * rms_scale(values) * gain[...]).astype(BF16)
    logits = dot(normed, w_router[...], NN)
    lanes = lax.broadcasted_iota(jnp.int32, logits.shape, 1)
    expert = lax.rem(lanes, experts)
    chosen = lanes < 0
    for k in range(routes.shape[1]):
        chosen = chosen | (routes[:, k : k + 1] == expert)
    chosen = chosen & (lanes < 2 * experts)
    logits = jnp.where(chosen, logits, masked_score)
    weights = jnp.exp(logits - jnp.max(logits, axis=1, keepdims=True))
    share = weights / (0.5 * jnp.sum(weights, axis=1, keepdims=True))
    gate[...] = share
    rows[:, :D] = normed
    rows[:, D:] = split_lanes(share, experts)


def route_call(experts, tokens, attn, w_out, gain, w_router, routes):
    rows = lambda cols: pl.BlockSpec((TILE, cols), lambda i: (i, 0))
    whole = lambda *shape: pl.BlockSpec(shape, lambda i: (0, 0), pipeline_mode=pl.Buffered(1))
    return pl.pallas_call(
        functools.partial(route_kernel, experts),
        grid=(LEN // TILE,),
        in_specs=[rows(D), pl.BlockSpec((D, TILE), lambda i: (0, i)), whole(D, D), whole(1, D), whole(D, LANES)]
        + [rows(routes.shape[1])],
        out_specs=[rows(D), rows(WIDTH), rows(LANES)],
        out_shape=[shaped((LEN, D), F32), shaped((LEN, WIDTH), BF16), shaped((LEN, LANES), F32)],
        compiler_params=pltpu.CompilerParams(vmem_limit_bytes=60 << 20),
        cost_estimate=estimate(5),
        name="route",
    )(tokens, attn, w_out, gain, w_router, routes)


def merge_kernel(experts, mark, kept, kept_share, landed, out):
    out[:, :D] = (kept[...].astype(F32) + landed[:, :D].astype(F32)).astype(BF16)
    if kept_share is not None:
        share = kept_share[...] + join_lanes(landed[:, D:].astype(F32), experts)
        share = jnp.where(lax.broadcasted_iota(jnp.int32, share.shape, 1) < experts, share, 0.0)
        out[:, D:] = split_lanes(share + pltpu.roll(share, experts, 1), experts)


def merge_call(experts, mark, kept, kept_share, landed):
    rows = lambda cols: pl.BlockSpec((TILE, cols), lambda i: (i, 0))
    width = landed.shape[1]
    kernel = functools.partial(merge_kernel, experts)
    if kept_share is None:
        kernel = lambda mark, kept, landed, out: merge_kernel(experts, mark, kept, None, landed, out)
    return pl.pallas_call(
        kernel,
        grid=(LEN // TILE,),
        in_specs=[ANY, rows(D)] + ([] if kept_share is None else [rows(LANES)]) + [rows(width)],
        out_specs=rows(width),
        out_shape=shaped((LEN, width), BF16),
        compiler_params=pltpu.CompilerParams(vmem_limit_bytes=32 << 20),
        cost_estimate=estimate(3),
        name="merge",
    )(*[ref for ref in (mark, kept, kept_share, landed) if ref is not None])


def back_kernel(
    experts, mark, kept, kept_share, core, chip, residual, cotangent, gate, gain, w_router, w_out, d_res, d_mix, d_attn, d_router
):
    @pl.when(pl.program_id(0) == 0)
    def _():
        d_router[...] = jnp.zeros_like(d_router)

    landed = core[:, D:].astype(F32) + chip[:, D:].astype(F32)
    share = kept_share[...] + join_lanes(landed, experts)
    first = lax.broadcasted_iota(jnp.int32, share.shape, 1) < experts
    gates = jnp.where(first, gate[...], 0.0)
    inner = jnp.sum(gates * share, axis=1, keepdims=True)
    d_logits = jnp.where(first, gates * (share - inner), 0.0).astype(BF16)
    d_normed = kept[...].astype(F32) + core[:, :D].astype(F32) + chip[:, :D].astype(F32) + dot(d_logits, w_router[...], NT)
    values, gains = residual[...], gain[...]
    scale = rms_scale(values)
    norm = values * scale
    d_gain = jnp.sum(d_normed * norm, axis=0, keepdims=True)
    scaled = d_normed * gains
    d_values = cotangent[...].astype(F32) + scale * (scaled - norm * jnp.mean(scaled * norm, axis=1, keepdims=True))
    d_res[...] = d_values
    mixed = d_values.astype(BF16)
    d_mix[...] = mixed
    d_attn[...] = dot(w_out[...], mixed, NT).astype(BF16)
    d_router[...] += dot(d_logits, (norm * gains).astype(BF16), TN)
    d_router[experts : experts + 1] += d_gain


def back_call(experts, mark, kept, kept_share, core, chip, residual, cotangent, gate, gain, w_router, w_out):
    rows = lambda cols: pl.BlockSpec((TILE, cols), lambda i: (i, 0))
    whole = lambda *shape: pl.BlockSpec(shape, lambda i: (0, 0), pipeline_mode=pl.Buffered(1))
    return pl.pallas_call(
        functools.partial(back_kernel, experts),
        grid=(LEN // TILE,),
        in_specs=[ANY, rows(D), rows(LANES), rows(WIDTH), rows(WIDTH), rows(D), rows(D), rows(LANES)]
        + [whole(1, D), whole(D, LANES), whole(D, D)],
        out_specs=[rows(D), rows(D), pl.BlockSpec((D, TILE), lambda i: (0, i)), whole(LANES, D)],
        out_shape=[
            shaped((LEN, D), F32),
            shaped((LEN, D), BF16),
            shaped((D, LEN), BF16),
            shaped((LANES, D), F32),
        ],
        compiler_params=pltpu.CompilerParams(vmem_limit_bytes=48 << 20),
        cost_estimate=estimate(8),
        name="back",
    )(mark, kept, kept_share, core, chip, residual, cotangent, gate, gain, w_router, w_out)


def out_kernel(mark, beat, attn, mixed, small, out):
    out[:, :D] = dot(attn[...], mixed[...], NN).astype(BF16)
    out[:, D:] = small[...].T.astype(BF16)


def out_call(marks, attn, mixed, small):
    return pl.pallas_call(
        out_kernel,
        grid=(D // TILE,),
        in_specs=[
            ANY,
            ANY,
            pl.BlockSpec((TILE, LEN), lambda i: (i, 0)),
            pl.BlockSpec((LEN, D), lambda i: (0, 0), pipeline_mode=pl.Buffered(1)),
            pl.BlockSpec((LANES, TILE), lambda i: (0, i)),
        ],
        out_specs=pl.BlockSpec((TILE, WIDTH), lambda i: (i, 0)),
        out_shape=shaped((D, WIDTH), BF16),
        compiler_params=pltpu.CompilerParams(vmem_limit_bytes=32 << 20),
        cost_estimate=estimate(5),
        name="out_grad",
    )(*marks, attn, mixed, small)


def pause_kernel(mark, beat, out):
    out[...] = mark[...] + beat[...]


def pause_call(mark, beat):
    return pl.pallas_call(
        pause_kernel, out_shape=shaped(mark.shape, mark.dtype), cost_estimate=estimate(10), name="pause"
    )(mark, beat)


def combine_kernel(residual, kept, core, chip, out):
    total = residual[...] + kept[...].astype(F32) + core[...].astype(F32) + chip[...].astype(F32)
    out[...] = total.astype(BF16)


def combine_call(residual, kept, core, chip):
    rows = pl.BlockSpec((TILE, D), lambda i: (i, 0))
    return pl.pallas_call(
        combine_kernel,
        grid=(LEN // TILE,),
        in_specs=[rows] * 4,
        out_specs=rows,
        out_shape=shaped((LEN, D), BF16),
        compiler_params=pltpu.CompilerParams(vmem_limit_bytes=48 << 20),
        cost_estimate=estimate(10),
        name="combine",
    )(residual, kept, core, chip)


def expert_kernel(count, experts, fresh, first, last_tokens, steps, ids, mark, beat, *rest):
    rest = list(rest)

    def take(number):
        taken = rest[:number]
        del rest[:number]
        return taken

    n2, up = take(2), take(2)
    w_in = [take(2) for _ in range(count)]
    sums_in = [[] if new else take(2) for new in fresh]
    carry_in = [] if first else take(3)
    outs = take(5) if last_tokens else take(3)
    sums_out = [take(2) for _ in range(count)]
    weights, sums = take(1)[0], take(1)[0]
    low, sem = rest
    half = weights.shape[1] // 6
    width = 2 * half
    step = pl.program_id(0)
    ahead = step < steps // 2

    def pieces_of(parts, whole):
        return [
            (ref.at[pl.ds(kind * half, half)], whole.at[pl.ds((2 * kind + part) * half, half)])
            for kind in range(3)
            for part, ref in enumerate(parts)
        ]

    def copies_of(pairs, lane):
        return [pltpu.make_async_copy(a, b, sem.at[lane, n]) for n, (a, b) in enumerate(pairs)]

    loads = [copies_of(pieces_of(w_in[e], weights.at[e]), e) for e in range(count)]
    prior = [[] if fresh[e] else copies_of(pieces_of(sums_in[e], low.at[e]), count + e) for e in range(count)]
    stores = [copies_of([(b, a) for a, b in pieces_of(sums_out[e], low.at[e])], e) for e in range(count)]

    @pl.when(step == 0)
    def _():
        for copy in sum(loads + prior, []):
            copy.start()
        sums[...] = jnp.zeros_like(sums)
        for copy in loads[0]:
            copy.wait()

    rows = jnp.where(ahead, n2[0][...], n2[1][...])
    grads = jnp.where(ahead, up[0][...], up[1][...])
    rows, gates = rows[:, :D], rows[:, D:].astype(F32)
    lanes = lax.broadcasted_iota(jnp.int32, gates.shape, 1)
    mixed = d_rows = d_shares = None
    add = lambda total, value: value if total is None else total + value
    for e in range(count):
        if e > 0:

            @pl.when(step == 0)
            def _(e=e):
                for copy in loads[e]:
                    copy.wait()

        w_both, w_down = weights.at[e, : 2 * width], weights.at[e, 2 * width :]
        hit = (lanes == ids[e]) | (lanes == ids[e] + experts)
        share = jnp.sum(jnp.where(hit, gates, 0.0), axis=1, keepdims=True)
        acts = dot(rows, w_both[...], NT)
        gate_act, up_act = acts[:, :width], acts[:, width:]
        d_plain = dot(grads, w_down[...], NT)
        sigmoid = 1.0 / (1.0 + jnp.exp(-gate_act))
        silu = gate_act * sigmoid
        hidden = silu * up_act
        shared = (share * hidden).astype(BF16)
        d_share = jnp.sum(hidden * d_plain, axis=1, keepdims=True)
        d_hidden = share * d_plain
        d_gate = (d_hidden * up_act * (sigmoid + silu * (1.0 - sigmoid))).astype(BF16)
        d_up = (d_hidden * silu).astype(BF16)
        d_both = jnp.concatenate([d_gate, d_up], axis=1)
        mixed = add(mixed, dot(shared, w_down[...], NN))
        d_rows = add(d_rows, dot(d_both, w_both[...], NN))
        d_shares = add(d_shares, jnp.where(hit, d_share, 0.0))
        sums[e, : 2 * width] += dot(d_both, rows, TN)
        sums[e, 2 * width :] += dot(shared, grads, TN)

        @pl.when(step == steps - 1)
        def _(e=e):
            for copy in prior[e]:
                copy.wait()
            low[e] = (sums[e] if fresh[e] else sums[e] + low[e].astype(F32)).astype(BF16)
            for copy in stores[e]:
                copy.start()

    results = [mixed, d_rows, d_shares]
    if not first:
        results = [result + ref[...].astype(F32) for result, ref in zip(results, carry_in)]
    if last_tokens:

        @pl.when(ahead)
        def _():
            for ref, result in zip(outs[:3], results):
                ref[...] = result.astype(ref.dtype)

        @pl.when(jnp.logical_not(ahead))
        def _():
            outs[3][...] = results[0].astype(BF16)
            outs[4][:, :D] = results[1].astype(BF16)
            outs[4][:, D:] = split_lanes(results[2], experts)
    else:
        for ref, result in zip(outs, results):
            ref[...] = result.astype(ref.dtype)

    @pl.when(step == steps - 1)
    def _():
        for copy in sum(stores, []):
            copy.wait()


def expert_call(ids, marks, experts, n2, up, weights, sums, carry, last_tokens):
    tokens, height, count = 2 * n2[0].shape[0], weights[0][0].shape[0], len(weights)
    steps = tokens // TILE
    rows = lambda cols: pl.BlockSpec((TILE, cols), lambda i: (i, 0))
    near = lambda cols: pl.BlockSpec((TILE, cols), lambda i: (jnp.minimum(i, steps // 2 - 1), 0))
    far = lambda cols: pl.BlockSpec((TILE, cols), lambda i: (jnp.maximum(i - steps // 2, 0), 0))
    ins = [ids, *marks, *n2, *up] + [w for pair in weights for w in pair]
    specs = [SMEM, ANY, ANY, near(WIDTH), far(WIDTH), near(D), far(D)] + [ANY] * (2 * count)
    fresh, first = [pair is None for pair in sums], carry is None
    columns = (D, D, LANES)
    if last_tokens:
        outs = [shaped((tokens // 2, c), t) for c, t in zip(columns, (BF16, BF16, F32))]
        outs += [shaped((tokens // 2, c), BF16) for c in (D, WIDTH)]
        out_specs = [near(c) for c in columns] + [far(D), far(WIDTH)]
    else:
        outs = [shaped((tokens, c), t) for c, t in zip(columns, (BF16, F32, F32))]
        out_specs = [rows(c) for c in columns]
    aliases = {}
    for pair in sums:
        if pair is not None:
            ins += pair
            specs += [ANY, ANY]
    if not first:
        if not last_tokens:
            aliases.update({len(ins) + k: k for k in range(3)})
        ins += carry
        specs += [rows(c) for c in columns]
    tokens_out = len(outs)
    for _ in range(count):
        outs += [shaped((height, D), BF16)] * 2
        out_specs += [ANY, ANY]
    scratch = [pltpu.VMEM((count, 2 * height, D), BF16), pltpu.VMEM((count, 2 * height, D), F32)]
    scratch.append(pltpu.VMEM((count, 2 * height, D), BF16))
    scratch.append(pltpu.SemaphoreType.DMA((2 * count, 6)))
    done = pl.pallas_call(
        functools.partial(expert_kernel, count, experts, fresh, first, last_tokens, steps),
        grid=(steps,),
        in_specs=specs,
        out_specs=out_specs,
        out_shape=outs,
        scratch_shapes=scratch,
        input_output_aliases=aliases,
        compiler_params=pltpu.CompilerParams(vmem_limit_bytes=63 << 20),
        cost_estimate=estimate(15 * count),
        name="expert",
    )(*ins)
    return list(done[:tokens_out]), [tuple(done[tokens_out + 2 * e : tokens_out + 2 * e + 2]) for e in range(count)]


def join_kernel(side, held, landed, gate, up, down):
    here = pl.program_id(0) == 0
    rows = jnp.where(here, held[...], landed[...]).astype(F32)
    half = down.shape[0]
    gate[...] = rows[:half].T
    up[...] = rows[half : 2 * half].T
    down[...] = rows[2 * half :]


def join_call(side, held, landed):
    half = held.shape[0] // 3
    whole = pl.BlockSpec(held.shape, lambda i, side: (0, 0))
    columns = pl.BlockSpec((D, half), lambda i, side: (0, lax.rem(side[0] + i, 2)))
    return pl.pallas_call(
        join_kernel,
        grid_spec=pltpu.PrefetchScalarGridSpec(
            num_scalar_prefetch=1,
            grid=(2,),
            in_specs=[whole, whole],
            out_specs=[columns, columns, pl.BlockSpec((half, D), lambda i, side: (lax.rem(side[0] + i, 2), 0))],
        ),
        out_shape=[shaped((D, 2 * half), F32), shaped((D, 2 * half), F32), shaped((2 * half, D), F32)],
        compiler_params=pltpu.CompilerParams(vmem_limit_bytes=48 << 20),
        cost_estimate=estimate(5),
        name="join",
    )(side, held, landed)


def after(values, *others):
    return lax.optimization_barrier((values, *others))[0]


class Task:
    def __init__(self, steps):
        self.steps, self.result, self.over = steps, None, False

    def step(self):
        if self.over:
            return []
        try:
            return [next(self.steps)]
        except StopIteration as stop:
            self.result, self.over = stop.value, True
            return [self.result]

    def finish(self):
        while not self.over:
            self.step()
        return self.result


def local(
    tokens,
    routes,
    pieces,
    attn_gain,
    w_query,
    w_key,
    w_value,
    w_out,
    ffn_gain,
    w_router,
    expert_gate,
    expert_up,
    expert_down,
    cotangent,
):
    shards, reps = lax.axis_size("ep"), lax.axis_size("rep")
    experts = w_router.shape[1]
    slots = shards // GROUP
    place = lax.axis_index("ep")
    side = lax.axis_index("rep") % 2

    def swap(values, bits):
        return lax.ppermute(values, "ep", [(i, i ^ bits) for i in range(shards)])

    def swap_rep(values, bits=1):
        return lax.ppermute(values, "rep", [(i, i ^ bits) for i in range(reps)])


    def reduce_reps(values, bits=1):
        while bits < reps:
            values = values.astype(BF16)
            landed = swap_rep(values, bits)
            yield values
            values = values.astype(F32) + hold(landed).astype(F32)
            bits *= 2
        return values

    def reduce_rows(values):
        values = values.reshape(shards, -1, values.shape[1])
        bits = 1
        while bits < shards:
            values = values.reshape(values.shape[0] // 2, 2, *values.shape[1:])
            bit = (place // bits) % 2
            kept, sent = [
                lax.dynamic_index_in_dim(values, index, axis=1, keepdims=False) for index in (bit, 1 - bit)
            ]
            landed = swap(sent, bits)
            yield sent
            values = (kept.astype(F32) + hold(landed).astype(F32)).astype(BF16)
            bits *= 2
        return (yield from reduce_reps(values[0]))

    def sum_steps(slot, own, other):
        other = hold(other)
        landed = swap_rep(other)
        yield other
        own = own.astype(F32) + hold(landed).astype(F32)
        if slot == 0:
            return own
        if slot == 2 and slots > 3:
            own = own + tasks[3].finish().astype(F32)
        own = own.astype(BF16)
        landed = swap(own, GROUP if slot == 3 else slot * GROUP)
        yield own
        return hold(landed)

    with jax.named_scope("weights_out"):
        turned = side.astype(jnp.int32).reshape(1)
        mine, theirs = halve_call(turned, expert_gate[0], expert_up[0], expert_down[0])
        tokens, mine, theirs = lax.optimization_barrier((tokens, mine, theirs))
        near = swap(mine, GROUP)

    with jax.named_scope("cotangent_out"):
        grads_next = swap(cotangent, 2)
        grads_in = [(cotangent, swap(cotangent, 1)), None]

    with jax.named_scope("attention"):
        inputs = tokens.astype(F32)
        scale_one = rms_scale(inputs)
        norm_one = inputs * scale_one
        normed_one = (norm_one * attn_gain).astype(BF16)
        w_dims = (((0,), (1,)), ((), ()))
        projections = (w_query, w_key, w_value)
        query, key, value = [dot(w, normed_one, w_dims) for w in projections]
        far = swap(after(mine, key, value, query), 2 * GROUP)
        cosine, sine = [jnp.asarray(table) for table in rotary_tables()]
        attn, query_rot, key_rot, value_low, lse = attend_call(pieces, query, key, value, cosine, sine)
        attn = after(attn, grads_next, grads_in[0][1])

    with jax.named_scope("cotangent_out"):
        grads_in[1] = (grads_next, swap(after(grads_next, attn), 1))

    with jax.named_scope("routing"):
        pad = jnp.zeros((D, LANES - 2 * experts), BF16)
        router_twice = jnp.concatenate([w_router, w_router, pad], axis=1)
        gain_two = ffn_gain.reshape(1, D)
        residual, rows, gate = route_call(experts, tokens, attn, w_out, gain_two, router_twice, routes)
        rows, _, near = lax.optimization_barrier((rows, grads_in[1][1], near))
        rows_next = swap(rows, 2)
        rows_in = [(rows, swap(rows, 1)), None]

    with jax.named_scope("weights_out"):
        weights = {0: (mine, theirs), 1: (near, swap_rep(near))}
        ids = [((place // GROUP) ^ slot) * GROUP + place % GROUP for slot in range(slots)]
        ids = [expert.astype(jnp.int32) for expert in ids]

    carry, sums, tasks = [None, None], [None] * slots, [None] * slots
    mark, point = after(jnp.zeros((8, LANES), F32), rows), rows
    beat = None

    def tick(*arrays):
        nonlocal mark
        mark = after(mark, *arrays)

    def hold(values):
        return after(values, point)

    def pause():
        nonlocal mark, beat
        mark, beat = pause_call(*marks()), None

    def marks():
        return [mark, mark if beat is None else beat]

    def passed(value, beats=False):
        nonlocal mark, point, beat
        beat = swap(mark, 1) if beats else None
        mark, point = after(mark, value), value

    def run(chip, group, last=False, beats=True):
        carry[chip], done = expert_call(
            jnp.stack([ids[slot] for slot in group]),
            marks(),
            experts,
            rows_in[chip],
            grads_in[chip],
            [weights[slot] for slot in group],
            [sums[slot] for slot in group],
            carry[chip],
            last,
        )
        passed(carry[chip][2], beats)
        for slot, pair in zip(group, done):
            if sums[slot] is not None:
                tasks[slot] = Task(sum_steps(slot, *pair))
            sums[slot] = pair

    with jax.named_scope("experts"):
        pause()
        run(0, [0], beats=False)
        tick(weights[1][1], far)
        far = hold(far)
        weights[2] = (far, swap_rep(far))
        landed = {slot: swap(far, GROUP) if slot == 3 else swap(hold(mine), slot * GROUP) for slot in range(3, slots)}
        run(0, [1])
        tick(rows_next, weights[2][1], *landed.values())
        for slot, held in landed.items():
            held = hold(held)
            weights[slot] = (held, swap_rep(held))
        rows_in[1] = (rows_next, swap(hold(rows_next), 1))
        pause()
        tick(rows_in[1][1])
        run(1, [0, 1])
        tick(*[weights[slot][1] for slot in landed])
        tasks[1].step()
        for slot in range(4, slots, 2):
            run(1, [slot, slot + 1])
            run(0, [slot])
            run(0, [slot + 1])
        run(1, [2, 3], True)
        there_landed = swap(hold(carry[1][4]), 1)
        pause()
        there = merge_call(experts, mark, carry[1][1], carry[1][2], there_landed)
        d_next = swap(there, 2)
        tick(there, *tasks[1].step())
        tasks[0].step()
        mix_landed = swap(hold(carry[1][3]), 1)
        run(0, [3])
        mix_there = merge_call(experts, mark, carry[1][0], None, mix_landed)
        tick(mix_there, *tasks[0].step())
        tasks[3].step()
        run(0, [2], True)

    with jax.named_scope("routing_back"):
        d_core = swap(hold(carry[0][4]), 1)
        tasks[2].step()
        pause()
        tick(d_core, d_next, *[array for task in tasks[3:] for array in task.step()])
        point = mark
        mix_home = swap(hold(mix_there), 2)
        mix_core = swap(hold(carry[0][3]), 1)
        d_residual, d_mixed, d_attn, d_small = back_call(
            experts, mark, carry[0][1], carry[0][2], d_core, d_next, residual, cotangent, gate, gain_two, router_twice, w_out
        )
        passed(d_small, True)
        tick(mix_core)
        d_out = out_call(marks(), attn, d_mixed, d_small)
        passed(d_out, True)

    with jax.named_scope("attention_back"):
        in_dims = (((0,), (1,)), ((), ()))
        sum_out = lax.psum_scatter(d_out, "ep", scatter_dimension=0, tiled=True)
        w_tasks, d_packed = [], []
        for part in range(PARTS):
            packed = None
            for turn in range(TURNS):
                packed = attend_back_call(
                    part, turn, marks(), pieces, query_rot, key_rot, value_low, d_attn, attn, lse, cosine, sine, packed
                )
                passed(packed, (part, turn) != (PARTS - 1, TURNS - 1))
                if (part, turn) == (0, 0):
                    tick(*tasks[2].step(), *tasks[1].step())
                if (part, turn) == (1, 0):
                    tick(mix_home)
                stepped = [array for task in w_tasks for array in task.step()]
                tick(*stepped)
            d_packed.append(packed)
            w_tasks.append(Task(reduce_rows(dot(normed_one, packed, in_dims).astype(BF16))))
            if part < PARTS - 1:
                tick(*w_tasks[-1].step())

    with jax.named_scope("tail"):
        last, other = w_tasks[1], w_tasks[0]
        out_task = Task(reduce_reps(hold(sum_out)))
        mix_home = after(mix_home, packed, *stepped, *last.step(), *out_task.step())
        output = point = combine_call(residual, carry[0][0], mix_core, mix_home)
        point = last.step()[0]
        total = tasks[0].finish()
        for task in tasks[1:3] + tasks[4:]:
            total = total + task.finish().astype(F32)
        total = Task(reduce_reps(total, 2)).finish().astype(BF16)
        total_landed = swap_rep(total)
        gain_one = after(attn_gain.reshape(1, D), output, total, point)
        d_tokens = point = finish_call(tokens, d_residual, projections, gain_one, d_packed)
        point = d_tokens = after(d_tokens, *other.step(), *last.step())
        s_mixed = out_task.finish()
        s_out, s_small = s_mixed[:, :D], s_mixed[:, D:]
        for task in (last, other, last):
            point = task.step()[0]
        total, total_landed, s_out = lax.optimization_barrier((total, total_landed, s_out, point))[:3]
        s_gate, s_up, s_down = join_call(turned, total, total_landed)
        point = s_down

    with jax.named_scope("sums_rest"):
        count = s_out.shape[0]
        first = place * count
        s_parts, s_attn, columns = [], 0.0, [[] for _ in projections]
        for task in w_tasks:
            part, cut = task.finish(), 0
            for group, w in zip(columns, projections):
                wide = w.shape[1] // PARTS
                own = lax.dynamic_slice(w, (first, len(group) * wide), (count, wide)).astype(F32)
                group.append(part[:, cut : cut + wide])
                s_attn += jnp.sum(group[-1] * own, axis=1)
                cut += wide
        s_query, s_key, s_value = [jnp.concatenate(group, axis=1) for group in columns]
        s_attn = s_attn / lax.dynamic_slice_in_dim(attn_gain, first, count)

    return (
        output,
        d_tokens,
        s_attn,
        s_query,
        s_key,
        s_value,
        s_out,
        s_small[:, experts],
        s_small[:, :experts],
        s_gate[None],
        s_up[None],
        s_down[None],
    )


def solution(mesh):
    rows, whole, slices = P(("rep", "ep"), None), P(), P("ep", None)
    expert = P("ep", None, None)
    return jax.shard_map(
        local,
        mesh=mesh,
        in_specs=(rows,) * 3 + (whole,) * 7 + (expert,) * 3 + (rows,),
        out_specs=(rows, rows, P("ep")) + (slices,) * 4 + (P("ep"), slices) + (expert,) * 3,
        check_vma=False,
    )
```

```python
import functools
import math

import jax
import jax.numpy as jnp
import numpy as np
from jax import lax
from jax.experimental import pallas as pl
from jax.experimental.pallas import tpu as pltpu
from jax.sharding import PartitionSpec as P

D = 1536
HEADS = 24
KV = 8
HEAD = 64
LEN = 1024
PIECE = 256
QUERIES = HEADS // KV
WIDE = 256
TILE = 256
GROUP = 4
PARTS = 2
TURNS = 2
LANES = 128
WIDTH = D + LANES

eps = 1e-06
theta_base = 10000.0
masked_score = -1e30
score_scale = HEAD ** (-0.5)
two_scale = score_scale * math.log2(math.e)

F32 = jnp.float32
BF16 = jnp.bfloat16
NN = (((1,), (0,)), ((), ()))
NT = (((1,), (1,)), ((), ()))
TN = (((0,), (0,)), ((), ()))
ANY = pl.BlockSpec(memory_space=pl.ANY)
SMEM = pl.BlockSpec(memory_space=pltpu.SMEM)


def dot(left, right, dims):
    return lax.dot_general(left, right, dims, preferred_element_type=F32)


def shaped(shape, dtype):
    return jax.ShapeDtypeStruct(shape, dtype)


def estimate(micros):
    return pl.CostEstimate(flops=int(micros * 1e10), bytes_accessed=int(micros * 1e6), transcendentals=0)


def rms_scale(values):
    return lax.rsqrt(jnp.mean(values * values, axis=-1, keepdims=True) + eps)


def rotary_tables():
    half_head = HEAD // 2
    frequency = theta_base ** (-(np.arange(half_head, dtype=np.float64) * 2.0) / HEAD)
    angles = frequency[:, None] * np.arange(LEN, dtype=np.float64)[None, :]
    return np.cos(angles).astype(np.float32), np.sin(angles).astype(np.float32)


def turn(values, cosine, sine):
    first, second = values[: HEAD // 2], values[HEAD // 2 :]
    return jnp.concatenate([first * cosine - second * sine, second * cosine + first * sine], axis=0)


def turn_back(grads, cosine, sine):
    first, second = grads[: HEAD // 2], grads[HEAD // 2 :]
    return jnp.concatenate([first * cosine + second * sine, second * cosine - first * sine], axis=0)


def fill_bias(pieces, bias):
    for block in range(LEN // WIDE):
        first = block * WIDE
        shape = bias.shape[1:]
        key = lax.broadcasted_iota(jnp.int32, shape, 0) + first
        query = lax.broadcasted_iota(jnp.int32, shape, 1) + first
        allowed = key <= query
        for piece in range(pieces.shape[1]):
            start = pieces[0, piece]
            low, high = jnp.minimum(key, query), jnp.maximum(key, query)
            allowed = allowed | ((low >= start) & (high < start + PIECE))
        bias[block] = jnp.where(allowed, 0.0, masked_score)


def key_span(block):
    return block * WIDE, min((block + 2) * WIDE, LEN)


def rows_at(place):
    return pl.BlockSpec((HEAD, LEN), lambda *grid: (place(*grid), 0))


def table_spec():
    return pl.BlockSpec((HEAD // 2, LEN), lambda *grid: (0, 0))


def attend_kernel(pieces, q0, q1, q2, k_in, v_in, cosine, sine, attn, q_out, k_out, v_out, lse, bias):
    @pl.when(pl.program_id(0) == 0)
    def _():
        fill_bias(pieces, bias)

    cos, sin = cosine[...], sine[...]
    k_rot = turn(k_in[...], cos, sin) * two_scale
    k_out[...] = k_rot.astype(BF16)
    keys = k_rot.T.astype(BF16)
    values = v_in[...].astype(BF16)
    v_out[...] = values
    for head, q_in in enumerate((q0, q1, q2)):
        rows = pl.ds(head * HEAD, HEAD)
        q_rot = turn(q_in[...], cos, sin).astype(BF16)
        q_out[rows, :] = q_rot
        for block in range(LEN // WIDE):
            columns = pl.ds(block * WIDE, WIDE)
            first, last = key_span(block)
            queries = q_rot[:, block * WIDE : (block + 1) * WIDE]
            spans = [(first, last)] + ([(0, first)] if first > 0 else [])
            scores = [dot(keys[a:b], queries, NN) for a, b in spans]
            scores[0] = scores[0] + bias[block, : last - first]
            highest = functools.reduce(jnp.maximum, [jnp.max(s, axis=0, keepdims=True) for s in scores])
            weights = [jnp.exp2(s - highest) for s in scores]
            total = sum(jnp.sum(w, axis=0, keepdims=True) for w in weights)
            mixed = sum(dot(values[:, a:b], w.astype(BF16), NN) for (a, b), w in zip(spans, weights)) / total
            attn[rows, columns] = mixed.astype(BF16)
            lse[head : head + 1, columns] = highest + jnp.log2(total)


def attend_call(pieces, query, key, value, cosine, sine):
    rows = lambda count: pl.BlockSpec((count, LEN), lambda i: (i, 0))
    width = QUERIES * HEAD
    return pl.pallas_call(
        attend_kernel,
        grid=(KV,),
        in_specs=[SMEM]
        + [rows_at(lambda i, head=head: QUERIES * i + head) for head in range(QUERIES)]
        + [rows_at(lambda i: i), rows_at(lambda i: i)]
        + [table_spec(), table_spec()],
        out_specs=[rows(width), rows(width), rows(HEAD), rows(HEAD), rows(8)],
        out_shape=[
            shaped((D, LEN), BF16),
            shaped((D, LEN), BF16),
            shaped((KV * HEAD, LEN), BF16),
            shaped((KV * HEAD, LEN), BF16),
            shaped((KV * 8, LEN), F32),
        ],
        scratch_shapes=[pltpu.VMEM((LEN // WIDE, 2 * WIDE, WIDE), F32)],
        compiler_params=pltpu.CompilerParams(vmem_limit_bytes=48 << 20),
        cost_estimate=estimate(25),
        name="attend",
    )(pieces, *[query] * QUERIES, key, value, cosine, sine)


def with_parts(columns, row):
    rank = lax.broadcasted_iota(jnp.int32, columns.shape, 0)
    high = row.astype(BF16).astype(F32)
    middle = (row - high).astype(BF16).astype(F32)
    parts = jnp.where(rank == 0, high, jnp.where(rank == 1, middle, jnp.where(rank == 2, row - high - middle, 0.0)))
    return jnp.concatenate([columns, parts.astype(BF16)], axis=0)


def attend_back_kernel(
    mark, beat, pieces, q_in, k_in, v_in, do_in, attn, lse, cosine, sine, *rest
):
    out, bias, keys_kept, values_kept, dk_sum, dv_sum = rest[-6:]
    kind = pl.program_id(1)

    @pl.when((pl.program_id(0) == 0) & (kind == 0))
    def _():
        fill_bias(pieces, bias)

    cos, sin = cosine[...], sine[...]

    @pl.when(kind == 0)
    def _():
        tail = jnp.where(lax.broadcasted_iota(jnp.int32, (LEN, HEAD), 1) < 3, -1.0, 0.0)
        for kept, ref in ((keys_kept, k_in), (values_kept, v_in)):
            kept[...] = jnp.concatenate([ref[...].astype(F32).T, tail], axis=1).astype(BF16)
        dk_sum[...] = jnp.zeros_like(dk_sum)
        dv_sum[...] = jnp.zeros_like(dv_sum)

    @pl.when(kind < QUERIES)
    def _():
        k_cols, keys, values = k_in[...], keys_kept[...], values_kept[...]
        q_cols, do_cols = q_in[...], do_in[...]
        q_rows = q_cols.astype(F32).T.astype(BF16)
        do_rows = do_cols.astype(F32).T.astype(BF16)
        delta = jnp.sum(do_cols.astype(F32) * attn[...].astype(F32), axis=0, keepdims=True)
        q_wide = with_parts(q_cols, lse[pl.ds(kind, 1), :])
        do_wide = with_parts(do_cols, delta)
        for block in range(LEN // WIDE):
            part = slice(block * WIDE, (block + 1) * WIDE)
            first, last = key_span(block)
            d_query = 0.0
            for a, b in [(first, last)] + ([(0, first)] if first > 0 else []):
                scores = dot(keys[a:b], q_wide[:, part], NN)
                if a == first:
                    scores = scores + bias[block, : b - a]
                probs = jnp.exp2(scores)
                d_scores = (probs * dot(values[a:b], do_wide[:, part], NN)).astype(BF16)
                dv_sum[a:b] += dot(probs.astype(BF16), do_rows[part], NN)
                dk_sum[a:b] += dot(d_scores, q_rows[part], NN)
                d_query = d_query + dot(k_cols[:, a:b], d_scores, NN)
            out[:, part] = turn_back(d_query * math.log(2.0), cos[:, part], sin[:, part]).astype(BF16)

    @pl.when(kind == QUERIES)
    def _():
        out[...] = turn_back(dk_sum[...].T * score_scale, cos, sin).astype(BF16)

    @pl.when(kind == QUERIES + 1)
    def _():
        out[...] = dv_sum[...].T.astype(BF16)


def attend_back_call(part, turn, marks, pieces, q_in, k_in, v_in, do_in, attn, lse, cosine, sine, before):
    group = KV // PARTS
    per = group // TURNS
    first = part * group + turn * per
    query = rows_at(lambda i, j: (first + i) * QUERIES + jnp.minimum(j, QUERIES - 1))
    key = rows_at(lambda i, j: first + i)

    def place(i, j):
        inner = turn * per + i
        tail = jnp.where(j == QUERIES, QUERIES * group + inner, (QUERIES + 1) * group + inner)
        return jnp.where(j < QUERIES, QUERIES * inner + j, tail)

    ins = [*marks, pieces, q_in, k_in, v_in, do_in, attn, lse, cosine, sine] + ([] if before is None else [before])
    return pl.pallas_call(
        attend_back_kernel,
        grid=(per, QUERIES + 2),
        in_specs=[ANY, ANY, SMEM, query, key, key, query, query, pl.BlockSpec((8, LEN), lambda i, j: (first + i, 0))]
        + [table_spec(), table_spec()]
        + ([] if before is None else [ANY]),
        out_specs=rows_at(place),
        out_shape=shaped(((QUERIES + 2) * group * HEAD, LEN), BF16),
        input_output_aliases={} if before is None else {len(ins) - 1: 0},
        scratch_shapes=[
            pltpu.VMEM((LEN // WIDE, 2 * WIDE, WIDE), F32),
            pltpu.VMEM((LEN, 2 * HEAD), BF16),
            pltpu.VMEM((LEN, 2 * HEAD), BF16),
            pltpu.VMEM((LEN, HEAD), F32),
            pltpu.VMEM((LEN, HEAD), F32),
        ],
        compiler_params=pltpu.CompilerParams(vmem_limit_bytes=48 << 20),
        cost_estimate=estimate(15),
        name="attend_back",
    )(*ins)


def halve_kernel(side, gate, up, down, mine, theirs):
    half = down.shape[0]

    def write(out):
        out[:half] = gate[...].T
        out[half : 2 * half] = up[...].T
        out[2 * half :] = down[...]

    pl.when(pl.program_id(0) == 0)(lambda: write(mine))
    pl.when(pl.program_id(0) == 1)(lambda: write(theirs))


def halve_call(side, gate, up, down):
    half = down.shape[0] // 2
    columns = pl.BlockSpec((D, half), lambda i, side: (0, lax.rem(side[0] + i, 2)))
    whole = pl.BlockSpec((3 * half, D), lambda i, side: (0, 0))
    return pl.pallas_call(
        halve_kernel,
        grid_spec=pltpu.PrefetchScalarGridSpec(
            num_scalar_prefetch=1,
            grid=(2,),
            in_specs=[columns, columns, pl.BlockSpec((half, D), lambda i, side: (lax.rem(side[0] + i, 2), 0))],
            out_specs=[whole, whole],
        ),
        out_shape=[shaped((3 * half, D), BF16)] * 2,
        compiler_params=pltpu.CompilerParams(vmem_limit_bytes=60 << 20),
        cost_estimate=estimate(5),
        name="halve",
    )(side, gate, up, down)


def finish_kernel(parts, tokens, residual, w_query, w_key, w_value, gain, *rest):
    grads, out = rest[:-1], rest[-1]
    total = 0.0
    for part, ref in enumerate(grads):
        columns = ref[...].T
        first = 0
        for weight in (w_query, w_key, w_value):
            wide = weight.shape[1] // parts
            total = total + dot(columns[:, first : first + wide], weight[:, part * wide : (part + 1) * wide], NT)
            first += wide
    values = tokens[...].astype(F32)
    scale = rms_scale(values)
    norm = values * scale
    scaled = total * gain[...]
    out[...] = residual[...] + scale * (scaled - norm * jnp.mean(scaled * norm, axis=1, keepdims=True))


def finish_call(tokens, residual, weights, gain, grads):
    rows = pl.BlockSpec((TILE, D), lambda i: (i, 0))
    whole = lambda array: pl.BlockSpec(array.shape, lambda i: (0, 0), pipeline_mode=pl.Buffered(1))
    return pl.pallas_call(
        functools.partial(finish_kernel, len(grads)),
        grid=(LEN // TILE,),
        in_specs=[rows, rows, *[whole(w) for w in weights], whole(gain)]
        + [pl.BlockSpec((g.shape[0], TILE), lambda i: (0, i)) for g in grads],
        out_specs=rows,
        out_shape=shaped((LEN, D), F32),
        compiler_params=pltpu.CompilerParams(vmem_limit_bytes=48 << 20),
        cost_estimate=estimate(5),
        name="finish",
    )(tokens, residual, *weights, gain, *grads)


def split_lanes(values, experts):
    lanes = lax.broadcasted_iota(jnp.int32, values.shape, 1)
    high = values.astype(BF16).astype(F32)
    return jnp.where(lanes < experts, high, jnp.where(lanes < 2 * experts, values - high, 0.0)).astype(BF16)


def join_lanes(parts, experts):
    return parts + pltpu.roll(parts, LANES - experts, 1)


def route_kernel(experts, tokens, attn, w_out, gain, w_router, routes, residual, rows, gate):
    values = tokens[...].astype(F32) + dot(attn[...], w_out[...], TN)
    residual[...] = values
    normed = (values * rms_scale(values) * gain[...]).astype(BF16)
    logits = dot(normed, w_router[...], NN)
    lanes = lax.broadcasted_iota(jnp.int32, logits.shape, 1)
    expert = lax.rem(lanes, experts)
    chosen = lanes < 0
    for k in range(routes.shape[1]):
        chosen = chosen | (routes[:, k : k + 1] == expert)
    chosen = chosen & (lanes < 2 * experts)
    logits = jnp.where(chosen, logits, masked_score)
    weights = jnp.exp(logits - jnp.max(logits, axis=1, keepdims=True))
    share = weights / (0.5 * jnp.sum(weights, axis=1, keepdims=True))
    gate[...] = share
    rows[:, :D] = normed
    rows[:, D:] = split_lanes(share, experts)


def route_call(experts, tokens, attn, w_out, gain, w_router, routes):
    rows = lambda cols: pl.BlockSpec((TILE, cols), lambda i: (i, 0))
    whole = lambda *shape: pl.BlockSpec(shape, lambda i: (0, 0), pipeline_mode=pl.Buffered(1))
    return pl.pallas_call(
        functools.partial(route_kernel, experts),
        grid=(LEN // TILE,),
        in_specs=[rows(D), pl.BlockSpec((D, TILE), lambda i: (0, i)), whole(D, D), whole(1, D), whole(D, LANES)]
        + [rows(routes.shape[1])],
        out_specs=[rows(D), rows(WIDTH), rows(LANES)],
        out_shape=[shaped((LEN, D), F32), shaped((LEN, WIDTH), BF16), shaped((LEN, LANES), F32)],
        compiler_params=pltpu.CompilerParams(vmem_limit_bytes=60 << 20),
        cost_estimate=estimate(5),
        name="route",
    )(tokens, attn, w_out, gain, w_router, routes)


def merge_kernel(experts, mark, kept, kept_share, landed, out):
    out[:, :D] = (kept[...].astype(F32) + landed[:, :D].astype(F32)).astype(BF16)
    if kept_share is not None:
        share = kept_share[...] + join_lanes(landed[:, D:].astype(F32), experts)
        share = jnp.where(lax.broadcasted_iota(jnp.int32, share.shape, 1) < experts, share, 0.0)
        out[:, D:] = split_lanes(share + pltpu.roll(share, experts, 1), experts)


def merge_call(experts, mark, kept, kept_share, landed):
    rows = lambda cols: pl.BlockSpec((TILE, cols), lambda i: (i, 0))
    width = landed.shape[1]
    kernel = functools.partial(merge_kernel, experts)
    if kept_share is None:
        kernel = lambda mark, kept, landed, out: merge_kernel(experts, mark, kept, None, landed, out)
    return pl.pallas_call(
        kernel,
        grid=(LEN // TILE,),
        in_specs=[ANY, rows(D)] + ([] if kept_share is None else [rows(LANES)]) + [rows(width)],
        out_specs=rows(width),
        out_shape=shaped((LEN, width), BF16),
        compiler_params=pltpu.CompilerParams(vmem_limit_bytes=32 << 20),
        cost_estimate=estimate(3),
        name="merge",
    )(*[ref for ref in (mark, kept, kept_share, landed) if ref is not None])


def back_kernel(
    experts, mark, kept, kept_share, core, chip, residual, cotangent, gate, gain, w_router, w_out, d_res, d_mix, d_attn, d_router
):
    @pl.when(pl.program_id(0) == 0)
    def _():
        d_router[...] = jnp.zeros_like(d_router)

    landed = core[:, D:].astype(F32) + chip[:, D:].astype(F32)
    share = kept_share[...] + join_lanes(landed, experts)
    first = lax.broadcasted_iota(jnp.int32, share.shape, 1) < experts
    gates = jnp.where(first, gate[...], 0.0)
    inner = jnp.sum(gates * share, axis=1, keepdims=True)
    d_logits = jnp.where(first, gates * (share - inner), 0.0).astype(BF16)
    d_normed = kept[...].astype(F32) + core[:, :D].astype(F32) + chip[:, :D].astype(F32) + dot(d_logits, w_router[...], NT)
    values, gains = residual[...], gain[...]
    scale = rms_scale(values)
    norm = values * scale
    d_gain = jnp.sum(d_normed * norm, axis=0, keepdims=True)
    scaled = d_normed * gains
    d_values = cotangent[...].astype(F32) + scale * (scaled - norm * jnp.mean(scaled * norm, axis=1, keepdims=True))
    d_res[...] = d_values
    mixed = d_values.astype(BF16)
    d_mix[...] = mixed
    d_attn[...] = dot(w_out[...], mixed, NT).astype(BF16)
    d_router[...] += dot(d_logits, (norm * gains).astype(BF16), TN)
    d_router[experts : experts + 1] += d_gain


def back_call(experts, mark, kept, kept_share, core, chip, residual, cotangent, gate, gain, w_router, w_out):
    rows = lambda cols: pl.BlockSpec((TILE, cols), lambda i: (i, 0))
    whole = lambda *shape: pl.BlockSpec(shape, lambda i: (0, 0), pipeline_mode=pl.Buffered(1))
    return pl.pallas_call(
        functools.partial(back_kernel, experts),
        grid=(LEN // TILE,),
        in_specs=[ANY, rows(D), rows(LANES), rows(WIDTH), rows(WIDTH), rows(D), rows(D), rows(LANES)]
        + [whole(1, D), whole(D, LANES), whole(D, D)],
        out_specs=[rows(D), rows(D), pl.BlockSpec((D, TILE), lambda i: (0, i)), whole(LANES, D)],
        out_shape=[
            shaped((LEN, D), F32),
            shaped((LEN, D), BF16),
            shaped((D, LEN), BF16),
            shaped((LANES, D), F32),
        ],
        compiler_params=pltpu.CompilerParams(vmem_limit_bytes=48 << 20),
        cost_estimate=estimate(8),
        name="back",
    )(mark, kept, kept_share, core, chip, residual, cotangent, gate, gain, w_router, w_out)


def out_kernel(mark, beat, attn, mixed, small, out):
    out[:, :D] = dot(attn[...], mixed[...], NN).astype(BF16)
    out[:, D:] = small[...].T.astype(BF16)


def out_call(marks, attn, mixed, small):
    return pl.pallas_call(
        out_kernel,
        grid=(D // TILE,),
        in_specs=[
            ANY,
            ANY,
            pl.BlockSpec((TILE, LEN), lambda i: (i, 0)),
            pl.BlockSpec((LEN, D), lambda i: (0, 0), pipeline_mode=pl.Buffered(1)),
            pl.BlockSpec((LANES, TILE), lambda i: (0, i)),
        ],
        out_specs=pl.BlockSpec((TILE, WIDTH), lambda i: (i, 0)),
        out_shape=shaped((D, WIDTH), BF16),
        compiler_params=pltpu.CompilerParams(vmem_limit_bytes=32 << 20),
        cost_estimate=estimate(5),
        name="out_grad",
    )(*marks, attn, mixed, small)


def pause_kernel(mark, beat, out):
    out[...] = mark[...] + beat[...]


def pause_call(mark, beat):
    return pl.pallas_call(
        pause_kernel, out_shape=shaped(mark.shape, mark.dtype), cost_estimate=estimate(10), name="pause"
    )(mark, beat)


def combine_kernel(residual, kept, core, chip, out):
    total = residual[...] + kept[...].astype(F32) + core[...].astype(F32) + chip[...].astype(F32)
    out[...] = total.astype(BF16)


def combine_call(residual, kept, core, chip):
    rows = pl.BlockSpec((TILE, D), lambda i: (i, 0))
    return pl.pallas_call(
        combine_kernel,
        grid=(LEN // TILE,),
        in_specs=[rows] * 4,
        out_specs=rows,
        out_shape=shaped((LEN, D), BF16),
        compiler_params=pltpu.CompilerParams(vmem_limit_bytes=48 << 20),
        cost_estimate=estimate(10),
        name="combine",
    )(residual, kept, core, chip)


def expert_kernel(count, experts, fresh, first, last_tokens, steps, ids, mark, beat, *rest):
    rest = list(rest)

    def take(number):
        taken = rest[:number]
        del rest[:number]
        return taken

    n2, up = take(2), take(2)
    w_in = [take(2) for _ in range(count)]
    sums_in = [[] if new else take(2) for new in fresh]
    carry_in = [] if first else take(3)
    outs = take(5) if last_tokens else take(3)
    sums_out = [take(2) for _ in range(count)]
    weights, sums = take(1)[0], take(1)[0]
    low, sem = rest
    half = weights.shape[1] // 6
    width = 2 * half
    step = pl.program_id(0)
    ahead = step < steps // 2

    def pieces_of(parts, whole):
        return [
            (ref.at[pl.ds(kind * half, half)], whole.at[pl.ds((2 * kind + part) * half, half)])
            for kind in range(3)
            for part, ref in enumerate(parts)
        ]

    def copies_of(pairs, lane):
        return [pltpu.make_async_copy(a, b, sem.at[lane, n]) for n, (a, b) in enumerate(pairs)]

    loads = [copies_of(pieces_of(w_in[e], weights.at[e]), e) for e in range(count)]
    prior = [[] if fresh[e] else copies_of(pieces_of(sums_in[e], low.at[e]), count + e) for e in range(count)]
    stores = [copies_of([(b, a) for a, b in pieces_of(sums_out[e], low.at[e])], e) for e in range(count)]

    @pl.when(step == 0)
    def _():
        for copy in sum(loads + prior, []):
            copy.start()
        sums[...] = jnp.zeros_like(sums)
        for copy in loads[0]:
            copy.wait()

    rows = jnp.where(ahead, n2[0][...], n2[1][...])
    grads = jnp.where(ahead, up[0][...], up[1][...])
    rows, gates = rows[:, :D], rows[:, D:].astype(F32)
    lanes = lax.broadcasted_iota(jnp.int32, gates.shape, 1)
    mixed = d_rows = d_shares = None
    add = lambda total, value: value if total is None else total + value
    for e in range(count):
        if e > 0:

            @pl.when(step == 0)
            def _(e=e):
                for copy in loads[e]:
                    copy.wait()

        w_both, w_down = weights.at[e, : 2 * width], weights.at[e, 2 * width :]
        hit = (lanes == ids[e]) | (lanes == ids[e] + experts)
        share = jnp.sum(jnp.where(hit, gates, 0.0), axis=1, keepdims=True)
        acts = dot(rows, w_both[...], NT)
        gate_act, up_act = acts[:, :width], acts[:, width:]
        d_plain = dot(grads, w_down[...], NT)
        sigmoid = 1.0 / (1.0 + jnp.exp(-gate_act))
        silu = gate_act * sigmoid
        hidden = silu * up_act
        shared = (share * hidden).astype(BF16)
        d_share = jnp.sum(hidden * d_plain, axis=1, keepdims=True)
        d_hidden = share * d_plain
        d_gate = (d_hidden * up_act * (sigmoid + silu * (1.0 - sigmoid))).astype(BF16)
        d_up = (d_hidden * silu).astype(BF16)
        d_both = jnp.concatenate([d_gate, d_up], axis=1)
        mixed = add(mixed, dot(shared, w_down[...], NN))
        d_rows = add(d_rows, dot(d_both, w_both[...], NN))
        d_shares = add(d_shares, jnp.where(hit, d_share, 0.0))
        sums[e, : 2 * width] += dot(d_both, rows, TN)
        sums[e, 2 * width :] += dot(shared, grads, TN)

        @pl.when(step == steps - 1)
        def _(e=e):
            for copy in prior[e]:
                copy.wait()
            low[e] = (sums[e] if fresh[e] else sums[e] + low[e].astype(F32)).astype(BF16)
            for copy in stores[e]:
                copy.start()

    results = [mixed, d_rows, d_shares]
    if not first:
        results = [result + ref[...].astype(F32) for result, ref in zip(results, carry_in)]
    if last_tokens:

        @pl.when(ahead)
        def _():
            for ref, result in zip(outs[:3], results):
                ref[...] = result.astype(ref.dtype)

        @pl.when(jnp.logical_not(ahead))
        def _():
            outs[3][...] = results[0].astype(BF16)
            outs[4][:, :D] = results[1].astype(BF16)
            outs[4][:, D:] = split_lanes(results[2], experts)
    else:
        for ref, result in zip(outs, results):
            ref[...] = result.astype(ref.dtype)

    @pl.when(step == steps - 1)
    def _():
        for copy in sum(stores, []):
            copy.wait()


def expert_call(ids, marks, experts, n2, up, weights, sums, carry, last_tokens):
    tokens, height, count = 2 * n2[0].shape[0], weights[0][0].shape[0], len(weights)
    steps = tokens // TILE
    rows = lambda cols: pl.BlockSpec((TILE, cols), lambda i: (i, 0))
    near = lambda cols: pl.BlockSpec((TILE, cols), lambda i: (jnp.minimum(i, steps // 2 - 1), 0))
    far = lambda cols: pl.BlockSpec((TILE, cols), lambda i: (jnp.maximum(i - steps // 2, 0), 0))
    ins = [ids, *marks, *n2, *up] + [w for pair in weights for w in pair]
    specs = [SMEM, ANY, ANY, near(WIDTH), far(WIDTH), near(D), far(D)] + [ANY] * (2 * count)
    fresh, first = [pair is None for pair in sums], carry is None
    columns = (D, D, LANES)
    if last_tokens:
        outs = [shaped((tokens // 2, c), t) for c, t in zip(columns, (BF16, BF16, F32))]
        outs += [shaped((tokens // 2, c), BF16) for c in (D, WIDTH)]
        out_specs = [near(c) for c in columns] + [far(D), far(WIDTH)]
    else:
        outs = [shaped((tokens, c), t) for c, t in zip(columns, (BF16, F32, F32))]
        out_specs = [rows(c) for c in columns]
    aliases = {}
    for pair in sums:
        if pair is not None:
            ins += pair
            specs += [ANY, ANY]
    if not first:
        if not last_tokens:
            aliases.update({len(ins) + k: k for k in range(3)})
        ins += carry
        specs += [rows(c) for c in columns]
    tokens_out = len(outs)
    for _ in range(count):
        outs += [shaped((height, D), BF16)] * 2
        out_specs += [ANY, ANY]
    scratch = [pltpu.VMEM((count, 2 * height, D), BF16), pltpu.VMEM((count, 2 * height, D), F32)]
    scratch.append(pltpu.VMEM((count, 2 * height, D), BF16))
    scratch.append(pltpu.SemaphoreType.DMA((2 * count, 6)))
    done = pl.pallas_call(
        functools.partial(expert_kernel, count, experts, fresh, first, last_tokens, steps),
        grid=(steps,),
        in_specs=specs,
        out_specs=out_specs,
        out_shape=outs,
        scratch_shapes=scratch,
        input_output_aliases=aliases,
        compiler_params=pltpu.CompilerParams(vmem_limit_bytes=63 << 20),
        cost_estimate=estimate(15 * count),
        name="expert",
    )(*ins)
    return list(done[:tokens_out]), [tuple(done[tokens_out + 2 * e : tokens_out + 2 * e + 2]) for e in range(count)]


def join_kernel(side, held, landed, gate, up, down):
    here = pl.program_id(0) == 0
    rows = jnp.where(here, held[...], landed[...]).astype(F32)
    half = down.shape[0]
    gate[...] = rows[:half].T
    up[...] = rows[half : 2 * half].T
    down[...] = rows[2 * half :]


def join_call(side, held, landed):
    half = held.shape[0] // 3
    whole = pl.BlockSpec(held.shape, lambda i, side: (0, 0))
    columns = pl.BlockSpec((D, half), lambda i, side: (0, lax.rem(side[0] + i, 2)))
    return pl.pallas_call(
        join_kernel,
        grid_spec=pltpu.PrefetchScalarGridSpec(
            num_scalar_prefetch=1,
            grid=(2,),
            in_specs=[whole, whole],
            out_specs=[columns, columns, pl.BlockSpec((half, D), lambda i, side: (lax.rem(side[0] + i, 2), 0))],
        ),
        out_shape=[shaped((D, 2 * half), F32), shaped((D, 2 * half), F32), shaped((2 * half, D), F32)],
        compiler_params=pltpu.CompilerParams(vmem_limit_bytes=48 << 20),
        cost_estimate=estimate(5),
        name="join",
    )(side, held, landed)


def after(values, *others):
    return lax.optimization_barrier((values, *others))[0]


class Task:
    def __init__(self, steps):
        self.steps, self.result, self.over = steps, None, False

    def step(self):
        if self.over:
            return []
        try:
            return [next(self.steps)]
        except StopIteration as stop:
            self.result, self.over = stop.value, True
            return [self.result]

    def finish(self):
        while not self.over:
            self.step()
        return self.result


def local(
    tokens,
    routes,
    pieces,
    attn_gain,
    w_query,
    w_key,
    w_value,
    w_out,
    ffn_gain,
    w_router,
    expert_gate,
    expert_up,
    expert_down,
    cotangent,
):
    shards, reps = lax.axis_size("ep"), lax.axis_size("rep")
    experts = w_router.shape[1]
    slots = shards // GROUP
    place = lax.axis_index("ep")
    side = lax.axis_index("rep") % 2

    def swap(values, bits):
        return lax.ppermute(values, "ep", [(i, i ^ bits) for i in range(shards)])

    def swap_rep(values, bits=1):
        return lax.ppermute(values, "rep", [(i, i ^ bits) for i in range(reps)])


    def reduce_reps(values, bits=1):
        while bits < reps:
            values = values.astype(BF16)
            landed = swap_rep(values, bits)
            yield values
            values = values.astype(F32) + hold(landed).astype(F32)
            bits *= 2
        return values

    def reduce_rows(values):
        values = values.reshape(shards, -1, values.shape[1])
        bits = 1
        while bits < shards:
            values = values.reshape(values.shape[0] // 2, 2, *values.shape[1:])
            bit = (place // bits) % 2
            kept, sent = [
                lax.dynamic_index_in_dim(values, index, axis=1, keepdims=False) for index in (bit, 1 - bit)
            ]
            landed = swap(sent, bits)
            yield sent
            values = (kept.astype(F32) + hold(landed).astype(F32)).astype(BF16)
            bits *= 2
        return (yield from reduce_reps(values[0]))

    def sum_steps(slot, own, other):
        other = hold(other)
        landed = swap_rep(other)
        yield other
        own = own.astype(F32) + hold(landed).astype(F32)
        if slot == 0:
            return own
        if slot == 2 and slots > 3:
            own = own + tasks[3].finish().astype(F32)
        own = own.astype(BF16)
        landed = swap(own, GROUP if slot == 3 else slot * GROUP)
        yield own
        return hold(landed)

    with jax.named_scope("weights_out"):
        turned = side.astype(jnp.int32).reshape(1)
        mine, theirs = halve_call(turned, expert_gate[0], expert_up[0], expert_down[0])
        tokens, mine, theirs = lax.optimization_barrier((tokens, mine, theirs))
        near = swap(mine, GROUP)

    with jax.named_scope("cotangent_out"):
        grads_next = swap(cotangent, 2)
        grads_in = [(cotangent, swap(cotangent, 1)), None]

    with jax.named_scope("attention"):
        inputs = tokens.astype(F32)
        scale_one = rms_scale(inputs)
        norm_one = inputs * scale_one
        normed_one = (norm_one * attn_gain).astype(BF16)
        w_dims = (((0,), (1,)), ((), ()))
        projections = (w_query, w_key, w_value)
        query, key, value = [dot(w, normed_one, w_dims) for w in projections]
        far = swap(after(mine, key, value, query), 2 * GROUP)
        cosine, sine = [jnp.asarray(table) for table in rotary_tables()]
        attn, query_rot, key_rot, value_low, lse = attend_call(pieces, query, key, value, cosine, sine)
        attn = after(attn, grads_next, grads_in[0][1])

    with jax.named_scope("cotangent_out"):
        grads_in[1] = (grads_next, swap(after(grads_next, attn), 1))

    with jax.named_scope("routing"):
        pad = jnp.zeros((D, LANES - 2 * experts), BF16)
        router_twice = jnp.concatenate([w_router, w_router, pad], axis=1)
        gain_two = ffn_gain.reshape(1, D)
        residual, rows, gate = route_call(experts, tokens, attn, w_out, gain_two, router_twice, routes)
        rows, _, near = lax.optimization_barrier((rows, grads_in[1][1], near))
        rows_next = swap(rows, 2)
        rows_in = [(rows, swap(rows, 1)), None]

    with jax.named_scope("weights_out"):
        weights = {0: (mine, theirs), 1: (near, swap_rep(near))}
        ids = [((place // GROUP) ^ slot) * GROUP + place % GROUP for slot in range(slots)]
        ids = [expert.astype(jnp.int32) for expert in ids]

    carry, sums, tasks = [None, None], [None] * slots, [None] * slots
    mark, point = after(jnp.zeros((8, LANES), F32), rows), rows
    beat = None

    def tick(*arrays):
        nonlocal mark
        mark = after(mark, *arrays)

    def hold(values):
        return after(values, point)

    def pause():
        nonlocal mark, beat
        mark, beat = pause_call(*marks()), None

    def marks():
        return [mark, mark if beat is None else beat]

    def passed(value, beats=False):
        nonlocal mark, point, beat
        beat = swap(mark, 1) if beats else None
        mark, point = after(mark, value), value

    def run(chip, group, last=False, beats=True):
        carry[chip], done = expert_call(
            jnp.stack([ids[slot] for slot in group]),
            marks(),
            experts,
            rows_in[chip],
            grads_in[chip],
            [weights[slot] for slot in group],
            [sums[slot] for slot in group],
            carry[chip],
            last,
        )
        passed(carry[chip][2], beats)
        for slot, pair in zip(group, done):
            if sums[slot] is not None:
                tasks[slot] = Task(sum_steps(slot, *pair))
            sums[slot] = pair

    with jax.named_scope("experts"):
        pause()
        run(0, [0], beats=False)
        tick(weights[1][1], far)
        far = hold(far)
        weights[2] = (far, swap_rep(far))
        landed = {slot: swap(far, GROUP) if slot == 3 else swap(hold(mine), slot * GROUP) for slot in range(3, slots)}
        run(0, [1])
        tick(rows_next, weights[2][1], *landed.values())
        for slot, held in landed.items():
            held = hold(held)
            weights[slot] = (held, swap_rep(held))
        rows_in[1] = (rows_next, swap(hold(rows_next), 1))
        pause()
        tick(rows_in[1][1])
        run(1, [0, 1])
        tick(*[weights[slot][1] for slot in landed])
        tasks[1].step()
        for slot in range(4, slots, 2):
            run(1, [slot, slot + 1])
            run(0, [slot])
            run(0, [slot + 1])
        run(1, [2, 3], True)
        there_landed = swap(hold(carry[1][4]), 1)
        pause()
        there = merge_call(experts, mark, carry[1][1], carry[1][2], there_landed)
        d_next = swap(there, 2)
        tick(there, *tasks[1].step())
        tasks[0].step()
        mix_landed = swap(hold(carry[1][3]), 1)
        run(0, [3])
        mix_there = merge_call(experts, mark, carry[1][0], None, mix_landed)
        tick(mix_there, *tasks[0].step())
        tasks[3].step()
        run(0, [2], True)

    with jax.named_scope("routing_back"):
        d_core = swap(hold(carry[0][4]), 1)
        tasks[2].step()
        pause()
        tick(d_core, d_next, *[array for task in tasks[3:] for array in task.step()])
        point = mark
        mix_home = swap(hold(mix_there), 2)
        mix_core = swap(hold(carry[0][3]), 1)
        d_residual, d_mixed, d_attn, d_small = back_call(
            experts, mark, carry[0][1], carry[0][2], d_core, d_next, residual, cotangent, gate, gain_two, router_twice, w_out
        )
        passed(d_small, True)
        tick(mix_core)
        d_out = out_call(marks(), attn, d_mixed, d_small)
        passed(d_out, True)

    with jax.named_scope("attention_back"):
        in_dims = (((0,), (1,)), ((), ()))
        sum_out = lax.psum_scatter(d_out, "ep", scatter_dimension=0, tiled=True)
        w_tasks, d_packed = [], []
        for part in range(PARTS):
            packed = None
            for turn in range(TURNS):
                packed = attend_back_call(
                    part, turn, marks(), pieces, query_rot, key_rot, value_low, d_attn, attn, lse, cosine, sine, packed
                )
                passed(packed, (part, turn) != (PARTS - 1, TURNS - 1))
                if (part, turn) == (0, 0):
                    tick(*tasks[2].step(), *tasks[1].step())
                if (part, turn) == (1, 0):
                    tick(mix_home)
                stepped = [array for task in w_tasks for array in task.step()]
                tick(*stepped)
            d_packed.append(packed)
            w_tasks.append(Task(reduce_rows(dot(normed_one, packed, in_dims).astype(BF16))))
            if part < PARTS - 1:
                tick(*w_tasks[-1].step())

    with jax.named_scope("tail"):
        last, other = w_tasks[1], w_tasks[0]
        mix_home = after(mix_home, packed, *stepped, *last.step())
        output = point = combine_call(residual, carry[0][0], mix_core, mix_home)
        point = last.step()[0]
        total = tasks[0].finish()
        for task in tasks[1:3] + tasks[4:]:
            total = total + task.finish().astype(F32)
        total = Task(reduce_reps(total, 2)).finish().astype(BF16)
        total_landed = swap_rep(total)
        gain_one = after(attn_gain.reshape(1, D), output, total, point)
        d_tokens = point = finish_call(tokens, d_residual, projections, gain_one, d_packed)
        point = d_tokens = after(d_tokens, *other.step(), *last.step())
        point = last.step()[0]
        out_task = Task(reduce_reps(hold(sum_out)))
        for task in (other, out_task, last):
            point = task.step()[0]
        total, total_landed = lax.optimization_barrier((total, total_landed, point))[:2]
        s_gate, s_up, s_down = join_call(turned, total, total_landed)
        point = s_down
        s_mixed = out_task.finish()
        s_out, s_small = s_mixed[:, :D], s_mixed[:, D:]

    with jax.named_scope("sums_rest"):
        count = s_out.shape[0]
        first = place * count
        s_parts, s_attn, columns = [], 0.0, [[] for _ in projections]
        for task in w_tasks:
            part, cut = task.finish(), 0
            for group, w in zip(columns, projections):
                wide = w.shape[1] // PARTS
                own = lax.dynamic_slice(w, (first, len(group) * wide), (count, wide)).astype(F32)
                group.append(part[:, cut : cut + wide])
                s_attn += jnp.sum(group[-1] * own, axis=1)
                cut += wide
        s_query, s_key, s_value = [jnp.concatenate(group, axis=1) for group in columns]
        s_attn = s_attn / lax.dynamic_slice_in_dim(attn_gain, first, count)

    return (
        output,
        d_tokens,
        s_attn,
        s_query,
        s_key,
        s_value,
        s_out,
        s_small[:, experts],
        s_small[:, :experts],
        s_gate[None],
        s_up[None],
        s_down[None],
    )


def solution(mesh):
    rows, whole, slices = P(("rep", "ep"), None), P(), P("ep", None)
    expert = P("ep", None, None)
    return jax.shard_map(
        local,
        mesh=mesh,
        in_specs=(rows,) * 3 + (whole,) * 7 + (expert,) * 3 + (rows,),
        out_specs=(rows, rows, P("ep")) + (slices,) * 4 + (P("ep"), slices) + (expert,) * 3,
        check_vma=False,
    )
```

```python
import functools
import math

import jax
import jax.numpy as jnp
import numpy as np
from jax import lax
from jax.experimental import pallas as pl
from jax.experimental.pallas import tpu as pltpu
from jax.sharding import PartitionSpec as P

D = 1536
HEADS = 24
KV = 8
HEAD = 64
LEN = 1024
PIECE = 256
QUERIES = HEADS // KV
WIDE = 256
TILE = 256
GROUP = 4
PARTS = 2
TURNS = 2
LANES = 128
WIDTH = D + LANES

eps = 1e-06
theta_base = 10000.0
masked_score = -1e30
score_scale = HEAD ** (-0.5)
two_scale = score_scale * math.log2(math.e)

F32 = jnp.float32
BF16 = jnp.bfloat16
NN = (((1,), (0,)), ((), ()))
NT = (((1,), (1,)), ((), ()))
TN = (((0,), (0,)), ((), ()))
ANY = pl.BlockSpec(memory_space=pl.ANY)
SMEM = pl.BlockSpec(memory_space=pltpu.SMEM)


def dot(left, right, dims):
    return lax.dot_general(left, right, dims, preferred_element_type=F32)


def shaped(shape, dtype):
    return jax.ShapeDtypeStruct(shape, dtype)


def estimate(micros):
    return pl.CostEstimate(flops=int(micros * 1e10), bytes_accessed=int(micros * 1e6), transcendentals=0)


def rms_scale(values):
    return lax.rsqrt(jnp.mean(values * values, axis=-1, keepdims=True) + eps)


def rotary_tables():
    half_head = HEAD // 2
    frequency = theta_base ** (-(np.arange(half_head, dtype=np.float64) * 2.0) / HEAD)
    angles = frequency[:, None] * np.arange(LEN, dtype=np.float64)[None, :]
    return np.cos(angles).astype(np.float32), np.sin(angles).astype(np.float32)


def turn(values, cosine, sine):
    first, second = values[: HEAD // 2], values[HEAD // 2 :]
    return jnp.concatenate([first * cosine - second * sine, second * cosine + first * sine], axis=0)


def turn_back(grads, cosine, sine):
    first, second = grads[: HEAD // 2], grads[HEAD // 2 :]
    return jnp.concatenate([first * cosine + second * sine, second * cosine - first * sine], axis=0)


def fill_bias(pieces, bias):
    for block in range(LEN // WIDE):
        first = block * WIDE
        shape = bias.shape[1:]
        key = lax.broadcasted_iota(jnp.int32, shape, 0) + first
        query = lax.broadcasted_iota(jnp.int32, shape, 1) + first
        allowed = key <= query
        for piece in range(pieces.shape[1]):
            start = pieces[0, piece]
            low, high = jnp.minimum(key, query), jnp.maximum(key, query)
            allowed = allowed | ((low >= start) & (high < start + PIECE))
        bias[block] = jnp.where(allowed, 0.0, masked_score)


def key_span(block):
    return block * WIDE, min((block + 2) * WIDE, LEN)


def rows_at(place):
    return pl.BlockSpec((HEAD, LEN), lambda *grid: (place(*grid), 0))


def table_spec():
    return pl.BlockSpec((HEAD // 2, LEN), lambda *grid: (0, 0))


def attend_kernel(pieces, q0, q1, q2, k_in, v_in, cosine, sine, attn, q_out, k_out, v_out, lse, bias):
    @pl.when(pl.program_id(0) == 0)
    def _():
        fill_bias(pieces, bias)

    cos, sin = cosine[...], sine[...]
    k_rot = turn(k_in[...], cos, sin) * two_scale
    k_out[...] = k_rot.astype(BF16)
    keys = k_rot.T.astype(BF16)
    values = v_in[...].astype(BF16)
    v_out[...] = values
    for head, q_in in enumerate((q0, q1, q2)):
        rows = pl.ds(head * HEAD, HEAD)
        q_rot = turn(q_in[...], cos, sin).astype(BF16)
        q_out[rows, :] = q_rot
        for block in range(LEN // WIDE):
            columns = pl.ds(block * WIDE, WIDE)
            first, last = key_span(block)
            queries = q_rot[:, block * WIDE : (block + 1) * WIDE]
            spans = [(first, last)] + ([(0, first)] if first > 0 else [])
            scores = [dot(keys[a:b], queries, NN) for a, b in spans]
            scores[0] = scores[0] + bias[block, : last - first]
            highest = functools.reduce(jnp.maximum, [jnp.max(s, axis=0, keepdims=True) for s in scores])
            weights = [jnp.exp2(s - highest) for s in scores]
            total = sum(jnp.sum(w, axis=0, keepdims=True) for w in weights)
            mixed = sum(dot(values[:, a:b], w.astype(BF16), NN) for (a, b), w in zip(spans, weights)) / total
            attn[rows, columns] = mixed.astype(BF16)
            lse[head : head + 1, columns] = highest + jnp.log2(total)


def attend_call(pieces, query, key, value, cosine, sine):
    rows = lambda count: pl.BlockSpec((count, LEN), lambda i: (i, 0))
    width = QUERIES * HEAD
    return pl.pallas_call(
        attend_kernel,
        grid=(KV,),
        in_specs=[SMEM]
        + [rows_at(lambda i, head=head: QUERIES * i + head) for head in range(QUERIES)]
        + [rows_at(lambda i: i), rows_at(lambda i: i)]
        + [table_spec(), table_spec()],
        out_specs=[rows(width), rows(width), rows(HEAD), rows(HEAD), rows(8)],
        out_shape=[
            shaped((D, LEN), BF16),
            shaped((D, LEN), BF16),
            shaped((KV * HEAD, LEN), BF16),
            shaped((KV * HEAD, LEN), BF16),
            shaped((KV * 8, LEN), F32),
        ],
        scratch_shapes=[pltpu.VMEM((LEN // WIDE, 2 * WIDE, WIDE), F32)],
        compiler_params=pltpu.CompilerParams(vmem_limit_bytes=48 << 20),
        cost_estimate=estimate(25),
        name="attend",
    )(pieces, *[query] * QUERIES, key, value, cosine, sine)


def with_parts(columns, row):
    rank = lax.broadcasted_iota(jnp.int32, columns.shape, 0)
    high = row.astype(BF16).astype(F32)
    middle = (row - high).astype(BF16).astype(F32)
    parts = jnp.where(rank == 0, high, jnp.where(rank == 1, middle, jnp.where(rank == 2, row - high - middle, 0.0)))
    return jnp.concatenate([columns, parts.astype(BF16)], axis=0)


def attend_back_kernel(
    mark, beat, pieces, q_in, k_in, v_in, do_in, attn, lse, cosine, sine, *rest
):
    out, bias, keys_kept, values_kept, dk_sum, dv_sum = rest[-6:]
    kind = pl.program_id(1)

    @pl.when((pl.program_id(0) == 0) & (kind == 0))
    def _():
        fill_bias(pieces, bias)

    cos, sin = cosine[...], sine[...]

    @pl.when(kind == 0)
    def _():
        tail = jnp.where(lax.broadcasted_iota(jnp.int32, (LEN, HEAD), 1) < 3, -1.0, 0.0)
        for kept, ref in ((keys_kept, k_in), (values_kept, v_in)):
            kept[...] = jnp.concatenate([ref[...].astype(F32).T, tail], axis=1).astype(BF16)
        dk_sum[...] = jnp.zeros_like(dk_sum)
        dv_sum[...] = jnp.zeros_like(dv_sum)

    @pl.when(kind < QUERIES)
    def _():
        k_cols, keys, values = k_in[...], keys_kept[...], values_kept[...]
        q_cols, do_cols = q_in[...], do_in[...]
        q_rows = q_cols.astype(F32).T.astype(BF16)
        do_rows = do_cols.astype(F32).T.astype(BF16)
        delta = jnp.sum(do_cols.astype(F32) * attn[...].astype(F32), axis=0, keepdims=True)
        q_wide = with_parts(q_cols, lse[pl.ds(kind, 1), :])
        do_wide = with_parts(do_cols, delta)
        for block in range(LEN // WIDE):
            part = slice(block * WIDE, (block + 1) * WIDE)
            first, last = key_span(block)
            d_query = 0.0
            for a, b in [(first, last)] + ([(0, first)] if first > 0 else []):
                scores = dot(keys[a:b], q_wide[:, part], NN)
                if a == first:
                    scores = scores + bias[block, : b - a]
                probs = jnp.exp2(scores)
                d_scores = (probs * dot(values[a:b], do_wide[:, part], NN)).astype(BF16)
                dv_sum[a:b] += dot(probs.astype(BF16), do_rows[part], NN)
                dk_sum[a:b] += dot(d_scores, q_rows[part], NN)
                d_query = d_query + dot(k_cols[:, a:b], d_scores, NN)
            out[:, part] = turn_back(d_query * math.log(2.0), cos[:, part], sin[:, part]).astype(BF16)

    @pl.when(kind == QUERIES)
    def _():
        out[...] = turn_back(dk_sum[...].T * score_scale, cos, sin).astype(BF16)

    @pl.when(kind == QUERIES + 1)
    def _():
        out[...] = dv_sum[...].T.astype(BF16)


def attend_back_call(part, turn, marks, pieces, q_in, k_in, v_in, do_in, attn, lse, cosine, sine, before):
    group = KV // PARTS
    per = group // TURNS
    first = part * group + turn * per
    query = rows_at(lambda i, j: (first + i) * QUERIES + jnp.minimum(j, QUERIES - 1))
    key = rows_at(lambda i, j: first + i)

    def place(i, j):
        inner = turn * per + i
        tail = jnp.where(j == QUERIES, QUERIES * group + inner, (QUERIES + 1) * group + inner)
        return jnp.where(j < QUERIES, QUERIES * inner + j, tail)

    ins = [*marks, pieces, q_in, k_in, v_in, do_in, attn, lse, cosine, sine] + ([] if before is None else [before])
    return pl.pallas_call(
        attend_back_kernel,
        grid=(per, QUERIES + 2),
        in_specs=[ANY, ANY, SMEM, query, key, key, query, query, pl.BlockSpec((8, LEN), lambda i, j: (first + i, 0))]
        + [table_spec(), table_spec()]
        + ([] if before is None else [ANY]),
        out_specs=rows_at(place),
        out_shape=shaped(((QUERIES + 2) * group * HEAD, LEN), BF16),
        input_output_aliases={} if before is None else {len(ins) - 1: 0},
        scratch_shapes=[
            pltpu.VMEM((LEN // WIDE, 2 * WIDE, WIDE), F32),
            pltpu.VMEM((LEN, 2 * HEAD), BF16),
            pltpu.VMEM((LEN, 2 * HEAD), BF16),
            pltpu.VMEM((LEN, HEAD), F32),
            pltpu.VMEM((LEN, HEAD), F32),
        ],
        compiler_params=pltpu.CompilerParams(vmem_limit_bytes=48 << 20),
        cost_estimate=estimate(15),
        name="attend_back",
    )(*ins)


def halve_kernel(side, gate, up, down, mine, theirs):
    half = down.shape[0]

    def write(out):
        out[:half] = gate[...].T
        out[half : 2 * half] = up[...].T
        out[2 * half :] = down[...]

    pl.when(pl.program_id(0) == 0)(lambda: write(mine))
    pl.when(pl.program_id(0) == 1)(lambda: write(theirs))


def halve_call(side, gate, up, down):
    half = down.shape[0] // 2
    columns = pl.BlockSpec((D, half), lambda i, side: (0, lax.rem(side[0] + i, 2)))
    whole = pl.BlockSpec((3 * half, D), lambda i, side: (0, 0))
    return pl.pallas_call(
        halve_kernel,
        grid_spec=pltpu.PrefetchScalarGridSpec(
            num_scalar_prefetch=1,
            grid=(2,),
            in_specs=[columns, columns, pl.BlockSpec((half, D), lambda i, side: (lax.rem(side[0] + i, 2), 0))],
            out_specs=[whole, whole],
        ),
        out_shape=[shaped((3 * half, D), BF16)] * 2,
        compiler_params=pltpu.CompilerParams(vmem_limit_bytes=60 << 20),
        cost_estimate=estimate(5),
        name="halve",
    )(side, gate, up, down)


def finish_kernel(parts, tokens, residual, w_query, w_key, w_value, gain, *rest):
    grads, out = rest[:-1], rest[-1]
    total = 0.0
    for part, ref in enumerate(grads):
        columns = ref[...].T
        first = 0
        for weight in (w_query, w_key, w_value):
            wide = weight.shape[1] // parts
            total = total + dot(columns[:, first : first + wide], weight[:, part * wide : (part + 1) * wide], NT)
            first += wide
    values = tokens[...].astype(F32)
    scale = rms_scale(values)
    norm = values * scale
    scaled = total * gain[...]
    out[...] = residual[...] + scale * (scaled - norm * jnp.mean(scaled * norm, axis=1, keepdims=True))


def finish_call(tokens, residual, weights, gain, grads):
    rows = pl.BlockSpec((TILE, D), lambda i: (i, 0))
    whole = lambda array: pl.BlockSpec(array.shape, lambda i: (0, 0), pipeline_mode=pl.Buffered(1))
    return pl.pallas_call(
        functools.partial(finish_kernel, len(grads)),
        grid=(LEN // TILE,),
        in_specs=[rows, rows, *[whole(w) for w in weights], whole(gain)]
        + [pl.BlockSpec((g.shape[0], TILE), lambda i: (0, i)) for g in grads],
        out_specs=rows,
        out_shape=shaped((LEN, D), F32),
        compiler_params=pltpu.CompilerParams(vmem_limit_bytes=48 << 20),
        cost_estimate=estimate(5),
        name="finish",
    )(tokens, residual, *weights, gain, *grads)


def split_lanes(values, experts):
    lanes = lax.broadcasted_iota(jnp.int32, values.shape, 1)
    high = values.astype(BF16).astype(F32)
    return jnp.where(lanes < experts, high, jnp.where(lanes < 2 * experts, values - high, 0.0)).astype(BF16)


def join_lanes(parts, experts):
    return parts + pltpu.roll(parts, LANES - experts, 1)


def route_kernel(experts, tokens, attn, w_out, gain, w_router, routes, residual, rows, gate):
    values = tokens[...].astype(F32) + dot(attn[...], w_out[...], TN)
    residual[...] = values
    normed = (values * rms_scale(values) * gain[...]).astype(BF16)
    logits = dot(normed, w_router[...], NN)
    lanes = lax.broadcasted_iota(jnp.int32, logits.shape, 1)
    expert = lax.rem(lanes, experts)
    chosen = lanes < 0
    for k in range(routes.shape[1]):
        chosen = chosen | (routes[:, k : k + 1] == expert)
    chosen = chosen & (lanes < 2 * experts)
    logits = jnp.where(chosen, logits, masked_score)
    weights = jnp.exp(logits - jnp.max(logits, axis=1, keepdims=True))
    share = weights / (0.5 * jnp.sum(weights, axis=1, keepdims=True))
    gate[...] = share
    rows[:, :D] = normed
    rows[:, D:] = split_lanes(share, experts)


def route_call(experts, tokens, attn, w_out, gain, w_router, routes):
    rows = lambda cols: pl.BlockSpec((TILE, cols), lambda i: (i, 0))
    whole = lambda *shape: pl.BlockSpec(shape, lambda i: (0, 0), pipeline_mode=pl.Buffered(1))
    return pl.pallas_call(
        functools.partial(route_kernel, experts),
        grid=(LEN // TILE,),
        in_specs=[rows(D), pl.BlockSpec((D, TILE), lambda i: (0, i)), whole(D, D), whole(1, D), whole(D, LANES)]
        + [rows(routes.shape[1])],
        out_specs=[rows(D), rows(WIDTH), rows(LANES)],
        out_shape=[shaped((LEN, D), F32), shaped((LEN, WIDTH), BF16), shaped((LEN, LANES), F32)],
        compiler_params=pltpu.CompilerParams(vmem_limit_bytes=60 << 20),
        cost_estimate=estimate(5),
        name="route",
    )(tokens, attn, w_out, gain, w_router, routes)


def merge_kernel(experts, mark, kept, kept_share, landed, out):
    out[:, :D] = (kept[...].astype(F32) + landed[:, :D].astype(F32)).astype(BF16)
    if kept_share is not None:
        share = kept_share[...] + join_lanes(landed[:, D:].astype(F32), experts)
        share = jnp.where(lax.broadcasted_iota(jnp.int32, share.shape, 1) < experts, share, 0.0)
        out[:, D:] = split_lanes(share + pltpu.roll(share, experts, 1), experts)


def merge_call(experts, mark, kept, kept_share, landed):
    rows = lambda cols: pl.BlockSpec((TILE, cols), lambda i: (i, 0))
    width = landed.shape[1]
    kernel = functools.partial(merge_kernel, experts)
    if kept_share is None:
        kernel = lambda mark, kept, landed, out: merge_kernel(experts, mark, kept, None, landed, out)
    return pl.pallas_call(
        kernel,
        grid=(LEN // TILE,),
        in_specs=[ANY, rows(D)] + ([] if kept_share is None else [rows(LANES)]) + [rows(width)],
        out_specs=rows(width),
        out_shape=shaped((LEN, width), BF16),
        compiler_params=pltpu.CompilerParams(vmem_limit_bytes=32 << 20),
        cost_estimate=estimate(3),
        name="merge",
    )(*[ref for ref in (mark, kept, kept_share, landed) if ref is not None])


def back_kernel(
    experts, mark, kept, kept_share, core, chip, residual, cotangent, gate, gain, w_router, w_out, d_res, d_mix, d_attn, d_router
):
    @pl.when(pl.program_id(0) == 0)
    def _():
        d_router[...] = jnp.zeros_like(d_router)

    landed = core[:, D:].astype(F32) + chip[:, D:].astype(F32)
    share = kept_share[...] + join_lanes(landed, experts)
    first = lax.broadcasted_iota(jnp.int32, share.shape, 1) < experts
    gates = jnp.where(first, gate[...], 0.0)
    inner = jnp.sum(gates * share, axis=1, keepdims=True)
    d_logits = jnp.where(first, gates * (share - inner), 0.0).astype(BF16)
    d_normed = kept[...].astype(F32) + core[:, :D].astype(F32) + chip[:, :D].astype(F32) + dot(d_logits, w_router[...], NT)
    values, gains = residual[...], gain[...]
    scale = rms_scale(values)
    norm = values * scale
    d_gain = jnp.sum(d_normed * norm, axis=0, keepdims=True)
    scaled = d_normed * gains
    d_values = cotangent[...].astype(F32) + scale * (scaled - norm * jnp.mean(scaled * norm, axis=1, keepdims=True))
    d_res[...] = d_values
    mixed = d_values.astype(BF16)
    d_mix[...] = mixed
    d_attn[...] = dot(w_out[...], mixed, NT).astype(BF16)
    d_router[...] += dot(d_logits, (norm * gains).astype(BF16), TN)
    d_router[experts : experts + 1] += d_gain


def back_call(experts, mark, kept, kept_share, core, chip, residual, cotangent, gate, gain, w_router, w_out):
    rows = lambda cols: pl.BlockSpec((TILE, cols), lambda i: (i, 0))
    whole = lambda *shape: pl.BlockSpec(shape, lambda i: (0, 0), pipeline_mode=pl.Buffered(1))
    return pl.pallas_call(
        functools.partial(back_kernel, experts),
        grid=(LEN // TILE,),
        in_specs=[ANY, rows(D), rows(LANES), rows(WIDTH), rows(WIDTH), rows(D), rows(D), rows(LANES)]
        + [whole(1, D), whole(D, LANES), whole(D, D)],
        out_specs=[rows(D), rows(D), pl.BlockSpec((D, TILE), lambda i: (0, i)), whole(LANES, D)],
        out_shape=[
            shaped((LEN, D), F32),
            shaped((LEN, D), BF16),
            shaped((D, LEN), BF16),
            shaped((LANES, D), F32),
        ],
        compiler_params=pltpu.CompilerParams(vmem_limit_bytes=48 << 20),
        cost_estimate=estimate(8),
        name="back",
    )(mark, kept, kept_share, core, chip, residual, cotangent, gate, gain, w_router, w_out)


def out_kernel(mark, beat, attn, mixed, small, out):
    out[:, :D] = dot(attn[...], mixed[...], NN).astype(BF16)
    out[:, D:] = small[...].T.astype(BF16)


def out_call(marks, attn, mixed, small):
    return pl.pallas_call(
        out_kernel,
        grid=(D // TILE,),
        in_specs=[
            ANY,
            ANY,
            pl.BlockSpec((TILE, LEN), lambda i: (i, 0)),
            pl.BlockSpec((LEN, D), lambda i: (0, 0), pipeline_mode=pl.Buffered(1)),
            pl.BlockSpec((LANES, TILE), lambda i: (0, i)),
        ],
        out_specs=pl.BlockSpec((TILE, WIDTH), lambda i: (i, 0)),
        out_shape=shaped((D, WIDTH), BF16),
        compiler_params=pltpu.CompilerParams(vmem_limit_bytes=32 << 20),
        cost_estimate=estimate(5),
        name="out_grad",
    )(*marks, attn, mixed, small)


def pause_kernel(mark, beat, out):
    out[...] = mark[...] + beat[...]


def pause_call(mark, beat):
    return pl.pallas_call(
        pause_kernel, out_shape=shaped(mark.shape, mark.dtype), cost_estimate=estimate(10), name="pause"
    )(mark, beat)


def combine_kernel(residual, kept, core, chip, out):
    total = residual[...] + kept[...].astype(F32) + core[...].astype(F32) + chip[...].astype(F32)
    out[...] = total.astype(BF16)


def combine_call(residual, kept, core, chip):
    rows = pl.BlockSpec((TILE, D), lambda i: (i, 0))
    return pl.pallas_call(
        combine_kernel,
        grid=(LEN // TILE,),
        in_specs=[rows] * 4,
        out_specs=rows,
        out_shape=shaped((LEN, D), BF16),
        compiler_params=pltpu.CompilerParams(vmem_limit_bytes=48 << 20),
        cost_estimate=estimate(10),
        name="combine",
    )(residual, kept, core, chip)


def expert_kernel(count, experts, fresh, first, last_tokens, steps, ids, mark, beat, *rest):
    rest = list(rest)

    def take(number):
        taken = rest[:number]
        del rest[:number]
        return taken

    n2, up = take(2), take(2)
    w_in = [take(2) for _ in range(count)]
    sums_in = [[] if new else take(2) for new in fresh]
    carry_in = [] if first else take(3)
    outs = take(5) if last_tokens else take(3)
    sums_out = [take(2) for _ in range(count)]
    weights, sums = take(1)[0], take(1)[0]
    low, sem = rest
    half = weights.shape[1] // 6
    width = 2 * half
    step = pl.program_id(0)
    ahead = step < steps // 2

    def pieces_of(parts, whole):
        return [
            (ref.at[pl.ds(kind * half, half)], whole.at[pl.ds((2 * kind + part) * half, half)])
            for kind in range(3)
            for part, ref in enumerate(parts)
        ]

    def copies_of(pairs, lane):
        return [pltpu.make_async_copy(a, b, sem.at[lane, n]) for n, (a, b) in enumerate(pairs)]

    loads = [copies_of(pieces_of(w_in[e], weights.at[e]), e) for e in range(count)]
    prior = [[] if fresh[e] else copies_of(pieces_of(sums_in[e], low.at[e]), count + e) for e in range(count)]
    stores = [copies_of([(b, a) for a, b in pieces_of(sums_out[e], low.at[e])], e) for e in range(count)]

    @pl.when(step == 0)
    def _():
        for copy in sum(loads + prior, []):
            copy.start()
        sums[...] = jnp.zeros_like(sums)
        for copy in loads[0]:
            copy.wait()

    rows = jnp.where(ahead, n2[0][...], n2[1][...])
    grads = jnp.where(ahead, up[0][...], up[1][...])
    rows, gates = rows[:, :D], rows[:, D:].astype(F32)
    lanes = lax.broadcasted_iota(jnp.int32, gates.shape, 1)
    mixed = d_rows = d_shares = None
    add = lambda total, value: value if total is None else total + value
    for e in range(count):
        if e > 0:

            @pl.when(step == 0)
            def _(e=e):
                for copy in loads[e]:
                    copy.wait()

        w_both, w_down = weights.at[e, : 2 * width], weights.at[e, 2 * width :]
        hit = (lanes == ids[e]) | (lanes == ids[e] + experts)
        share = jnp.sum(jnp.where(hit, gates, 0.0), axis=1, keepdims=True)
        acts = dot(rows, w_both[...], NT)
        gate_act, up_act = acts[:, :width], acts[:, width:]
        d_plain = dot(grads, w_down[...], NT)
        sigmoid = 1.0 / (1.0 + jnp.exp(-gate_act))
        silu = gate_act * sigmoid
        hidden = silu * up_act
        shared = (share * hidden).astype(BF16)
        d_share = jnp.sum(hidden * d_plain, axis=1, keepdims=True)
        d_hidden = share * d_plain
        d_gate = (d_hidden * up_act * (sigmoid + silu * (1.0 - sigmoid))).astype(BF16)
        d_up = (d_hidden * silu).astype(BF16)
        d_both = jnp.concatenate([d_gate, d_up], axis=1)
        mixed = add(mixed, dot(shared, w_down[...], NN))
        d_rows = add(d_rows, dot(d_both, w_both[...], NN))
        d_shares = add(d_shares, jnp.where(hit, d_share, 0.0))
        sums[e, : 2 * width] += dot(d_both, rows, TN)
        sums[e, 2 * width :] += dot(shared, grads, TN)

        @pl.when(step == steps - 1)
        def _(e=e):
            for copy in prior[e]:
                copy.wait()
            low[e] = (sums[e] if fresh[e] else sums[e] + low[e].astype(F32)).astype(BF16)
            for copy in stores[e]:
                copy.start()

    results = [mixed, d_rows, d_shares]
    if not first:
        results = [result + ref[...].astype(F32) for result, ref in zip(results, carry_in)]
    if last_tokens:

        @pl.when(ahead)
        def _():
            for ref, result in zip(outs[:3], results):
                ref[...] = result.astype(ref.dtype)

        @pl.when(jnp.logical_not(ahead))
        def _():
            outs[3][...] = results[0].astype(BF16)
            outs[4][:, :D] = results[1].astype(BF16)
            outs[4][:, D:] = split_lanes(results[2], experts)
    else:
        for ref, result in zip(outs, results):
            ref[...] = result.astype(ref.dtype)

    @pl.when(step == steps - 1)
    def _():
        for copy in sum(stores, []):
            copy.wait()


def expert_call(ids, marks, experts, n2, up, weights, sums, carry, last_tokens):
    tokens, height, count = 2 * n2[0].shape[0], weights[0][0].shape[0], len(weights)
    steps = tokens // TILE
    rows = lambda cols: pl.BlockSpec((TILE, cols), lambda i: (i, 0))
    near = lambda cols: pl.BlockSpec((TILE, cols), lambda i: (jnp.minimum(i, steps // 2 - 1), 0))
    far = lambda cols: pl.BlockSpec((TILE, cols), lambda i: (jnp.maximum(i - steps // 2, 0), 0))
    ins = [ids, *marks, *n2, *up] + [w for pair in weights for w in pair]
    specs = [SMEM, ANY, ANY, near(WIDTH), far(WIDTH), near(D), far(D)] + [ANY] * (2 * count)
    fresh, first = [pair is None for pair in sums], carry is None
    columns = (D, D, LANES)
    if last_tokens:
        outs = [shaped((tokens // 2, c), t) for c, t in zip(columns, (BF16, BF16, F32))]
        outs += [shaped((tokens // 2, c), BF16) for c in (D, WIDTH)]
        out_specs = [near(c) for c in columns] + [far(D), far(WIDTH)]
    else:
        outs = [shaped((tokens, c), t) for c, t in zip(columns, (BF16, F32, F32))]
        out_specs = [rows(c) for c in columns]
    aliases = {}
    for pair in sums:
        if pair is not None:
            ins += pair
            specs += [ANY, ANY]
    if not first:
        if not last_tokens:
            aliases.update({len(ins) + k: k for k in range(3)})
        ins += carry
        specs += [rows(c) for c in columns]
    tokens_out = len(outs)
    for _ in range(count):
        outs += [shaped((height, D), BF16)] * 2
        out_specs += [ANY, ANY]
    scratch = [pltpu.VMEM((count, 2 * height, D), BF16), pltpu.VMEM((count, 2 * height, D), F32)]
    scratch.append(pltpu.VMEM((count, 2 * height, D), BF16))
    scratch.append(pltpu.SemaphoreType.DMA((2 * count, 6)))
    done = pl.pallas_call(
        functools.partial(expert_kernel, count, experts, fresh, first, last_tokens, steps),
        grid=(steps,),
        in_specs=specs,
        out_specs=out_specs,
        out_shape=outs,
        scratch_shapes=scratch,
        input_output_aliases=aliases,
        compiler_params=pltpu.CompilerParams(vmem_limit_bytes=63 << 20),
        cost_estimate=estimate(15 * count),
        name="expert",
    )(*ins)
    return list(done[:tokens_out]), [tuple(done[tokens_out + 2 * e : tokens_out + 2 * e + 2]) for e in range(count)]


def join_kernel(side, held, landed, gate, up, down):
    here = pl.program_id(0) == 0
    rows = jnp.where(here, held[...], landed[...]).astype(F32)
    half = down.shape[0]
    gate[...] = rows[:half].T
    up[...] = rows[half : 2 * half].T
    down[...] = rows[2 * half :]


def join_call(side, held, landed):
    half = held.shape[0] // 3
    whole = pl.BlockSpec(held.shape, lambda i, side: (0, 0))
    columns = pl.BlockSpec((D, half), lambda i, side: (0, lax.rem(side[0] + i, 2)))
    return pl.pallas_call(
        join_kernel,
        grid_spec=pltpu.PrefetchScalarGridSpec(
            num_scalar_prefetch=1,
            grid=(2,),
            in_specs=[whole, whole],
            out_specs=[columns, columns, pl.BlockSpec((half, D), lambda i, side: (lax.rem(side[0] + i, 2), 0))],
        ),
        out_shape=[shaped((D, 2 * half), F32), shaped((D, 2 * half), F32), shaped((2 * half, D), F32)],
        compiler_params=pltpu.CompilerParams(vmem_limit_bytes=48 << 20),
        cost_estimate=estimate(5),
        name="join",
    )(side, held, landed)


def after(values, *others):
    return lax.optimization_barrier((values, *others))[0]


class Task:
    def __init__(self, steps):
        self.steps, self.result, self.over = steps, None, False

    def step(self):
        if self.over:
            return []
        try:
            return [next(self.steps)]
        except StopIteration as stop:
            self.result, self.over = stop.value, True
            return [self.result]

    def finish(self):
        while not self.over:
            self.step()
        return self.result


def local(
    tokens,
    routes,
    pieces,
    attn_gain,
    w_query,
    w_key,
    w_value,
    w_out,
    ffn_gain,
    w_router,
    expert_gate,
    expert_up,
    expert_down,
    cotangent,
):
    shards, reps = lax.axis_size("ep"), lax.axis_size("rep")
    experts = w_router.shape[1]
    slots = shards // GROUP
    place = lax.axis_index("ep")
    side = lax.axis_index("rep") % 2

    def swap(values, bits):
        return lax.ppermute(values, "ep", [(i, i ^ bits) for i in range(shards)])

    def swap_rep(values, bits=1):
        return lax.ppermute(values, "rep", [(i, i ^ bits) for i in range(reps)])


    def reduce_reps(values, bits=1):
        while bits < reps:
            values = values.astype(BF16)
            landed = swap_rep(values, bits)
            yield values
            values = values.astype(F32) + hold(landed).astype(F32)
            bits *= 2
        return values

    def reduce_rows(values):
        values = values.reshape(shards, -1, values.shape[1])
        bits = 1
        while bits < shards:
            values = values.reshape(values.shape[0] // 2, 2, *values.shape[1:])
            bit = (place // bits) % 2
            kept, sent = [
                lax.dynamic_index_in_dim(values, index, axis=1, keepdims=False) for index in (bit, 1 - bit)
            ]
            landed = swap(sent, bits)
            yield sent
            values = (kept.astype(F32) + hold(landed).astype(F32)).astype(BF16)
            bits *= 2
        return (yield from reduce_reps(values[0]))

    def sum_steps(slot, own, other):
        other = hold(other)
        landed = swap_rep(other)
        yield other
        own = own.astype(F32) + hold(landed).astype(F32)
        if slot == 0:
            return own
        if slot == 2 and slots > 3:
            own = own + tasks[3].finish().astype(F32)
        own = own.astype(BF16)
        landed = swap(own, GROUP if slot == 3 else slot * GROUP)
        yield own
        return hold(landed)

    with jax.named_scope("weights_out"):
        turned = side.astype(jnp.int32).reshape(1)
        mine, theirs = halve_call(turned, expert_gate[0], expert_up[0], expert_down[0])
        tokens, mine, theirs = lax.optimization_barrier((tokens, mine, theirs))
        near = swap(mine, GROUP)

    with jax.named_scope("cotangent_out"):
        grads_next = swap(cotangent, 2)
        grads_in = [(cotangent, swap(cotangent, 1)), None]

    with jax.named_scope("attention"):
        inputs = tokens.astype(F32)
        scale_one = rms_scale(inputs)
        norm_one = inputs * scale_one
        normed_one = (norm_one * attn_gain).astype(BF16)
        w_dims = (((0,), (1,)), ((), ()))
        projections = (w_query, w_key, w_value)
        query, key, value = [dot(w, normed_one, w_dims) for w in projections]
        far = swap(after(mine, key, value, query), 2 * GROUP)
        cosine, sine = [jnp.asarray(table) for table in rotary_tables()]
        attn, query_rot, key_rot, value_low, lse = attend_call(pieces, query, key, value, cosine, sine)
        attn = after(attn, grads_next, grads_in[0][1])

    with jax.named_scope("cotangent_out"):
        grads_in[1] = (grads_next, swap(after(grads_next, attn), 1))

    with jax.named_scope("routing"):
        pad = jnp.zeros((D, LANES - 2 * experts), BF16)
        router_twice = jnp.concatenate([w_router, w_router, pad], axis=1)
        gain_two = ffn_gain.reshape(1, D)
        residual, rows, gate = route_call(experts, tokens, attn, w_out, gain_two, router_twice, routes)
        rows, _, near = lax.optimization_barrier((rows, grads_in[1][1], near))
        rows_next = swap(rows, 2)
        rows_in = [(rows, swap(rows, 1)), None]

    with jax.named_scope("weights_out"):
        weights = {0: (mine, theirs), 1: (near, swap_rep(near))}
        ids = [((place // GROUP) ^ slot) * GROUP + place % GROUP for slot in range(slots)]
        ids = [expert.astype(jnp.int32) for expert in ids]

    carry, sums, tasks = [None, None], [None] * slots, [None] * slots
    mark, point = after(jnp.zeros((8, LANES), F32), rows), rows
    beat = None

    def tick(*arrays):
        nonlocal mark
        mark = after(mark, *arrays)

    def hold(values):
        return after(values, point)

    def pause():
        nonlocal mark, beat
        mark, beat = pause_call(*marks()), None

    def marks():
        return [mark, mark if beat is None else beat]

    def passed(value, beats=False):
        nonlocal mark, point, beat
        beat = swap(mark, 1) if beats else None
        mark, point = after(mark, value), value

    def run(chip, group, last=False, beats=True):
        carry[chip], done = expert_call(
            jnp.stack([ids[slot] for slot in group]),
            marks(),
            experts,
            rows_in[chip],
            grads_in[chip],
            [weights[slot] for slot in group],
            [sums[slot] for slot in group],
            carry[chip],
            last,
        )
        passed(carry[chip][2], beats)
        for slot, pair in zip(group, done):
            if sums[slot] is not None:
                tasks[slot] = Task(sum_steps(slot, *pair))
            sums[slot] = pair

    with jax.named_scope("experts"):
        pause()
        run(0, [0], beats=False)
        tick(weights[1][1], far)
        far = hold(far)
        weights[2] = (far, swap_rep(far))
        landed = {slot: swap(far, GROUP) if slot == 3 else swap(hold(mine), slot * GROUP) for slot in range(3, slots)}
        run(0, [1])
        tick(rows_next, weights[2][1], *landed.values())
        for slot, held in landed.items():
            held = hold(held)
            weights[slot] = (held, swap_rep(held))
        rows_in[1] = (rows_next, swap(hold(rows_next), 1))
        pause()
        tick(rows_in[1][1])
        run(1, [0, 1])
        tick(*[weights[slot][1] for slot in landed])
        tasks[1].step()
        for slot in range(4, slots, 2):
            run(1, [slot, slot + 1])
            run(0, [slot])
            run(0, [slot + 1])
        run(1, [2, 3], True)
        there_landed = swap(hold(carry[1][4]), 1)
        pause()
        there = merge_call(experts, mark, carry[1][1], carry[1][2], there_landed)
        d_next = swap(there, 2)
        tick(there, *tasks[1].step())
        tasks[0].step()
        mix_landed = swap(hold(carry[1][3]), 1)
        run(0, [3])
        mix_there = merge_call(experts, mark, carry[1][0], None, mix_landed)
        tick(mix_there, *tasks[0].step(), *tasks[1].step())
        mix_home = swap(hold(mix_there), 2)
        tasks[3].step()
        run(0, [2], True)

    with jax.named_scope("routing_back"):
        d_core = swap(hold(carry[0][4]), 1)
        tasks[2].step()
        pause()
        tick(d_core, d_next, *[array for task in tasks[3:] for array in task.step()])
        point = mark
        d_residual, d_mixed, d_attn, d_small = back_call(
            experts, mark, carry[0][1], carry[0][2], d_core, d_next, residual, cotangent, gate, gain_two, router_twice, w_out
        )
        passed(d_small, True)
        mix_core = swap(hold(carry[0][3]), 1)
        d_out = out_call(marks(), attn, d_mixed, d_small)
        passed(d_out, True)
        tick(mix_core)

    with jax.named_scope("attention_back"):
        in_dims = (((0,), (1,)), ((), ()))
        out_task, w_tasks, d_packed = Task(reduce_rows(d_out)), [], []
        tick(*out_task.step())
        for part in range(PARTS):
            packed = None
            for turn in range(TURNS):
                packed = attend_back_call(
                    part, turn, marks(), pieces, query_rot, key_rot, value_low, d_attn, attn, lse, cosine, sine, packed
                )
                passed(packed, (part, turn) != (PARTS - 1, TURNS - 1))
                if (part, turn) == (0, 0):
                    tick(mix_home, *tasks[2].step())
                stepped = [array for task in w_tasks for array in task.step()]
                stepped += out_task.step() if (part, turn) != (1, 0) else []
                tick(*stepped)
            d_packed.append(packed)
            w_tasks.append(Task(reduce_rows(dot(normed_one, packed, in_dims).astype(BF16))))
            if part < PARTS - 1:
                tick(*w_tasks[-1].step())

    with jax.named_scope("tail"):
        last, other = w_tasks[1], w_tasks[0]
        mix_home = after(mix_home, packed, *stepped, *last.step())
        output = point = combine_call(residual, carry[0][0], mix_core, mix_home)
        point = last.step()[0]
        total = tasks[0].finish()
        for task in tasks[1:3] + tasks[4:]:
            total = total + task.finish().astype(F32)
        total = Task(reduce_reps(total, 2)).finish().astype(BF16)
        total_landed = swap_rep(total)
        gain_one = after(attn_gain.reshape(1, D), output, total, point)
        d_tokens = point = finish_call(tokens, d_residual, projections, gain_one, d_packed)
        point = d_tokens = after(d_tokens, *other.step(), *last.step())
        point = last.step()[0]
        for task in (other, out_task, last):
            point = task.step()[0]
        total, total_landed = lax.optimization_barrier((total, total_landed, point))[:2]
        s_gate, s_up, s_down = join_call(turned, total, total_landed)
        point = s_down
        s_mixed = out_task.finish()
        s_out, s_small = s_mixed[:, :D], s_mixed[:, D:]

    with jax.named_scope("sums_rest"):
        count = s_out.shape[0]
        first = place * count
        s_parts, s_attn, columns = [], 0.0, [[] for _ in projections]
        for task in w_tasks:
            part, cut = task.finish(), 0
            for group, w in zip(columns, projections):
                wide = w.shape[1] // PARTS
                own = lax.dynamic_slice(w, (first, len(group) * wide), (count, wide)).astype(F32)
                group.append(part[:, cut : cut + wide])
                s_attn += jnp.sum(group[-1] * own, axis=1)
                cut += wide
        s_query, s_key, s_value = [jnp.concatenate(group, axis=1) for group in columns]
        s_attn = s_attn / lax.dynamic_slice_in_dim(attn_gain, first, count)

    return (
        output,
        d_tokens,
        s_attn,
        s_query,
        s_key,
        s_value,
        s_out,
        s_small[:, experts],
        s_small[:, :experts],
        s_gate[None],
        s_up[None],
        s_down[None],
    )


def solution(mesh):
    rows, whole, slices = P(("rep", "ep"), None), P(), P("ep", None)
    expert = P("ep", None, None)
    return jax.shard_map(
        local,
        mesh=mesh,
        in_specs=(rows,) * 3 + (whole,) * 7 + (expert,) * 3 + (rows,),
        out_specs=(rows, rows, P("ep")) + (slices,) * 4 + (P("ep"), slices) + (expert,) * 3,
        check_vma=False,
    )
```

```python
import functools
import math

import jax
import jax.numpy as jnp
import numpy as np
from jax import lax
from jax.experimental import pallas as pl
from jax.experimental.pallas import tpu as pltpu
from jax.sharding import PartitionSpec as P

D = 1536
HEADS = 24
KV = 8
HEAD = 64
LEN = 1024
PIECE = 256
QUERIES = HEADS // KV
WIDE = 256
TILE = 256
GROUP = 4
PARTS = 2
TURNS = 2
LANES = 128
WIDTH = D + LANES

eps = 1e-06
theta_base = 10000.0
masked_score = -1e30
score_scale = HEAD ** (-0.5)
two_scale = score_scale * math.log2(math.e)

F32 = jnp.float32
BF16 = jnp.bfloat16
NN = (((1,), (0,)), ((), ()))
NT = (((1,), (1,)), ((), ()))
TN = (((0,), (0,)), ((), ()))
ANY = pl.BlockSpec(memory_space=pl.ANY)
SMEM = pl.BlockSpec(memory_space=pltpu.SMEM)


def dot(left, right, dims):
    return lax.dot_general(left, right, dims, preferred_element_type=F32)


def shaped(shape, dtype):
    return jax.ShapeDtypeStruct(shape, dtype)


def estimate(micros):
    return pl.CostEstimate(flops=int(micros * 1e10), bytes_accessed=int(micros * 1e6), transcendentals=0)


def rms_scale(values):
    return lax.rsqrt(jnp.mean(values * values, axis=-1, keepdims=True) + eps)


def rotary_tables():
    half_head = HEAD // 2
    frequency = theta_base ** (-(np.arange(half_head, dtype=np.float64) * 2.0) / HEAD)
    angles = frequency[:, None] * np.arange(LEN, dtype=np.float64)[None, :]
    return np.cos(angles).astype(np.float32), np.sin(angles).astype(np.float32)


def turn(values, cosine, sine):
    first, second = values[: HEAD // 2], values[HEAD // 2 :]
    return jnp.concatenate([first * cosine - second * sine, second * cosine + first * sine], axis=0)


def turn_back(grads, cosine, sine):
    first, second = grads[: HEAD // 2], grads[HEAD // 2 :]
    return jnp.concatenate([first * cosine + second * sine, second * cosine - first * sine], axis=0)


def fill_bias(pieces, bias):
    for block in range(LEN // WIDE):
        first = block * WIDE
        shape = bias.shape[1:]
        key = lax.broadcasted_iota(jnp.int32, shape, 0) + first
        query = lax.broadcasted_iota(jnp.int32, shape, 1) + first
        allowed = key <= query
        for piece in range(pieces.shape[1]):
            start = pieces[0, piece]
            low, high = jnp.minimum(key, query), jnp.maximum(key, query)
            allowed = allowed | ((low >= start) & (high < start + PIECE))
        bias[block] = jnp.where(allowed, 0.0, masked_score)


def key_span(block):
    return block * WIDE, min((block + 2) * WIDE, LEN)


def rows_at(place):
    return pl.BlockSpec((HEAD, LEN), lambda *grid: (place(*grid), 0))


def table_spec():
    return pl.BlockSpec((HEAD // 2, LEN), lambda *grid: (0, 0))


def attend_kernel(pieces, q0, q1, q2, k_in, v_in, cosine, sine, attn, q_out, k_out, v_out, lse, bias):
    @pl.when(pl.program_id(0) == 0)
    def _():
        fill_bias(pieces, bias)

    cos, sin = cosine[...], sine[...]
    k_rot = turn(k_in[...], cos, sin) * two_scale
    k_out[...] = k_rot.astype(BF16)
    keys = k_rot.T.astype(BF16)
    values = v_in[...].astype(BF16)
    v_out[...] = values
    for head, q_in in enumerate((q0, q1, q2)):
        rows = pl.ds(head * HEAD, HEAD)
        q_rot = turn(q_in[...], cos, sin).astype(BF16)
        q_out[rows, :] = q_rot
        for block in range(LEN // WIDE):
            columns = pl.ds(block * WIDE, WIDE)
            first, last = key_span(block)
            queries = q_rot[:, block * WIDE : (block + 1) * WIDE]
            spans = [(first, last)] + ([(0, first)] if first > 0 else [])
            scores = [dot(keys[a:b], queries, NN) for a, b in spans]
            scores[0] = scores[0] + bias[block, : last - first]
            highest = functools.reduce(jnp.maximum, [jnp.max(s, axis=0, keepdims=True) for s in scores])
            weights = [jnp.exp2(s - highest) for s in scores]
            total = sum(jnp.sum(w, axis=0, keepdims=True) for w in weights)
            mixed = sum(dot(values[:, a:b], w.astype(BF16), NN) for (a, b), w in zip(spans, weights)) / total
            attn[rows, columns] = mixed.astype(BF16)
            lse[head : head + 1, columns] = highest + jnp.log2(total)


def attend_call(pieces, query, key, value, cosine, sine):
    rows = lambda count: pl.BlockSpec((count, LEN), lambda i: (i, 0))
    width = QUERIES * HEAD
    return pl.pallas_call(
        attend_kernel,
        grid=(KV,),
        in_specs=[SMEM]
        + [rows_at(lambda i, head=head: QUERIES * i + head) for head in range(QUERIES)]
        + [rows_at(lambda i: i), rows_at(lambda i: i)]
        + [table_spec(), table_spec()],
        out_specs=[rows(width), rows(width), rows(HEAD), rows(HEAD), rows(8)],
        out_shape=[
            shaped((D, LEN), BF16),
            shaped((D, LEN), BF16),
            shaped((KV * HEAD, LEN), BF16),
            shaped((KV * HEAD, LEN), BF16),
            shaped((KV * 8, LEN), F32),
        ],
        scratch_shapes=[pltpu.VMEM((LEN // WIDE, 2 * WIDE, WIDE), F32)],
        compiler_params=pltpu.CompilerParams(vmem_limit_bytes=48 << 20),
        cost_estimate=estimate(25),
        name="attend",
    )(pieces, *[query] * QUERIES, key, value, cosine, sine)


def with_parts(columns, row):
    rank = lax.broadcasted_iota(jnp.int32, columns.shape, 0)
    high = row.astype(BF16).astype(F32)
    middle = (row - high).astype(BF16).astype(F32)
    parts = jnp.where(rank == 0, high, jnp.where(rank == 1, middle, jnp.where(rank == 2, row - high - middle, 0.0)))
    return jnp.concatenate([columns, parts.astype(BF16)], axis=0)


def attend_back_kernel(
    mark, beat, pieces, q_in, k_in, v_in, do_in, attn, lse, cosine, sine, *rest
):
    out, bias, keys_kept, values_kept, dk_sum, dv_sum = rest[-6:]
    kind = pl.program_id(1)

    @pl.when((pl.program_id(0) == 0) & (kind == 0))
    def _():
        fill_bias(pieces, bias)

    cos, sin = cosine[...], sine[...]

    @pl.when(kind == 0)
    def _():
        tail = jnp.where(lax.broadcasted_iota(jnp.int32, (LEN, HEAD), 1) < 3, -1.0, 0.0)
        for kept, ref in ((keys_kept, k_in), (values_kept, v_in)):
            kept[...] = jnp.concatenate([ref[...].astype(F32).T, tail], axis=1).astype(BF16)
        dk_sum[...] = jnp.zeros_like(dk_sum)
        dv_sum[...] = jnp.zeros_like(dv_sum)

    @pl.when(kind < QUERIES)
    def _():
        k_cols, keys, values = k_in[...], keys_kept[...], values_kept[...]
        q_cols, do_cols = q_in[...], do_in[...]
        q_rows = q_cols.astype(F32).T.astype(BF16)
        do_rows = do_cols.astype(F32).T.astype(BF16)
        delta = jnp.sum(do_cols.astype(F32) * attn[...].astype(F32), axis=0, keepdims=True)
        q_wide = with_parts(q_cols, lse[pl.ds(kind, 1), :])
        do_wide = with_parts(do_cols, delta)
        for block in range(LEN // WIDE):
            part = slice(block * WIDE, (block + 1) * WIDE)
            first, last = key_span(block)
            d_query = 0.0
            for a, b in [(first, last)] + ([(0, first)] if first > 0 else []):
                scores = dot(keys[a:b], q_wide[:, part], NN)
                if a == first:
                    scores = scores + bias[block, : b - a]
                probs = jnp.exp2(scores)
                d_scores = (probs * dot(values[a:b], do_wide[:, part], NN)).astype(BF16)
                dv_sum[a:b] += dot(probs.astype(BF16), do_rows[part], NN)
                dk_sum[a:b] += dot(d_scores, q_rows[part], NN)
                d_query = d_query + dot(k_cols[:, a:b], d_scores, NN)
            out[:, part] = turn_back(d_query * math.log(2.0), cos[:, part], sin[:, part]).astype(BF16)

    @pl.when(kind == QUERIES)
    def _():
        out[...] = turn_back(dk_sum[...].T * score_scale, cos, sin).astype(BF16)

    @pl.when(kind == QUERIES + 1)
    def _():
        out[...] = dv_sum[...].T.astype(BF16)


def attend_back_call(part, turn, marks, pieces, q_in, k_in, v_in, do_in, attn, lse, cosine, sine, before):
    group = KV // PARTS
    per = group // TURNS
    first = part * group + turn * per
    query = rows_at(lambda i, j: (first + i) * QUERIES + jnp.minimum(j, QUERIES - 1))
    key = rows_at(lambda i, j: first + i)

    def place(i, j):
        inner = turn * per + i
        tail = jnp.where(j == QUERIES, QUERIES * group + inner, (QUERIES + 1) * group + inner)
        return jnp.where(j < QUERIES, QUERIES * inner + j, tail)

    ins = [*marks, pieces, q_in, k_in, v_in, do_in, attn, lse, cosine, sine] + ([] if before is None else [before])
    return pl.pallas_call(
        attend_back_kernel,
        grid=(per, QUERIES + 2),
        in_specs=[ANY, ANY, SMEM, query, key, key, query, query, pl.BlockSpec((8, LEN), lambda i, j: (first + i, 0))]
        + [table_spec(), table_spec()]
        + ([] if before is None else [ANY]),
        out_specs=rows_at(place),
        out_shape=shaped(((QUERIES + 2) * group * HEAD, LEN), BF16),
        input_output_aliases={} if before is None else {len(ins) - 1: 0},
        scratch_shapes=[
            pltpu.VMEM((LEN // WIDE, 2 * WIDE, WIDE), F32),
            pltpu.VMEM((LEN, 2 * HEAD), BF16),
            pltpu.VMEM((LEN, 2 * HEAD), BF16),
            pltpu.VMEM((LEN, HEAD), F32),
            pltpu.VMEM((LEN, HEAD), F32),
        ],
        compiler_params=pltpu.CompilerParams(vmem_limit_bytes=48 << 20),
        cost_estimate=estimate(15),
        name="attend_back",
    )(*ins)


def halve_kernel(side, gate, up, down, mine, theirs):
    half = down.shape[0]

    def write(out):
        out[:half] = gate[...].T
        out[half : 2 * half] = up[...].T
        out[2 * half :] = down[...]

    pl.when(pl.program_id(0) == 0)(lambda: write(mine))
    pl.when(pl.program_id(0) == 1)(lambda: write(theirs))


def halve_call(side, gate, up, down):
    half = down.shape[0] // 2
    columns = pl.BlockSpec((D, half), lambda i, side: (0, lax.rem(side[0] + i, 2)))
    whole = pl.BlockSpec((3 * half, D), lambda i, side: (0, 0))
    return pl.pallas_call(
        halve_kernel,
        grid_spec=pltpu.PrefetchScalarGridSpec(
            num_scalar_prefetch=1,
            grid=(2,),
            in_specs=[columns, columns, pl.BlockSpec((half, D), lambda i, side: (lax.rem(side[0] + i, 2), 0))],
            out_specs=[whole, whole],
        ),
        out_shape=[shaped((3 * half, D), BF16)] * 2,
        compiler_params=pltpu.CompilerParams(vmem_limit_bytes=60 << 20),
        cost_estimate=estimate(5),
        name="halve",
    )(side, gate, up, down)


def finish_kernel(parts, tokens, residual, w_query, w_key, w_value, gain, *rest):
    grads, out = rest[:-1], rest[-1]
    total = 0.0
    for part, ref in enumerate(grads):
        columns = ref[...].T
        first = 0
        for weight in (w_query, w_key, w_value):
            wide = weight.shape[1] // parts
            total = total + dot(columns[:, first : first + wide], weight[:, part * wide : (part + 1) * wide], NT)
            first += wide
    values = tokens[...].astype(F32)
    scale = rms_scale(values)
    norm = values * scale
    scaled = total * gain[...]
    out[...] = residual[...] + scale * (scaled - norm * jnp.mean(scaled * norm, axis=1, keepdims=True))


def finish_call(tokens, residual, weights, gain, grads):
    rows = pl.BlockSpec((TILE, D), lambda i: (i, 0))
    whole = lambda array: pl.BlockSpec(array.shape, lambda i: (0, 0), pipeline_mode=pl.Buffered(1))
    return pl.pallas_call(
        functools.partial(finish_kernel, len(grads)),
        grid=(LEN // TILE,),
        in_specs=[rows, rows, *[whole(w) for w in weights], whole(gain)]
        + [pl.BlockSpec((g.shape[0], TILE), lambda i: (0, i)) for g in grads],
        out_specs=rows,
        out_shape=shaped((LEN, D), F32),
        compiler_params=pltpu.CompilerParams(vmem_limit_bytes=48 << 20),
        cost_estimate=estimate(5),
        name="finish",
    )(tokens, residual, *weights, gain, *grads)


def split_lanes(values, experts):
    lanes = lax.broadcasted_iota(jnp.int32, values.shape, 1)
    high = values.astype(BF16).astype(F32)
    return jnp.where(lanes < experts, high, jnp.where(lanes < 2 * experts, values - high, 0.0)).astype(BF16)


def join_lanes(parts, experts):
    return parts + pltpu.roll(parts, LANES - experts, 1)


def route_kernel(experts, tokens, attn, w_out, gain, w_router, routes, residual, rows, gate):
    values = tokens[...].astype(F32) + dot(attn[...], w_out[...], TN)
    residual[...] = values
    normed = (values * rms_scale(values) * gain[...]).astype(BF16)
    logits = dot(normed, w_router[...], NN)
    lanes = lax.broadcasted_iota(jnp.int32, logits.shape, 1)
    expert = lax.rem(lanes, experts)
    chosen = lanes < 0
    for k in range(routes.shape[1]):
        chosen = chosen | (routes[:, k : k + 1] == expert)
    chosen = chosen & (lanes < 2 * experts)
    logits = jnp.where(chosen, logits, masked_score)
    weights = jnp.exp(logits - jnp.max(logits, axis=1, keepdims=True))
    share = weights / (0.5 * jnp.sum(weights, axis=1, keepdims=True))
    gate[...] = share
    rows[:, :D] = normed
    rows[:, D:] = split_lanes(share, experts)


def route_call(experts, tokens, attn, w_out, gain, w_router, routes):
    rows = lambda cols: pl.BlockSpec((TILE, cols), lambda i: (i, 0))
    whole = lambda *shape: pl.BlockSpec(shape, lambda i: (0, 0), pipeline_mode=pl.Buffered(1))
    return pl.pallas_call(
        functools.partial(route_kernel, experts),
        grid=(LEN // TILE,),
        in_specs=[rows(D), pl.BlockSpec((D, TILE), lambda i: (0, i)), whole(D, D), whole(1, D), whole(D, LANES)]
        + [rows(routes.shape[1])],
        out_specs=[rows(D), rows(WIDTH), rows(LANES)],
        out_shape=[shaped((LEN, D), F32), shaped((LEN, WIDTH), BF16), shaped((LEN, LANES), F32)],
        compiler_params=pltpu.CompilerParams(vmem_limit_bytes=60 << 20),
        cost_estimate=estimate(5),
        name="route",
    )(tokens, attn, w_out, gain, w_router, routes)


def merge_kernel(experts, mark, kept, kept_share, landed, out):
    out[:, :D] = (kept[...].astype(F32) + landed[:, :D].astype(F32)).astype(BF16)
    if kept_share is not None:
        share = kept_share[...] + join_lanes(landed[:, D:].astype(F32), experts)
        share = jnp.where(lax.broadcasted_iota(jnp.int32, share.shape, 1) < experts, share, 0.0)
        out[:, D:] = split_lanes(share + pltpu.roll(share, experts, 1), experts)


def merge_call(experts, mark, kept, kept_share, landed):
    rows = lambda cols: pl.BlockSpec((TILE, cols), lambda i: (i, 0))
    width = landed.shape[1]
    kernel = functools.partial(merge_kernel, experts)
    if kept_share is None:
        kernel = lambda mark, kept, landed, out: merge_kernel(experts, mark, kept, None, landed, out)
    return pl.pallas_call(
        kernel,
        grid=(LEN // TILE,),
        in_specs=[ANY, rows(D)] + ([] if kept_share is None else [rows(LANES)]) + [rows(width)],
        out_specs=rows(width),
        out_shape=shaped((LEN, width), BF16),
        compiler_params=pltpu.CompilerParams(vmem_limit_bytes=32 << 20),
        cost_estimate=estimate(3),
        name="merge",
    )(*[ref for ref in (mark, kept, kept_share, landed) if ref is not None])


def back_kernel(
    experts, mark, kept, kept_share, core, chip, residual, cotangent, gate, gain, w_router, w_out, d_res, d_mix, d_attn, d_router
):
    @pl.when(pl.program_id(0) == 0)
    def _():
        d_router[...] = jnp.zeros_like(d_router)

    landed = core[:, D:].astype(F32) + chip[:, D:].astype(F32)
    share = kept_share[...] + join_lanes(landed, experts)
    first = lax.broadcasted_iota(jnp.int32, share.shape, 1) < experts
    gates = jnp.where(first, gate[...], 0.0)
    inner = jnp.sum(gates * share, axis=1, keepdims=True)
    d_logits = jnp.where(first, gates * (share - inner), 0.0).astype(BF16)
    d_normed = kept[...].astype(F32) + core[:, :D].astype(F32) + chip[:, :D].astype(F32) + dot(d_logits, w_router[...], NT)
    values, gains = residual[...], gain[...]
    scale = rms_scale(values)
    norm = values * scale
    d_gain = jnp.sum(d_normed * norm, axis=0, keepdims=True)
    scaled = d_normed * gains
    d_values = cotangent[...].astype(F32) + scale * (scaled - norm * jnp.mean(scaled * norm, axis=1, keepdims=True))
    d_res[...] = d_values
    mixed = d_values.astype(BF16)
    d_mix[...] = mixed
    d_attn[...] = dot(w_out[...], mixed, NT).astype(BF16)
    d_router[...] += dot(d_logits, (norm * gains).astype(BF16), TN)
    d_router[experts : experts + 1] += d_gain


def back_call(experts, mark, kept, kept_share, core, chip, residual, cotangent, gate, gain, w_router, w_out):
    rows = lambda cols: pl.BlockSpec((TILE, cols), lambda i: (i, 0))
    whole = lambda *shape: pl.BlockSpec(shape, lambda i: (0, 0), pipeline_mode=pl.Buffered(1))
    return pl.pallas_call(
        functools.partial(back_kernel, experts),
        grid=(LEN // TILE,),
        in_specs=[ANY, rows(D), rows(LANES), rows(WIDTH), rows(WIDTH), rows(D), rows(D), rows(LANES)]
        + [whole(1, D), whole(D, LANES), whole(D, D)],
        out_specs=[rows(D), rows(D), pl.BlockSpec((D, TILE), lambda i: (0, i)), whole(LANES, D)],
        out_shape=[
            shaped((LEN, D), F32),
            shaped((LEN, D), BF16),
            shaped((D, LEN), BF16),
            shaped((LANES, D), F32),
        ],
        compiler_params=pltpu.CompilerParams(vmem_limit_bytes=48 << 20),
        cost_estimate=estimate(8),
        name="back",
    )(mark, kept, kept_share, core, chip, residual, cotangent, gate, gain, w_router, w_out)


def out_kernel(mark, beat, attn, mixed, small, out):
    out[:, :D] = dot(attn[...], mixed[...], NN).astype(BF16)
    out[:, D:] = small[...].T.astype(BF16)


def out_call(marks, attn, mixed, small):
    return pl.pallas_call(
        out_kernel,
        grid=(D // TILE,),
        in_specs=[
            ANY,
            ANY,
            pl.BlockSpec((TILE, LEN), lambda i: (i, 0)),
            pl.BlockSpec((LEN, D), lambda i: (0, 0), pipeline_mode=pl.Buffered(1)),
            pl.BlockSpec((LANES, TILE), lambda i: (0, i)),
        ],
        out_specs=pl.BlockSpec((TILE, WIDTH), lambda i: (i, 0)),
        out_shape=shaped((D, WIDTH), BF16),
        compiler_params=pltpu.CompilerParams(vmem_limit_bytes=32 << 20),
        cost_estimate=estimate(5),
        name="out_grad",
    )(*marks, attn, mixed, small)


def pause_kernel(mark, beat, out):
    out[...] = mark[...] + beat[...]


def pause_call(mark, beat):
    return pl.pallas_call(
        pause_kernel, out_shape=shaped(mark.shape, mark.dtype), cost_estimate=estimate(10), name="pause"
    )(mark, beat)


def combine_kernel(residual, kept, core, chip, out):
    total = residual[...] + kept[...].astype(F32) + core[...].astype(F32) + chip[...].astype(F32)
    out[...] = total.astype(BF16)


def combine_call(residual, kept, core, chip):
    rows = pl.BlockSpec((TILE, D), lambda i: (i, 0))
    return pl.pallas_call(
        combine_kernel,
        grid=(LEN // TILE,),
        in_specs=[rows] * 4,
        out_specs=rows,
        out_shape=shaped((LEN, D), BF16),
        compiler_params=pltpu.CompilerParams(vmem_limit_bytes=48 << 20),
        cost_estimate=estimate(10),
        name="combine",
    )(residual, kept, core, chip)


def expert_kernel(count, experts, fresh, first, last_tokens, steps, ids, mark, beat, *rest):
    rest = list(rest)

    def take(number):
        taken = rest[:number]
        del rest[:number]
        return taken

    n2, up = take(2), take(2)
    w_in = [take(2) for _ in range(count)]
    sums_in = [[] if new else take(2) for new in fresh]
    carry_in = [] if first else take(3)
    outs = take(5) if last_tokens else take(3)
    sums_out = [take(2) for _ in range(count)]
    weights, sums = take(1)[0], take(1)[0]
    low, sem = rest
    half = weights.shape[1] // 6
    width = 2 * half
    step = pl.program_id(0)
    ahead = step < steps // 2

    def pieces_of(parts, whole):
        return [
            (ref.at[pl.ds(kind * half, half)], whole.at[pl.ds((2 * kind + part) * half, half)])
            for kind in range(3)
            for part, ref in enumerate(parts)
        ]

    def copies_of(pairs, lane):
        return [pltpu.make_async_copy(a, b, sem.at[lane, n]) for n, (a, b) in enumerate(pairs)]

    loads = [copies_of(pieces_of(w_in[e], weights.at[e]), e) for e in range(count)]
    prior = [[] if fresh[e] else copies_of(pieces_of(sums_in[e], low.at[e]), count + e) for e in range(count)]
    stores = [copies_of([(b, a) for a, b in pieces_of(sums_out[e], low.at[e])], e) for e in range(count)]

    @pl.when(step == 0)
    def _():
        for copy in sum(loads + prior, []):
            copy.start()
        sums[...] = jnp.zeros_like(sums)
        for copy in loads[0]:
            copy.wait()

    rows = jnp.where(ahead, n2[0][...], n2[1][...])
    grads = jnp.where(ahead, up[0][...], up[1][...])
    rows, gates = rows[:, :D], rows[:, D:].astype(F32)
    lanes = lax.broadcasted_iota(jnp.int32, gates.shape, 1)
    mixed = d_rows = d_shares = None
    add = lambda total, value: value if total is None else total + value
    for e in range(count):
        if e > 0:

            @pl.when(step == 0)
            def _(e=e):
                for copy in loads[e]:
                    copy.wait()

        w_both, w_down = weights.at[e, : 2 * width], weights.at[e, 2 * width :]
        hit = (lanes == ids[e]) | (lanes == ids[e] + experts)
        share = jnp.sum(jnp.where(hit, gates, 0.0), axis=1, keepdims=True)
        acts = dot(rows, w_both[...], NT)
        gate_act, up_act = acts[:, :width], acts[:, width:]
        d_plain = dot(grads, w_down[...], NT)
        sigmoid = 1.0 / (1.0 + jnp.exp(-gate_act))
        silu = gate_act * sigmoid
        hidden = silu * up_act
        shared = (share * hidden).astype(BF16)
        d_share = jnp.sum(hidden * d_plain, axis=1, keepdims=True)
        d_hidden = share * d_plain
        d_gate = (d_hidden * up_act * (sigmoid + silu * (1.0 - sigmoid))).astype(BF16)
        d_up = (d_hidden * silu).astype(BF16)
        d_both = jnp.concatenate([d_gate, d_up], axis=1)
        mixed = add(mixed, dot(shared, w_down[...], NN))
        d_rows = add(d_rows, dot(d_both, w_both[...], NN))
        d_shares = add(d_shares, jnp.where(hit, d_share, 0.0))
        sums[e, : 2 * width] += dot(d_both, rows, TN)
        sums[e, 2 * width :] += dot(shared, grads, TN)

        @pl.when(step == steps - 1)
        def _(e=e):
            for copy in prior[e]:
                copy.wait()
            low[e] = (sums[e] if fresh[e] else sums[e] + low[e].astype(F32)).astype(BF16)
            for copy in stores[e]:
                copy.start()

    results = [mixed, d_rows, d_shares]
    if not first:
        results = [result + ref[...].astype(F32) for result, ref in zip(results, carry_in)]
    if last_tokens:

        @pl.when(ahead)
        def _():
            for ref, result in zip(outs[:3], results):
                ref[...] = result.astype(ref.dtype)

        @pl.when(jnp.logical_not(ahead))
        def _():
            outs[3][...] = results[0].astype(BF16)
            outs[4][:, :D] = results[1].astype(BF16)
            outs[4][:, D:] = split_lanes(results[2], experts)
    else:
        for ref, result in zip(outs, results):
            ref[...] = result.astype(ref.dtype)

    @pl.when(step == steps - 1)
    def _():
        for copy in sum(stores, []):
            copy.wait()


def expert_call(ids, marks, experts, n2, up, weights, sums, carry, last_tokens):
    tokens, height, count = 2 * n2[0].shape[0], weights[0][0].shape[0], len(weights)
    steps = tokens // TILE
    rows = lambda cols: pl.BlockSpec((TILE, cols), lambda i: (i, 0))
    near = lambda cols: pl.BlockSpec((TILE, cols), lambda i: (jnp.minimum(i, steps // 2 - 1), 0))
    far = lambda cols: pl.BlockSpec((TILE, cols), lambda i: (jnp.maximum(i - steps // 2, 0), 0))
    ins = [ids, *marks, *n2, *up] + [w for pair in weights for w in pair]
    specs = [SMEM, ANY, ANY, near(WIDTH), far(WIDTH), near(D), far(D)] + [ANY] * (2 * count)
    fresh, first = [pair is None for pair in sums], carry is None
    columns = (D, D, LANES)
    if last_tokens:
        outs = [shaped((tokens // 2, c), t) for c, t in zip(columns, (BF16, BF16, F32))]
        outs += [shaped((tokens // 2, c), BF16) for c in (D, WIDTH)]
        out_specs = [near(c) for c in columns] + [far(D), far(WIDTH)]
    else:
        outs = [shaped((tokens, c), t) for c, t in zip(columns, (BF16, F32, F32))]
        out_specs = [rows(c) for c in columns]
    aliases = {}
    for pair in sums:
        if pair is not None:
            ins += pair
            specs += [ANY, ANY]
    if not first:
        if not last_tokens:
            aliases.update({len(ins) + k: k for k in range(3)})
        ins += carry
        specs += [rows(c) for c in columns]
    tokens_out = len(outs)
    for _ in range(count):
        outs += [shaped((height, D), BF16)] * 2
        out_specs += [ANY, ANY]
    scratch = [pltpu.VMEM((count, 2 * height, D), BF16), pltpu.VMEM((count, 2 * height, D), F32)]
    scratch.append(pltpu.VMEM((count, 2 * height, D), BF16))
    scratch.append(pltpu.SemaphoreType.DMA((2 * count, 6)))
    done = pl.pallas_call(
        functools.partial(expert_kernel, count, experts, fresh, first, last_tokens, steps),
        grid=(steps,),
        in_specs=specs,
        out_specs=out_specs,
        out_shape=outs,
        scratch_shapes=scratch,
        input_output_aliases=aliases,
        compiler_params=pltpu.CompilerParams(vmem_limit_bytes=63 << 20),
        cost_estimate=estimate(15 * count),
        name="expert",
    )(*ins)
    return list(done[:tokens_out]), [tuple(done[tokens_out + 2 * e : tokens_out + 2 * e + 2]) for e in range(count)]


def join_kernel(side, held, landed, gate, up, down):
    here = pl.program_id(0) == 0
    rows = jnp.where(here, held[...], landed[...]).astype(F32)
    half = down.shape[0]
    gate[...] = rows[:half].T
    up[...] = rows[half : 2 * half].T
    down[...] = rows[2 * half :]


def join_call(side, held, landed):
    half = held.shape[0] // 3
    whole = pl.BlockSpec(held.shape, lambda i, side: (0, 0))
    columns = pl.BlockSpec((D, half), lambda i, side: (0, lax.rem(side[0] + i, 2)))
    return pl.pallas_call(
        join_kernel,
        grid_spec=pltpu.PrefetchScalarGridSpec(
            num_scalar_prefetch=1,
            grid=(2,),
            in_specs=[whole, whole],
            out_specs=[columns, columns, pl.BlockSpec((half, D), lambda i, side: (lax.rem(side[0] + i, 2), 0))],
        ),
        out_shape=[shaped((D, 2 * half), F32), shaped((D, 2 * half), F32), shaped((2 * half, D), F32)],
        compiler_params=pltpu.CompilerParams(vmem_limit_bytes=48 << 20),
        cost_estimate=estimate(5),
        name="join",
    )(side, held, landed)


def after(values, *others):
    return lax.optimization_barrier((values, *others))[0]


class Task:
    def __init__(self, steps):
        self.steps, self.result, self.over = steps, None, False

    def step(self):
        if self.over:
            return []
        try:
            return [next(self.steps)]
        except StopIteration as stop:
            self.result, self.over = stop.value, True
            return [self.result]

    def finish(self):
        while not self.over:
            self.step()
        return self.result


def local(
    tokens,
    routes,
    pieces,
    attn_gain,
    w_query,
    w_key,
    w_value,
    w_out,
    ffn_gain,
    w_router,
    expert_gate,
    expert_up,
    expert_down,
    cotangent,
):
    shards, reps = lax.axis_size("ep"), lax.axis_size("rep")
    experts = w_router.shape[1]
    slots = shards // GROUP
    place = lax.axis_index("ep")
    side = lax.axis_index("rep") % 2

    def swap(values, bits):
        return lax.ppermute(values, "ep", [(i, i ^ bits) for i in range(shards)])

    def swap_rep(values, bits=1):
        return lax.ppermute(values, "rep", [(i, i ^ bits) for i in range(reps)])


    def reduce_reps(values, bits=1):
        while bits < reps:
            values = values.astype(BF16)
            landed = swap_rep(values, bits)
            yield values
            values = values.astype(F32) + hold(landed).astype(F32)
            bits *= 2
        return values

    def reduce_rows(values):
        values = values.reshape(shards, -1, values.shape[1])
        bits = 1
        while bits < shards:
            values = values.reshape(values.shape[0] // 2, 2, *values.shape[1:])
            bit = (place // bits) % 2
            kept, sent = [
                lax.dynamic_index_in_dim(values, index, axis=1, keepdims=False) for index in (bit, 1 - bit)
            ]
            landed = swap(sent, bits)
            yield sent
            values = (kept.astype(F32) + hold(landed).astype(F32)).astype(BF16)
            bits *= 2
        return (yield from reduce_reps(values[0]))

    def sum_steps(slot, own, other):
        other = hold(other)
        landed = swap_rep(other)
        yield other
        own = own.astype(F32) + hold(landed).astype(F32)
        if slot == 0:
            return own
        if slot == 2 and slots > 3:
            own = own + tasks[3].finish().astype(F32)
        own = own.astype(BF16)
        landed = swap(own, GROUP if slot == 3 else slot * GROUP)
        yield own
        return hold(landed)

    with jax.named_scope("weights_out"):
        turned = side.astype(jnp.int32).reshape(1)
        mine, theirs = halve_call(turned, expert_gate[0], expert_up[0], expert_down[0])
        tokens, mine, theirs = lax.optimization_barrier((tokens, mine, theirs))
        near = swap(mine, GROUP)

    with jax.named_scope("cotangent_out"):
        grads_next = swap(cotangent, 2)
        grads_in = [(cotangent, swap(cotangent, 1)), None]

    with jax.named_scope("attention"):
        inputs = tokens.astype(F32)
        scale_one = rms_scale(inputs)
        norm_one = inputs * scale_one
        normed_one = (norm_one * attn_gain).astype(BF16)
        w_dims = (((0,), (1,)), ((), ()))
        projections = (w_query, w_key, w_value)
        query, key, value = [dot(w, normed_one, w_dims) for w in projections]
        far = swap(after(mine, key, value, query), 2 * GROUP)
        cosine, sine = [jnp.asarray(table) for table in rotary_tables()]
        attn, query_rot, key_rot, value_low, lse = attend_call(pieces, query, key, value, cosine, sine)
        attn = after(attn, grads_next, grads_in[0][1])

    with jax.named_scope("cotangent_out"):
        grads_in[1] = (grads_next, swap(after(grads_next, attn), 1))

    with jax.named_scope("routing"):
        pad = jnp.zeros((D, LANES - 2 * experts), BF16)
        router_twice = jnp.concatenate([w_router, w_router, pad], axis=1)
        gain_two = ffn_gain.reshape(1, D)
        residual, rows, gate = route_call(experts, tokens, attn, w_out, gain_two, router_twice, routes)
        rows, _, near = lax.optimization_barrier((rows, grads_in[1][1], near))
        rows_next = swap(rows, 2)
        rows_in = [(rows, swap(rows, 1)), None]

    with jax.named_scope("weights_out"):
        weights = {0: (mine, theirs), 1: (near, swap_rep(near))}
        ids = [((place // GROUP) ^ slot) * GROUP + place % GROUP for slot in range(slots)]
        ids = [expert.astype(jnp.int32) for expert in ids]

    carry, sums, tasks = [None, None], [None] * slots, [None] * slots
    mark, point = after(jnp.zeros((8, LANES), F32), rows), rows
    beat = None

    def tick(*arrays):
        nonlocal mark
        mark = after(mark, *arrays)

    def hold(values):
        return after(values, point)

    def pause():
        nonlocal mark, beat
        mark, beat = pause_call(*marks()), None

    def marks():
        return [mark, mark if beat is None else beat]

    def passed(value, beats=False):
        nonlocal mark, point, beat
        beat = swap(mark, 1) if beats else None
        mark, point = after(mark, value), value

    def run(chip, group, last=False, beats=True):
        carry[chip], done = expert_call(
            jnp.stack([ids[slot] for slot in group]),
            marks(),
            experts,
            rows_in[chip],
            grads_in[chip],
            [weights[slot] for slot in group],
            [sums[slot] for slot in group],
            carry[chip],
            last,
        )
        passed(carry[chip][2], beats)
        for slot, pair in zip(group, done):
            if sums[slot] is not None:
                tasks[slot] = Task(sum_steps(slot, *pair))
            sums[slot] = pair

    with jax.named_scope("experts"):
        pause()
        run(0, [0], beats=False)
        tick(weights[1][1], far)
        far = hold(far)
        weights[2] = (far, swap_rep(far))
        landed = {slot: swap(far, GROUP) if slot == 3 else swap(hold(mine), slot * GROUP) for slot in range(3, slots)}
        run(0, [1])
        tick(rows_next, weights[2][1], *landed.values())
        for slot, held in landed.items():
            held = hold(held)
            weights[slot] = (held, swap_rep(held))
        rows_in[1] = (rows_next, swap(hold(rows_next), 1))
        pause()
        tick(rows_in[1][1])
        run(1, [0, 1])
        tick(*[weights[slot][1] for slot in landed])
        tasks[1].step()
        for slot in range(4, slots, 2):
            run(1, [slot, slot + 1])
            run(0, [slot])
            run(0, [slot + 1])
        run(1, [2, 3], True)
        there_landed = swap(hold(carry[1][4]), 1)
        pause()
        there = merge_call(experts, mark, carry[1][1], carry[1][2], there_landed)
        d_next = swap(there, 2)
        tick(there, *tasks[1].step())
        tasks[0].step()
        mix_landed = swap(hold(carry[1][3]), 1)
        run(0, [3])
        mix_there = merge_call(experts, mark, carry[1][0], None, mix_landed)
        tick(mix_there, *tasks[0].step(), *tasks[1].step())
        mix_home = swap(hold(mix_there), 2)
        tasks[3].step()
        run(0, [2], True)

    with jax.named_scope("routing_back"):
        d_core = swap(hold(carry[0][4]), 1)
        tasks[2].step()
        pause()
        tick(d_core, d_next, *[array for task in tasks[3:] for array in task.step()])
        point = mark
        d_residual, d_mixed, d_attn, d_small = back_call(
            experts, mark, carry[0][1], carry[0][2], d_core, d_next, residual, cotangent, gate, gain_two, router_twice, w_out
        )
        passed(d_small, True)
        mix_core = swap(hold(carry[0][3]), 1)
        d_out = out_call(marks(), attn, d_mixed, d_small)
        passed(d_out, True)
        tick(mix_core)

    with jax.named_scope("attention_back"):
        in_dims = (((0,), (1,)), ((), ()))
        out_task, w_tasks, d_packed = Task(reduce_rows(d_out)), [], []
        tick(*out_task.step())
        for part in range(PARTS):
            packed = None
            for turn in range(TURNS):
                packed = attend_back_call(
                    part, turn, marks(), pieces, query_rot, key_rot, value_low, d_attn, attn, lse, cosine, sine, packed
                )
                passed(packed, (part, turn) != (PARTS - 1, TURNS - 1))
                if (part, turn) == (0, 0):
                    tick(mix_home, *tasks[2].step())
                stepped = [array for task in w_tasks for array in task.step()]
                stepped += out_task.step() if part == turn else []
                tick(*stepped)
            d_packed.append(packed)
            w_tasks.append(Task(reduce_rows(dot(normed_one, packed, in_dims).astype(BF16))))
            if part < PARTS - 1:
                tick(*w_tasks[-1].step())

    with jax.named_scope("tail"):
        last, other = w_tasks[1], w_tasks[0]
        mix_home = after(mix_home, packed, *stepped, *last.step())
        output = point = combine_call(residual, carry[0][0], mix_core, mix_home)
        point = last.step()[0]
        total = tasks[0].finish()
        for task in tasks[1:3] + tasks[4:]:
            total = total + task.finish().astype(F32)
        total = Task(reduce_reps(total, 2)).finish().astype(BF16)
        total_landed = swap_rep(total)
        gain_one = after(attn_gain.reshape(1, D), output, total, point)
        d_tokens = point = finish_call(tokens, d_residual, projections, gain_one, d_packed)
        point = d_tokens = after(d_tokens, *other.step(), *out_task.step(), *last.step())
        point = last.step()[0]
        for task in (other, out_task, last):
            point = task.step()[0]
        total, total_landed = lax.optimization_barrier((total, total_landed, point))[:2]
        s_gate, s_up, s_down = join_call(turned, total, total_landed)
        point = s_down
        s_mixed = out_task.finish()
        s_out, s_small = s_mixed[:, :D], s_mixed[:, D:]

    with jax.named_scope("sums_rest"):
        count = s_out.shape[0]
        first = place * count
        s_parts, s_attn, columns = [], 0.0, [[] for _ in projections]
        for task in w_tasks:
            part, cut = task.finish(), 0
            for group, w in zip(columns, projections):
                wide = w.shape[1] // PARTS
                own = lax.dynamic_slice(w, (first, len(group) * wide), (count, wide)).astype(F32)
                group.append(part[:, cut : cut + wide])
                s_attn += jnp.sum(group[-1] * own, axis=1)
                cut += wide
        s_query, s_key, s_value = [jnp.concatenate(group, axis=1) for group in columns]
        s_attn = s_attn / lax.dynamic_slice_in_dim(attn_gain, first, count)

    return (
        output,
        d_tokens,
        s_attn,
        s_query,
        s_key,
        s_value,
        s_out,
        s_small[:, experts],
        s_small[:, :experts],
        s_gate[None],
        s_up[None],
        s_down[None],
    )


def solution(mesh):
    rows, whole, slices = P(("rep", "ep"), None), P(), P("ep", None)
    expert = P("ep", None, None)
    return jax.shard_map(
        local,
        mesh=mesh,
        in_specs=(rows,) * 3 + (whole,) * 7 + (expert,) * 3 + (rows,),
        out_specs=(rows, rows, P("ep")) + (slices,) * 4 + (P("ep"), slices) + (expert,) * 3,
        check_vma=False,
    )
```
